32 devices in a mesh: dp: 2 (over x), section: 16 (over z, y, core).
Axes of the slice: x: 2, y: 2, z: 4, core: 2. Of those that a mesh axis runs over, the one named last changes fastest.
Arguments:
- edge_rows: bfloat16 [16, 6144, 256], P('dp', 'section'), may hold values from -6 to 6
- lengths: int32 [16], P('dp'), may hold values from 512 to 3072, as said below
- norm_gain: float32 [2, 2, 256], replicated, may hold values from 0.5 to 1.5
- norm_bias: float32 [2, 2, 256], replicated, may hold values from -3 to 3
- w_qkv: bfloat16 [2, 256, 512], replicated, may hold values from -0.375 to 0.375
- w_out: bfloat16 [2, 256, 256], replicated, may hold values from -1 to 1
- w_up: bfloat16 [2, 256, 512], replicated, may hold values from -0.375 to 0.375
- w_down: bfloat16 [2, 512, 256], replicated, may hold values from -0.25 to 0.25
Outputs:
- forward_rows: float32 [16, 6144, 256], P('dp', 'section')
- backward_rows: float32 [16, 6144, 256], P('dp', 'section')
- rms_values: float32 [6, 16], P(None, 'dp')
- grad_gain: float32 [2, 2, 256], replicated
- grad_bias: float32 [2, 2, 256], replicated
- grad_qkv: float32 [2, 256, 512], replicated
- grad_out: float32 [2, 256, 256], replicated
- grad_up: float32 [2, 256, 512], replicated
- grad_down: float32 [2, 512, 256], replicated
The draws below stay inside these ranges and needn't reach their ends.
Inputs may be any that keep to these rules, and one draw needn't show every extreme that they name: `lengths`: in every group of 2 consecutive images one image has length 3072.
All inputs are finite; a program needn't handle non-finite values.
Results may differ from the reference program's by a relative error of at most 0.01.
Values may be sent and summed in bfloat16 or wider, within the bound.
No kernel may reach another device: no remote copies, remote signals or barrier semaphores. Data moves between devices by JAX's collectives and lax.ppermute only.
A program may use at most 384 MiB of HBM per device.

```python
import math
import jax
import jax.numpy as jnp
from jax import lax

D = 256
HEADS = 2
HD = 128
QKD = 64
FF = 512
WIN = 128
STRIDE = 128
SEQ = 3072
IMG_MB = 2
MIN_LEN = 512
IMAGES = 16
QK = 128


def draw_lengths(key, part):
    key = jax.random.fold_in(key, 11)
    first_key, second_key = jax.random.split(key)
    drawn = jax.random.randint(first_key, (IMAGES,), MIN_LEN, SEQ + 1, dtype=jnp.int32)
    chosen = jax.random.randint(second_key, (IMAGES // IMG_MB, 1), 0, IMG_MB, dtype=jnp.int32)
    slots = jnp.arange(IMG_MB, dtype=jnp.int32)[None, :]
    filled = jnp.where(slots == chosen, SEQ, drawn.reshape(IMAGES // IMG_MB, IMG_MB))
    return filled.reshape(IMAGES).astype(jnp.int32)


def block_scale(own_key, extent, shards, least, top_value):
    def one(axis_at, parts):
        heights = jax.random.uniform(jax.random.fold_in(jax.random.fold_in(own_key, 6), axis_at), (parts,), jnp.float32, least / len(shards), top_value / len(shards))
        return jnp.repeat(jnp.exp(heights), extent[axis_at] // parts).reshape((-1,) + (1,) * (len(extent) - axis_at - 1))

    gain = one(*shards[0])
    for cut in shards[1:]:
        gain = gain * one(*cut)
    return gain


def noise(rng, dims, scale, reach, cuts=(), kind=jnp.bfloat16):
    result = jax.random.normal(rng, dims, jnp.float32) * scale
    if len(cuts) > 0:
        result = block_scale(rng, dims, cuts, -0.22, 0.18) * result
    return jnp.clip(result, min=-reach, max=reach).astype(kind)


def setup_inputs(seed: int = 0) -> dict:
    key_list = jax.random.split(jax.random.key(seed), 9)
    return {
        "edge_rows": noise(key_list[0], (IMAGES, 2 * SEQ, D), 1.0, 6.0, ((0, 2), (1, 16))),
        "lengths": draw_lengths(jax.random.fold_in(key_list[8], 71), 0),
        "norm_gain": jnp.clip(1.0 + 0.1 * jax.random.normal(key_list[2], (2, 2, D), jnp.float32), 0.5, 1.5),
        "norm_bias": noise(key_list[3], (2, 2, D), 0.5, 3.0, (), jnp.float32),
        "w_qkv": noise(key_list[4], (2, D, 2 * QK + D), D ** -0.5, 0.375),
        "w_out": noise(key_list[5], (2, D, D), (D // 8) ** -0.5, 1.0),
        "w_up": noise(key_list[6], (2, D, FF), D ** -0.5, 0.375),
        "w_down": noise(key_list[7], (2, FF, D), FF ** -0.5, 0.25),
    }


@jax.custom_vjp
def low(v):
    return lax.optimization_barrier(v.astype(jnp.bfloat16)).astype(jnp.float32)

@jax.custom_vjp
def low_back(v):
    return v

def low_keep(v):
    return (low(v), None)

def low_pass(kept, grad):
    return (grad,)

def back_keep(v):
    return (v, None)

def back_low(kept, grad):
    return (low(grad),)
low.defvjp(low_keep, low_pass)
low_back.defvjp(back_keep, back_low)

def product(left, right):
    return jnp.dot(left, right, precision=lax.Precision.HIGHEST, preferred_element_type=jnp.float32)

def normalize(stream, gain_row, offset):
    centre = stream - lax.optimization_barrier(jnp.mean(stream, axis=-1, keepdims=True))
    spread = lax.optimization_barrier(jnp.mean(centre * centre, axis=-1, keepdims=True))
    return centre * lax.rsqrt(spread + 1e-05) * gain_row + offset

def masked_softmax(scores, allowed):
    masked = jnp.where(allowed, scores, -1e+30)
    largest = lax.optimization_barrier(jnp.max(masked, axis=-1, keepdims=True))
    powers = jnp.where(allowed, jnp.exp(masked - largest), 0.0)
    return powers / lax.optimization_barrier(jnp.sum(powers, axis=-1, keepdims=True))

def local_attention(queries, key_rows, values, length):
    block_rows = math.gcd(SEQ, 512)
    padded_keys = jnp.concatenate([jnp.zeros((WIN, HEADS, QKD), jnp.float32), key_rows], axis=0)
    padded_values = jnp.concatenate([jnp.zeros((WIN, HEADS, HD), jnp.float32), values], axis=0)

    def one_block(start):
        block_queries = lax.dynamic_slice_in_dim(queries, start, block_rows, 0)
        block_keys = lax.dynamic_slice_in_dim(padded_keys, start, block_rows + WIN, 0)
        block_values = lax.dynamic_slice_in_dim(padded_values, start, block_rows + WIN, 0)
        query_pos = (start + jnp.arange(block_rows, dtype=jnp.int32))[:, None]
        key_pos = (start - WIN + jnp.arange(block_rows + WIN, dtype=jnp.int32))[None, :]
        allowed = (key_pos <= query_pos) & (key_pos > query_pos - WIN) & (key_pos >= 0) & ((key_pos < length) | (key_pos == query_pos))
        scores = low_back(jnp.einsum('ihd,jhd->hij', block_queries, block_keys, precision=lax.Precision.HIGHEST))
        weights = low(masked_softmax(scores, allowed[None]))
        return jnp.einsum('hij,jhd->ihd', weights, block_values, precision=lax.Precision.HIGHEST)
    starts = jnp.arange(SEQ // block_rows, dtype=jnp.int32) * block_rows
    return lax.map(jax.checkpoint(one_block), starts).reshape(SEQ, HEADS, HD)

def strided_attention(queries, key_rows, values, length):
    block_rows = math.gcd(SEQ, 512)
    grid_count = SEQ // STRIDE
    padded_keys = jnp.concatenate([jnp.zeros((WIN, HEADS, QKD), jnp.float32), key_rows], axis=0)
    padded_values = jnp.concatenate([jnp.zeros((WIN, HEADS, HD), jnp.float32), values], axis=0)
    grid_keys = key_rows.reshape(grid_count, STRIDE, HEADS, QKD)
    grid_values = values.reshape(grid_count, STRIDE, HEADS, HD)

    def one_block(start):
        block_queries = lax.dynamic_slice_in_dim(queries, start, block_rows, 0)
        block_keys = lax.dynamic_slice_in_dim(padded_keys, start, block_rows + WIN, 0)
        block_values = lax.dynamic_slice_in_dim(padded_values, start, block_rows + WIN, 0)
        query_line = start + jnp.arange(block_rows, dtype=jnp.int32)
        query_pos = query_line[:, None]
        key_pos = (start - WIN + jnp.arange(block_rows + WIN, dtype=jnp.int32))[None, :]
        near_allowed = (key_pos <= query_pos) & (key_pos > query_pos - WIN) & (key_pos >= 0) & ((key_pos < length) | (key_pos == query_pos))
        residue = query_line % STRIDE
        far_keys = jnp.take(grid_keys, residue, axis=1)
        far_values = jnp.take(grid_values, residue, axis=1)
        far_pos = jnp.arange(grid_count, dtype=jnp.int32)[None, :] * STRIDE + residue[:, None]
        far_allowed = (far_pos < query_pos) & (far_pos < length)
        near_scores = jnp.einsum('ihd,jhd->hij', block_queries, block_keys, precision=lax.Precision.HIGHEST)
        far_scores = jnp.einsum('ihd,gihd->hig', block_queries, far_keys, precision=lax.Precision.HIGHEST)
        scores = low_back(jnp.concatenate([near_scores, far_scores], axis=-1))
        allowed = jnp.concatenate([near_allowed, far_allowed], axis=-1)
        weights = low(masked_softmax(scores, allowed[None]))
        near_weights = weights[..., :block_rows + WIN]
        far_weights = weights[..., block_rows + WIN:]
        near_out = jnp.einsum('hij,jhd->ihd', near_weights, block_values, precision=lax.Precision.HIGHEST)
        far_out = jnp.einsum('hig,gihd->ihd', far_weights, far_values, precision=lax.Precision.HIGHEST)
        return near_out + far_out
    starts = jnp.arange(SEQ // block_rows, dtype=jnp.int32) * block_rows
    return lax.map(jax.checkpoint(one_block), starts).reshape(SEQ, HEADS, HD)

def residual_layer(stream, weights, length, attend):
    gain_rows, offsets, w_mix, w_proj, w_in, w_back = weights
    score_scale = 1.0 / math.sqrt(QKD)
    normed = low(normalize(stream, gain_rows[0], offsets[0]))
    mixed_rows = low_back(product(normed, w_mix))
    queries = low(mixed_rows[:, :QK] * score_scale).reshape(SEQ, HEADS, QKD)
    key_rows = low(mixed_rows[:, QK:2 * QK]).reshape(SEQ, HEADS, QKD)
    values = low(mixed_rows[:, 2 * QK:]).reshape(SEQ, HEADS, HD)
    attended = low_back(low(attend(queries, key_rows, values, length).reshape(SEQ, D)))
    branch = low_back(product(attended, w_proj))
    middle = stream + branch
    normed_two = low(normalize(middle, gain_rows[1], offsets[1]))
    hidden = low_back(product(normed_two, w_in))
    active = low(jax.nn.gelu(hidden, approximate=True))
    feed_out = low_back(product(active, w_back))
    return (middle + feed_out, (branch, feed_out))

def reference(edge_rows, lengths, norm_gain, norm_bias, w_qkv, w_out, w_up, w_down):
    stacks = (norm_gain.astype(jnp.float32), norm_bias.astype(jnp.float32), w_qkv.astype(jnp.float32), w_out.astype(jnp.float32), w_up.astype(jnp.float32), w_down.astype(jnp.float32))
    first_weights = tuple((member[0] for member in stacks))
    second_weights = tuple((member[1] for member in stacks))
    row_index = jnp.arange(SEQ, dtype=jnp.int32)
    zeros = tuple((jnp.zeros(member.shape, jnp.float32) for member in stacks))

    def per_image(totals, entry):
        image_rows, length = entry
        stream = image_rows[:SEQ].astype(jnp.float32)
        cotangent = image_rows[SEQ:].astype(jnp.float32)
        in_length = (row_index < length).astype(jnp.float32)[:, None]
        first_out, first_back, first_aux = jax.vjp(lambda inputs, weights: residual_layer(inputs, weights, length, local_attention), stream, first_weights, has_aux=True)
        handed = low(first_out)
        second_out, second_back, second_aux = jax.vjp(lambda inputs, weights: residual_layer(inputs, weights, length, strided_attention), handed, second_weights, has_aux=True)
        handed_grad, second_grads = second_back(cotangent * in_length)
        stream_grad, first_grads = first_back(low(handed_grad))
        counted = length.astype(jnp.float32) * D
        measured = [stream, first_aux[0], first_aux[1], handed, second_aux[0], second_aux[1]]
        root_means = jnp.stack([jnp.sqrt(jnp.sum(in_length * measure * measure) / counted) for measure in measured])
        totals = tuple((running + jnp.stack([former, latter]) for running, former, latter in zip(totals, first_grads, second_grads)))
        return (totals, (first_out, second_out, stream_grad, handed_grad, root_means))
    totals, collected = lax.scan(per_image, zeros, (edge_rows, lengths))
    forward_rows = jnp.concatenate([collected[0], collected[1]], axis=1)
    backward_rows = jnp.concatenate([collected[2], collected[3]], axis=1)
    rms_values = jnp.transpose(collected[4])
    return (forward_rows, backward_rows, rms_values, totals[0], totals[1], totals[2], totals[3], totals[4], totals[5])
```

```python
import functools
import math

import jax
import jax.numpy as jnp
from jax import lax
from jax.experimental import pallas as pl
from jax.experimental.pallas import tpu as pltpu
from jax.sharding import PartitionSpec as P

HEADS = 2
WIN = 128
STRIDE = 128
NEG = -1e30
F32 = jnp.float32
BF16 = jnp.bfloat16
TB = 256
RES = 4
UNROLL = 2
VMEM_LIMIT = 56 * 1024 * 1024


def dot(left, right):
    return lax.dot_general(left, right, (((1,), (0,)), ((), ())), preferred_element_type=F32)


def dot_t(left, right):
    return lax.dot_general(left, right, (((1,), (1,)), ((), ())), preferred_element_type=F32)


def t_dot(left, right):
    return lax.dot_general(left, right, (((0,), (0,)), ((), ())), preferred_element_type=F32)


def score_scale(query_width):
    return 1.0 / math.sqrt(query_width // HEADS)


def norm_parts(rows):
    centre = rows - jnp.mean(rows, axis=-1, keepdims=True)
    scale = lax.rsqrt(jnp.mean(centre * centre, axis=-1, keepdims=True) + 1e-05)
    return centre * scale, scale


def norm_back(grad, unit, scale, gain):
    scaled = grad * gain
    first = jnp.mean(scaled, axis=-1, keepdims=True)
    second = jnp.mean(scaled * unit, axis=-1, keepdims=True)
    return scale * (scaled - first - unit * second)


def col_sum(rows):
    return jnp.sum(rows.reshape(rows.shape[0] // 8, 8, rows.shape[1]), axis=0)


def gelu_pair(hidden):
    c0 = math.sqrt(2.0 / math.pi)
    square = hidden * hidden
    share = 0.5 + 0.5 * jnp.tanh(hidden * (c0 + (c0 * 0.044715) * square))
    active = hidden * share
    slope = share + active * (1.0 - share) * (2.0 * c0 + (6.0 * c0 * 0.044715) * square)
    return active, slope


def head_split(rows):
    lane = lax.broadcasted_iota(jnp.int32, rows.shape, 1)
    zero = jnp.zeros_like(rows)
    low = lane < rows.shape[1] // HEADS
    return jnp.concatenate([jnp.where(low, rows, zero), jnp.where(low, zero, rows)], axis=0)


def head_join(stacked):
    half = stacked.shape[0] // 2
    lane = lax.broadcasted_iota(jnp.int32, (half, stacked.shape[1]), 1)
    return jnp.where(lane < stacked.shape[1] // HEADS, stacked[:half], stacked[half:])


def near_masks(base, limit):
    row = lax.broadcasted_iota(jnp.int32, (2 * WIN, WIN), 0)
    row = jnp.where(row >= WIN, row - WIN, row)
    col = lax.broadcasted_iota(jnp.int32, (2 * WIN, WIN), 1)
    own = col <= row
    key = base + col - jnp.where(own, 0, WIN)
    allowed = (key >= 0) & ((key < limit) | (col == row))
    return own, allowed


def near_scores(split_q, keys, own, allowed):
    scores = dot_t(split_q, keys)
    folded = jnp.where(own, scores[:, WIN:], scores[:, :WIN])
    return jnp.where(allowed, folded, NEG)


def unfold(folded, own):
    return jnp.concatenate([jnp.where(own, 0.0, folded), jnp.where(own, folded, 0.0)], axis=1).astype(BF16)


def near_forward(queries, keys, values, base, limit):
    own, allowed = near_masks(base, limit)
    scores = near_scores(head_split(queries), keys, own, allowed)
    largest = jnp.max(scores, axis=-1, keepdims=True)
    powers = jnp.exp(scores - largest)
    total = jnp.sum(powers, axis=-1, keepdims=True)
    weights = unfold(powers, own)
    hd = values.shape[1] // HEADS
    out = [dot(weights[h * WIN : (h + 1) * WIN], values[:, h * hd : (h + 1) * hd]) for h in range(HEADS)]
    return out, largest, total


def near_backward(queries, keys, values, grad_out, log_total, delta, base, limit):
    own, allowed = near_masks(base, limit)
    split_q = head_split(queries)
    weights = jnp.exp(near_scores(split_q, keys, own, allowed) - log_total)
    hd = values.shape[1] // HEADS
    pull = jnp.concatenate(
        [dot_t(grad_out[:, h * hd : (h + 1) * hd], values[:, h * hd : (h + 1) * hd]) for h in range(HEADS)], axis=0
    )
    pull = jnp.where(own, pull[:, WIN:], pull[:, :WIN])
    slope = unfold(weights * (pull - delta), own)
    weights = unfold(weights, own)
    grad_q = head_join(dot(slope, keys))
    grad_k = t_dot(slope, split_q)
    grad_v = jnp.concatenate(
        [t_dot(weights[h * WIN : (h + 1) * WIN], grad_out[:, h * hd : (h + 1) * hd]) for h in range(HEADS)], axis=1
    )
    return grad_q, grad_k, grad_v


def stack_stat(stat, width=128):
    return jnp.concatenate([stat[:, 0:1], stat[:, width // 2 : width // 2 + 1]], axis=0)


def spread_stat(stacked, width=128):
    half = stacked.shape[0] // 2
    lane = lax.broadcasted_iota(jnp.int32, (half, width), 1)
    return jnp.where(lane < width // 2, stacked[:half], stacked[half:])


def masked_squares(rows, base, limit):
    pos = base + lax.broadcasted_iota(jnp.int32, (rows.shape[0], 1), 0)
    return col_sum(jnp.where(pos < limit, rows * rows, 0.0))


def gather_pieces(info, pieces, target, sems, want_low):
    quarter = len(pieces) // 2
    rows = pieces[0].shape[0]

    def each(act):
        for t in range(quarter):
            place = target.at[pl.ds((t ^ info[2]) * rows, rows)]
            low, high = (t, t + quarter) if want_low else (t + quarter, t)

            @pl.when(info[3] == 0)
            def _():
                act(pltpu.make_async_copy(pieces[low], place, sems.at[t]))

            @pl.when(info[3] != 0)
            def _():
                act(pltpu.make_async_copy(pieces[high], place, sems.at[t]))

    each(lambda c: c.start())
    each(lambda c: c.wait())


def first_kernel(info, *refs):
    pieces = refs[:8]
    gain, bias, w_mix, x_out, q_out, kv_out, sems = refs[8:]
    gather_pieces(info, pieces, x_out, sems, True)
    qw = q_out.shape[1]

    def block(i, _):
        at = pl.ds(pl.multiple_of(i * TB, TB), TB)
        unit, _ = norm_parts(x_out[at].astype(F32))
        normed = (unit * gain[0:1] + bias[0:1]).astype(BF16)
        mixed = dot(normed, w_mix[...])
        q_out[at] = (mixed[:, :qw] * score_scale(qw)).astype(BF16)
        kv_out[at] = mixed[:, qw:].astype(BF16)
        return 0

    lax.fori_loop(0, x_out.shape[0] // TB, block, 0)


def load_extended(halo, kv, ext):
    ext[: halo.shape[0]] = halo[...]
    ext[halo.shape[0] :] = kv[...]


def second_kernel(
    info, x, q, kv, halo, gain, bias, w_proj, w_in, w_back, gain_next, bias_next, w_mix_next,
    z_out, q_next, kv_next, o_out, lse_out, active_out, slope_out, mid_out, squares, ext,
):
    step = pl.program_id(0)
    qw = q.shape[1]
    n = kv.shape[0]

    @pl.when(step == 0)
    def _():
        load_extended(halo, kv, ext)
        squares[...] = jnp.zeros_like(squares)

    limit = info[1]
    start = step * TB
    base = info[0] * n + start
    outs = []
    for sub in range(TB // WIN):
        near = pl.ds(pl.multiple_of(start + sub * WIN, WIN), 2 * WIN)
        keys = ext[near, :qw]
        values = ext[near, qw:]
        queries = q[sub * WIN : (sub + 1) * WIN]
        out, largest, total = near_forward(queries, keys, values, base + sub * WIN, limit)
        inverse = 1.0 / total
        lse_out[sub * WIN : (sub + 1) * WIN] = spread_stat(largest + jnp.log(total))
        outs.append(jnp.concatenate([out[0] * inverse[:WIN], out[1] * inverse[WIN:]], axis=1))
    attended = jnp.concatenate(outs, axis=0).astype(BF16)
    o_out[...] = attended
    stream = x[...].astype(F32)
    branch = dot(attended, w_proj[...])
    middle = stream + branch
    mid_out[...] = middle
    unit, _ = norm_parts(middle)
    normed = (unit * gain[1:2] + bias[1:2]).astype(BF16)
    active, slope = gelu_pair(dot(normed, w_in[...]))
    active = active.astype(BF16)
    active_out[...] = active
    slope_out[...] = slope.astype(BF16)
    feed = dot(active, w_back[...])
    z = (middle + feed).astype(BF16)
    z_out[...] = z
    squares[0] += masked_squares(stream, base, limit)
    squares[1] += masked_squares(branch, base, limit)
    squares[2] += masked_squares(feed, base, limit)
    unit, _ = norm_parts(z.astype(F32))
    normed = (unit * gain_next[0:1] + bias_next[0:1]).astype(BF16)
    mixed = dot(normed, w_mix_next[...])
    q_next[...] = (mixed[:, :qw] * score_scale(qw)).astype(BF16)
    kv_next[...] = mixed[:, qw:].astype(BF16)


def far_mask(grid_q, grid_k, part_grid):
    shape = (HEADS * RES * grid_q, RES * grid_k)
    row = lax.broadcasted_iota(jnp.int32, shape, 0)
    col = lax.broadcasted_iota(jnp.int32, shape, 1)
    row = jnp.where(row >= RES * grid_q, row - RES * grid_q, row)
    row_res = jnp.zeros(shape, jnp.int32)
    col_res = jnp.zeros(shape, jnp.int32)
    for r in range(1, RES):
        row_res += (row >= r * grid_q).astype(jnp.int32)
        col_res += (col >= r * grid_k).astype(jnp.int32)
    row_grid = row - row_res * grid_q + part_grid
    col_grid = col - col_res * grid_k
    allowed = (row_res == col_res) & (col_grid < row_grid)
    return allowed, col_grid * STRIDE + col_res


def far_forward_kernel(info, q, kv, other, qr, kr, vr, o_far, lse_far, q_s, k_s, v_s, o_s, lse_s):
    n, qw = q.shape
    grid_q = n // STRIDE
    grid_k = 2 * grid_q
    part = info[0]
    limit = info[1]

    def place(g, _):
        at = pl.ds(pl.multiple_of(g * STRIDE, STRIDE), STRIDE)
        own = kv[at].astype(F32)
        early = jnp.where(part == 0, own, other[at].astype(F32))
        q_s[pl.ds(g, STRIDE, stride=grid_q), :] = q[at].astype(F32)
        k_s[pl.ds(g, STRIDE, stride=grid_k), :] = early[:, :qw]
        k_s[pl.ds(g + grid_q, STRIDE, stride=grid_k), :] = own[:, :qw]
        hd = v_s.shape[1]
        for h in range(HEADS):
            v_s[h, pl.ds(g, STRIDE, stride=grid_k), :] = early[:, qw + h * 128 : qw + (h + 1) * 128]
            v_s[h, pl.ds(g + grid_q, STRIDE, stride=grid_k), :] = own[:, qw + h * 128 : qw + (h + 1) * 128]
        return 0

    lax.fori_loop(0, grid_q, place, 0)
    base_mask, key_pos = far_mask(grid_q, grid_k, part * grid_q)
    rows_q = RES * grid_q
    rows_k = RES * grid_k

    def one(i):
        at_q = pl.ds(pl.multiple_of(i * rows_q, rows_q), rows_q)
        at_k = pl.ds(pl.multiple_of(i * rows_k, rows_k), rows_k)
        queries = q_s[at_q].astype(BF16)
        keys = k_s[at_k].astype(BF16)
        values = [v_s[h, at_k].astype(BF16) for h in range(HEADS)]
        qr[at_q] = queries
        kr[at_k] = keys
        for h in range(HEADS):
            vr[at_k, h * 128 : (h + 1) * 128] = values[h]
        allowed = base_mask & (key_pos + i * RES < limit)
        scores = jnp.where(allowed, dot_t(head_split(queries), keys), NEG)
        largest = jnp.max(scores, axis=-1, keepdims=True)
        powers = jnp.where(allowed, jnp.exp(scores - largest), 0.0)
        total = jnp.sum(powers, axis=-1, keepdims=True)
        safe = jnp.maximum(total, 1e-30)
        weights = (powers * (1.0 / safe)).astype(BF16)
        lse = jnp.where(total > 0.0, largest + jnp.log(safe), NEG)
        lse_s[at_q] = spread_stat(lse)
        for h in range(HEADS):
            o_s[h, at_q] = dot(weights[h * rows_q : (h + 1) * rows_q], values[h])

    def group(i, _):
        for u in range(UNROLL):
            one(i * UNROLL + u)
        return 0

    lax.fori_loop(0, STRIDE // RES // UNROLL, group, 0)

    def back(g, _):
        at = pl.ds(pl.multiple_of(g * STRIDE, STRIDE), STRIDE)
        pick = pl.ds(g, STRIDE, stride=grid_q)
        lse_far[at] = lse_s[pick, :]
        for h in range(HEADS):
            o_far[at, h * 128 : (h + 1) * 128] = o_s[h, pick, :]
        return 0

    lax.fori_loop(0, grid_q, back, 0)


def third_kernel(
    info, *refs,
):
    pieces = refs[:8]
    (q, kv, halo, o_far, lse_far, z, gain, bias, w_proj, w_in, w_back,
     y_out, go_out, stat_out, gq_out, gk_out, gv_out, gmid_out, d_proj, d_in, d_back, d_gain, d_bias, squares,
     ext, cot, sems) = refs[8:]
    step = pl.program_id(0)
    qw = q.shape[1]
    n = kv.shape[0]

    @pl.when(step == 0)
    def _():
        gather_pieces(info, pieces, cot, sems, False)
        load_extended(halo, kv, ext)
        for ref in (squares, gk_out, gv_out, d_proj, d_in, d_back, d_gain, d_bias):
            ref[...] = jnp.zeros_like(ref)

    limit = info[1]
    start = pl.multiple_of(step * TB, TB)
    base = info[0] * n + start
    outs = []
    logs = []
    for sub in range(TB // WIN):
        rows = slice(sub * WIN, (sub + 1) * WIN)
        near = pl.ds(pl.multiple_of(start + sub * WIN, WIN), 2 * WIN)
        out, largest, total = near_forward(q[rows], ext[near, :qw], ext[near, qw:], base + sub * WIN, limit)
        far_log = stack_stat(lse_far[rows])
        top = jnp.maximum(largest, far_log)
        near_share = jnp.exp(largest - top)
        far_share = jnp.exp(far_log - top)
        whole = total * near_share + far_share
        inverse = 1.0 / whole
        near_share = near_share * inverse
        far_share = far_share * inverse
        logs.append(top + jnp.log(whole))
        far = o_far[rows]
        outs.append(
            jnp.concatenate(
                [
                    out[h] * near_share[h * WIN : (h + 1) * WIN]
                    + far[:, h * 128 : (h + 1) * 128] * far_share[h * WIN : (h + 1) * WIN]
                    for h in range(HEADS)
                ],
                axis=1,
            )
        )
    attended_wide = jnp.concatenate(outs, axis=0)
    attended = attended_wide.astype(BF16)
    stream = z[...].astype(F32)
    branch = dot(attended, w_proj[...])
    middle = stream + branch
    unit, scale = norm_parts(middle)
    normed = (unit * gain[1:2] + bias[1:2]).astype(BF16)
    active, slope = gelu_pair(dot(normed, w_in[...]))
    active = active.astype(BF16)
    feed = dot(active, w_back[...])
    y_out[...] = (middle + feed).astype(BF16)
    squares[0] += masked_squares(stream, base, limit)
    squares[1] += masked_squares(branch, base, limit)
    squares[2] += masked_squares(feed, base, limit)

    pos = base + lax.broadcasted_iota(jnp.int32, (TB, 1), 0)
    upstream = jnp.where(pos < limit, cot[pl.ds(start, TB)].astype(F32), 0.0)
    grad_out, grad_mid = feed_backward(
        upstream, active, slope, normed, unit, scale, attended, gain, w_proj, w_in, w_back,
        d_proj, d_in, d_back, d_gain, d_bias,
    )
    gmid_out[...] = grad_mid
    go_out[...] = grad_out
    weighted = grad_out.astype(F32) * attended_wide
    for sub in range(TB // WIN):
        rows = slice(sub * WIN, (sub + 1) * WIN)
        near = pl.ds(pl.multiple_of(start + sub * WIN, WIN), 2 * WIN)
        delta = jnp.concatenate(
            [jnp.sum(weighted[rows, h * 128 : (h + 1) * 128], axis=-1, keepdims=True) for h in range(HEADS)], axis=0
        )
        stat_out[rows] = pack_stats(logs[sub], delta)
        gq, gk, gv = near_backward(
            q[rows], ext[near, :qw], ext[near, qw:], grad_out[rows], logs[sub], delta, base + sub * WIN, limit
        )
        gq_out[rows] = gq
        gk_out[near] += gk
        gv_out[near] += gv


def pack_stats(lse, delta):
    half = lse.shape[0] // 2
    lane = lax.broadcasted_iota(jnp.int32, (half, 128), 1)
    low = jnp.where(lane < 32, lse[:half], lse[half:])
    high = jnp.where(lane < 96, delta[:half], delta[half:])
    return jnp.where(lane < 64, low, high)


def feed_backward(
    upstream, active, slope, normed, unit, scale, attended, gain, w_proj, w_in, w_back,
    d_proj, d_in, d_back, d_gain, d_bias,
):
    low = upstream.astype(BF16)
    d_back[...] += t_dot(active, low)
    grad_hidden = (dot_t(low, w_back[...]) * slope).astype(BF16)
    d_in[...] += t_dot(normed, grad_hidden)
    grad_normed = dot_t(grad_hidden, w_in[...])
    d_gain[...] += col_sum(grad_normed * unit)
    d_bias[...] += col_sum(grad_normed)
    grad_mid = upstream + norm_back(grad_normed, unit, scale, gain[1:2])
    branch_low = grad_mid.astype(BF16)
    d_proj[...] += t_dot(attended, branch_low)
    grad_out = dot_t(branch_low, w_proj[...]).astype(BF16)
    return grad_out, grad_mid


def far_backward_kernel(
    info, qr, kr, vr, go, stat, gq_near, gk_near, gv_near, gq_out, gkv_own, gkv_send,
    go_s, stat_s, gq_s, gk_s, gv_s,
):
    n, qw = gq_near.shape
    grid_q = n // STRIDE
    grid_k = 2 * grid_q
    part = info[0]
    limit = info[1]

    def place(g, _):
        at = pl.ds(pl.multiple_of(g * STRIDE, STRIDE), STRIDE)
        pick = pl.ds(g, STRIDE, stride=grid_q)
        rows = go[at].astype(F32)
        for h in range(HEADS):
            go_s[h, pick, :] = rows[:, h * 128 : (h + 1) * 128]
        stat_s[pick, :] = stat[at]
        return 0

    lax.fori_loop(0, grid_q, place, 0)
    base_mask, key_pos = far_mask(grid_q, grid_k, part * grid_q)
    rows_q = RES * grid_q
    rows_k = RES * grid_k

    def one(i):
        at_q = pl.ds(pl.multiple_of(i * rows_q, rows_q), rows_q)
        at_k = pl.ds(pl.multiple_of(i * rows_k, rows_k), rows_k)
        keys = kr[at_k]
        split_q = head_split(qr[at_q])
        grads = [go_s[h, at_q].astype(BF16) for h in range(HEADS)]
        stats = stat_s[at_q]
        lse = jnp.concatenate([stats[:, 0:1], stats[:, 32:33]], axis=0)
        delta = jnp.concatenate([stats[:, 64:65], stats[:, 96:97]], axis=0)
        allowed = base_mask & (key_pos + i * RES < limit)
        weights = jnp.exp(jnp.where(allowed, dot_t(split_q, keys), NEG) - lse)
        pull = jnp.concatenate([dot_t(grads[h], vr[at_k, h * 128 : (h + 1) * 128]) for h in range(HEADS)], axis=0)
        slope = (weights * (pull - delta)).astype(BF16)
        weights = weights.astype(BF16)
        gq_s[at_q] = head_join(dot(slope, keys))
        gk_s[at_k] = t_dot(slope, split_q)
        for h in range(HEADS):
            gv_s[h, at_k] = t_dot(weights[h * rows_q : (h + 1) * rows_q], grads[h])

    def group(i, _):
        for u in range(UNROLL):
            one(i * UNROLL + u)
        return 0

    lax.fori_loop(0, STRIDE // RES // UNROLL, group, 0)

    def back(g, _):
        at = pl.ds(pl.multiple_of(g * STRIDE, STRIDE), STRIDE)
        shifted = pl.ds(pl.multiple_of(g * STRIDE + WIN, STRIDE), STRIDE)
        gq_out[at] = gq_near[at] + gq_s[pl.ds(g, STRIDE, stride=grid_q), :]
        mine = pl.ds(g + part * grid_q, STRIDE, stride=grid_k)
        sent = pl.ds(g, STRIDE, stride=grid_k)
        last = jnp.where(g == grid_q - 1, 1.0, 0.0)
        gkv_own[at, :qw] = gk_near[shifted] + gk_s[mine, :]
        gkv_send[at, :qw] = (gk_s[sent, :] + last * gk_near[:WIN]).astype(BF16)
        for h in range(HEADS):
            cols = slice(h * 128, (h + 1) * 128)
            wide = slice(qw + h * 128, qw + (h + 1) * 128)
            gkv_own[at, wide] = gv_near[shifted, cols] + gv_s[h, mine, :]
            gkv_send[at, wide] = (gv_s[h, sent, :] + last * gv_near[:WIN, cols]).astype(BF16)
        return 0

    lax.fori_loop(0, grid_q, back, 0)


def mix_backward(grad_q, grad_kv, rows, gain, bias, w_mix, d_mix, d_gain, d_bias, carried):
    grad_mixed = jnp.concatenate([grad_q * score_scale(grad_q.shape[1]), grad_kv], axis=1).astype(BF16)
    unit, scale = norm_parts(rows)
    normed = (unit * gain[0:1] + bias[0:1]).astype(BF16)
    d_mix[...] += t_dot(normed, grad_mixed)
    grad_normed = dot_t(grad_mixed, w_mix[...])
    d_gain[...] += col_sum(grad_normed * unit)
    d_bias[...] += col_sum(grad_normed)
    return carried + norm_back(grad_normed, unit, scale, gain[0:1])


def fourth_kernel(
    info, gq, gkv, got, z, gmid, gain_next, bias_next, w_mix_next,
    q, kv, halo, o, lse, active, slope, mid, gain, bias, w_proj, w_in, w_back,
    gz_out, gq_out, gk_out, gv_out, gmid_out, d_mix, dn_gain, dn_bias, d_proj, d_in, d_back, d_gain, d_bias,
    ext,
):
    step = pl.program_id(0)
    qw = q.shape[1]
    n = kv.shape[0]

    @pl.when(step == 0)
    def _():
        load_extended(halo, kv, ext)
        for ref in (gk_out, gv_out, d_mix, dn_gain, dn_bias, d_proj, d_in, d_back, d_gain, d_bias):
            ref[...] = jnp.zeros_like(ref)

    limit = info[1]
    start = pl.multiple_of(step * TB, TB)
    base = info[0] * n + start
    grad_kv = gkv[...] + got[...].astype(F32)
    grad_z = mix_backward(
        gq[...], grad_kv, z[...].astype(F32), gain_next, bias_next, w_mix_next, d_mix, dn_gain, dn_bias, gmid[...]
    )
    grad_low = grad_z.astype(BF16)
    gz_out[...] = grad_low
    unit, scale = norm_parts(mid[...])
    normed = (unit * gain[1:2] + bias[1:2]).astype(BF16)
    attended = o[...]
    grad_out, grad_mid = feed_backward(
        grad_low.astype(F32), active[...], slope[...].astype(F32), normed, unit, scale, attended, gain,
        w_proj, w_in, w_back, d_proj, d_in, d_back, d_gain, d_bias,
    )
    gmid_out[...] = grad_mid
    weighted = grad_out.astype(F32) * attended.astype(F32)
    for sub in range(TB // WIN):
        rows = slice(sub * WIN, (sub + 1) * WIN)
        near = pl.ds(pl.multiple_of(start + sub * WIN, WIN), 2 * WIN)
        delta = jnp.concatenate(
            [jnp.sum(weighted[rows, h * 128 : (h + 1) * 128], axis=-1, keepdims=True) for h in range(HEADS)], axis=0
        )
        g_q, g_k, g_v = near_backward(
            q[rows], ext[near, :qw], ext[near, qw:], grad_out[rows], stack_stat(lse[rows]), delta,
            base + sub * WIN, limit,
        )
        gq_out[rows] = g_q
        gk_out[near] += g_k
        gv_out[near] += g_v


def fifth_kernel(info, gq, gk, gv, got, x, gmid, gain, bias, w_mix, gx_out, d_mix, d_gain, d_bias):
    step = pl.program_id(0)

    @pl.when(step == 0)
    def _():
        for ref in (d_mix, d_gain, d_bias):
            ref[...] = jnp.zeros_like(ref)

    at = pl.ds(pl.multiple_of(step * TB + WIN, WIN), TB)
    last = jnp.where(step == pl.num_programs(0) - 1, 1.0, 0.0)
    tail = got[...].astype(F32) * last
    extra = jnp.concatenate([jnp.zeros((TB - WIN, got.shape[1]), F32), tail], axis=0)
    grad_kv = jnp.concatenate([gk[at], gv[at]], axis=1) + extra
    grad_x = mix_backward(
        gq[...], grad_kv, x[...].astype(F32), gain, bias, w_mix, d_mix, d_gain, d_bias, gmid[...]
    )
    gx_out[...] = grad_x.astype(BF16)


def assemble_kernel(info, *refs):
    count = 8
    low, high, out, narrow, wide, sem_in, sem_out = refs[:count], refs[count : 2 * count], *refs[2 * count :]

    def each(t, act):
        @pl.when(info[5] == 0)
        def _():
            act(pltpu.make_async_copy(low[t], narrow.at[t], sem_in.at[t]))

        @pl.when(info[5] != 0)
        def _():
            act(pltpu.make_async_copy(high[t], narrow.at[t], sem_in.at[t]))

    def leave(t):
        return pltpu.make_async_copy(wide.at[t], out.at[t ^ info[4]], sem_out.at[t])

    for t in range(count):
        each(t, lambda c: c.start())
    for t in range(count):
        each(t, lambda c: c.wait())
        wide[t] = narrow[t].astype(F32)
        leave(t).start()
    for t in range(count):
        leave(t).wait()


def call(kernel, info, operands, specs, outs, out_specs, scratch=(), grid=()):
    return pl.pallas_call(
        kernel,
        grid_spec=pltpu.PrefetchScalarGridSpec(
            num_scalar_prefetch=1, grid=grid, in_specs=specs, out_specs=out_specs, scratch_shapes=list(scratch)
        ),
        out_shape=outs,
        compiler_params=pltpu.CompilerParams(vmem_limit_bytes=VMEM_LIMIT),
    )(info, *operands)


def whole(array):
    zeros = (0,) * len(array.shape)
    return pl.BlockSpec(array.shape, lambda *_: zeros)


def tiled(array):
    return pl.BlockSpec((TB, array.shape[1]), lambda i, *_: (i, 0))


ANY = pl.BlockSpec(memory_space=pl.ANY)


def shape(dims, kind):
    return jax.ShapeDtypeStruct(dims, kind)


def body(edge_rows, lengths, norm_gain, norm_bias, w_qkv, w_out, w_up, w_down):
    sections = lax.axis_size("section")
    index = lax.axis_index("section")
    images, rows_dev, width = edge_rows.shape
    seats = 2 * images
    rep = sections // seats
    seat = index // rep
    twin = index % rep
    rows_piece = rows_dev * rep
    qw = (w_qkv.shape[2] - width) // 2
    kvw = w_qkv.shape[2] - qw
    hidden = w_up.shape[2]
    n = rows_piece * images // 2
    quarter = images // 2
    steps = (n // TB,)

    def route(pairs):
        return [(s * rep + e, d * rep + e) for s, d in pairs for e in range(rep)]

    if rep > 1:
        groups = [[s * rep + e for e in range(rep)] for s in range(seats)]
        edge_rows = lax.all_gather(edge_rows, "section", axis_index_groups=groups, axis=1, tiled=True)

    def source_key(s):
        return (s // images) * quarter + s % quarter, (s % images) // quarter

    def source_seat(key, core):
        return (key // quarter) * images + core * quarter + key % quarter

    half = seat // images
    my_key = half * quarter + seat % quarter
    chip = seat // 2
    part = seat % 2
    limit = lengths[chip]
    info = jnp.stack([part, limit, chip % quarter, chip // quarter, my_key, half]).astype(jnp.int32)

    def scatter_route(t):
        return route([(s, 2 * (source_key(s)[0] ^ t) + source_key(s)[1]) for s in range(seats)])

    def return_route(t, to_half):
        pairs = []
        for s in range(seats):
            key = (s // 2) ^ t
            if key // quarter == to_half:
                pairs.append((s, source_seat(key, s % 2)))
        return route(pairs)

    received = [None] * images
    for t in list(range(quarter, images)) + list(range(quarter)):
        piece = lax.dynamic_index_in_dim(edge_rows, my_key ^ t, 0, keepdims=False)
        received[t] = lax.ppermute(piece, "section", scatter_route(t))

    def send_back(rows, to_half):
        blocks = rows.reshape(quarter, rows_piece, width)
        out = []
        for t in range(images):
            piece = lax.dynamic_index_in_dim(blocks, (chip ^ t) % quarter, 0, keepdims=False)
            out.append(lax.ppermute(piece, "section", return_route(t, to_half)))
        return out

    first_to_second = route([(2 * c, 2 * c + 1) for c in range(images)])
    second_to_first = route([(2 * c + 1, 2 * c) for c in range(images)])

    dma = pltpu.SemaphoreType.DMA
    rows_q = shape((n, qw), BF16)
    rows_kv = shape((n, kvw), BF16)
    rows_low = shape((n, width), BF16)
    rows_wide = shape((n, width), F32)
    rows_stat = shape((n, 128), F32)
    rows_hidden = shape((n, hidden), BF16)
    grad_k_shape = shape((n + WIN, qw), F32)
    grad_v_shape = shape((n + WIN, width), F32)
    d_mix_shape = shape(w_qkv.shape[1:], F32)
    d_proj_shape = shape(w_out.shape[1:], F32)
    d_in_shape = shape(w_up.shape[1:], F32)
    d_back_shape = shape(w_down.shape[1:], F32)
    vec_shape = shape((8, width), F32)
    squares_shape = shape((3, 8, width), F32)
    ext = pltpu.VMEM((n + WIN, kvw), BF16)

    g0, g1, b0, b1 = norm_gain[0], norm_gain[1], norm_bias[0], norm_bias[1]

    outs = [rows_low, rows_q, rows_kv]
    x, q0, kv0 = call(
        first_kernel, info, received + [g0, b0, w_qkv[0]],
        [ANY] * images + [whole(g0), whole(b0), whole(w_qkv[0])],
        outs, [whole(o) for o in outs], [dma((quarter,))],
    )
    halo0 = lax.ppermute(kv0[n - WIN :], "section", first_to_second)

    outs = [rows_low, rows_q, rows_kv, rows_low, rows_stat, rows_hidden, rows_hidden, rows_wide, squares_shape]
    z, q1, kv1, o0, lse0, active0, slope0, mid0, squares0 = call(
        second_kernel, info, [x, q0, kv0, halo0, g0, b0, w_out[0], w_up[0], w_down[0], g1, b1, w_qkv[1]],
        [tiled(x), tiled(q0)] + [whole(a) for a in (kv0, halo0, g0, b0, w_out[0], w_up[0], w_down[0], g1, b1, w_qkv[1])],
        outs, [tiled(o) for o in outs[:-1]] + [whole(outs[-1])], [ext], steps,
    )
    kv_other = lax.ppermute(kv1, "section", first_to_second)
    y0_back = send_back(z, 0)

    rows_k_all = shape((2 * n, qw), BF16)
    rows_v_all = shape((2 * n, width), BF16)
    outs = [rows_q, rows_k_all, rows_v_all, rows_wide, rows_stat]
    qr, kr, vr, o_far, lse_far = call(
        far_forward_kernel, info, [q1, kv1, kv_other], [whole(a) for a in (q1, kv1, kv_other)],
        outs, [whole(o) for o in outs],
        [pltpu.VMEM((n, qw), F32), pltpu.VMEM((2 * n, qw), F32), pltpu.VMEM((HEADS, 2 * n, 128), F32),
         pltpu.VMEM((HEADS, n, 128), F32), pltpu.VMEM((n, 128), F32)],
    )

    halo1 = kv_other[n - WIN :]
    outs = [rows_low, rows_low, rows_stat, shape((n, qw), F32), grad_k_shape, grad_v_shape, rows_wide,
            d_proj_shape, d_in_shape, d_back_shape, vec_shape, vec_shape, squares_shape]
    (y1, go1, stat1, gq_near, gk_near, gv_near, gmid1, d_proj1, d_in1, d_back1, d_gain11, d_bias11, squares1) = call(
        third_kernel, info,
        received + [q1, kv1, halo1, o_far, lse_far, z, g1, b1, w_out[1], w_up[1], w_down[1]],
        [ANY] * images + [tiled(q1), whole(kv1), whole(halo1), tiled(o_far), tiled(lse_far), tiled(z)]
        + [whole(a) for a in (g1, b1, w_out[1], w_up[1], w_down[1])],
        outs,
        [tiled(o) for o in outs[:4]] + [whole(outs[4]), whole(outs[5]), tiled(outs[6])] + [whole(o) for o in outs[7:]],
        [ext, pltpu.VMEM((n, width), BF16), dma((quarter,))], steps,
    )
    y1_back = send_back(y1, 1)

    outs = [shape((n, qw), F32), shape((n, kvw), F32), rows_kv]
    operands = [qr, kr, vr, go1, stat1, gq_near, gk_near, gv_near]
    gq1, gkv1, gkv_send = call(
        far_backward_kernel, info, operands, [whole(a) for a in operands], outs, [whole(o) for o in outs],
        [pltpu.VMEM((HEADS, n, 128), F32), pltpu.VMEM((n, 128), F32), pltpu.VMEM((n, qw), F32),
         pltpu.VMEM((2 * n, qw), F32), pltpu.VMEM((HEADS, 2 * n, 128), F32)],
    )
    gkv_got = lax.ppermute(gkv_send, "section", second_to_first)

    outs = [rows_low, shape((n, qw), F32), grad_k_shape, grad_v_shape, rows_wide,
            d_mix_shape, vec_shape, vec_shape, d_proj_shape, d_in_shape, d_back_shape, vec_shape, vec_shape]
    (gz, gq0, gk0, gv0, gmid0, d_mix1, d_gain10, d_bias10, d_proj0, d_in0, d_back0, d_gain01, d_bias01) = call(
        fourth_kernel, info,
        [gq1, gkv1, gkv_got, z, gmid1, g1, b1, w_qkv[1], q0, kv0, halo0, o0, lse0, active0, slope0, mid0, g0, b0,
         w_out[0], w_up[0], w_down[0]],
        [tiled(a) for a in (gq1, gkv1, gkv_got, z, gmid1)] + [whole(a) for a in (g1, b1, w_qkv[1])]
        + [tiled(q0), whole(kv0), whole(halo0)] + [tiled(a) for a in (o0, lse0, active0, slope0, mid0)]
        + [whole(a) for a in (g0, b0, w_out[0], w_up[0], w_down[0])],
        outs,
        [tiled(outs[0]), tiled(outs[1]), whole(outs[2]), whole(outs[3]), tiled(outs[4])] + [whole(o) for o in outs[5:]],
        [ext], steps,
    )
    halo_send = jnp.concatenate([gk0[:WIN], gv0[:WIN]], axis=1).astype(BF16)
    halo_got = lax.ppermute(halo_send, "section", second_to_first)
    gz_back = send_back(gz, 1)

    outs = [rows_low, d_mix_shape, vec_shape, vec_shape]
    gx, d_mix0, d_gain00, d_bias00 = call(
        fifth_kernel, info, [gq0, gk0, gv0, halo_got, x, gmid0, g0, b0, w_qkv[0]],
        [tiled(gq0), whole(gk0), whole(gv0), whole(halo_got), tiled(x), tiled(gmid0), whole(g0), whole(b0), whole(w_qkv[0])],
        outs, [tiled(outs[0])] + [whole(o) for o in outs[1:]], (), steps,
    )
    gx_back = send_back(gx, 0)

    def assemble(low, high):
        out = call(
            assemble_kernel, info, low + high, [ANY] * (2 * images),
            shape((images, rows_piece, width), F32), ANY,
            [pltpu.VMEM((images, rows_piece, width), BF16), pltpu.VMEM((images, rows_piece, width), F32),
             dma((images,)), dma((images,))],
        )
        if rep > 1:
            out = lax.dynamic_slice_in_dim(out, twin * rows_dev, rows_dev, 1)
        return out

    forward_rows = assemble(y0_back, y1_back)
    backward_rows = assemble(gx_back, gz_back)

    once = (twin == 0).astype(F32)
    squares = jnp.concatenate([squares0, squares1]).sum(axis=(1, 2))
    spread = squares[:, None] * (jnp.arange(images) == chip).astype(F32)[None, :] * once
    summed = lax.psum(spread, "section")
    rms_values = jnp.sqrt(summed / (lengths.astype(F32)[None, :] * width))

    d_gain = jnp.stack([jnp.stack([d_gain00, d_gain01]), jnp.stack([d_gain10, d_gain11])]).sum(axis=2)
    d_bias = jnp.stack([jnp.stack([d_bias00, d_bias01]), jnp.stack([d_bias10, d_bias11])]).sum(axis=2)
    grads = (
        d_gain, d_bias, jnp.stack([d_mix0, d_mix1]), jnp.stack([d_proj0, d_proj1]),
        jnp.stack([d_in0, d_in1]), jnp.stack([d_back0, d_back1]),
    )
    grads = lax.psum(tuple(g * once for g in grads), ("dp", "section"))
    return (forward_rows, backward_rows, rms_values) + tuple(grads)


def solution(mesh):
    placed = (P("dp", "section", None), P("dp"), P(), P(), P(), P(), P(), P())
    return jax.shard_map(
        body,
        mesh=mesh,
        in_specs=placed,
        out_specs=(P("dp", "section", None), P("dp", "section", None), P(None, "dp"), P(), P(), P(), P(), P(), P()),
        check_vma=False,
    )
```

```python
import functools
import math

import jax
import jax.numpy as jnp
from jax import lax
from jax.experimental import pallas as pl
from jax.experimental.pallas import tpu as pltpu
from jax.sharding import PartitionSpec as P

HEADS = 2
WIN = 128
STRIDE = 128
NEG = -1e30
F32 = jnp.float32
BF16 = jnp.bfloat16
TB = 512
RES = 8
UNROLL = 16
VMEM_LIMIT = 56 * 1024 * 1024


def dot(left, right):
    return lax.dot_general(left, right, (((1,), (0,)), ((), ())), preferred_element_type=F32)


def dot_t(left, right):
    return lax.dot_general(left, right, (((1,), (1,)), ((), ())), preferred_element_type=F32)


def t_dot(left, right):
    return lax.dot_general(left, right, (((0,), (0,)), ((), ())), preferred_element_type=F32)


def score_scale(query_width):
    return 1.0 / math.sqrt(query_width // HEADS)


def norm_parts(rows):
    centre = rows - jnp.mean(rows, axis=-1, keepdims=True)
    scale = lax.rsqrt(jnp.mean(centre * centre, axis=-1, keepdims=True) + 1e-05)
    return centre * scale, scale


def norm_back(grad, unit, scale, gain):
    scaled = grad * gain
    first = jnp.mean(scaled, axis=-1, keepdims=True)
    second = jnp.mean(scaled * unit, axis=-1, keepdims=True)
    return scale * (scaled - first - unit * second)


def col_sum(rows):
    return jnp.sum(rows.reshape(rows.shape[0] // 8, 8, rows.shape[1]), axis=0)


def gelu_pair(hidden):
    c0 = math.sqrt(2.0 / math.pi)
    square = hidden * hidden
    share = 0.5 + 0.5 * jnp.tanh(hidden * (c0 + (c0 * 0.044715) * square))
    active = hidden * share
    slope = share + active * (1.0 - share) * (2.0 * c0 + (6.0 * c0 * 0.044715) * square)
    return active, slope


def head_split(rows):
    lane = lax.broadcasted_iota(jnp.int32, rows.shape, 1)
    zero = jnp.zeros_like(rows)
    low = lane < rows.shape[1] // HEADS
    return jnp.concatenate([jnp.where(low, rows, zero), jnp.where(low, zero, rows)], axis=0)


def head_join(stacked):
    half = stacked.shape[0] // 2
    lane = lax.broadcasted_iota(jnp.int32, (half, stacked.shape[1]), 1)
    return jnp.where(lane < stacked.shape[1] // HEADS, stacked[:half], stacked[half:])


def near_masks(base, limit):
    row = lax.broadcasted_iota(jnp.int32, (2 * WIN, WIN), 0)
    row = jnp.where(row >= WIN, row - WIN, row)
    col = lax.broadcasted_iota(jnp.int32, (2 * WIN, WIN), 1)
    own = col <= row
    key = base + col - jnp.where(own, 0, WIN)
    allowed = (key >= 0) & ((key < limit) | (col == row))
    return own, allowed


def near_scores(split_q, keys, own, allowed):
    scores = dot_t(split_q, keys)
    folded = jnp.where(own, scores[:, WIN:], scores[:, :WIN])
    return jnp.where(allowed, folded, NEG)


def unfold(folded, own):
    return jnp.concatenate([jnp.where(own, 0.0, folded), jnp.where(own, folded, 0.0)], axis=1).astype(BF16)


def near_forward(queries, keys, values, base, limit):
    own, allowed = near_masks(base, limit)
    scores = near_scores(head_split(queries), keys, own, allowed)
    largest = jnp.max(scores, axis=-1, keepdims=True)
    powers = jnp.exp(scores - largest)
    total = jnp.sum(powers, axis=-1, keepdims=True)
    weights = unfold(powers, own)
    hd = values.shape[1] // HEADS
    out = [dot(weights[h * WIN : (h + 1) * WIN], values[:, h * hd : (h + 1) * hd]) for h in range(HEADS)]
    return out, largest, total


def near_backward(queries, keys, values, grad_out, log_total, delta, base, limit):
    own, allowed = near_masks(base, limit)
    split_q = head_split(queries)
    weights = jnp.exp(near_scores(split_q, keys, own, allowed) - log_total)
    hd = values.shape[1] // HEADS
    pull = jnp.concatenate(
        [dot_t(grad_out[:, h * hd : (h + 1) * hd], values[:, h * hd : (h + 1) * hd]) for h in range(HEADS)], axis=0
    )
    pull = jnp.where(own, pull[:, WIN:], pull[:, :WIN])
    slope = unfold(weights * (pull - delta), own)
    weights = unfold(weights, own)
    grad_q = head_join(dot(slope, keys))
    grad_k = t_dot(slope, split_q)
    grad_v = jnp.concatenate(
        [t_dot(weights[h * WIN : (h + 1) * WIN], grad_out[:, h * hd : (h + 1) * hd]) for h in range(HEADS)], axis=1
    )
    return grad_q, grad_k, grad_v


def stack_stat(stat, width=128):
    return jnp.concatenate([stat[:, 0:1], stat[:, width // 2 : width // 2 + 1]], axis=0)


def spread_stat(stacked, width=128):
    half = stacked.shape[0] // 2
    lane = lax.broadcasted_iota(jnp.int32, (half, width), 1)
    return jnp.where(lane < width // 2, stacked[:half], stacked[half:])


def masked_squares(rows, base, limit):
    pos = base + lax.broadcasted_iota(jnp.int32, (rows.shape[0], 1), 0)
    return col_sum(jnp.where(pos < limit, rows * rows, 0.0))


def gather_pieces(info, pieces, target, sems, want_low):
    quarter = len(pieces) // 2
    rows = pieces[0].shape[0]

    def each(act):
        for t in range(quarter):
            place = target.at[pl.ds((t ^ info[2]) * rows, rows)]
            low, high = (t, t + quarter) if want_low else (t + quarter, t)

            @pl.when(info[3] == 0)
            def _():
                act(pltpu.make_async_copy(pieces[low], place, sems.at[t]))

            @pl.when(info[3] != 0)
            def _():
                act(pltpu.make_async_copy(pieces[high], place, sems.at[t]))

    each(lambda c: c.start())
    each(lambda c: c.wait())


def first_kernel(info, *refs):
    pieces = refs[:8]
    gain, bias, w_mix, x_out, q_out, kv_out, sems = refs[8:]
    gather_pieces(info, pieces, x_out, sems, True)
    qw = q_out.shape[1]

    def block(i, _):
        at = pl.ds(pl.multiple_of(i * TB, TB), TB)
        unit, _ = norm_parts(x_out[at].astype(F32))
        normed = (unit * gain[0:1] + bias[0:1]).astype(BF16)
        mixed = dot(normed, w_mix[...])
        q_out[at] = (mixed[:, :qw] * score_scale(qw)).astype(BF16)
        kv_out[at] = mixed[:, qw:].astype(BF16)
        return 0

    lax.fori_loop(0, x_out.shape[0] // TB, block, 0)


def load_extended(halo, kv, ext):
    ext[: halo.shape[0]] = halo[...]
    ext[halo.shape[0] :] = kv[...]


def second_kernel(
    info, x, q, kv, halo, gain, bias, w_proj, w_in, w_back, gain_next, bias_next, w_mix_next,
    z_out, q_next, kv_next, o_out, lse_out, active_out, slope_out, mid_out, squares, ext,
):
    step = pl.program_id(0)
    qw = q.shape[1]
    n = kv.shape[0]

    @pl.when(step == 0)
    def _():
        load_extended(halo, kv, ext)
        squares[...] = jnp.zeros_like(squares)

    limit = info[1]
    start = step * TB
    base = info[0] * n + start
    outs = []
    for sub in range(TB // WIN):
        near = pl.ds(pl.multiple_of(start + sub * WIN, WIN), 2 * WIN)
        keys = ext[near, :qw]
        values = ext[near, qw:]
        queries = q[sub * WIN : (sub + 1) * WIN]
        out, largest, total = near_forward(queries, keys, values, base + sub * WIN, limit)
        inverse = 1.0 / total
        lse_out[sub * WIN : (sub + 1) * WIN] = spread_stat(largest + jnp.log(total))
        outs.append(jnp.concatenate([out[0] * inverse[:WIN], out[1] * inverse[WIN:]], axis=1))
    attended = jnp.concatenate(outs, axis=0).astype(BF16)
    o_out[...] = attended
    stream = x[...].astype(F32)
    branch = dot(attended, w_proj[...])
    middle = stream + branch
    mid_out[...] = middle
    unit, _ = norm_parts(middle)
    normed = (unit * gain[1:2] + bias[1:2]).astype(BF16)
    active, slope = gelu_pair(dot(normed, w_in[...]))
    active = active.astype(BF16)
    active_out[...] = active
    slope_out[...] = slope.astype(BF16)
    feed = dot(active, w_back[...])
    z = (middle + feed).astype(BF16)
    z_out[...] = z
    squares[0] += masked_squares(stream, base, limit)
    squares[1] += masked_squares(branch, base, limit)
    squares[2] += masked_squares(feed, base, limit)
    unit, _ = norm_parts(z.astype(F32))
    normed = (unit * gain_next[0:1] + bias_next[0:1]).astype(BF16)
    mixed = dot(normed, w_mix_next[...])
    q_next[...] = (mixed[:, :qw] * score_scale(qw)).astype(BF16)
    kv_next[...] = mixed[:, qw:].astype(BF16)


def far_mask(grid_q, grid_k, part_grid):
    shape = (HEADS * RES * grid_q, RES * grid_k)
    row = lax.broadcasted_iota(jnp.int32, shape, 0)
    col = lax.broadcasted_iota(jnp.int32, shape, 1)
    row = jnp.where(row >= RES * grid_q, row - RES * grid_q, row)
    row_res = jnp.zeros(shape, jnp.int32)
    col_res = jnp.zeros(shape, jnp.int32)
    for r in range(1, RES):
        row_res += (row >= r * grid_q).astype(jnp.int32)
        col_res += (col >= r * grid_k).astype(jnp.int32)
    row_grid = row - row_res * grid_q + part_grid
    col_grid = col - col_res * grid_k
    allowed = (row_res == col_res) & (col_grid < row_grid)
    return allowed, col_grid * STRIDE + col_res


def far_forward_kernel(info, q, kv, other, qr, kr, vr, o_far, lse_far, q_s, k_s, v_s, o_s, lse_s):
    n, qw = q.shape
    grid_q = n // STRIDE
    grid_k = 2 * grid_q
    part = info[0]
    limit = info[1]

    def place(g, _):
        at = pl.ds(pl.multiple_of(g * STRIDE, STRIDE), STRIDE)
        own = kv[at].astype(F32)
        early = jnp.where(part == 0, own, other[at].astype(F32))
        q_s[pl.ds(g, STRIDE, stride=grid_q), :] = q[at].astype(F32)
        k_s[pl.ds(g, STRIDE, stride=grid_k), :] = early[:, :qw]
        k_s[pl.ds(g + grid_q, STRIDE, stride=grid_k), :] = own[:, :qw]
        hd = v_s.shape[1]
        for h in range(HEADS):
            v_s[h, pl.ds(g, STRIDE, stride=grid_k), :] = early[:, qw + h * 128 : qw + (h + 1) * 128]
            v_s[h, pl.ds(g + grid_q, STRIDE, stride=grid_k), :] = own[:, qw + h * 128 : qw + (h + 1) * 128]
        return 0

    lax.fori_loop(0, grid_q, place, 0)
    base_mask, key_pos = far_mask(grid_q, grid_k, part * grid_q)
    rows_q = RES * grid_q
    rows_k = RES * grid_k

    def one(i):
        at_q = pl.ds(pl.multiple_of(i * rows_q, rows_q), rows_q)
        at_k = pl.ds(pl.multiple_of(i * rows_k, rows_k), rows_k)
        queries = q_s[at_q].astype(BF16)
        keys = k_s[at_k].astype(BF16)
        values = [v_s[h, at_k].astype(BF16) for h in range(HEADS)]
        qr[at_q] = queries
        kr[at_k] = keys
        for h in range(HEADS):
            vr[at_k, h * 128 : (h + 1) * 128] = values[h]
        allowed = base_mask & (key_pos + i * RES < limit)
        scores = jnp.where(allowed, dot_t(head_split(queries), keys), NEG)
        largest = jnp.max(scores, axis=-1, keepdims=True)
        powers = jnp.where(allowed, jnp.exp(scores - largest), 0.0)
        total = jnp.sum(powers, axis=-1, keepdims=True)
        safe = jnp.maximum(total, 1e-30)
        weights = (powers * (1.0 / safe)).astype(BF16)
        lse = jnp.where(total > 0.0, largest + jnp.log(safe), NEG)
        lse_s[at_q] = spread_stat(lse)
        for h in range(HEADS):
            o_s[h, at_q] = dot(weights[h * rows_q : (h + 1) * rows_q], values[h])

    def group(i, _):
        for u in range(UNROLL):
            one(i * UNROLL + u)
        return 0

    lax.fori_loop(0, STRIDE // RES // UNROLL, group, 0)

    def back(g, _):
        at = pl.ds(pl.multiple_of(g * STRIDE, STRIDE), STRIDE)
        pick = pl.ds(g, STRIDE, stride=grid_q)
        lse_far[at] = lse_s[pick, :]
        for h in range(HEADS):
            o_far[at, h * 128 : (h + 1) * 128] = o_s[h, pick, :]
        return 0

    lax.fori_loop(0, grid_q, back, 0)


def third_kernel(
    info, *refs,
):
    pieces = refs[:8]
    (q, kv, halo, o_far, lse_far, z, gain, bias, w_proj, w_in, w_back,
     y_out, go_out, stat_out, gq_out, gk_out, gv_out, gmid_out, slab, d_gain, d_bias, squares,
     ext, cot, sems) = refs[8:]
    step = pl.program_id(0)
    qw = q.shape[1]
    n = kv.shape[0]

    @pl.when(step == 0)
    def _():
        gather_pieces(info, pieces, cot, sems, False)
        load_extended(halo, kv, ext)
        for ref in (squares, gk_out, gv_out, slab, d_gain, d_bias):
            ref[...] = jnp.zeros_like(ref)

    limit = info[1]
    start = pl.multiple_of(step * TB, TB)
    base = info[0] * n + start
    outs = []
    logs = []
    for sub in range(TB // WIN):
        rows = slice(sub * WIN, (sub + 1) * WIN)
        near = pl.ds(pl.multiple_of(start + sub * WIN, WIN), 2 * WIN)
        out, largest, total = near_forward(q[rows], ext[near, :qw], ext[near, qw:], base + sub * WIN, limit)
        far_log = stack_stat(lse_far[rows])
        top = jnp.maximum(largest, far_log)
        near_share = jnp.exp(largest - top)
        far_share = jnp.exp(far_log - top)
        whole = total * near_share + far_share
        inverse = 1.0 / whole
        near_share = near_share * inverse
        far_share = far_share * inverse
        logs.append(top + jnp.log(whole))
        far = o_far[rows]
        outs.append(
            jnp.concatenate(
                [
                    out[h] * near_share[h * WIN : (h + 1) * WIN]
                    + far[:, h * 128 : (h + 1) * 128] * far_share[h * WIN : (h + 1) * WIN]
                    for h in range(HEADS)
                ],
                axis=1,
            )
        )
    attended_wide = jnp.concatenate(outs, axis=0)
    attended = attended_wide.astype(BF16)
    stream = z[...].astype(F32)
    branch = dot(attended, w_proj[...])
    middle = stream + branch
    unit, scale = norm_parts(middle)
    normed = (unit * gain[1:2] + bias[1:2]).astype(BF16)
    active, slope = gelu_pair(dot(normed, w_in[...]))
    active = active.astype(BF16)
    feed = dot(active, w_back[...])
    y_out[...] = (middle + feed).astype(BF16)
    squares[0] += masked_squares(stream, base, limit)
    squares[1] += masked_squares(branch, base, limit)
    squares[2] += masked_squares(feed, base, limit)

    pos = base + lax.broadcasted_iota(jnp.int32, (TB, 1), 0)
    upstream = jnp.where(pos < limit, cot[pl.ds(start, TB)].astype(F32), 0.0)
    grad_out, grad_mid = feed_backward(
        upstream, active, slope, normed, unit, scale, attended, gain, w_proj, w_in, w_back, slab, 0, d_gain, d_bias
    )
    gmid_out[...] = grad_mid
    go_out[...] = grad_out
    weighted = grad_out.astype(F32) * attended_wide
    for sub in range(TB // WIN):
        rows = slice(sub * WIN, (sub + 1) * WIN)
        near = pl.ds(pl.multiple_of(start + sub * WIN, WIN), 2 * WIN)
        delta = jnp.concatenate(
            [jnp.sum(weighted[rows, h * 128 : (h + 1) * 128], axis=-1, keepdims=True) for h in range(HEADS)], axis=0
        )
        stat_out[rows] = pack_stats(logs[sub], delta)
        gq, gk, gv = near_backward(
            q[rows], ext[near, :qw], ext[near, qw:], grad_out[rows], logs[sub], delta, base + sub * WIN, limit
        )
        gq_out[rows] = gq
        gk_out[near] += gk
        gv_out[near] += gv


def pack_stats(lse, delta):
    half = lse.shape[0] // 2
    lane = lax.broadcasted_iota(jnp.int32, (half, 128), 1)
    low = jnp.where(lane < 32, lse[:half], lse[half:])
    high = jnp.where(lane < 96, delta[:half], delta[half:])
    return jnp.where(lane < 64, low, high)


def add_columns(slab, at, grad):
    rows, cols = grad.shape
    width = slab.shape[1]
    for i in range(cols // width):
        slab[at + i * rows : at + (i + 1) * rows] += grad[:, i * width : (i + 1) * width]


def feed_backward(
    upstream, active, slope, normed, unit, scale, attended, gain, w_proj, w_in, w_back, slab, at, d_gain, d_bias,
):
    low = upstream.astype(BF16)
    width = low.shape[1]
    hidden = active.shape[1]
    slab[at + width + hidden : at + width + 2 * hidden] += t_dot(active, low)
    grad_hidden = (dot_t(low, w_back[...]) * slope).astype(BF16)
    add_columns(slab, at + width, t_dot(normed, grad_hidden))
    grad_normed = dot_t(grad_hidden, w_in[...])
    d_gain[...] += col_sum(grad_normed * unit)
    d_bias[...] += col_sum(grad_normed)
    grad_mid = upstream + norm_back(grad_normed, unit, scale, gain[1:2])
    branch_low = grad_mid.astype(BF16)
    slab[at : at + width] += t_dot(attended, branch_low)
    grad_out = dot_t(branch_low, w_proj[...]).astype(BF16)
    return grad_out, grad_mid


def far_backward_kernel(
    info, qr, kr, vr, go, stat, gq_near, gk_near, gv_near, gq_out, gkv_own, gkv_send,
    go_s, stat_s, gq_s, gk_s, gv_s,
):
    n, qw = gq_near.shape
    grid_q = n // STRIDE
    grid_k = 2 * grid_q
    part = info[0]
    limit = info[1]

    def place(g, _):
        at = pl.ds(pl.multiple_of(g * STRIDE, STRIDE), STRIDE)
        pick = pl.ds(g, STRIDE, stride=grid_q)
        rows = go[at].astype(F32)
        for h in range(HEADS):
            go_s[h, pick, :] = rows[:, h * 128 : (h + 1) * 128]
        stat_s[pick, :] = stat[at]
        return 0

    lax.fori_loop(0, grid_q, place, 0)
    base_mask, key_pos = far_mask(grid_q, grid_k, part * grid_q)
    rows_q = RES * grid_q
    rows_k = RES * grid_k

    def one(i):
        at_q = pl.ds(pl.multiple_of(i * rows_q, rows_q), rows_q)
        at_k = pl.ds(pl.multiple_of(i * rows_k, rows_k), rows_k)
        keys = kr[at_k]
        split_q = head_split(qr[at_q])
        grads = [go_s[h, at_q].astype(BF16) for h in range(HEADS)]
        stats = stat_s[at_q]
        lse = jnp.concatenate([stats[:, 0:1], stats[:, 32:33]], axis=0)
        delta = jnp.concatenate([stats[:, 64:65], stats[:, 96:97]], axis=0)
        allowed = base_mask & (key_pos + i * RES < limit)
        weights = jnp.exp(jnp.where(allowed, dot_t(split_q, keys), NEG) - lse)
        pull = jnp.concatenate([dot_t(grads[h], vr[at_k, h * 128 : (h + 1) * 128]) for h in range(HEADS)], axis=0)
        slope = (weights * (pull - delta)).astype(BF16)
        weights = weights.astype(BF16)
        gq_s[at_q] = head_join(dot(slope, keys))
        gk_s[at_k] = t_dot(slope, split_q)
        for h in range(HEADS):
            gv_s[h, at_k] = t_dot(weights[h * rows_q : (h + 1) * rows_q], grads[h])

    def group(i, _):
        for u in range(UNROLL):
            one(i * UNROLL + u)
        return 0

    lax.fori_loop(0, STRIDE // RES // UNROLL, group, 0)

    def back(g, _):
        at = pl.ds(pl.multiple_of(g * STRIDE, STRIDE), STRIDE)
        shifted = pl.ds(pl.multiple_of(g * STRIDE + WIN, STRIDE), STRIDE)
        gq_out[at] = gq_near[at] + gq_s[pl.ds(g, STRIDE, stride=grid_q), :]
        mine = pl.ds(g + part * grid_q, STRIDE, stride=grid_k)
        sent = pl.ds(g, STRIDE, stride=grid_k)
        last = jnp.where(g == grid_q - 1, 1.0, 0.0)
        gkv_own[at, :qw] = gk_near[shifted] + gk_s[mine, :]
        gkv_send[at, :qw] = (gk_s[sent, :] + last * gk_near[:WIN]).astype(BF16)
        for h in range(HEADS):
            cols = slice(h * 128, (h + 1) * 128)
            wide = slice(qw + h * 128, qw + (h + 1) * 128)
            gkv_own[at, wide] = gv_near[shifted, cols] + gv_s[h, mine, :]
            gkv_send[at, wide] = (gv_s[h, sent, :] + last * gv_near[:WIN, cols]).astype(BF16)
        return 0

    lax.fori_loop(0, grid_q, back, 0)


def mix_backward(grad_q, grad_kv, rows, gain, bias, w_mix, slab, d_gain, d_bias, carried):
    grad_mixed = jnp.concatenate([grad_q * score_scale(grad_q.shape[1]), grad_kv], axis=1).astype(BF16)
    unit, scale = norm_parts(rows)
    normed = (unit * gain[0:1] + bias[0:1]).astype(BF16)
    add_columns(slab, 0, t_dot(normed, grad_mixed))
    grad_normed = dot_t(grad_mixed, w_mix[...])
    d_gain[...] += col_sum(grad_normed * unit)
    d_bias[...] += col_sum(grad_normed)
    return carried + norm_back(grad_normed, unit, scale, gain[0:1])


def fourth_kernel(
    info, gq, gkv, got, z, gmid, gain_next, bias_next, w_mix_next,
    q, kv, halo, o, lse, active, slope, mid, gain, bias, w_proj, w_in, w_back,
    gz_out, gq_out, gk_out, gv_out, gmid_out, slab, dn_gain, dn_bias, d_gain, d_bias,
    ext,
):
    step = pl.program_id(0)
    qw = q.shape[1]
    n = kv.shape[0]

    @pl.when(step == 0)
    def _():
        load_extended(halo, kv, ext)
        for ref in (gk_out, gv_out, slab, dn_gain, dn_bias, d_gain, d_bias):
            ref[...] = jnp.zeros_like(ref)

    limit = info[1]
    start = pl.multiple_of(step * TB, TB)
    base = info[0] * n + start
    grad_kv = gkv[...] + got[...].astype(F32)
    grad_z = mix_backward(
        gq[...], grad_kv, z[...].astype(F32), gain_next, bias_next, w_mix_next, slab, dn_gain, dn_bias, gmid[...]
    )
    grad_low = grad_z.astype(BF16)
    gz_out[...] = grad_low
    unit, scale = norm_parts(mid[...])
    normed = (unit * gain[1:2] + bias[1:2]).astype(BF16)
    attended = o[...]
    grad_out, grad_mid = feed_backward(
        grad_low.astype(F32), active[...], slope[...].astype(F32), normed, unit, scale, attended, gain,
        w_proj, w_in, w_back, slab, w_mix_next.size // w_proj.shape[1], d_gain, d_bias,
    )
    gmid_out[...] = grad_mid
    weighted = grad_out.astype(F32) * attended.astype(F32)
    for sub in range(TB // WIN):
        rows = slice(sub * WIN, (sub + 1) * WIN)
        near = pl.ds(pl.multiple_of(start + sub * WIN, WIN), 2 * WIN)
        delta = jnp.concatenate(
            [jnp.sum(weighted[rows, h * 128 : (h + 1) * 128], axis=-1, keepdims=True) for h in range(HEADS)], axis=0
        )
        g_q, g_k, g_v = near_backward(
            q[rows], ext[near, :qw], ext[near, qw:], grad_out[rows], stack_stat(lse[rows]), delta,
            base + sub * WIN, limit,
        )
        gq_out[rows] = g_q
        gk_out[near] += g_k
        gv_out[near] += g_v


def fifth_kernel(info, gq, gk, gv, got, x, gmid, gain, bias, w_mix, *rest):
    gx_out, slab, d_gain, d_bias = rest[-4:]
    step = pl.program_id(0)

    @pl.when(step == 0)
    def _():
        for ref in (slab, d_gain, d_bias):
            ref[...] = jnp.zeros_like(ref)

    at = pl.ds(pl.multiple_of(step * TB + WIN, WIN), TB)
    last = jnp.where(step == pl.num_programs(0) - 1, 1.0, 0.0)
    tail = got[...].astype(F32) * last
    extra = jnp.concatenate([jnp.zeros((TB - WIN, got.shape[1]), F32), tail], axis=0)
    grad_kv = jnp.concatenate([gk[at], gv[at]], axis=1) + extra
    grad_x = mix_backward(
        gq[...], grad_kv, x[...].astype(F32), gain, bias, w_mix, slab, d_gain, d_bias, gmid[...]
    )
    gx_out[...] = grad_x.astype(BF16)


def assemble_kernel(info, *refs):
    half = info[5]
    core = info[0]
    own, other, out, narrow, wide, sem_in, sem_out = refs[:4], *refs[4:]
    rows = out.shape[1]
    place = info[4]

    def enter(t):
        if t < 4:
            return pltpu.make_async_copy(own[t].at[pl.ds(core * rows, rows)], narrow.at[t], sem_in.at[t])
        return pltpu.make_async_copy(other.at[t - 4], narrow.at[t], sem_in.at[t])

    def leave(t):
        tz, ty = (t % 4) // 2, t % 2
        column = core if t < 4 else 1 - core
        image = (half ^ tz) * 4 + column * 2 + (place ^ ty)
        return pltpu.make_async_copy(wide.at[t], out.at[image], sem_out.at[t])

    for t in range(8):
        enter(t).start()
    for t in range(8):
        enter(t).wait()
        wide[t] = narrow[t].astype(F32)
        leave(t).start()
    for t in range(8):
        leave(t).wait()


def small_kernel(info, *refs):
    vectors, (first, second, out) = refs[:8], refs[8:]
    width = out.shape[1]
    once = jnp.where(info[7] == 0, 1.0, 0.0)
    lane = lax.broadcasted_iota(jnp.int32, (1, width), 1)
    out[...] = jnp.zeros_like(out)
    for i, vector in enumerate(vectors):
        out[i : i + 1] = jnp.sum(vector[...], axis=0, keepdims=True) * once
    for i in range(6):
        rows = (first if i < 3 else second)[i % 3]
        total = jnp.sum(jnp.sum(rows, axis=0, keepdims=True), axis=1, keepdims=True)
        out[8 + i : 9 + i] = jnp.where(lane == info[6], total * once, 0.0)


def unpack_kernel(info, mine, theirs, small, mix, proj, up, down, gain, bias, wide, *, sizes):
    core = info[0]
    wide[core] = mine[...].astype(F32)
    wide[1 - core] = theirs[...].astype(F32)
    rows_a, rows_b, rows_c, ways = sizes
    early = (rows_a + rows_b) // 2 // ways
    late = rows_c // 2 // ways
    rows_mix = rows_c

    def pieces(slab, start, stop):
        total = {"a": rows_a, "b": rows_b, "c": rows_c}[slab] // 2
        size, shift, skip = (late, early, 0) if slab == "c" else (early, 0, rows_a // 2 if slab == "b" else 0)
        at = start
        while at < stop:
            half, row = at // total, at % total
            along = row + skip
            count = min(stop - at, total - row, size - along % size)
            yield at - start, half, along // size * (early + late) + shift + along % size, count
            at += count

    width = wide.shape[2]
    places = {0: (("c", 0), ("b", rows_mix)), 1: (("b", 0), ("a", 0))}
    for layer in range(2):
        (slab, at), (feed, feed_at) = places[layer]
        for out, name in ((mix, slab), (proj, feed), (up, feed), (down, feed)):
            if name == feed and out is not mix:
                at = feed_at
            rows, cols = out.shape[1:]
            for i in range(cols // width):
                for offset, half, row, count in pieces(name, at + i * rows, at + (i + 1) * rows):
                    out[layer, offset : offset + count, i * width : (i + 1) * width] = wide[half, row : row + count]
            if out is not mix:
                feed_at = at + rows * cols // width
    for layer in range(2):
        for norm in range(2):
            gain[layer, norm : norm + 1] = small[2 * layer + norm : 2 * layer + norm + 1]
            bias[layer, norm : norm + 1] = small[4 + 2 * layer + norm : 5 + 2 * layer + norm]


def call(kernel, info, operands, specs, outs, out_specs, scratch=(), grid=(), work=0):
    moved = sum(math.prod(a.shape) * a.dtype.itemsize for a in list(operands) + jax.tree.leaves(outs))
    return pl.pallas_call(
        kernel,
        grid_spec=pltpu.PrefetchScalarGridSpec(
            num_scalar_prefetch=1, grid=grid, in_specs=specs, out_specs=out_specs, scratch_shapes=list(scratch)
        ),
        out_shape=outs,
        compiler_params=pltpu.CompilerParams(vmem_limit_bytes=VMEM_LIMIT),
        cost_estimate=pl.CostEstimate(flops=int(work * 1.15e9), bytes_accessed=moved, transcendentals=0),
    )(info, *operands)


def whole(array):
    zeros = (0,) * len(array.shape)
    return pl.BlockSpec(array.shape, lambda *_: zeros)


def tiled(array):
    return pl.BlockSpec((TB, array.shape[1]), lambda i, *_: (i, 0))


ANY = pl.BlockSpec(memory_space=pl.ANY)


def shape(dims, kind):
    return jax.ShapeDtypeStruct(dims, kind)


def after(value, *others):
    return lax.optimization_barrier((value, others))[0]


def body(edge_rows, lengths, norm_gain, norm_bias, w_qkv, w_out, w_up, w_down):
    sections = lax.axis_size("section")
    index = lax.axis_index("section")
    images, rows_dev, width = edge_rows.shape
    seats = 2 * images
    rep = sections // seats
    seat = index // rep
    twin = index % rep
    rows_piece = rows_dev * rep
    qw = (w_qkv.shape[2] - width) // 2
    kvw = w_qkv.shape[2] - qw
    hidden = w_up.shape[2]
    n = rows_piece * images // 2
    quarter = images // 2
    steps = (n // TB,)

    def route(pairs):
        return [(s * rep + e, d * rep + e) for s, d in pairs for e in range(rep)]

    if rep > 1:
        groups = [[s * rep + e for e in range(rep)] for s in range(seats)]
        edge_rows = lax.all_gather(edge_rows, "section", axis_index_groups=groups, axis=1, tiled=True)

    def source_key(s):
        return (s // images) * quarter + s % quarter, (s % images) // quarter

    def source_seat(key, core):
        return (key // quarter) * images + core * quarter + key % quarter

    half = seat // images
    my_key = half * quarter + seat % quarter
    chip = seat // 2
    part = seat % 2
    limit = lengths[chip]
    spot = lax.axis_index("dp") * images + chip
    info = jnp.stack([part, limit, chip % quarter, chip // quarter, chip % 2, half, spot, twin]).astype(jnp.int32)

    def scatter_route(t):
        return route([(s, 2 * (source_key(s)[0] ^ t) + source_key(s)[1]) for s in range(seats)])

    received = [None] * images
    for t in list(range(quarter, images)) + list(range(quarter)):
        piece = lax.dynamic_index_in_dim(edge_rows, my_key ^ t, 0, keepdims=False)
        received[t] = lax.ppermute(piece, "section", scatter_route(t))

    fz, fl, fy = chip // 4, (chip // 2) % 2, chip % 2
    swap = route([(s, s ^ 1) for s in range(seats)])

    def return_route(tz, ty):
        pairs = []
        for s in range(seats):
            z, l, y, p = s // 8, (s // 4) % 2, (s // 2) % 2, s % 2
            pairs.append((s, ((z ^ tz) * 4 + p * 2 + (y ^ ty)) * 2 + l))
        return route(pairs)

    def send_back(low, high, which=(2, 3, 0, 1)):
        low = low.reshape(2, 2 * rows_piece, width)
        high = high.reshape(2, 2 * rows_piece, width)
        out = []
        for t in which:
            tz, ty = t // 2, t % 2
            piece = jnp.where(
                (fz ^ tz) == 0,
                lax.dynamic_index_in_dim(low, fy ^ ty, 0, keepdims=False),
                lax.dynamic_index_in_dim(high, fy ^ ty, 0, keepdims=False),
            )
            out.append((t, lax.ppermute(piece, "section", return_route(tz, ty))))
        return [piece for _, piece in sorted(out, key=lambda p: p[0])]

    def trade(got):
        send = jnp.stack([lax.dynamic_slice_in_dim(g, (1 - part) * rows_piece, rows_piece, 0) for g in got])
        return lax.ppermute(send, "section", swap)

    first_to_second = route([(2 * c, 2 * c + 1) for c in range(images)])
    second_to_first = route([(2 * c + 1, 2 * c) for c in range(images)])

    dma = pltpu.SemaphoreType.DMA
    rows_q = shape((n, qw), BF16)
    rows_kv = shape((n, kvw), BF16)
    rows_low = shape((n, width), BF16)
    rows_wide = shape((n, width), F32)
    rows_stat = shape((n, 128), F32)
    rows_hidden = shape((n, hidden), BF16)
    grad_k_shape = shape((n + WIN, qw), F32)
    grad_v_shape = shape((n + WIN, width), F32)
    mix_rows = w_qkv.shape[1] * w_qkv.shape[2] // width
    feed_rows = (w_out[0].size + w_up[0].size + w_down[0].size) // width
    feed_slab = shape((feed_rows, width), F32)
    both_slab = shape((mix_rows + feed_rows, width), F32)
    mix_slab = shape((mix_rows, width), F32)
    vec_shape = shape((8, width), F32)
    squares_shape = shape((3, 8, width), F32)
    ext = pltpu.VMEM((n + WIN, kvw), BF16)

    g0, g1, b0, b1 = norm_gain[0], norm_gain[1], norm_bias[0], norm_bias[1]

    outs = [rows_low, rows_q, rows_kv]
    x, q0, kv0 = call(
        first_kernel, info, received + [g0, b0, w_qkv[0]],
        [ANY] * images + [whole(g0), whole(b0), whole(w_qkv[0])],
        outs, [whole(o) for o in outs], [dma((quarter,))], work=6,
    )
    halo0 = lax.ppermute(kv0[n - WIN :], "section", first_to_second)

    outs = [rows_low, rows_q, rows_kv, rows_low, rows_stat, rows_hidden, rows_hidden, rows_wide, squares_shape]
    z, q1, kv1, o0, lse0, active0, slope0, mid0, squares0 = call(
        second_kernel, info, [x, q0, kv0, halo0, g0, b0, w_out[0], w_up[0], w_down[0], g1, b1, w_qkv[1]],
        [tiled(x), tiled(q0)] + [whole(a) for a in (kv0, halo0, g0, b0, w_out[0], w_up[0], w_down[0], g1, b1, w_qkv[1])],
        outs, [tiled(o) for o in outs[:-1]] + [whole(outs[-1])], [ext], steps, work=15,
    )
    kv_other = lax.ppermute(kv1, "section", first_to_second)

    rows_k_all = shape((2 * n, qw), BF16)
    rows_v_all = shape((2 * n, width), BF16)
    outs = [rows_q, rows_k_all, rows_v_all, rows_wide, rows_stat]
    qr, kr, vr, o_far, lse_far = call(
        far_forward_kernel, info, [q1, kv1, kv_other], [whole(a) for a in (q1, kv1, kv_other)],
        outs, [whole(o) for o in outs],
        [pltpu.VMEM((n, qw), F32), pltpu.VMEM((2 * n, qw), F32), pltpu.VMEM((HEADS, 2 * n, 128), F32),
         pltpu.VMEM((HEADS, n, 128), F32), pltpu.VMEM((n, 128), F32)], work=14,
    )

    halo1 = kv_other[n - WIN :]
    outs = [rows_low, rows_low, rows_stat, shape((n, qw), F32), grad_k_shape, grad_v_shape, rows_wide,
            feed_slab, vec_shape, vec_shape, squares_shape]
    (y1, go1, stat1, gq_near, gk_near, gv_near, gmid1, slab_a, d_gain11, d_bias11, squares1) = call(
        third_kernel, info,
        received + [q1, kv1, halo1, o_far, lse_far, z, g1, b1, w_out[1], w_up[1], w_down[1]],
        [ANY] * images + [tiled(q1), whole(kv1), whole(halo1), tiled(o_far), tiled(lse_far), tiled(z)]
        + [whole(a) for a in (g1, b1, w_out[1], w_up[1], w_down[1])],
        outs,
        [tiled(o) for o in outs[:4]] + [whole(outs[4]), whole(outs[5]), tiled(outs[6])] + [whole(o) for o in outs[7:]],
        [ext, pltpu.VMEM((n, width), BF16), dma((quarter,))], steps, work=24,
    )
    second_way = send_back(z, y1, (2,))

    outs = [shape((n, qw), F32), shape((n, kvw), F32), rows_kv]
    operands = [qr, kr, vr, go1, stat1, gq_near, gk_near, gv_near]
    gq1, gkv1, gkv_send = call(
        far_backward_kernel, info, operands, [whole(a) for a in operands], outs, [whole(o) for o in outs],
        [pltpu.VMEM((HEADS, n, 128), F32), pltpu.VMEM((n, 128), F32), pltpu.VMEM((n, qw), F32),
         pltpu.VMEM((2 * n, qw), F32), pltpu.VMEM((HEADS, 2 * n, 128), F32)], work=18,
    )
    gkv_got = lax.ppermute(after(gkv_send, *second_way), "section", second_to_first)
    first_way, other_way, third_way = send_back(after(z, *second_way), y1, (3, 0, 1))
    forward_back = [first_way, other_way, *second_way, third_way]

    outs = [rows_low, shape((n, qw), F32), grad_k_shape, grad_v_shape, rows_wide,
            both_slab, vec_shape, vec_shape, vec_shape, vec_shape]
    (gz, gq0, gk0, gv0, gmid0, slab_b, d_gain10, d_bias10, d_gain01, d_bias01) = call(
        fourth_kernel, info,
        [gq1, gkv1, gkv_got, z, gmid1, g1, b1, w_qkv[1], q0, kv0, halo0, o0, lse0, active0, slope0, mid0, g0, b0,
         w_out[0], w_up[0], w_down[0]],
        [tiled(a) for a in (gq1, gkv1, gkv_got, z, gmid1)] + [whole(a) for a in (g1, b1, w_qkv[1])]
        + [tiled(q0), whole(kv0), whole(halo0)] + [tiled(a) for a in (o0, lse0, active0, slope0, mid0)]
        + [whole(a) for a in (g0, b0, w_out[0], w_up[0], w_down[0])],
        outs,
        [tiled(outs[0]), tiled(outs[1]), whole(outs[2]), whole(outs[3]), tiled(outs[4])] + [whole(o) for o in outs[5:]],
        [ext], steps, work=20,
    )
    gk0, gv0, slab_b = after((gk0, gv0, slab_b), *forward_back)
    halo_send = jnp.concatenate([gk0[:WIN], gv0[:WIN]], axis=1).astype(BF16)
    halo_got = lax.ppermute(halo_send, "section", second_to_first)

    once = (twin == 0).astype(F32)
    dp_count = lax.axis_size("dp")
    dp_index = lax.axis_index("dp")

    def partners(masks):
        total = dp_count * sections
        spot = dp_index * sections + index
        digit = sum(((spot // m) % 2) << i for i, m in enumerate(masks))
        routes = []
        for c in range(1, 1 << len(masks)):
            flips = sum(m for i, m in enumerate(masks) if (c >> i) & 1)
            routes.append((c, [(s, s ^ flips) for s in range(total)]))
        return digit, routes

    def chunk(slabs, which, ways):
        return jnp.concatenate(
            [lax.dynamic_slice_in_dim(s, which * (s.shape[0] // ways), s.shape[0] // ways, 0) for s in slabs]
        )

    def scatter(slabs, masks, vectors=None):
        digit, routes = partners(masks)
        ways = 1 << len(masks)
        kept = chunk(slabs, digit, ways)
        count = kept.shape[0]
        riders = []
        if vectors is not None:
            coarse = vectors.astype(BF16)
            riders = [coarse, (vectors - coarse.astype(F32)).astype(BF16)]
        got = [
            lax.ppermute(jnp.concatenate([chunk(slabs, digit ^ c, ways).astype(BF16)] + riders), ("dp", "section"), way)
            for c, way in routes
        ]
        for g in got:
            kept = kept + g[:count].astype(F32)
            if vectors is not None:
                rest = g[count:].astype(F32)
                vectors = vectors + (rest[: vectors.shape[0]] + rest[vectors.shape[0] :])
        return kept if vectors is None else (kept, vectors)

    def gather(piece, masks):
        digit, routes = partners(masks)
        pieces = [piece] + [lax.ppermute(piece, ("dp", "section"), way) for _, way in routes]
        stacked = jnp.stack(pieces)
        return jnp.concatenate(
            [lax.dynamic_index_in_dim(stacked, digit ^ j, 0, keepdims=False) for j in range(len(pieces))]
        )

    dp_masks = [sections << b for b in range(dp_count.bit_length() - 1)]
    section_masks = [1 << b for b in range(1, sections.bit_length() - 1)]
    plane = [dp_masks[0], section_masks[0]]
    rest = section_masks[1:] + dp_masks[1:]
    rest = [rest[i : i + 2] for i in range(0, len(rest), 2)]
    early = scatter([slab_a * once, slab_b * once] if rep > 1 else [slab_a, slab_b], [1])
    gq0 = after(gq0, early)
    early = scatter([early], plane)

    outs = [rows_low, mix_slab, vec_shape, vec_shape]
    gx, slab_c, d_gain00, d_bias00 = call(
        fifth_kernel, info, [gq0, gk0, gv0, halo_got, x, gmid0, g0, b0, w_qkv[0]],
        [tiled(gq0), whole(gk0), whole(gv0), whole(halo_got), tiled(x), tiled(gmid0), whole(g0), whole(b0), whole(w_qkv[0])],
        outs, [tiled(outs[0])] + [whole(o) for o in outs[1:]], (), steps, work=8,
    )
    forward_trade = trade(after(forward_back, gx))

    operands = [d_gain00, d_gain01, d_gain10, d_gain11, d_bias00, d_bias01, d_bias10, d_bias11, squares0, squares1]
    small_shape = shape((16, width), F32)
    small = call(small_kernel, info, operands, [whole(a) for a in operands], small_shape, whole(small_shape))

    def assemble(own, other):
        out = call(
            assemble_kernel, info, own + [other], [ANY] * 5, shape((images, rows_piece, width), F32), ANY,
            [pltpu.VMEM((images, rows_piece, width), BF16), pltpu.VMEM((images, rows_piece, width), F32),
             dma((images,)), dma((images,))],
        )
        if rep > 1:
            out = lax.dynamic_slice_in_dim(out, twin * rows_dev, rows_dev, 1)
        return out

    crossing = send_back(gx, gz, (2, 3))
    late, small = scatter([after(slab_c * once if rep > 1 else slab_c, early)], [1], small)
    late, small = scatter([late], plane, small)
    early_rows = early.shape[0]
    forward_rows = assemble(forward_back, forward_trade)
    both, _ = after((jnp.concatenate([early, late]), forward_rows), *crossing)
    staying = send_back(after(gx, *crossing), gz, (0, 1))
    for masks in rest:
        both, small = scatter([both], masks, small)
    both = both.astype(BF16)
    for masks in rest[::-1]:
        both = gather(both, masks)
    backward_back = staying + crossing
    backward_trade = trade(backward_back)
    both = gather(both, plane)
    backward_rows = assemble(backward_back, backward_trade)
    both = after(both, backward_rows)
    (theirs,) = (lax.ppermute(both, ("dp", "section"), way) for _, way in partners([1])[1])
    sums = lax.dynamic_slice_in_dim(small[8:14], dp_index * images, images, 1)
    rms_values = jnp.sqrt(sums / (lengths.astype(F32)[None, :] * width))
    outs = [shape(w.shape, F32) for w in (w_qkv, w_out, w_up, w_down, norm_gain, norm_bias)]
    sizes = (slab_a.shape[0], slab_b.shape[0], slab_c.shape[0], 1 << len(plane))
    grads = call(
        functools.partial(unpack_kernel, sizes=sizes), jnp.stack([index % 2]).astype(jnp.int32), [both, theirs, small],
        [whole(both), whole(theirs), whole(small)], outs, [whole(o) for o in outs],
        [pltpu.VMEM((2,) + both.shape, F32)],
    )
    return (forward_rows, backward_rows, rms_values, grads[4], grads[5]) + tuple(grads[:4])


def solution(mesh):
    placed = (P("dp", "section", None), P("dp"), P(), P(), P(), P(), P(), P())
    return jax.shard_map(
        body,
        mesh=mesh,
        in_specs=placed,
        out_specs=(P("dp", "section", None), P("dp", "section", None), P(None, "dp"), P(), P(), P(), P(), P(), P()),
        check_vma=False,
    )
```

```python
import functools
import math

import jax
import jax.numpy as jnp
from jax import lax
from jax.experimental import pallas as pl
from jax.experimental.pallas import tpu as pltpu
from jax.sharding import PartitionSpec as P

HEADS = 2
WIN = 128
STRIDE = 128
NEG = -1e30
F32 = jnp.float32
BF16 = jnp.bfloat16
TB = 512
RES = 8
UNROLL = 16
VMEM_LIMIT = 16 * 1024 * 1024


def dot(left, right):
    return lax.dot_general(left, right, (((1,), (0,)), ((), ())), preferred_element_type=F32)


def dot_t(left, right):
    return lax.dot_general(left, right, (((1,), (1,)), ((), ())), preferred_element_type=F32)


def t_dot(left, right):
    return lax.dot_general(left, right, (((0,), (0,)), ((), ())), preferred_element_type=F32)


def score_scale(query_width):
    return 1.0 / math.sqrt(query_width // HEADS)


def norm_parts(rows):
    centre = rows - jnp.mean(rows, axis=-1, keepdims=True)
    scale = lax.rsqrt(jnp.mean(centre * centre, axis=-1, keepdims=True) + 1e-05)
    return centre * scale, scale


def norm_back(grad, unit, scale, gain):
    scaled = grad * gain
    first = jnp.mean(scaled, axis=-1, keepdims=True)
    second = jnp.mean(scaled * unit, axis=-1, keepdims=True)
    return scale * (scaled - first - unit * second)


def col_sum(rows):
    return jnp.sum(rows.reshape(rows.shape[0] // 8, 8, rows.shape[1]), axis=0)


def gelu_pair(hidden):
    c0 = math.sqrt(2.0 / math.pi)
    square = hidden * hidden
    share = 0.5 + 0.5 * jnp.tanh(hidden * (c0 + (c0 * 0.044715) * square))
    active = hidden * share
    slope = share + active * (1.0 - share) * (2.0 * c0 + (6.0 * c0 * 0.044715) * square)
    return active, slope


def head_split(rows):
    lane = lax.broadcasted_iota(jnp.int32, rows.shape, 1)
    zero = jnp.zeros_like(rows)
    low = lane < rows.shape[1] // HEADS
    return jnp.concatenate([jnp.where(low, rows, zero), jnp.where(low, zero, rows)], axis=0)


def head_join(stacked):
    half = stacked.shape[0] // 2
    lane = lax.broadcasted_iota(jnp.int32, (half, stacked.shape[1]), 1)
    return jnp.where(lane < stacked.shape[1] // HEADS, stacked[:half], stacked[half:])


def near_masks(base, limit):
    row = lax.broadcasted_iota(jnp.int32, (2 * WIN, WIN), 0)
    row = jnp.where(row >= WIN, row - WIN, row)
    col = lax.broadcasted_iota(jnp.int32, (2 * WIN, WIN), 1)
    own = col <= row
    key = base + col - jnp.where(own, 0, WIN)
    allowed = (key >= 0) & ((key < limit) | (col == row))
    return own, allowed


def near_scores(split_q, keys, own, allowed):
    scores = dot_t(split_q, keys)
    folded = jnp.where(own, scores[:, WIN:], scores[:, :WIN])
    return jnp.where(allowed, folded, NEG)


def unfold(folded, own):
    return jnp.concatenate([jnp.where(own, 0.0, folded), jnp.where(own, folded, 0.0)], axis=1).astype(BF16)


def near_forward(queries, keys, values, base, limit):
    own, allowed = near_masks(base, limit)
    scores = near_scores(head_split(queries), keys, own, allowed)
    largest = jnp.max(scores, axis=-1, keepdims=True)
    powers = jnp.exp(scores - largest)
    total = jnp.sum(powers, axis=-1, keepdims=True)
    weights = unfold(powers, own)
    hd = values.shape[1] // HEADS
    out = [dot(weights[h * WIN : (h + 1) * WIN], values[:, h * hd : (h + 1) * hd]) for h in range(HEADS)]
    return out, largest, total


def near_backward(queries, keys, values, grad_out, log_total, delta, base, limit):
    own, allowed = near_masks(base, limit)
    split_q = head_split(queries)
    weights = jnp.exp(near_scores(split_q, keys, own, allowed) - log_total)
    hd = values.shape[1] // HEADS
    pull = jnp.concatenate(
        [dot_t(grad_out[:, h * hd : (h + 1) * hd], values[:, h * hd : (h + 1) * hd]) for h in range(HEADS)], axis=0
    )
    pull = jnp.where(own, pull[:, WIN:], pull[:, :WIN])
    slope = unfold(weights * (pull - delta), own)
    weights = unfold(weights, own)
    grad_q = head_join(dot(slope, keys))
    grad_k = t_dot(slope, split_q)
    grad_v = jnp.concatenate(
        [t_dot(weights[h * WIN : (h + 1) * WIN], grad_out[:, h * hd : (h + 1) * hd]) for h in range(HEADS)], axis=1
    )
    return grad_q, grad_k, grad_v


def stack_stat(stat, width=128):
    return jnp.concatenate([stat[:, 0:1], stat[:, width // 2 : width // 2 + 1]], axis=0)


def spread_stat(stacked, width=128):
    half = stacked.shape[0] // 2
    lane = lax.broadcasted_iota(jnp.int32, (half, width), 1)
    return jnp.where(lane < width // 2, stacked[:half], stacked[half:])


def masked_squares(rows, base, limit):
    pos = base + lax.broadcasted_iota(jnp.int32, (rows.shape[0], 1), 0)
    return col_sum(jnp.where(pos < limit, rows * rows, 0.0))


def gather_pieces(info, pieces, target, sems, low):
    rows = pieces[0].shape[0]

    def each(act):
        for ty in range(2):
            place = target.at[pl.ds((ty ^ info[4]) * rows, rows)]

            @pl.when(info[5] == (0 if low else 1))
            def _():
                act(pltpu.make_async_copy(pieces[ty], place, sems.at[ty]))

            @pl.when(info[5] == (1 if low else 0))
            def _():
                act(pltpu.make_async_copy(pieces[2 + ty], place, sems.at[ty]))

    each(lambda c: c.start())
    each(lambda c: c.wait())


def emit_messages(info, step, cross, local, low, high):
    half = cross[0].shape[0]
    lower = info[5] == 0
    for sub in range(TB // 256):
        rows = slice(sub * 256, (sub + 1) * 256)
        number = step * (TB // 256) + sub
        block = number // (half // 256)
        at = pl.ds(pl.multiple_of((number - block * (half // 256)) * 256, 256), 256)
        leaving = jnp.where(lower, high[rows], low[rows])
        staying = jnp.where(lower, low[rows], high[rows])
        for ty in range(2):

            @pl.when((block ^ info[4]) == ty)
            def _():
                cross[ty][at] = leaving
                local[ty][at] = staying


def split_slab(info, slab, keep, send):
    once = jnp.where(info[7] == 0, 1.0, 0.0)
    half = keep.shape[0]
    mine = info[8]
    keep[...] = slab[pl.ds(pl.multiple_of(mine * half, 8), half)] * once
    send[:half] = (slab[pl.ds(pl.multiple_of((1 - mine) * half, 8), half)] * once).astype(BF16)


def first_kernel(info, *refs):
    pieces = refs[:4]
    gain, bias, w_mix, x_out, q_out, kv_out, halo_out, sems = refs[4:]
    gather_pieces(info, pieces, x_out, sems, True)
    qw = q_out.shape[1]

    def block(i, _):
        at = pl.ds(pl.multiple_of(i * TB, TB), TB)
        unit, _ = norm_parts(x_out[at].astype(F32))
        normed = (unit * gain[0:1] + bias[0:1]).astype(BF16)
        mixed = dot(normed, w_mix[...])
        q_out[at] = (mixed[:, :qw] * score_scale(qw)).astype(BF16)
        kv_out[at] = mixed[:, qw:].astype(BF16)
        return 0

    lax.fori_loop(0, x_out.shape[0] // TB, block, 0)
    halo_out[...] = kv_out[kv_out.shape[0] - WIN :]


def load_extended(halo, kv, ext):
    ext[: halo.shape[0]] = halo[...]
    ext[halo.shape[0] :] = kv[...]


def second_kernel(
    info, x, q, kv, halo, gain, bias, w_proj, w_in, w_back, gain_next, bias_next, w_mix_next,
    z_out, q_next, kv_next, o_out, lse_out, active_out, slope_out, mid_out, squares, ext,
):
    step = pl.program_id(0)
    qw = q.shape[1]
    n = kv.shape[0]

    @pl.when(step == 0)
    def _():
        load_extended(halo, kv, ext)
        squares[...] = jnp.zeros_like(squares)

    limit = info[1]
    start = step * TB
    base = info[0] * n + start
    outs = []
    for sub in range(TB // WIN):
        near = pl.ds(pl.multiple_of(start + sub * WIN, WIN), 2 * WIN)
        keys = ext[near, :qw]
        values = ext[near, qw:]
        queries = q[sub * WIN : (sub + 1) * WIN]
        out, largest, total = near_forward(queries, keys, values, base + sub * WIN, limit)
        inverse = 1.0 / total
        lse_out[sub * WIN : (sub + 1) * WIN] = spread_stat(largest + jnp.log(total))
        outs.append(jnp.concatenate([out[0] * inverse[:WIN], out[1] * inverse[WIN:]], axis=1))
    attended = jnp.concatenate(outs, axis=0).astype(BF16)
    o_out[...] = attended
    stream = x[...].astype(F32)
    branch = dot(attended, w_proj[...])
    middle = stream + branch
    mid_out[...] = middle
    unit, _ = norm_parts(middle)
    normed = (unit * gain[1:2] + bias[1:2]).astype(BF16)
    active, slope = gelu_pair(dot(normed, w_in[...]))
    active = active.astype(BF16)
    active_out[...] = active
    slope_out[...] = slope.astype(BF16)
    feed = dot(active, w_back[...])
    z = (middle + feed).astype(BF16)
    z_out[...] = z
    squares[0] += masked_squares(stream, base, limit)
    squares[1] += masked_squares(branch, base, limit)
    squares[2] += masked_squares(feed, base, limit)
    unit, _ = norm_parts(z.astype(F32))
    normed = (unit * gain_next[0:1] + bias_next[0:1]).astype(BF16)
    mixed = dot(normed, w_mix_next[...])
    q_next[...] = (mixed[:, :qw] * score_scale(qw)).astype(BF16)
    kv_next[...] = mixed[:, qw:].astype(BF16)


def far_mask(grid_q, grid_k, part_grid):
    shape = (HEADS * RES * grid_q, RES * grid_k)
    row = lax.broadcasted_iota(jnp.int32, shape, 0)
    col = lax.broadcasted_iota(jnp.int32, shape, 1)
    row = jnp.where(row >= RES * grid_q, row - RES * grid_q, row)
    row_res = jnp.zeros(shape, jnp.int32)
    col_res = jnp.zeros(shape, jnp.int32)
    for r in range(1, RES):
        row_res += (row >= r * grid_q).astype(jnp.int32)
        col_res += (col >= r * grid_k).astype(jnp.int32)
    row_grid = row - row_res * grid_q + part_grid
    col_grid = col - col_res * grid_k
    allowed = (row_res == col_res) & (col_grid < row_grid)
    return allowed, col_grid * STRIDE + col_res


def far_forward_kernel(info, q, kv, other, qr, kr, vr, o_far, lse_far, q_s, k_s, v_s, o_s, lse_s):
    n, qw = q.shape
    grid_q = n // STRIDE
    grid_k = 2 * grid_q
    part = info[0]
    limit = info[1]

    def place(g, _):
        at = pl.ds(pl.multiple_of(g * STRIDE, STRIDE), STRIDE)
        own = kv[at].astype(F32)
        early = jnp.where(part == 0, own, other[at].astype(F32))
        q_s[pl.ds(g, STRIDE, stride=grid_q), :] = q[at].astype(F32)
        k_s[pl.ds(g, STRIDE, stride=grid_k), :] = early[:, :qw]
        k_s[pl.ds(g + grid_q, STRIDE, stride=grid_k), :] = own[:, :qw]
        hd = v_s.shape[1]
        for h in range(HEADS):
            v_s[h, pl.ds(g, STRIDE, stride=grid_k), :] = early[:, qw + h * 128 : qw + (h + 1) * 128]
            v_s[h, pl.ds(g + grid_q, STRIDE, stride=grid_k), :] = own[:, qw + h * 128 : qw + (h + 1) * 128]
        return 0

    lax.fori_loop(0, grid_q, place, 0)
    base_mask, key_pos = far_mask(grid_q, grid_k, part * grid_q)
    rows_q = RES * grid_q
    rows_k = RES * grid_k

    def one(i):
        at_q = pl.ds(pl.multiple_of(i * rows_q, rows_q), rows_q)
        at_k = pl.ds(pl.multiple_of(i * rows_k, rows_k), rows_k)
        queries = q_s[at_q].astype(BF16)
        keys = k_s[at_k].astype(BF16)
        values = [v_s[h, at_k].astype(BF16) for h in range(HEADS)]
        qr[at_q] = queries
        kr[at_k] = keys
        for h in range(HEADS):
            vr[at_k, h * 128 : (h + 1) * 128] = values[h]
        allowed = base_mask & (key_pos + i * RES < limit)
        scores = jnp.where(allowed, dot_t(head_split(queries), keys), NEG)
        largest = jnp.max(scores, axis=-1, keepdims=True)
        powers = jnp.where(allowed, jnp.exp(scores - largest), 0.0)
        total = jnp.sum(powers, axis=-1, keepdims=True)
        safe = jnp.maximum(total, 1e-30)
        weights = (powers * (1.0 / safe)).astype(BF16)
        lse = jnp.where(total > 0.0, largest + jnp.log(safe), NEG)
        lse_s[at_q] = spread_stat(lse)
        for h in range(HEADS):
            o_s[h, at_q] = dot(weights[h * rows_q : (h + 1) * rows_q], values[h])

    def group(i, _):
        for u in range(UNROLL):
            one(i * UNROLL + u)
        return 0

    lax.fori_loop(0, STRIDE // RES // UNROLL, group, 0)

    def back(g, _):
        at = pl.ds(pl.multiple_of(g * STRIDE, STRIDE), STRIDE)
        pick = pl.ds(g, STRIDE, stride=grid_q)
        lse_far[at] = lse_s[pick, :]
        for h in range(HEADS):
            o_far[at, h * 128 : (h + 1) * 128] = o_s[h, pick, :]
        return 0

    lax.fori_loop(0, grid_q, back, 0)


def third_kernel(
    info, *refs,
):
    pieces = refs[:4]
    (q, kv, halo, o_far, lse_far, z, gain, bias, w_proj, w_in, w_back,
     cross0, cross1, local0, local1, go_out, stat_out, gq_out, gk_out, gv_out, gmid_out, keep, send,
     d_gain, d_bias, squares, ext, cot, slab, sems) = refs[4:]
    step = pl.program_id(0)
    qw = q.shape[1]
    n = kv.shape[0]

    @pl.when(step == 0)
    def _():
        gather_pieces(info, pieces, cot, sems, False)
        load_extended(halo, kv, ext)
        for ref in (squares, gk_out, gv_out, slab, d_gain, d_bias):
            ref[...] = jnp.zeros_like(ref)

    limit = info[1]
    start = pl.multiple_of(step * TB, TB)
    base = info[0] * n + start
    outs = []
    logs = []
    for sub in range(TB // WIN):
        rows = slice(sub * WIN, (sub + 1) * WIN)
        near = pl.ds(pl.multiple_of(start + sub * WIN, WIN), 2 * WIN)
        out, largest, total = near_forward(q[rows], ext[near, :qw], ext[near, qw:], base + sub * WIN, limit)
        far_log = stack_stat(lse_far[rows])
        top = jnp.maximum(largest, far_log)
        near_share = jnp.exp(largest - top)
        far_share = jnp.exp(far_log - top)
        whole = total * near_share + far_share
        inverse = 1.0 / whole
        near_share = near_share * inverse
        far_share = far_share * inverse
        logs.append(top + jnp.log(whole))
        far = o_far[rows]
        outs.append(
            jnp.concatenate(
                [
                    out[h] * near_share[h * WIN : (h + 1) * WIN]
                    + far[:, h * 128 : (h + 1) * 128] * far_share[h * WIN : (h + 1) * WIN]
                    for h in range(HEADS)
                ],
                axis=1,
            )
        )
    attended_wide = jnp.concatenate(outs, axis=0)
    attended = attended_wide.astype(BF16)
    stream = z[...].astype(F32)
    branch = dot(attended, w_proj[...])
    middle = stream + branch
    unit, scale = norm_parts(middle)
    normed = (unit * gain[1:2] + bias[1:2]).astype(BF16)
    active, slope = gelu_pair(dot(normed, w_in[...]))
    active = active.astype(BF16)
    feed = dot(active, w_back[...])
    emit_messages(info, step, (cross0, cross1), (local0, local1), z[...], (middle + feed).astype(BF16))
    squares[0] += masked_squares(stream, base, limit)
    squares[1] += masked_squares(branch, base, limit)
    squares[2] += masked_squares(feed, base, limit)

    pos = base + lax.broadcasted_iota(jnp.int32, (TB, 1), 0)
    upstream = jnp.where(pos < limit, cot[pl.ds(start, TB)].astype(F32), 0.0)
    grad_out, grad_mid = feed_backward(
        upstream, active, slope, normed, unit, scale, attended, gain, w_proj, w_in, w_back, slab, 0, d_gain, d_bias
    )
    gmid_out[...] = grad_mid
    go_out[...] = grad_out
    weighted = grad_out.astype(F32) * attended_wide
    for sub in range(TB // WIN):
        rows = slice(sub * WIN, (sub + 1) * WIN)
        near = pl.ds(pl.multiple_of(start + sub * WIN, WIN), 2 * WIN)
        delta = jnp.concatenate(
            [jnp.sum(weighted[rows, h * 128 : (h + 1) * 128], axis=-1, keepdims=True) for h in range(HEADS)], axis=0
        )
        stat_out[rows] = pack_stats(logs[sub], delta)
        gq, gk, gv = near_backward(
            q[rows], ext[near, :qw], ext[near, qw:], grad_out[rows], logs[sub], delta, base + sub * WIN, limit
        )
        gq_out[rows] = gq
        gk_out[near] += gk
        gv_out[near] += gv

    @pl.when(step == pl.num_programs(0) - 1)
    def _():
        split_slab(info, slab, keep, send)


def pack_stats(lse, delta):
    half = lse.shape[0] // 2
    lane = lax.broadcasted_iota(jnp.int32, (half, 128), 1)
    low = jnp.where(lane < 32, lse[:half], lse[half:])
    high = jnp.where(lane < 96, delta[:half], delta[half:])
    return jnp.where(lane < 64, low, high)


def add_columns(slab, at, grad):
    rows, cols = grad.shape
    width = slab.shape[1]
    for i in range(cols // width):
        slab[at + i * rows : at + (i + 1) * rows] += grad[:, i * width : (i + 1) * width]


def feed_backward(
    upstream, active, slope, normed, unit, scale, attended, gain, w_proj, w_in, w_back, slab, at, d_gain, d_bias,
):
    low = upstream.astype(BF16)
    width = low.shape[1]
    hidden = active.shape[1]
    slab[at + width + hidden : at + width + 2 * hidden] += t_dot(active, low)
    grad_hidden = (dot_t(low, w_back[...]) * slope).astype(BF16)
    add_columns(slab, at + width, t_dot(normed, grad_hidden))
    grad_normed = dot_t(grad_hidden, w_in[...])
    d_gain[...] += col_sum(grad_normed * unit)
    d_bias[...] += col_sum(grad_normed)
    grad_mid = upstream + norm_back(grad_normed, unit, scale, gain[1:2])
    branch_low = grad_mid.astype(BF16)
    slab[at : at + width] += t_dot(attended, branch_low)
    grad_out = dot_t(branch_low, w_proj[...]).astype(BF16)
    return grad_out, grad_mid


def far_backward_kernel(
    info, qr, kr, vr, go, stat, gq_near, gk_near, gv_near, gq_out, gkv_own, gkv_send,
    go_s, stat_s, gq_s, gk_s, gv_s,
):
    n, qw = gq_near.shape
    grid_q = n // STRIDE
    grid_k = 2 * grid_q
    part = info[0]
    limit = info[1]

    def place(g, _):
        at = pl.ds(pl.multiple_of(g * STRIDE, STRIDE), STRIDE)
        pick = pl.ds(g, STRIDE, stride=grid_q)
        rows = go[at].astype(F32)
        for h in range(HEADS):
            go_s[h, pick, :] = rows[:, h * 128 : (h + 1) * 128]
        stat_s[pick, :] = stat[at]
        return 0

    lax.fori_loop(0, grid_q, place, 0)
    base_mask, key_pos = far_mask(grid_q, grid_k, part * grid_q)
    rows_q = RES * grid_q
    rows_k = RES * grid_k

    def one(i):
        at_q = pl.ds(pl.multiple_of(i * rows_q, rows_q), rows_q)
        at_k = pl.ds(pl.multiple_of(i * rows_k, rows_k), rows_k)
        keys = kr[at_k]
        split_q = head_split(qr[at_q])
        grads = [go_s[h, at_q].astype(BF16) for h in range(HEADS)]
        stats = stat_s[at_q]
        lse = jnp.concatenate([stats[:, 0:1], stats[:, 32:33]], axis=0)
        delta = jnp.concatenate([stats[:, 64:65], stats[:, 96:97]], axis=0)
        allowed = base_mask & (key_pos + i * RES < limit)
        weights = jnp.exp(jnp.where(allowed, dot_t(split_q, keys), NEG) - lse)
        pull = jnp.concatenate([dot_t(grads[h], vr[at_k, h * 128 : (h + 1) * 128]) for h in range(HEADS)], axis=0)
        slope = (weights * (pull - delta)).astype(BF16)
        weights = weights.astype(BF16)
        gq_s[at_q] = head_join(dot(slope, keys))
        gk_s[at_k] = t_dot(slope, split_q)
        for h in range(HEADS):
            gv_s[h, at_k] = t_dot(weights[h * rows_q : (h + 1) * rows_q], grads[h])

    def group(i, _):
        for u in range(UNROLL):
            one(i * UNROLL + u)
        return 0

    lax.fori_loop(0, STRIDE // RES // UNROLL, group, 0)

    def back(g, _):
        at = pl.ds(pl.multiple_of(g * STRIDE, STRIDE), STRIDE)
        shifted = pl.ds(pl.multiple_of(g * STRIDE + WIN, STRIDE), STRIDE)
        gq_out[at] = gq_near[at] + gq_s[pl.ds(g, STRIDE, stride=grid_q), :]
        mine = pl.ds(g + part * grid_q, STRIDE, stride=grid_k)
        sent = pl.ds(g, STRIDE, stride=grid_k)
        last = jnp.where(g == grid_q - 1, 1.0, 0.0)
        gkv_own[at, :qw] = gk_near[shifted] + gk_s[mine, :]
        gkv_send[at, :qw] = (gk_s[sent, :] + last * gk_near[:WIN]).astype(BF16)
        for h in range(HEADS):
            cols = slice(h * 128, (h + 1) * 128)
            wide = slice(qw + h * 128, qw + (h + 1) * 128)
            gkv_own[at, wide] = gv_near[shifted, cols] + gv_s[h, mine, :]
            gkv_send[at, wide] = (gv_s[h, sent, :] + last * gv_near[:WIN, cols]).astype(BF16)
        return 0

    lax.fori_loop(0, grid_q, back, 0)


def mix_backward(grad_q, grad_kv, rows, gain, bias, w_mix, slab, d_gain, d_bias, carried):
    grad_mixed = jnp.concatenate([grad_q * score_scale(grad_q.shape[1]), grad_kv], axis=1).astype(BF16)
    unit, scale = norm_parts(rows)
    normed = (unit * gain[0:1] + bias[0:1]).astype(BF16)
    add_columns(slab, 0, t_dot(normed, grad_mixed))
    grad_normed = dot_t(grad_mixed, w_mix[...])
    d_gain[...] += col_sum(grad_normed * unit)
    d_bias[...] += col_sum(grad_normed)
    return carried + norm_back(grad_normed, unit, scale, gain[0:1])


def fourth_kernel(
    info, gq, gkv, got, z, gmid, gain_next, bias_next, w_mix_next,
    q, kv, halo, o, lse, active, slope, mid, gain, bias, w_proj, w_in, w_back,
    gz_out, gq_out, gk_out, gv_out, gmid_out, halo_out, keep, send, dn_gain, dn_bias, d_gain, d_bias,
    ext, slab,
):
    step = pl.program_id(0)
    qw = q.shape[1]
    n = kv.shape[0]

    @pl.when(step == 0)
    def _():
        load_extended(halo, kv, ext)
        for ref in (gk_out, gv_out, slab, dn_gain, dn_bias, d_gain, d_bias):
            ref[...] = jnp.zeros_like(ref)

    limit = info[1]
    start = pl.multiple_of(step * TB, TB)
    base = info[0] * n + start
    grad_kv = gkv[...] + got[...].astype(F32)
    grad_z = mix_backward(
        gq[...], grad_kv, z[...].astype(F32), gain_next, bias_next, w_mix_next, slab, dn_gain, dn_bias, gmid[...]
    )
    grad_low = grad_z.astype(BF16)
    gz_out[...] = grad_low
    unit, scale = norm_parts(mid[...])
    normed = (unit * gain[1:2] + bias[1:2]).astype(BF16)
    attended = o[...]
    grad_out, grad_mid = feed_backward(
        grad_low.astype(F32), active[...], slope[...].astype(F32), normed, unit, scale, attended, gain,
        w_proj, w_in, w_back, slab, w_mix_next.size // w_proj.shape[1], d_gain, d_bias,
    )
    gmid_out[...] = grad_mid
    weighted = grad_out.astype(F32) * attended.astype(F32)
    for sub in range(TB // WIN):
        rows = slice(sub * WIN, (sub + 1) * WIN)
        near = pl.ds(pl.multiple_of(start + sub * WIN, WIN), 2 * WIN)
        delta = jnp.concatenate(
            [jnp.sum(weighted[rows, h * 128 : (h + 1) * 128], axis=-1, keepdims=True) for h in range(HEADS)], axis=0
        )
        g_q, g_k, g_v = near_backward(
            q[rows], ext[near, :qw], ext[near, qw:], grad_out[rows], stack_stat(lse[rows]), delta,
            base + sub * WIN, limit,
        )
        gq_out[rows] = g_q
        gk_out[near] += g_k
        gv_out[near] += g_v

    @pl.when(step == pl.num_programs(0) - 1)
    def _():
        halo_out[...] = jnp.concatenate([gk_out[:WIN], gv_out[:WIN]], axis=1).astype(BF16)
        split_slab(info, slab, keep, send)


def fifth_kernel(
    info, gq, gk, gv, got, x, gmid, gz, gain, bias, w_mix, *refs,
):
    vectors, squares = refs[:6], refs[6:8]
    cross0, cross1, local0, local1, keep, send, small, slab, d_gain, d_bias = refs[8:]
    step = pl.program_id(0)

    @pl.when(step == 0)
    def _():
        for ref in (slab, d_gain, d_bias):
            ref[...] = jnp.zeros_like(ref)

    at = pl.ds(pl.multiple_of(step * TB + WIN, WIN), TB)
    last = jnp.where(step == pl.num_programs(0) - 1, 1.0, 0.0)
    tail = got[...].astype(F32) * last
    extra = jnp.concatenate([jnp.zeros((TB - WIN, got.shape[1]), F32), tail], axis=0)
    grad_kv = jnp.concatenate([gk[at], gv[at]], axis=1) + extra
    grad_x = mix_backward(
        gq[...], grad_kv, x[...].astype(F32), gain, bias, w_mix, slab, d_gain, d_bias, gmid[...]
    )
    emit_messages(info, step, (cross0, cross1), (local0, local1), grad_x.astype(BF16), gz[...])

    @pl.when(step == pl.num_programs(0) - 1)
    def _():
        split_slab(info, slab, keep, send)
        small_rows(info, (d_gain,) + vectors[:3] + (d_bias,) + vectors[3:], squares, small)
        half = keep.shape[0]
        count = small.shape[0]
        coarse = small[...].astype(BF16)
        send[half : half + count] = coarse
        send[half + count :] = (small[...] - coarse.astype(F32)).astype(BF16)


def assemble_kernel(info, *refs):
    own, other, out, wide, sems = refs[:4], *refs[4:]
    core = info[0]
    rows = out.shape[1]

    def leave(t):
        column = core if t < 4 else 1 - core
        image = (info[5] ^ (t % 4 // 2)) * 4 + column * 2 + (info[4] ^ (t % 2))
        return pltpu.make_async_copy(wide.at[t], out.at[image], sems.at[t])

    for t in range(8):
        if t < 4:
            block = own[t][pl.ds(pl.multiple_of(core * rows, rows), rows)]
        else:
            block = other[t - 4]
        wide[t] = block.astype(F32)
        leave(t).start()
    for t in range(8):
        leave(t).wait()


def small_rows(info, vectors, squares, out):
    width = out.shape[1]
    once = jnp.where(info[7] == 0, 1.0, 0.0)
    lane = lax.broadcasted_iota(jnp.int32, (1, width), 1)
    out[...] = jnp.zeros_like(out)
    for i, vector in enumerate(vectors):
        out[i : i + 1] = jnp.sum(vector[...], axis=0, keepdims=True) * once
    for i in range(6):
        total = jnp.sum(jnp.sum(squares[i // 3][i % 3], axis=0, keepdims=True), axis=1, keepdims=True)
        out[8 + i : 9 + i] = jnp.where(lane == info[6], total * once, 0.0)


def trade_kernel(info, *refs):
    pieces, out = refs[:4], refs[4]
    rows = out.shape[1]
    for t in range(4):
        out[t] = pieces[t][pl.ds(pl.multiple_of((1 - info[0]) * rows, rows), rows)]


def unpack_kernel(info, mine, theirs, small, mix, proj, up, down, gain, bias, wide, *, sizes):
    core = info[0]
    wide[core] = mine[...].astype(F32)
    wide[1 - core] = theirs[...].astype(F32)
    rows_a, rows_b, rows_c, ways = sizes
    early = (rows_a + rows_b) // 2 // ways
    late = rows_c // 2 // ways
    rows_mix = rows_c

    def pieces(slab, start, stop):
        total = {"a": rows_a, "b": rows_b, "c": rows_c}[slab] // 2
        size, shift, skip = (late, early, 0) if slab == "c" else (early, 0, rows_a // 2 if slab == "b" else 0)
        at = start
        while at < stop:
            half, row = at // total, at % total
            along = row + skip
            count = min(stop - at, total - row, size - along % size)
            yield at - start, half, along // size * (early + late) + shift + along % size, count
            at += count

    width = wide.shape[2]
    places = {0: (("c", 0), ("b", rows_mix)), 1: (("b", 0), ("a", 0))}
    for layer in range(2):
        (slab, at), (feed, feed_at) = places[layer]
        for out, name in ((mix, slab), (proj, feed), (up, feed), (down, feed)):
            if name == feed and out is not mix:
                at = feed_at
            rows, cols = out.shape[1:]
            for i in range(cols // width):
                for offset, half, row, count in pieces(name, at + i * rows, at + (i + 1) * rows):
                    out[layer, offset : offset + count, i * width : (i + 1) * width] = wide[half, row : row + count]
            if out is not mix:
                feed_at = at + rows * cols // width
    for layer in range(2):
        for norm in range(2):
            gain[layer, norm : norm + 1] = small[2 * layer + norm : 2 * layer + norm + 1]
            bias[layer, norm : norm + 1] = small[4 + 2 * layer + norm : 5 + 2 * layer + norm]


VMEM = pl.BlockSpec(memory_space=pltpu.VMEM)


def call(kernel, info, operands, specs, outs, out_specs, scratch=(), grid=(), work=0):
    moved = sum(math.prod(a.shape) * a.dtype.itemsize for a in list(operands) + jax.tree.leaves(outs))
    single = not isinstance(outs, list)
    views = list(specs) + ([out_specs] if single else list(out_specs))

    def body_of(info, *refs):
        seen = [view(ref) if callable(view) else ref for view, ref in zip(views, refs)]
        kernel(info, *seen, *refs[len(views) :])

    def plain(view):
        return VMEM if callable(view) else view

    return pl.pallas_call(
        body_of,
        grid_spec=pltpu.PrefetchScalarGridSpec(
            num_scalar_prefetch=1,
            grid=grid,
            in_specs=[plain(v) for v in specs],
            out_specs=plain(out_specs) if single else [plain(v) for v in out_specs],
            scratch_shapes=list(scratch),
        ),
        out_shape=outs,
        compiler_params=pltpu.CompilerParams(vmem_limit_bytes=VMEM_LIMIT),
        cost_estimate=pl.CostEstimate(flops=int(work * 1.15e9), bytes_accessed=moved, transcendentals=0),
    )(info, *operands)


def whole(array):
    return VMEM


def tiled(array):
    return lambda ref: ref.at[pl.ds(pl.multiple_of(pl.program_id(0) * TB, TB), TB)]


def last_rows(ref):
    return ref.at[pl.ds(ref.shape[0] - WIN, WIN)]


ANY = pl.BlockSpec(memory_space=pl.ANY)


def shape(dims, kind):
    return jax.ShapeDtypeStruct(dims, kind)


def after(value, *others):
    return lax.optimization_barrier((value, others))[0]


def body(edge_rows, lengths, norm_gain, norm_bias, w_qkv, w_out, w_up, w_down):
    sections = lax.axis_size("section")
    index = lax.axis_index("section")
    images, rows_dev, width = edge_rows.shape
    seats = 2 * images
    rep = sections // seats
    seat = index // rep
    twin = index % rep
    rows_piece = rows_dev * rep
    qw = (w_qkv.shape[2] - width) // 2
    kvw = w_qkv.shape[2] - qw
    hidden = w_up.shape[2]
    n = rows_piece * images // 2
    quarter = images // 2
    steps = (n // TB,)

    def route(pairs):
        return [(s * rep + e, d * rep + e) for s, d in pairs for e in range(rep)]

    if rep > 1:
        groups = [[s * rep + e for e in range(rep)] for s in range(seats)]
        edge_rows = lax.all_gather(edge_rows, "section", axis_index_groups=groups, axis=1, tiled=True)

    chip = seat // 2
    part = seat % 2
    fz, fl, fy = chip // 4, (chip // 2) % 2, chip % 2
    limit = lengths[chip]
    spot = lax.axis_index("dp") * images + chip
    info = jnp.stack([part, limit, chip % quarter, fz, fy, fz, spot, twin, index % 2]).astype(jnp.int32)
    swap = route([(s, s ^ 1) for s in range(seats)])

    def bits(s):
        return s // 8, (s // 4) % 2, (s // 2) % 2, s % 2

    by_column = edge_rows.reshape(2, 2, 2, rows_piece, width)
    traded = lax.dynamic_index_in_dim(by_column, 1 - part, 1, keepdims=False).reshape(4, rows_piece, width)
    traded = lax.ppermute(traded, "section", swap)
    column = lax.dynamic_index_in_dim(by_column, part, 1, keepdims=False).reshape(4, rows_piece, width)
    received = [None] * 4
    for t in (2, 3, 0, 1):
        tz, ty = t // 2, t % 2
        image = (fz ^ tz) * 2 + (fy ^ ty)
        own = lax.dynamic_index_in_dim(column, image, 0, keepdims=False)
        got = lax.dynamic_index_in_dim(traded, image, 0, keepdims=False)
        message = jnp.where(part == 0, jnp.concatenate([own, got]), jnp.concatenate([got, own]))
        pairs = []
        for s in range(seats):
            z, l, y, k = bits(s)
            pairs.append((s, ((z ^ tz) * 4 + k * 2 + (y ^ ty)) * 2 + l))
        received[t] = lax.ppermute(message, "section", route(pairs))

    def send_back(message, tz, ty):
        pairs = []
        for s in range(seats):
            z, l, y, p = bits(s)
            pairs.append((s, ((z ^ tz) * 4 + p * 2 + (y ^ ty)) * 2 + l))
        return lax.ppermute(message, "section", route(pairs))

    def trade(got):
        out = shape((4, rows_piece, width), BF16)
        send = call(trade_kernel, info, got, [VMEM] * 4, out, whole(out))
        return lax.ppermute(send, "section", swap)

    first_to_second = route([(2 * c, 2 * c + 1) for c in range(images)])
    second_to_first = route([(2 * c + 1, 2 * c) for c in range(images)])

    dma = pltpu.SemaphoreType.DMA
    rows_q = shape((n, qw), BF16)
    rows_kv = shape((n, kvw), BF16)
    rows_low = shape((n, width), BF16)
    rows_wide = shape((n, width), F32)
    rows_stat = shape((n, 128), F32)
    rows_hidden = shape((n, hidden), BF16)
    grad_k_shape = shape((n + WIN, qw), F32)
    grad_v_shape = shape((n + WIN, width), F32)
    mix_rows = w_qkv.shape[1] * w_qkv.shape[2] // width
    feed_rows = (w_out[0].size + w_up[0].size + w_down[0].size) // width
    vec_shape = shape((8, width), F32)
    squares_shape = shape((3, 8, width), F32)
    ext = pltpu.VMEM((n + WIN, kvw), BF16)

    g0, g1, b0, b1 = norm_gain[0], norm_gain[1], norm_bias[0], norm_bias[1]

    halo_shape = shape((WIN, kvw), BF16)
    outs = [rows_low, rows_q, rows_kv, halo_shape]
    x, q0, kv0, halo0 = call(
        first_kernel, info, received + [g0, b0, w_qkv[0]], [ANY] * 4 + [whole(g0), whole(b0), whole(w_qkv[0])],
        outs, [whole(o) for o in outs], [dma((2,))], work=6,
    )
    halo0 = lax.ppermute(halo0, "section", first_to_second)

    outs = [rows_low, rows_q, rows_kv, rows_low, rows_stat, rows_hidden, rows_hidden, rows_wide, squares_shape]
    z, q1, kv1, o0, lse0, active0, slope0, mid0, squares0 = call(
        second_kernel, info, [x, q0, kv0, halo0, g0, b0, w_out[0], w_up[0], w_down[0], g1, b1, w_qkv[1]],
        [tiled(x), tiled(q0)] + [whole(a) for a in (kv0, halo0, g0, b0, w_out[0], w_up[0], w_down[0], g1, b1, w_qkv[1])],
        outs, [tiled(o) for o in outs[:-1]] + [whole(outs[-1])], [ext], steps, work=15,
    )
    kv_other = lax.ppermute(kv1, "section", first_to_second)

    rows_k_all = shape((2 * n, qw), BF16)
    rows_v_all = shape((2 * n, width), BF16)
    outs = [rows_q, rows_k_all, rows_v_all, rows_wide, rows_stat]
    qr, kr, vr, o_far, lse_far = call(
        far_forward_kernel, info, [q1, kv1, kv_other], [whole(a) for a in (q1, kv1, kv_other)],
        outs, [whole(o) for o in outs],
        [pltpu.VMEM((n, qw), F32), pltpu.VMEM((2 * n, qw), F32), pltpu.VMEM((HEADS, 2 * n, 128), F32),
         pltpu.VMEM((HEADS, n, 128), F32), pltpu.VMEM((n, 128), F32)], work=14,
    )

    message = shape((2 * rows_piece, width), BF16)
    outs = [message] * 4 + [rows_low, rows_stat, shape((n, qw), F32), grad_k_shape, grad_v_shape, rows_wide,
            shape((feed_rows // 2, width), F32), shape((feed_rows // 2, width), BF16),
            vec_shape, vec_shape, squares_shape]
    (cross0, cross1, local0, local1, go1, stat1, gq_near, gk_near, gv_near, gmid1, keep_a, send_a,
     d_gain11, d_bias11, squares1) = call(
        third_kernel, info,
        received + [q1, kv1, kv_other, o_far, lse_far, z, g1, b1, w_out[1], w_up[1], w_down[1]],
        [ANY] * 4
        + [tiled(q1), whole(kv1), last_rows]
        + [tiled(o_far), tiled(lse_far), tiled(z)]
        + [whole(a) for a in (g1, b1, w_out[1], w_up[1], w_down[1])],
        outs,
        [whole(message)] * 4 + [tiled(o) for o in outs[4:7]] + [whole(outs[7]), whole(outs[8]), tiled(outs[9])]
        + [whole(o) for o in outs[10:]],
        [ext, pltpu.VMEM((n, width), BF16), pltpu.VMEM((feed_rows, width), F32), dma((2,))], steps, work=24,
    )
    forward_back = [None, None, send_back(cross0, 1, 0), None]

    outs = [shape((n, qw), F32), shape((n, kvw), F32), rows_kv]
    operands = [qr, kr, vr, go1, stat1, gq_near, gk_near, gv_near]
    gq1, gkv1, gkv_send = call(
        far_backward_kernel, info, operands, [whole(a) for a in operands], outs, [whole(o) for o in outs],
        [pltpu.VMEM((HEADS, n, 128), F32), pltpu.VMEM((n, 128), F32), pltpu.VMEM((n, qw), F32),
         pltpu.VMEM((2 * n, qw), F32), pltpu.VMEM((HEADS, 2 * n, 128), F32)], work=18,
    )
    gkv_got = lax.ppermute(after(gkv_send, forward_back[2]), "section", second_to_first)
    forward_back[3] = send_back(after(cross1, forward_back[2]), 1, 1)
    forward_back[0] = send_back(after(local0, forward_back[2]), 0, 0)
    forward_back[1] = send_back(after(local1, forward_back[2]), 0, 1)

    slab_rows = mix_rows + feed_rows
    outs = [rows_low, shape((n, qw), F32), grad_k_shape, grad_v_shape, rows_wide, halo_shape,
            shape((slab_rows // 2, width), F32), shape((slab_rows // 2, width), BF16),
            vec_shape, vec_shape, vec_shape, vec_shape]
    (gz, gq0, gk0, gv0, gmid0, halo_send, keep_b, send_b, d_gain10, d_bias10, d_gain01, d_bias01) = call(
        fourth_kernel, info,
        [gq1, gkv1, gkv_got, z, gmid1, g1, b1, w_qkv[1], q0, kv0, halo0, o0, lse0, active0, slope0, mid0, g0, b0,
         w_out[0], w_up[0], w_down[0]],
        [tiled(a) for a in (gq1, gkv1, gkv_got, z, gmid1)] + [whole(a) for a in (g1, b1, w_qkv[1])]
        + [tiled(q0), whole(kv0), whole(halo0)] + [tiled(a) for a in (o0, lse0, active0, slope0, mid0)]
        + [whole(a) for a in (g0, b0, w_out[0], w_up[0], w_down[0])],
        outs,
        [tiled(outs[0]), tiled(outs[1]), whole(outs[2]), whole(outs[3]), tiled(outs[4])] + [whole(o) for o in outs[5:]],
        [ext, pltpu.VMEM((slab_rows, width), F32)], steps, work=20,
    )
    halo_send, send_b = after((halo_send, send_b), *forward_back)
    halo_got = lax.ppermute(halo_send, "section", second_to_first)

    dp_count = lax.axis_size("dp")
    dp_index = lax.axis_index("dp")

    def partners(masks):
        total = dp_count * sections
        spot = dp_index * sections + index
        digit = sum(((spot // m) % 2) << i for i, m in enumerate(masks))
        routes = []
        for c in range(1, 1 << len(masks)):
            flips = sum(m for i, m in enumerate(masks) if (c >> i) & 1)
            routes.append((c, [(s, s ^ flips) for s in range(total)]))
        return digit, routes

    def chunk(slabs, which, ways):
        return jnp.concatenate(
            [lax.dynamic_slice_in_dim(s, which * (s.shape[0] // ways), s.shape[0] // ways, 0) for s in slabs]
        )

    def scatter(slabs, masks, vectors=None):
        digit, routes = partners(masks)
        ways = 1 << len(masks)
        kept = chunk(slabs, digit, ways)
        count = kept.shape[0]
        riders = []
        if vectors is not None:
            coarse = vectors.astype(BF16)
            riders = [coarse, (vectors - coarse.astype(F32)).astype(BF16)]
        got = [
            lax.ppermute(jnp.concatenate([chunk(slabs, digit ^ c, ways).astype(BF16)] + riders), ("dp", "section"), way)
            for c, way in routes
        ]
        for g in got:
            kept = kept + g[:count].astype(F32)
            if vectors is not None:
                rest = g[count:].astype(F32)
                vectors = vectors + (rest[: vectors.shape[0]] + rest[vectors.shape[0] :])
        return kept if vectors is None else (kept, vectors)

    def gather(piece, masks):
        digit, routes = partners(masks)
        pieces = [piece] + [lax.ppermute(piece, ("dp", "section"), way) for _, way in routes]
        stacked = jnp.stack(pieces)
        return jnp.concatenate(
            [lax.dynamic_index_in_dim(stacked, digit ^ j, 0, keepdims=False) for j in range(len(pieces))]
        )

    def pair(message):
        return lax.ppermute(message, ("dp", "section"), partners([1])[1][0][1])

    def riders_of(vectors):
        coarse = vectors.astype(BF16)
        return [coarse, (vectors - coarse.astype(F32)).astype(BF16)]

    def ridden(rest):
        rest = rest.astype(F32)
        return rest[: rest.shape[0] // 2] + rest[rest.shape[0] // 2 :]

    def exchange(rows, masks, vectors):
        rows = rows.astype(BF16)
        count = rows.shape[0]
        riders = riders_of(vectors)
        got = lax.ppermute(jnp.concatenate([rows] + riders), ("dp", "section"), partners(masks)[1][0][1])
        rows = (rows.astype(F32) + got[:count].astype(F32)).astype(BF16)
        return rows, ridden(jnp.concatenate(riders)) + ridden(got[count:])

    dp_masks = [sections << b for b in range(dp_count.bit_length() - 1)]
    section_masks = [1 << b for b in range(1, sections.bit_length() - 1)]
    plane = [dp_masks[0], section_masks[0]]
    rest = section_masks[1:] + dp_masks[1:]
    got_early = pair(jnp.concatenate([send_a, send_b]))
    early = jnp.concatenate([keep_a, keep_b]) + got_early.astype(F32)
    gq0 = after(gq0, early)
    early = scatter([early], plane)

    small_shape = shape((16, width), F32)
    outs = [message] * 4 + [shape((mix_rows // 2, width), F32),
            shape((mix_rows // 2 + 2 * small_shape.shape[0], width), BF16), small_shape]
    operands = [gq0, gk0, gv0, halo_got, x, gmid0, gz, g0, b0, w_qkv[0]]
    partial = [d_gain01, d_gain10, d_gain11, d_bias01, d_bias10, d_bias11, squares0, squares1]
    cross0, cross1, local0, local1, late, send_c, small = call(
        fifth_kernel, info, operands + partial,
        [tiled(gq0), whole(gk0), whole(gv0), whole(halo_got), tiled(x), tiled(gmid0), tiled(gz)]
        + [whole(a) for a in operands[7:] + partial],
        outs, [whole(o) for o in outs],
        [pltpu.VMEM((mix_rows, width), F32), pltpu.VMEM((8, width), F32), pltpu.VMEM((8, width), F32)], steps, work=8,
    )

    def assemble(own, other):
        out = call(
            assemble_kernel, info, own + [other], [VMEM] * 5, shape((images, rows_piece, width), F32), ANY,
            [pltpu.VMEM((images, rows_piece, width), F32), dma((images,))],
        )
        if rep > 1:
            out = lax.dynamic_slice_in_dim(out, twin * rows_dev, rows_dev, 1)
        return out

    backward_back = [send_back(local0, 0, 0), None, send_back(cross0, 1, 0), None]
    got_late = pair(after(send_c, early))
    late_rows = late.shape[0]
    late = late + got_late[:late_rows].astype(F32)
    small = small + ridden(got_late[late_rows:])
    late, small = scatter([late], plane, small)
    early_rows = early.shape[0]
    forward_trade = trade(after(forward_back, late))
    forward_rows = assemble(forward_back, forward_trade)
    both = after(jnp.concatenate([early, late]), backward_back[0], backward_back[2])
    backward_back[3] = send_back(after(cross1, backward_back[2]), 1, 1)
    backward_back[1] = send_back(after(local1, backward_back[2]), 0, 1)
    for mask in rest[:-1]:
        both, small = scatter([both], [mask], small)
    both = after(both, forward_rows)
    both, small = exchange(both, rest[-1:], small)
    for mask in rest[-2::-1]:
        both = gather(both, [mask])
    both = after(both, backward_back[1], backward_back[3])
    both = gather(both, plane)
    backward_trade = trade(backward_back)
    both = after(both, backward_trade)
    theirs = pair(both)
    backward_rows = assemble(backward_back, backward_trade)
    sums = lax.dynamic_slice_in_dim(small[8:14], dp_index * images, images, 1)
    rms_values = jnp.sqrt(sums / (lengths.astype(F32)[None, :] * width))
    outs = [shape(w.shape, F32) for w in (w_qkv, w_out, w_up, w_down, norm_gain, norm_bias)]
    sizes = (feed_rows, slab_rows, mix_rows, 1 << len(plane))
    grads = call(
        functools.partial(unpack_kernel, sizes=sizes), jnp.stack([index % 2]).astype(jnp.int32), [both, theirs, small],
        [whole(both), whole(theirs), whole(small)], outs, [whole(o) for o in outs],
        [pltpu.VMEM((2,) + both.shape, F32)],
    )
    return (forward_rows, backward_rows, rms_values, grads[4], grads[5]) + tuple(grads[:4])


def solution(mesh):
    placed = (P("dp", "section", None), P("dp"), P(), P(), P(), P(), P(), P())
    return jax.shard_map(
        body,
        mesh=mesh,
        in_specs=placed,
        out_specs=(P("dp", "section", None), P("dp", "section", None), P(None, "dp"), P(), P(), P(), P(), P(), P()),
        check_vma=False,
    )
```

```python
import functools
import math

import jax
import jax.numpy as jnp
from jax import lax
from jax.experimental import pallas as pl
from jax.experimental.pallas import tpu as pltpu
from jax.sharding import PartitionSpec as P

HEADS = 2
WIN = 128
STRIDE = 128
NEG = -1e30
F32 = jnp.float32
BF16 = jnp.bfloat16
TB = 512
RES = 8
UNROLL = 16
VMEM_LIMIT = 16 * 1024 * 1024


def dot(left, right):
    return lax.dot_general(left, right, (((1,), (0,)), ((), ())), preferred_element_type=F32)


def dot_t(left, right):
    return lax.dot_general(left, right, (((1,), (1,)), ((), ())), preferred_element_type=F32)


def t_dot(left, right):
    return lax.dot_general(left, right, (((0,), (0,)), ((), ())), preferred_element_type=F32)


def score_scale(query_width):
    return 1.0 / math.sqrt(query_width // HEADS)


def norm_parts(rows):
    centre = rows - jnp.mean(rows, axis=-1, keepdims=True)
    scale = lax.rsqrt(jnp.mean(centre * centre, axis=-1, keepdims=True) + 1e-05)
    return centre * scale, scale


def norm_back(grad, unit, scale, gain):
    scaled = grad * gain
    first = jnp.mean(scaled, axis=-1, keepdims=True)
    second = jnp.mean(scaled * unit, axis=-1, keepdims=True)
    return scale * (scaled - first - unit * second)


def col_sum(rows):
    return jnp.sum(rows.reshape(rows.shape[0] // 8, 8, rows.shape[1]), axis=0)


def gelu_pair(hidden):
    c0 = math.sqrt(2.0 / math.pi)
    square = hidden * hidden
    share = 0.5 + 0.5 * jnp.tanh(hidden * (c0 + (c0 * 0.044715) * square))
    active = hidden * share
    slope = share + active * (1.0 - share) * (2.0 * c0 + (6.0 * c0 * 0.044715) * square)
    return active, slope


def head_split(rows):
    lane = lax.broadcasted_iota(jnp.int32, rows.shape, 1)
    zero = jnp.zeros_like(rows)
    low = lane < rows.shape[1] // HEADS
    return jnp.concatenate([jnp.where(low, rows, zero), jnp.where(low, zero, rows)], axis=0)


def head_join(stacked):
    half = stacked.shape[0] // 2
    lane = lax.broadcasted_iota(jnp.int32, (half, stacked.shape[1]), 1)
    return jnp.where(lane < stacked.shape[1] // HEADS, stacked[:half], stacked[half:])


def near_masks(base, limit):
    row = lax.broadcasted_iota(jnp.int32, (2 * WIN, WIN), 0)
    row = jnp.where(row >= WIN, row - WIN, row)
    col = lax.broadcasted_iota(jnp.int32, (2 * WIN, WIN), 1)
    own = col <= row
    key = base + col - jnp.where(own, 0, WIN)
    allowed = (key >= 0) & ((key < limit) | (col == row))
    return own, allowed


def near_scores(split_q, keys, own, allowed):
    scores = dot_t(split_q, keys)
    folded = jnp.where(own, scores[:, WIN:], scores[:, :WIN])
    return jnp.where(allowed, folded, NEG)


def unfold(folded, own):
    return jnp.concatenate([jnp.where(own, 0.0, folded), jnp.where(own, folded, 0.0)], axis=1).astype(BF16)


def near_forward(queries, keys, values, base, limit):
    own, allowed = near_masks(base, limit)
    scores = near_scores(head_split(queries), keys, own, allowed)
    largest = jnp.max(scores, axis=-1, keepdims=True)
    powers = jnp.exp(scores - largest)
    total = jnp.sum(powers, axis=-1, keepdims=True)
    weights = unfold(powers, own)
    hd = values.shape[1] // HEADS
    out = [dot(weights[h * WIN : (h + 1) * WIN], values[:, h * hd : (h + 1) * hd]) for h in range(HEADS)]
    return out, largest, total


def near_backward(queries, keys, values, grad_out, log_total, delta, base, limit):
    own, allowed = near_masks(base, limit)
    split_q = head_split(queries)
    weights = jnp.exp(near_scores(split_q, keys, own, allowed) - log_total)
    hd = values.shape[1] // HEADS
    pull = jnp.concatenate(
        [dot_t(grad_out[:, h * hd : (h + 1) * hd], values[:, h * hd : (h + 1) * hd]) for h in range(HEADS)], axis=0
    )
    pull = jnp.where(own, pull[:, WIN:], pull[:, :WIN])
    slope = unfold(weights * (pull - delta), own)
    weights = unfold(weights, own)
    grad_q = head_join(dot(slope, keys))
    grad_k = t_dot(slope, split_q)
    grad_v = jnp.concatenate(
        [t_dot(weights[h * WIN : (h + 1) * WIN], grad_out[:, h * hd : (h + 1) * hd]) for h in range(HEADS)], axis=1
    )
    return grad_q, grad_k, grad_v


def stack_stat(stat, width=128):
    return jnp.concatenate([stat[:, 0:1], stat[:, width // 2 : width // 2 + 1]], axis=0)


def spread_stat(stacked, width=128):
    half = stacked.shape[0] // 2
    lane = lax.broadcasted_iota(jnp.int32, (half, width), 1)
    return jnp.where(lane < width // 2, stacked[:half], stacked[half:])


def masked_squares(rows, base, limit):
    pos = base + lax.broadcasted_iota(jnp.int32, (rows.shape[0], 1), 0)
    return col_sum(jnp.where(pos < limit, rows * rows, 0.0))


def gather_pieces(info, pieces, target, sems, low):
    rows = pieces[0].shape[0]

    def each(act):
        for ty in range(2):
            place = target.at[pl.ds((ty ^ info[4]) * rows, rows)]

            @pl.when(info[5] == (0 if low else 1))
            def _():
                act(pltpu.make_async_copy(pieces[ty], place, sems.at[ty]))

            @pl.when(info[5] == (1 if low else 0))
            def _():
                act(pltpu.make_async_copy(pieces[2 + ty], place, sems.at[ty]))

    each(lambda c: c.start())
    each(lambda c: c.wait())


def emit_rows(info, first, rows, to_lower, cross, local):
    units = cross[0].shape[0] // WIN
    stays = info[5] == (0 if to_lower else 1)
    for sub in range(rows.shape[0] // WIN):
        number = first + sub
        block = number // units
        at = pl.ds(pl.multiple_of((number - block * units) * WIN, WIN), WIN)
        value = rows[sub * WIN : (sub + 1) * WIN]
        for ty in range(2):
            fits = (number >= 0) & ((block ^ info[4]) == ty)

            @pl.when(fits & stays)
            def _():
                local[ty][at] = value

            @pl.when(fits & jnp.logical_not(stays))
            def _():
                cross[ty][at] = value


def split_slab(info, slab, keep, send):
    once = jnp.where(info[7] == 0, 1.0, 0.0)
    half = keep.shape[0]
    mine = info[8]
    keep[...] = slab[pl.ds(pl.multiple_of(mine * half, 8), half)] * once
    send[:half] = (slab[pl.ds(pl.multiple_of((1 - mine) * half, 8), half)] * once).astype(BF16)


def first_kernel(info, *refs):
    pieces = refs[:4]
    gain, bias, w_mix, x_out, q_out, kv_out, halo_out, sems = refs[4:]
    gather_pieces(info, pieces, x_out.at[pl.ds(WIN, x_out.shape[0] - WIN)], sems, True)
    x_out[:WIN] = jnp.zeros((WIN, x_out.shape[1]), BF16)
    qw = q_out.shape[1]

    def block(i, _):
        at = pl.ds(pl.multiple_of(i * TB, TB), TB)
        unit, _ = norm_parts(x_out[pl.ds(pl.multiple_of(i * TB + WIN, WIN), TB)].astype(F32))
        normed = (unit * gain[0:1] + bias[0:1]).astype(BF16)
        mixed = dot(normed, w_mix[...])
        q_out[at] = (mixed[:, :qw] * score_scale(qw)).astype(BF16)
        kv_out[at] = mixed[:, qw:].astype(BF16)
        return 0

    lax.fori_loop(0, q_out.shape[0] // TB, block, 0)
    halo_out[...] = kv_out[kv_out.shape[0] - WIN :]


def load_extended(halo, kv, ext):
    ext[: halo.shape[0]] = halo[...]
    ext[halo.shape[0] :] = kv[...]


def second_kernel(
    info, x, q, kv, halo, gain, bias, w_proj, w_in, w_back, gain_next, bias_next, w_mix_next,
    z_out, q_next, kv_next, o_out, lse_out, active_out, slope_out, mid_out, squares, ext,
):
    step = pl.program_id(0)
    qw = q.shape[1]
    n = kv.shape[0]

    @pl.when(step == 0)
    def _():
        load_extended(halo, kv, ext)
        squares[...] = jnp.zeros_like(squares)

    limit = info[1]
    start = step * TB
    base = info[0] * n + start
    outs = []
    for sub in range(TB // WIN):
        near = pl.ds(pl.multiple_of(start + sub * WIN, WIN), 2 * WIN)
        keys = ext[near, :qw]
        values = ext[near, qw:]
        queries = q[sub * WIN : (sub + 1) * WIN]
        out, largest, total = near_forward(queries, keys, values, base + sub * WIN, limit)
        inverse = 1.0 / total
        lse_out[sub * WIN : (sub + 1) * WIN] = spread_stat(largest + jnp.log(total))
        outs.append(jnp.concatenate([out[0] * inverse[:WIN], out[1] * inverse[WIN:]], axis=1))
    attended = jnp.concatenate(outs, axis=0).astype(BF16)
    o_out[...] = attended
    stream = x[...].astype(F32)
    branch = dot(attended, w_proj[...])
    middle = stream + branch
    mid_out[...] = middle
    unit, _ = norm_parts(middle)
    normed = (unit * gain[1:2] + bias[1:2]).astype(BF16)
    active, slope = gelu_pair(dot(normed, w_in[...]))
    active = active.astype(BF16)
    active_out[...] = active
    slope_out[...] = slope.astype(BF16)
    feed = dot(active, w_back[...])
    z = (middle + feed).astype(BF16)
    z_out[...] = z
    squares[0] += masked_squares(stream, base, limit)
    squares[1] += masked_squares(branch, base, limit)
    squares[2] += masked_squares(feed, base, limit)
    unit, _ = norm_parts(z.astype(F32))
    normed = (unit * gain_next[0:1] + bias_next[0:1]).astype(BF16)
    mixed = dot(normed, w_mix_next[...])
    q_next[...] = (mixed[:, :qw] * score_scale(qw)).astype(BF16)
    kv_next[...] = mixed[:, qw:].astype(BF16)


def far_mask(grid_q, grid_k, part_grid):
    shape = (HEADS * RES * grid_q, RES * grid_k)
    row = lax.broadcasted_iota(jnp.int32, shape, 0)
    col = lax.broadcasted_iota(jnp.int32, shape, 1)
    row = jnp.where(row >= RES * grid_q, row - RES * grid_q, row)
    row_res = jnp.zeros(shape, jnp.int32)
    col_res = jnp.zeros(shape, jnp.int32)
    for r in range(1, RES):
        row_res += (row >= r * grid_q).astype(jnp.int32)
        col_res += (col >= r * grid_k).astype(jnp.int32)
    row_grid = row - row_res * grid_q + part_grid
    col_grid = col - col_res * grid_k
    allowed = (row_res == col_res) & (col_grid < row_grid)
    return allowed, col_grid * STRIDE + col_res


def far_forward_kernel(info, q, kv, other, qr, kr, vr, o_far, lse_far, q_s, k_s, v_s, o_s, lse_s):
    n, qw = q.shape
    grid_q = n // STRIDE
    grid_k = 2 * grid_q
    part = info[0]
    limit = info[1]

    def place(g, _):
        at = pl.ds(pl.multiple_of(g * STRIDE, STRIDE), STRIDE)
        own = kv[at].astype(F32)
        early = jnp.where(part == 0, own, other[at].astype(F32))
        q_s[pl.ds(g, STRIDE, stride=grid_q), :] = q[at].astype(F32)
        k_s[pl.ds(g, STRIDE, stride=grid_k), :] = early[:, :qw]
        k_s[pl.ds(g + grid_q, STRIDE, stride=grid_k), :] = own[:, :qw]
        hd = v_s.shape[1]
        for h in range(HEADS):
            v_s[h, pl.ds(g, STRIDE, stride=grid_k), :] = early[:, qw + h * 128 : qw + (h + 1) * 128]
            v_s[h, pl.ds(g + grid_q, STRIDE, stride=grid_k), :] = own[:, qw + h * 128 : qw + (h + 1) * 128]
        return 0

    lax.fori_loop(0, grid_q, place, 0)
    base_mask, key_pos = far_mask(grid_q, grid_k, part * grid_q)
    rows_q = RES * grid_q
    rows_k = RES * grid_k

    def one(i):
        at_q = pl.ds(pl.multiple_of(i * rows_q, rows_q), rows_q)
        at_k = pl.ds(pl.multiple_of(i * rows_k, rows_k), rows_k)
        queries = q_s[at_q].astype(BF16)
        keys = k_s[at_k].astype(BF16)
        values = [v_s[h, at_k].astype(BF16) for h in range(HEADS)]
        qr[at_q] = queries
        kr[at_k] = keys
        for h in range(HEADS):
            vr[at_k, h * 128 : (h + 1) * 128] = values[h]
        allowed = base_mask & (key_pos + i * RES < limit)
        scores = jnp.where(allowed, dot_t(head_split(queries), keys), NEG)
        largest = jnp.max(scores, axis=-1, keepdims=True)
        powers = jnp.where(allowed, jnp.exp(scores - largest), 0.0)
        total = jnp.sum(powers, axis=-1, keepdims=True)
        safe = jnp.maximum(total, 1e-30)
        weights = (powers * (1.0 / safe)).astype(BF16)
        lse = jnp.where(total > 0.0, largest + jnp.log(safe), NEG)
        lse_s[at_q] = spread_stat(lse)
        for h in range(HEADS):
            o_s[h, at_q] = dot(weights[h * rows_q : (h + 1) * rows_q], values[h])

    def group(i, _):
        for u in range(UNROLL):
            one(i * UNROLL + u)
        return 0

    lax.fori_loop(0, STRIDE // RES // UNROLL, group, 0)

    def back(g, _):
        at = pl.ds(pl.multiple_of(g * STRIDE, STRIDE), STRIDE)
        pick = pl.ds(g, STRIDE, stride=grid_q)
        lse_far[at] = lse_s[pick, :]
        for h in range(HEADS):
            o_far[at, h * 128 : (h + 1) * 128] = o_s[h, pick, :]
        return 0

    lax.fori_loop(0, grid_q, back, 0)


def third_kernel(
    info, *refs,
):
    pieces = refs[:4]
    (q, kv, halo, o_far, lse_far, z, gain, bias, w_proj, w_in, w_back,
     cross0, cross1, local0, local1, go_out, stat_out, gq_out, gk_out, gv_out, gmid_out, keep, send,
     d_gain, d_bias, squares, ext, cot, slab, sems) = refs[4:]
    step = pl.program_id(0)
    qw = q.shape[1]
    n = kv.shape[0]

    @pl.when(step == 0)
    def _():
        gather_pieces(info, pieces, cot, sems, False)
        load_extended(halo, kv, ext)
        for ref in (squares, gk_out, gv_out, slab, d_gain, d_bias):
            ref[...] = jnp.zeros_like(ref)

    limit = info[1]
    start = pl.multiple_of(step * TB, TB)
    base = info[0] * n + start
    outs = []
    logs = []
    for sub in range(TB // WIN):
        rows = slice(sub * WIN, (sub + 1) * WIN)
        near = pl.ds(pl.multiple_of(start + sub * WIN, WIN), 2 * WIN)
        out, largest, total = near_forward(q[rows], ext[near, :qw], ext[near, qw:], base + sub * WIN, limit)
        far_log = stack_stat(lse_far[rows])
        top = jnp.maximum(largest, far_log)
        near_share = jnp.exp(largest - top)
        far_share = jnp.exp(far_log - top)
        whole = total * near_share + far_share
        inverse = 1.0 / whole
        near_share = near_share * inverse
        far_share = far_share * inverse
        logs.append(top + jnp.log(whole))
        far = o_far[rows]
        outs.append(
            jnp.concatenate(
                [
                    out[h] * near_share[h * WIN : (h + 1) * WIN]
                    + far[:, h * 128 : (h + 1) * 128] * far_share[h * WIN : (h + 1) * WIN]
                    for h in range(HEADS)
                ],
                axis=1,
            )
        )
    attended_wide = jnp.concatenate(outs, axis=0)
    attended = attended_wide.astype(BF16)
    stream = z[...].astype(F32)
    branch = dot(attended, w_proj[...])
    middle = stream + branch
    unit, scale = norm_parts(middle)
    normed = (unit * gain[1:2] + bias[1:2]).astype(BF16)
    active, slope = gelu_pair(dot(normed, w_in[...]))
    active = active.astype(BF16)
    feed = dot(active, w_back[...])
    number = step * (TB // WIN)
    emit_rows(info, number, z[...], True, (cross0, cross1), (local0, local1))
    emit_rows(info, number, (middle + feed).astype(BF16), False, (cross0, cross1), (local0, local1))
    squares[0] += masked_squares(stream, base, limit)
    squares[1] += masked_squares(branch, base, limit)
    squares[2] += masked_squares(feed, base, limit)

    pos = base + lax.broadcasted_iota(jnp.int32, (TB, 1), 0)
    upstream = jnp.where(pos < limit, cot[pl.ds(start, TB)].astype(F32), 0.0)
    grad_out, grad_mid = feed_backward(
        upstream, active, slope, normed, unit, scale, attended, gain, w_proj, w_in, w_back, slab, 0, d_gain, d_bias
    )
    gmid_out[...] = grad_mid
    go_out[...] = grad_out
    weighted = grad_out.astype(F32) * attended_wide
    for sub in range(TB // WIN):
        rows = slice(sub * WIN, (sub + 1) * WIN)
        near = pl.ds(pl.multiple_of(start + sub * WIN, WIN), 2 * WIN)
        delta = jnp.concatenate(
            [jnp.sum(weighted[rows, h * 128 : (h + 1) * 128], axis=-1, keepdims=True) for h in range(HEADS)], axis=0
        )
        stat_out[rows] = pack_stats(logs[sub], delta)
        gq, gk, gv = near_backward(
            q[rows], ext[near, :qw], ext[near, qw:], grad_out[rows], logs[sub], delta, base + sub * WIN, limit
        )
        gq_out[rows] = gq
        gk_out[near] += gk
        gv_out[near] += gv

    @pl.when(step == pl.num_programs(0) - 1)
    def _():
        split_slab(info, slab, keep, send)


def pack_stats(lse, delta):
    half = lse.shape[0] // 2
    lane = lax.broadcasted_iota(jnp.int32, (half, 128), 1)
    low = jnp.where(lane < 32, lse[:half], lse[half:])
    high = jnp.where(lane < 96, delta[:half], delta[half:])
    return jnp.where(lane < 64, low, high)


def add_columns(slab, at, grad):
    rows, cols = grad.shape
    width = slab.shape[1]
    for i in range(cols // width):
        slab[at + i * rows : at + (i + 1) * rows] += grad[:, i * width : (i + 1) * width]


def feed_backward(
    upstream, active, slope, normed, unit, scale, attended, gain, w_proj, w_in, w_back, slab, at, d_gain, d_bias,
):
    low = upstream.astype(BF16)
    width = low.shape[1]
    hidden = active.shape[1]
    slab[at + width + hidden : at + width + 2 * hidden] += t_dot(active, low)
    grad_hidden = (dot_t(low, w_back[...]) * slope).astype(BF16)
    add_columns(slab, at + width, t_dot(normed, grad_hidden))
    grad_normed = dot_t(grad_hidden, w_in[...])
    d_gain[...] += col_sum(grad_normed * unit)
    d_bias[...] += col_sum(grad_normed)
    grad_mid = upstream + norm_back(grad_normed, unit, scale, gain[1:2])
    branch_low = grad_mid.astype(BF16)
    slab[at : at + width] += t_dot(attended, branch_low)
    grad_out = dot_t(branch_low, w_proj[...]).astype(BF16)
    return grad_out, grad_mid


def far_backward_kernel(
    info, qr, kr, vr, go, stat, gq_near, gk_near, gv_near, gq_out, gkv_own, gkv_send,
    go_s, stat_s, gq_s, gk_s, gv_s,
):
    n, qw = gq_near.shape
    grid_q = n // STRIDE
    grid_k = 2 * grid_q
    part = info[0]
    limit = info[1]

    def place(g, _):
        at = pl.ds(pl.multiple_of(g * STRIDE, STRIDE), STRIDE)
        pick = pl.ds(g, STRIDE, stride=grid_q)
        rows = go[at].astype(F32)
        for h in range(HEADS):
            go_s[h, pick, :] = rows[:, h * 128 : (h + 1) * 128]
        stat_s[pick, :] = stat[at]
        return 0

    lax.fori_loop(0, grid_q, place, 0)
    base_mask, key_pos = far_mask(grid_q, grid_k, part * grid_q)
    rows_q = RES * grid_q
    rows_k = RES * grid_k

    def one(i):
        at_q = pl.ds(pl.multiple_of(i * rows_q, rows_q), rows_q)
        at_k = pl.ds(pl.multiple_of(i * rows_k, rows_k), rows_k)
        keys = kr[at_k]
        split_q = head_split(qr[at_q])
        grads = [go_s[h, at_q].astype(BF16) for h in range(HEADS)]
        stats = stat_s[at_q]
        lse = jnp.concatenate([stats[:, 0:1], stats[:, 32:33]], axis=0)
        delta = jnp.concatenate([stats[:, 64:65], stats[:, 96:97]], axis=0)
        allowed = base_mask & (key_pos + i * RES < limit)
        weights = jnp.exp(jnp.where(allowed, dot_t(split_q, keys), NEG) - lse)
        pull = jnp.concatenate([dot_t(grads[h], vr[at_k, h * 128 : (h + 1) * 128]) for h in range(HEADS)], axis=0)
        slope = (weights * (pull - delta)).astype(BF16)
        weights = weights.astype(BF16)
        gq_s[at_q] = head_join(dot(slope, keys))
        gk_s[at_k] = t_dot(slope, split_q)
        for h in range(HEADS):
            gv_s[h, at_k] = t_dot(weights[h * rows_q : (h + 1) * rows_q], grads[h])

    def group(i, _):
        for u in range(UNROLL):
            one(i * UNROLL + u)
        return 0

    lax.fori_loop(0, STRIDE // RES // UNROLL, group, 0)

    def back(g, _):
        at = pl.ds(pl.multiple_of(g * STRIDE, STRIDE), STRIDE)
        shifted = pl.ds(pl.multiple_of(g * STRIDE + WIN, STRIDE), STRIDE)
        gq_out[at] = gq_near[at] + gq_s[pl.ds(g, STRIDE, stride=grid_q), :]
        mine = pl.ds(g + part * grid_q, STRIDE, stride=grid_k)
        sent = pl.ds(g, STRIDE, stride=grid_k)
        last = jnp.where(g == grid_q - 1, 1.0, 0.0)
        gkv_own[at, :qw] = gk_near[shifted] + gk_s[mine, :]
        gkv_send[at, :qw] = (gk_s[sent, :] + last * gk_near[:WIN]).astype(BF16)
        for h in range(HEADS):
            cols = slice(h * 128, (h + 1) * 128)
            wide = slice(qw + h * 128, qw + (h + 1) * 128)
            gkv_own[at, wide] = gv_near[shifted, cols] + gv_s[h, mine, :]
            gkv_send[at, wide] = (gv_s[h, sent, :] + last * gv_near[:WIN, cols]).astype(BF16)
        return 0

    lax.fori_loop(0, grid_q, back, 0)


def mix_backward(grad_q, grad_kv, rows, gain, bias, w_mix, slab, d_gain, d_bias, carried):
    grad_mixed = jnp.concatenate([grad_q * score_scale(grad_q.shape[1]), grad_kv], axis=1).astype(BF16)
    unit, scale = norm_parts(rows)
    normed = (unit * gain[0:1] + bias[0:1]).astype(BF16)
    add_columns(slab, 0, t_dot(normed, grad_mixed))
    grad_normed = dot_t(grad_mixed, w_mix[...])
    d_gain[...] += col_sum(grad_normed * unit)
    d_bias[...] += col_sum(grad_normed)
    return carried + norm_back(grad_normed, unit, scale, gain[0:1])


def fourth_kernel(
    info, gq, gkv, got, z, gmid, gain_next, bias_next, w_mix_next,
    q, kv, halo, o, lse, active, slope, mid, x, gain, bias, w_mix, w_proj, w_in, w_back, keep_a, send_a,
    cross0, cross1, local0, local1, gq_last, gkv_last, gmid_last, halo_out, keep, send, slab_last,
    dn_gain, dn_bias, d_gain, d_bias, d_gain_first, d_bias_first,
    ext, slab, gq_ext, gk_ext, gv_ext, gmid_ext,
):
    step = pl.program_id(0)
    qw = q.shape[1]
    n = kv.shape[0]

    @pl.when(step == 0)
    def _():
        load_extended(halo, kv, ext)
        for ref in (
            slab, slab_last, dn_gain, dn_bias, d_gain, d_bias, d_gain_first, d_bias_first, gq_ext, gk_ext, gv_ext, gmid_ext
        ):
            ref[...] = jnp.zeros_like(ref)

    limit = info[1]
    start = pl.multiple_of(step * TB, TB)
    base = info[0] * n + start
    grad_kv = gkv[...] + got[...].astype(F32)
    grad_z = mix_backward(
        gq[...], grad_kv, z[...].astype(F32), gain_next, bias_next, w_mix_next, slab, dn_gain, dn_bias, gmid[...]
    )
    grad_low = grad_z.astype(BF16)
    emit_rows(info, step * (TB // WIN), grad_low, False, (cross0, cross1), (local0, local1))
    unit, scale = norm_parts(mid[...])
    normed = (unit * gain[1:2] + bias[1:2]).astype(BF16)
    attended = o[...]
    grad_out, grad_mid = feed_backward(
        grad_low.astype(F32), active[...], slope[...].astype(F32), normed, unit, scale, attended, gain,
        w_proj, w_in, w_back, slab, w_mix_next.size // w_proj.shape[1], d_gain, d_bias,
    )
    shifted = pl.ds(pl.multiple_of(start + WIN, WIN), TB)
    gmid_ext[shifted] = grad_mid
    weighted = grad_out.astype(F32) * attended.astype(F32)
    for sub in range(TB // WIN):
        rows = slice(sub * WIN, (sub + 1) * WIN)
        near = pl.ds(pl.multiple_of(start + sub * WIN, WIN), 2 * WIN)
        delta = jnp.concatenate(
            [jnp.sum(weighted[rows, h * 128 : (h + 1) * 128], axis=-1, keepdims=True) for h in range(HEADS)], axis=0
        )
        g_q, g_k, g_v = near_backward(
            q[rows], ext[near, :qw], ext[near, qw:], grad_out[rows], stack_stat(lse[rows]), delta,
            base + sub * WIN, limit,
        )
        gq_ext[pl.ds(pl.multiple_of(start + (sub + 1) * WIN, WIN), WIN)] = g_q
        gk_ext[near] += g_k
        gv_ext[near] += g_v

    @pl.when(step == 0)
    def _():
        halo_out[...] = jnp.concatenate([gk_ext[:WIN], gv_ext[:WIN]], axis=1).astype(BF16)
        gk_ext[:WIN] = jnp.zeros((WIN, gk_ext.shape[1]), F32)
        gv_ext[:WIN] = jnp.zeros((WIN, gv_ext.shape[1]), F32)

    whole_rows = pl.ds(start, TB)
    grad_x = mix_backward(
        gq_ext[whole_rows], jnp.concatenate([gk_ext[whole_rows], gv_ext[whole_rows]], axis=1),
        x[whole_rows].astype(F32), gain, bias, w_mix, slab_last, d_gain_first, d_bias_first, gmid_ext[whole_rows],
    )
    emit_rows(info, step * (TB // WIN) - 1, grad_x.astype(BF16), True, (cross0, cross1), (local0, local1))

    @pl.when(step == pl.num_programs(0) - 1)
    def _():
        gq_last[...] = gq_ext[n:]
        gkv_last[...] = jnp.concatenate([gk_ext[n:], gv_ext[n:]], axis=1)
        gmid_last[...] = gmid_ext[n:]
        half = keep_a.shape[0]
        keep[:half] = keep_a[...]
        send[:half] = send_a[...]
        split_slab(info, slab, keep.at[pl.ds(half, keep.shape[0] - half)], send.at[pl.ds(half, send.shape[0] - half)])


def fifth_kernel(info, gq, gkv, got, x, gmid, gain, bias, w_mix, slab_in, *refs):
    vectors, squares = refs[:8], refs[8:10]
    cross, local, (keep, send, small, slab, d_gain, d_bias) = refs[-10:-8], refs[-8:-6], refs[-6:]
    slab[...] = slab_in[...]
    d_gain[...] = vectors[0][...]
    d_bias[...] = vectors[4][...]
    n = x.shape[0] - WIN
    grad_x = mix_backward(
        gq[...], gkv[...] + got[...].astype(F32), x[n:].astype(F32), gain, bias, w_mix, slab, d_gain, d_bias, gmid[...]
    )
    emit_rows(info, n // WIN - 1, grad_x.astype(BF16), True, cross, local)
    split_slab(info, slab, keep, send)
    small_rows(info, (d_gain,) + vectors[1:4] + (d_bias,) + vectors[5:], squares, small)
    put_riders(small[...], send, keep.shape[0])


def put_riders(rows, send, at):
    count = rows.shape[0]
    coarse = rows.astype(BF16)
    send[at : at + count] = coarse
    send[at + count :] = (rows - coarse.astype(F32)).astype(BF16)


def riders_of(got, at):
    count = (got.shape[0] - at) // 2
    return got[at : at + count].astype(F32) + got[at + count :].astype(F32)


def stage_kernel(digits, *refs, groups, ways, stage, riders):
    refs = list(refs)
    parts = [(refs.pop(0), [refs.pop(0) for _ in range(count)]) for count in groups]
    small = refs.pop(0) if riders else None
    messages = [refs.pop(0) for _ in range(max(ways - 1, 1))]
    kept_out = refs.pop(0) if ways > 1 else None
    small_out = refs.pop(0) if riders else None
    total = refs.pop(0)
    vectors = small[...] if riders else None
    at = 0
    for kept, got in parts:
        rows = kept.shape[0]
        value = kept[...]
        for g in got:
            value = value + g[:rows].astype(F32)
            if g.shape[0] > rows:
                vectors = vectors + riders_of(g, rows)
        total[at : at + rows] = value
        at += rows
    chunk = at // ways

    def piece(which):
        return total[pl.ds(pl.multiple_of(which * chunk, 16), chunk)]

    mine = digits[9 + stage] if ways > 1 else 0
    for i, message in enumerate(messages):
        message[:chunk] = piece(mine ^ (i + 1) if ways > 1 else 0).astype(BF16)
        if riders:
            put_riders(vectors, message, chunk)
    if ways > 1:
        kept_out[...] = piece(mine)
    if riders:
        small_out[...] = vectors


def exchange_kernel(digits, mine, theirs, rows_out, small_out):
    count = rows_out.shape[0]
    rows_out[...] = (mine[:count].astype(F32) + theirs[:count].astype(F32)).astype(BF16)
    small_out[...] = riders_of(mine, count) + riders_of(theirs, count)


def again_kernel(digits, rows, small, message):
    message[: rows.shape[0]] = rows[...]
    put_riders(small[...], message, rows.shape[0])


def order_kernel(digits, *refs, stage):
    pieces, out = refs[:-1], refs[-1]
    rows = pieces[0].shape[0]
    for c, piece in enumerate(pieces):
        out[pl.ds(pl.multiple_of((digits[9 + stage] ^ c) * rows, 16), rows)] = piece[...]


def assemble_kernel(info, *refs):
    own, other, out, wide, sems = refs[:4], *refs[4:]
    core = info[0]
    rows = out.shape[1]

    def leave(t):
        column = core if t < 4 else 1 - core
        image = (info[5] ^ (t % 4 // 2)) * 4 + column * 2 + (info[4] ^ (t % 2))
        return pltpu.make_async_copy(wide.at[t], out.at[image], sems.at[t])

    for t in range(8):
        if t < 4:
            block = own[t][pl.ds(pl.multiple_of(core * rows, rows), rows)]
        else:
            block = other[t - 4]
        wide[t] = block.astype(F32)
        leave(t).start()
    for t in range(8):
        leave(t).wait()


def hold_kernel(info, first, second, *refs):
    refs[-2][...] = first[...]
    refs[-1][...] = second[...]


def small_rows(info, vectors, squares, out):
    width = out.shape[1]
    once = jnp.where(info[7] == 0, 1.0, 0.0)
    lane = lax.broadcasted_iota(jnp.int32, (1, width), 1)
    out[...] = jnp.zeros_like(out)
    for i, vector in enumerate(vectors):
        out[i : i + 1] = jnp.sum(vector[...], axis=0, keepdims=True) * once
    for i in range(6):
        total = jnp.sum(jnp.sum(squares[i // 3][i % 3], axis=0, keepdims=True), axis=1, keepdims=True)
        out[8 + i : 9 + i] = jnp.where(lane == info[6], total * once, 0.0)


def trade_kernel(info, *refs):
    pieces, out = refs[:4], refs[4]
    rows = out.shape[1]
    for t in range(4):
        out[t] = pieces[t][pl.ds(pl.multiple_of((1 - info[0]) * rows, rows), rows)]


def unpack_kernel(info, mine, theirs, small, counted, mix, proj, up, down, gain, bias, rms, wide, *, sizes):
    core = info[9]
    wide[core] = mine[...].astype(F32)
    wide[1 - core] = theirs[...].astype(F32)
    rows_a, rows_b, rows_c, ways = sizes
    early = (rows_a + rows_b) // 2 // ways
    late = rows_c // 2 // ways
    rows_mix = rows_c

    def pieces(slab, start, stop):
        total = {"a": rows_a, "b": rows_b, "c": rows_c}[slab] // 2
        size, shift, skip = (late, early, 0) if slab == "c" else (early, 0, rows_a // 2 if slab == "b" else 0)
        at = start
        while at < stop:
            half, row = at // total, at % total
            along = row + skip
            count = min(stop - at, total - row, size - along % size)
            yield at - start, half, along // size * (early + late) + shift + along % size, count
            at += count

    width = wide.shape[2]
    places = {0: (("c", 0), ("b", rows_mix)), 1: (("b", 0), ("a", 0))}
    for layer in range(2):
        (slab, at), (feed, feed_at) = places[layer]
        for out, name in ((mix, slab), (proj, feed), (up, feed), (down, feed)):
            if name == feed and out is not mix:
                at = feed_at
            rows, cols = out.shape[1:]
            for i in range(cols // width):
                for offset, half, row, count in pieces(name, at + i * rows, at + (i + 1) * rows):
                    out[layer, offset : offset + count, i * width : (i + 1) * width] = wide[half, row : row + count]
            if out is not mix:
                feed_at = at + rows * cols // width
    for layer in range(2):
        for norm in range(2):
            gain[layer, norm : norm + 1] = small[2 * layer + norm : 2 * layer + norm + 1]
            bias[layer, norm : norm + 1] = small[4 + 2 * layer + norm : 5 + 2 * layer + norm]
    images = rms.shape[1]
    sums = pltpu.roll(small[8:16], small.shape[1] - (info[6] - info[6] % images), 1)
    rms[...] = jnp.sqrt(sums[: rms.shape[0], :images] / counted[...])


VMEM = pl.BlockSpec(memory_space=pltpu.VMEM)


def call(kernel, info, operands, specs, outs, out_specs, scratch=(), grid=(), work=0, aliases={}):
    moved = sum(math.prod(a.shape) * a.dtype.itemsize for a in list(operands) + jax.tree.leaves(outs))
    single = not isinstance(outs, list)
    views = list(specs) + ([out_specs] if single else list(out_specs))

    def body_of(info, *refs):
        seen = [view(ref) if callable(view) else ref for view, ref in zip(views, refs)]
        kernel(info, *seen, *refs[len(views) :])

    def plain(view):
        return VMEM if callable(view) else view

    return pl.pallas_call(
        body_of,
        grid_spec=pltpu.PrefetchScalarGridSpec(
            num_scalar_prefetch=1,
            grid=grid,
            in_specs=[plain(v) for v in specs],
            out_specs=plain(out_specs) if single else [plain(v) for v in out_specs],
            scratch_shapes=list(scratch),
        ),
        out_shape=outs,
        input_output_aliases=aliases,
        compiler_params=pltpu.CompilerParams(vmem_limit_bytes=VMEM_LIMIT),
        cost_estimate=pl.CostEstimate(flops=int(work * 1.15e9), bytes_accessed=moved, transcendentals=0),
    )(info, *operands)


def whole(array):
    return VMEM


def tiled(array):
    return lambda ref: ref.at[pl.ds(pl.multiple_of(pl.program_id(0) * TB, TB), TB)]


def tiled_after_window(ref):
    return ref.at[pl.ds(pl.multiple_of(pl.program_id(0) * TB + WIN, WIN), TB)]


def last_rows(ref):
    return ref.at[pl.ds(ref.shape[0] - WIN, WIN)]


ANY = pl.BlockSpec(memory_space=pl.ANY)


def shape(dims, kind):
    return jax.ShapeDtypeStruct(dims, kind)


def after(value, *others):
    return lax.optimization_barrier((value, others))[0]


def body(edge_rows, lengths, norm_gain, norm_bias, w_qkv, w_out, w_up, w_down):
    sections = lax.axis_size("section")
    index = lax.axis_index("section")
    images, rows_dev, width = edge_rows.shape
    seats = 2 * images
    rep = sections // seats
    seat = index // rep
    twin = index % rep
    rows_piece = rows_dev * rep
    qw = (w_qkv.shape[2] - width) // 2
    kvw = w_qkv.shape[2] - qw
    hidden = w_up.shape[2]
    n = rows_piece * images // 2
    quarter = images // 2
    steps = (n // TB,)

    def route(pairs):
        return [(s * rep + e, d * rep + e) for s, d in pairs for e in range(rep)]

    if rep > 1:
        groups = [[s * rep + e for e in range(rep)] for s in range(seats)]
        edge_rows = lax.all_gather(edge_rows, "section", axis_index_groups=groups, axis=1, tiled=True)

    chip = seat // 2
    part = seat % 2
    fz, fl, fy = chip // 4, (chip // 2) % 2, chip % 2
    limit = lengths[chip]
    spot = lax.axis_index("dp") * images + chip
    dp_count = lax.axis_size("dp")
    dp_index = lax.axis_index("dp")

    def partners(masks):
        total = dp_count * sections
        spot = dp_index * sections + index
        digit = sum(((spot // m) % 2) << i for i, m in enumerate(masks))
        routes = []
        for c in range(1, 1 << len(masks)):
            flips = sum(m for i, m in enumerate(masks) if (c >> i) & 1)
            routes.append((c, [(s, s ^ flips) for s in range(total)]))
        return digit, routes

    dp_masks = [sections << b for b in range(dp_count.bit_length() - 1)]
    section_masks = [1 << b for b in range(1, sections.bit_length() - 1)]
    plane = [dp_masks[0], section_masks[0]]
    rest = section_masks[1:] + dp_masks[1:]
    digits = [partners(masks)[0] for masks in [[1], plane] + [[m] for m in rest]]
    counted = (lengths.astype(F32) * width)[None, :]
    info = jnp.stack([part, limit, chip % quarter, fz, fy, fz, spot, twin, index % 2] + digits).astype(jnp.int32)
    swap = route([(s, s ^ 1) for s in range(seats)])

    def bits(s):
        return s // 8, (s // 4) % 2, (s // 2) % 2, s % 2

    by_column = edge_rows.reshape(2, 2, 2, rows_piece, width)
    traded = lax.dynamic_index_in_dim(by_column, 1 - part, 1, keepdims=False).reshape(4, rows_piece, width)
    traded = lax.ppermute(traded, "section", swap)
    column = lax.dynamic_index_in_dim(by_column, part, 1, keepdims=False).reshape(4, rows_piece, width)
    received = [None] * 4
    for t in (2, 3, 0, 1):
        tz, ty = t // 2, t % 2
        image = (fz ^ tz) * 2 + (fy ^ ty)
        own = lax.dynamic_index_in_dim(column, image, 0, keepdims=False)
        got = lax.dynamic_index_in_dim(traded, image, 0, keepdims=False)
        message = jnp.where(part == 0, jnp.concatenate([own, got]), jnp.concatenate([got, own]))
        pairs = []
        for s in range(seats):
            z, l, y, k = bits(s)
            pairs.append((s, ((z ^ tz) * 4 + k * 2 + (y ^ ty)) * 2 + l))
        received[t] = lax.ppermute(message, "section", route(pairs))

    def send_back(message, tz, ty):
        pairs = []
        for s in range(seats):
            z, l, y, p = bits(s)
            pairs.append((s, ((z ^ tz) * 4 + p * 2 + (y ^ ty)) * 2 + l))
        return lax.ppermute(message, "section", route(pairs))

    def trade(got):
        out = shape((4, rows_piece, width), BF16)
        send = call(trade_kernel, info, got, [VMEM] * 4, out, whole(out))
        return lax.ppermute(send, "section", swap)

    first_to_second = route([(2 * c, 2 * c + 1) for c in range(images)])
    second_to_first = route([(2 * c + 1, 2 * c) for c in range(images)])

    dma = pltpu.SemaphoreType.DMA
    rows_q = shape((n, qw), BF16)
    rows_kv = shape((n, kvw), BF16)
    rows_low = shape((n, width), BF16)
    rows_wide = shape((n, width), F32)
    rows_stat = shape((n, 128), F32)
    rows_hidden = shape((n, hidden), BF16)
    grad_k_shape = shape((n + WIN, qw), F32)
    grad_v_shape = shape((n + WIN, width), F32)
    mix_rows = w_qkv.shape[1] * w_qkv.shape[2] // width
    feed_rows = (w_out[0].size + w_up[0].size + w_down[0].size) // width
    vec_shape = shape((8, width), F32)
    squares_shape = shape((3, 8, width), F32)
    ext = pltpu.VMEM((n + WIN, kvw), BF16)

    g0, g1, b0, b1 = norm_gain[0], norm_gain[1], norm_bias[0], norm_bias[1]

    halo_shape = shape((WIN, kvw), BF16)
    outs = [shape((n + WIN, width), BF16), rows_q, rows_kv, halo_shape]
    x, q0, kv0, halo0 = call(
        first_kernel, info, received + [g0, b0, w_qkv[0]], [ANY] * 4 + [whole(g0), whole(b0), whole(w_qkv[0])],
        outs, [whole(o) for o in outs], [dma((2,))], work=6,
    )
    halo0 = lax.ppermute(halo0, "section", first_to_second)

    outs = [rows_low, rows_q, rows_kv, rows_low, rows_stat, rows_hidden, rows_hidden, rows_wide, squares_shape]
    z, q1, kv1, o0, lse0, active0, slope0, mid0, squares0 = call(
        second_kernel, info, [x, q0, kv0, halo0, g0, b0, w_out[0], w_up[0], w_down[0], g1, b1, w_qkv[1]],
        [tiled_after_window, tiled(q0)] + [whole(a) for a in (kv0, halo0, g0, b0, w_out[0], w_up[0], w_down[0], g1, b1, w_qkv[1])],
        outs, [tiled(o) for o in outs[:-1]] + [whole(outs[-1])], [ext], steps, work=15,
    )
    kv_other = lax.ppermute(kv1, "section", first_to_second)

    rows_k_all = shape((2 * n, qw), BF16)
    rows_v_all = shape((2 * n, width), BF16)
    outs = [rows_q, rows_k_all, rows_v_all, rows_wide, rows_stat]
    qr, kr, vr, o_far, lse_far = call(
        far_forward_kernel, info, [q1, kv1, kv_other], [whole(a) for a in (q1, kv1, kv_other)],
        outs, [whole(o) for o in outs],
        [pltpu.VMEM((n, qw), F32), pltpu.VMEM((2 * n, qw), F32), pltpu.VMEM((HEADS, 2 * n, 128), F32),
         pltpu.VMEM((HEADS, n, 128), F32), pltpu.VMEM((n, 128), F32)], work=14,
    )

    message = shape((2 * rows_piece, width), BF16)
    outs = [message] * 4 + [rows_low, rows_stat, shape((n, qw), F32), grad_k_shape, grad_v_shape, rows_wide,
            shape((feed_rows // 2, width), F32), shape((feed_rows // 2, width), BF16),
            vec_shape, vec_shape, squares_shape]
    (cross0, cross1, local0, local1, go1, stat1, gq_near, gk_near, gv_near, gmid1, keep_a, send_a,
     d_gain11, d_bias11, squares1) = call(
        third_kernel, info,
        received + [q1, kv1, kv_other, o_far, lse_far, z, g1, b1, w_out[1], w_up[1], w_down[1]],
        [ANY] * 4
        + [tiled(q1), whole(kv1), last_rows]
        + [tiled(o_far), tiled(lse_far), tiled(z)]
        + [whole(a) for a in (g1, b1, w_out[1], w_up[1], w_down[1])],
        outs,
        [whole(message)] * 4 + [tiled(o) for o in outs[4:7]] + [whole(outs[7]), whole(outs[8]), tiled(outs[9])]
        + [whole(o) for o in outs[10:]],
        [ext, pltpu.VMEM((n, width), BF16), pltpu.VMEM((feed_rows, width), F32), dma((2,))], steps, work=24,
    )
    forward_back = [None, None, send_back(cross0, 1, 0), None]

    outs = [shape((n, qw), F32), shape((n, kvw), F32), rows_kv]
    operands = [qr, kr, vr, go1, stat1, gq_near, gk_near, gv_near]
    gq1, gkv1, gkv_send = call(
        far_backward_kernel, info, operands, [whole(a) for a in operands], outs, [whole(o) for o in outs],
        [pltpu.VMEM((HEADS, n, 128), F32), pltpu.VMEM((n, 128), F32), pltpu.VMEM((n, qw), F32),
         pltpu.VMEM((2 * n, qw), F32), pltpu.VMEM((HEADS, 2 * n, 128), F32)], work=18,
    )
    gkv_got = lax.ppermute(after(gkv_send, forward_back[2]), "section", second_to_first)
    forward_back[3] = send_back(after(cross1, forward_back[2]), 1, 1)
    forward_back[0] = send_back(after(local0, forward_back[2]), 0, 0)
    forward_back[1] = send_back(after(local1, forward_back[2]), 0, 1)

    slab_rows = mix_rows + feed_rows
    early_shape = (feed_rows + slab_rows) // 2, width
    mix_slab = shape((mix_rows, width), F32)
    outs = [message] * 4 + [shape((WIN, qw), F32), shape((WIN, kvw), F32), shape((WIN, width), F32), halo_shape,
            shape(early_shape, F32), shape(early_shape, BF16), mix_slab] + [vec_shape] * 6
    operands = [gq1, gkv1, gkv_got, z, gmid1, g1, b1, w_qkv[1], q0, kv0, halo0, o0, lse0, active0, slope0, mid0, x, g0,
                b0, w_qkv[0], w_out[0], w_up[0], w_down[0], keep_a, send_a]
    (cross0, cross1, local0, local1, gq_last, gkv_last, gmid_last, halo_send, keep_early, send_early, slab_last,
     d_gain10, d_bias10, d_gain01, d_bias01, d_gain00, d_bias00) = call(
        fourth_kernel, info, operands,
        [tiled(a) for a in operands[:5]] + [VMEM] * 3 + [tiled(q0), VMEM, VMEM] + [tiled(a) for a in operands[11:16]]
        + [VMEM] * 9,
        outs, [VMEM] * len(outs),
        [ext, pltpu.VMEM((slab_rows, width), F32), pltpu.VMEM((n + WIN, qw), F32), pltpu.VMEM((n + WIN, qw), F32),
         pltpu.VMEM((n + WIN, width), F32), pltpu.VMEM((n + WIN, width), F32)], steps, work=20,
    )
    outs = [halo_shape, shape(early_shape, BF16)]
    halo_send, send_early = call(
        hold_kernel, info, [halo_send, send_early] + forward_back, [VMEM] * 2 + [ANY] * 4, outs, [VMEM] * 2
    )
    halo_got = lax.ppermute(halo_send, "section", second_to_first)

    def pair(message):
        return lax.ppermute(message, ("dp", "section"), partners([1])[1][0][1])

    def send_all(messages, masks):
        return [lax.ppermute(m, ("dp", "section"), way) for m, (_, way) in zip(messages, partners(masks)[1])]

    small_shape = shape((16, width), F32)
    rider_rows = 2 * small_shape.shape[0]

    def stage(groups, small, ways, number):
        operands = [a for kept, got in groups for a in [kept] + got] + ([] if small is None else [small])
        rows = sum(kept.shape[0] for kept, _ in groups)
        riders = small is not None
        outs = [shape((rows // ways + rider_rows * riders, width), BF16)] * max(ways - 1, 1)
        outs += [shape((rows // ways, width), F32)] * (ways > 1) + [small_shape] * riders
        kernel = functools.partial(
            stage_kernel, groups=[len(got) for _, got in groups], ways=ways, stage=number, riders=riders
        )
        made = call(
            kernel, info, operands, [VMEM] * len(operands), outs, [VMEM] * len(outs), [pltpu.VMEM((rows, width), F32)]
        )
        sent = max(ways - 1, 1)
        return made[:sent], made[sent] if ways > 1 else None, made[-1] if riders else None

    def gather(piece, masks, number):
        pieces = [piece] + [lax.ppermute(piece, ("dp", "section"), way) for _, way in partners(masks)[1]]
        out = shape((len(pieces) * piece.shape[0], width), BF16)
        return call(functools.partial(order_kernel, stage=number), info, pieces, [VMEM] * len(pieces), out, VMEM)

    early, kept_early, _ = stage([(keep_early, [pair(send_early)])], None, 4, 1)
    early_sent = early
    early = send_all(early, plane)

    outs = [message] * 4 + [shape((mix_rows // 2, width), F32), shape((mix_rows // 2 + rider_rows, width), BF16), small_shape]
    operands = [gq_last, gkv_last, halo_got, x, gmid_last, g0, b0, w_qkv[0], slab_last]
    operands += [d_gain00, d_gain01, d_gain10, d_gain11, d_bias00, d_bias01, d_bias10, d_bias11, squares0, squares1]
    aliases = {1 + len(operands) + i: i for i in range(4)}
    operands += [cross0, cross1, local0, local1]
    awaited = list(early_sent)
    cross0, cross1, local0, local1, keep_late, send_late, small = call(
        fifth_kernel, info, operands + awaited, [VMEM] * len(operands) + [ANY] * len(awaited), outs, [VMEM] * len(outs),
        [pltpu.VMEM((mix_rows, width), F32), pltpu.VMEM((8, width), F32), pltpu.VMEM((8, width), F32)],
        aliases=aliases,
    )

    def assemble(own, other):
        out = call(
            assemble_kernel, info, own + [other], [VMEM] * 5, shape((images, rows_piece, width), F32), ANY,
            [pltpu.VMEM((images, rows_piece, width), F32), dma((images,))],
        )
        if rep > 1:
            out = lax.dynamic_slice_in_dim(out, twin * rows_dev, rows_dev, 1)
        return out

    backward_back = [send_back(local0, 0, 0), None, send_back(cross0, 1, 0), None]
    late, kept_late, small = stage([(keep_late, [pair(after(send_late, *early))])], small, 4, 1)
    late = send_all(late, plane)
    forward_trade = trade(forward_back)
    forward_rows = assemble(forward_back, forward_trade)
    groups = [(kept_early, early), (kept_late, late)]
    number = 2
    scattered = []
    while number - 1 < len(rest) and sum(kept.shape[0] for kept, _ in groups) % 32 == 0:
        messages, kept, small = stage(groups, small, 2, number)
        groups = [(kept, send_all(messages, [rest[number - 2]]))]
        scattered.append(number)
        number += 1
    scattered_rows = groups[-1][1]
    backward_back[3] = send_back(after(cross1, backward_back[2], *scattered_rows, forward_rows), 1, 1)
    backward_back[1] = send_back(after(local1, backward_back[2], *scattered_rows, forward_rows), 0, 1)
    (both,), _, small = stage(groups, small, 1, 0)
    both = after(both, backward_back[0], backward_back[2])
    rows_shape = shape((both.shape[0] - rider_rows, width), BF16)
    while number - 2 < len(rest):
        (got,) = send_all([both], [rest[number - 2]])
        rows, small = call(exchange_kernel, info, [both, got], [VMEM] * 2, [rows_shape, small_shape], [VMEM] * 2)
        number += 1
        if number - 2 < len(rest):
            both = call(again_kernel, info, [rows, small], [VMEM] * 2, shape(both.shape, BF16), VMEM)
    both = after(rows, backward_back[1], backward_back[3])
    for number in scattered[::-1]:
        both = gather(both, [rest[number - 2]], number)
    backward_trade = trade(after(backward_back, rows))
    both = gather(both, plane, 1)
    both = after(both, backward_trade)
    theirs = pair(both)
    backward_rows = assemble(backward_back, backward_trade)
    outs = [shape(w.shape, F32) for w in (w_qkv, w_out, w_up, w_down, norm_gain, norm_bias)] + [shape((6, images), F32)]
    sizes = (feed_rows, slab_rows, mix_rows, 1 << len(plane))
    grads = call(
        functools.partial(unpack_kernel, sizes=sizes), info, [both, theirs, small, counted],
        [VMEM] * 4, outs, [whole(o) for o in outs],
        [pltpu.VMEM((2,) + both.shape, F32)],
    )
    return (forward_rows, backward_rows, grads[6], grads[4], grads[5]) + tuple(grads[:4])


def solution(mesh):
    placed = (P("dp", "section", None), P("dp"), P(), P(), P(), P(), P(), P())
    return jax.shard_map(
        body,
        mesh=mesh,
        in_specs=placed,
        out_specs=(P("dp", "section", None), P("dp", "section", None), P(None, "dp"), P(), P(), P(), P(), P(), P()),
        check_vma=False,
    )
```

```python
import functools
import math

import jax
import jax.numpy as jnp
from jax import lax
from jax.experimental import pallas as pl
from jax.experimental.pallas import tpu as pltpu
from jax.sharding import PartitionSpec as P

HEADS = 2
WIN = 128
STRIDE = 128
NEG = -1e30
F32 = jnp.float32
BF16 = jnp.bfloat16
TB = 768
RES = 8
UNROLL = 16
RES_BACK = 16
UNROLL_BACK = 8
VMEM_LIMIT = 16 * 1024 * 1024


def dot(left, right):
    return lax.dot_general(left, right, (((1,), (0,)), ((), ())), preferred_element_type=F32)


def dot_t(left, right):
    return lax.dot_general(left, right, (((1,), (1,)), ((), ())), preferred_element_type=F32)


def t_dot(left, right):
    return lax.dot_general(left, right, (((0,), (0,)), ((), ())), preferred_element_type=F32)


def score_scale(query_width):
    return 1.0 / math.sqrt(query_width // HEADS)


def norm_parts(rows):
    centre = rows - jnp.mean(rows, axis=-1, keepdims=True)
    scale = lax.rsqrt(jnp.mean(centre * centre, axis=-1, keepdims=True) + 1e-05)
    return centre * scale, scale


def norm_back(grad, unit, scale, gain):
    scaled = grad * gain
    first = jnp.mean(scaled, axis=-1, keepdims=True)
    second = jnp.mean(scaled * unit, axis=-1, keepdims=True)
    return scale * (scaled - first - unit * second)


def col_sum(rows):
    return jnp.sum(rows.reshape(rows.shape[0] // 8, 8, rows.shape[1]), axis=0)


def gelu_pair(hidden):
    c0 = math.sqrt(2.0 / math.pi)
    square = hidden * hidden
    share = 0.5 + 0.5 * jnp.tanh(hidden * (c0 + (c0 * 0.044715) * square))
    active = hidden * share
    slope = share + active * (1.0 - share) * (2.0 * c0 + (6.0 * c0 * 0.044715) * square)
    return active, slope


def head_split(rows):
    lane = lax.broadcasted_iota(jnp.int32, rows.shape, 1)
    zero = jnp.zeros_like(rows)
    low = lane < rows.shape[1] // HEADS
    return jnp.concatenate([jnp.where(low, rows, zero), jnp.where(low, zero, rows)], axis=0)


def head_join(stacked):
    half = stacked.shape[0] // 2
    lane = lax.broadcasted_iota(jnp.int32, (half, stacked.shape[1]), 1)
    return jnp.where(lane < stacked.shape[1] // HEADS, stacked[:half], stacked[half:])


def near_masks(base, limit):
    row = lax.broadcasted_iota(jnp.int32, (2 * WIN, WIN), 0)
    row = jnp.where(row >= WIN, row - WIN, row)
    col = lax.broadcasted_iota(jnp.int32, (2 * WIN, WIN), 1)
    own = col <= row
    key = base + col - jnp.where(own, 0, WIN)
    allowed = (key >= 0) & ((key < limit) | (col == row))
    return own, allowed


def near_scores(split_q, keys, own, allowed):
    scores = dot_t(split_q, keys)
    folded = jnp.where(own, scores[:, WIN:], scores[:, :WIN])
    return jnp.where(allowed, folded, NEG)


def unfold(folded, own):
    return jnp.concatenate([jnp.where(own, 0.0, folded), jnp.where(own, folded, 0.0)], axis=1).astype(BF16)


def near_forward(queries, keys, values, base, limit):
    own, allowed = near_masks(base, limit)
    scores = near_scores(head_split(queries), keys, own, allowed)
    largest = jnp.max(scores, axis=-1, keepdims=True)
    powers = jnp.exp(scores - largest)
    total = jnp.sum(powers, axis=-1, keepdims=True)
    weights = unfold(powers, own)
    hd = values.shape[1] // HEADS
    out = [dot(weights[h * WIN : (h + 1) * WIN], values[:, h * hd : (h + 1) * hd]) for h in range(HEADS)]
    return out, largest, total, powers


def near_backward(queries, keys, values, grad_out, log_total, delta, base, limit, weights=None):
    own, allowed = near_masks(base, limit)
    split_q = head_split(queries)
    if weights is None:
        weights = jnp.exp(near_scores(split_q, keys, own, allowed) - log_total)
    hd = values.shape[1] // HEADS
    pull = jnp.concatenate(
        [dot_t(grad_out[:, h * hd : (h + 1) * hd], values[:, h * hd : (h + 1) * hd]) for h in range(HEADS)], axis=0
    )
    pull = jnp.where(own, pull[:, WIN:], pull[:, :WIN])
    slope = weights * (pull - delta)
    grad_q = head_join(dot(unfold(slope, own), keys))
    row = lax.broadcasted_iota(jnp.int32, (WIN, 2 * WIN), 0)
    col = lax.broadcasted_iota(jnp.int32, (WIN, 2 * WIN), 1)
    here = (row <= jnp.where(col >= WIN, col - WIN, col)).astype(F32).astype(BF16)

    def turned(folded):
        flat = folded.astype(BF16).T
        current = flat * here
        return jnp.concatenate([flat - current, current], axis=0)

    grad_k = dot(turned(slope), split_q)
    weights = turned(weights)
    grad_v = jnp.concatenate(
        [dot(weights[:, h * WIN : (h + 1) * WIN], grad_out[:, h * hd : (h + 1) * hd]) for h in range(HEADS)], axis=1
    )
    return grad_q, grad_k, grad_v


def stack_stat(stat, width=128):
    return jnp.concatenate([stat[:, 0:1], stat[:, width // 2 : width // 2 + 1]], axis=0)


def spread_stat(stacked, width=128):
    half = stacked.shape[0] // 2
    lane = lax.broadcasted_iota(jnp.int32, (half, width), 1)
    return jnp.where(lane < width // 2, stacked[:half], stacked[half:])


def masked_squares(rows, base, limit):
    pos = base + lax.broadcasted_iota(jnp.int32, (rows.shape[0], 1), 0)
    return col_sum(jnp.where(pos < limit, rows * rows, 0.0))


def gather_pieces(info, pieces, target, sems, low):
    rows = pieces[0].shape[0]

    def each(act):
        for ty in range(2):
            place = target.at[pl.ds((ty ^ info[4]) * rows, rows)]

            @pl.when(info[5] == (0 if low else 1))
            def _():
                act(pltpu.make_async_copy(pieces[ty], place, sems.at[ty]))

            @pl.when(info[5] == (1 if low else 0))
            def _():
                act(pltpu.make_async_copy(pieces[2 + ty], place, sems.at[ty]))

    each(lambda c: c.start())
    each(lambda c: c.wait())


def emit_rows(info, first, rows, to_lower, cross, local):
    units = cross[0].shape[0] // WIN
    stays = info[5] == (0 if to_lower else 1)
    for sub in range(rows.shape[0] // WIN):
        number = first + sub
        block = number // units
        at = pl.ds(pl.multiple_of((number - block * units) * WIN, WIN), WIN)
        value = rows[sub * WIN : (sub + 1) * WIN]
        for ty in range(2):
            fits = (number >= 0) & ((block ^ info[4]) == ty)

            @pl.when(fits & stays)
            def _():
                local[ty][at] = value

            @pl.when(fits & jnp.logical_not(stays))
            def _():
                cross[ty][at] = value


def split_slab(info, slab, keep, send):
    once = jnp.where(info[7] == 0, 1.0, 0.0)
    half = keep.shape[0]
    mine = info[8]
    keep[...] = slab[pl.ds(pl.multiple_of(mine * half, 8), half)] * once
    send[:half] = (slab[pl.ds(pl.multiple_of((1 - mine) * half, 8), half)] * once).astype(BF16)


def first_kernel(info, *refs):
    pieces = refs[:4]
    gain, bias, w_mix, x_out, q_out, kv_out, halo_out, sems = refs[4:]
    gather_pieces(info, pieces, x_out.at[pl.ds(WIN, x_out.shape[0] - WIN)], sems, True)
    x_out[:WIN] = jnp.zeros((WIN, x_out.shape[1]), BF16)
    qw = q_out.shape[1]

    def block(i, _):
        at = pl.ds(pl.multiple_of(i * TB, TB), TB)
        unit, _ = norm_parts(x_out[pl.ds(pl.multiple_of(i * TB + WIN, WIN), TB)].astype(F32))
        normed = (unit * gain[0:1] + bias[0:1]).astype(BF16)
        mixed = dot(normed, w_mix[...])
        q_out[at] = (mixed[:, :qw] * score_scale(qw)).astype(BF16)
        kv_out[at] = mixed[:, qw:].astype(BF16)
        return 0

    lax.fori_loop(0, q_out.shape[0] // TB, block, 0)
    halo_out[...] = kv_out[kv_out.shape[0] - WIN :]


def load_extended(halo, kv, ext):
    ext[: halo.shape[0]] = halo[...]
    ext[halo.shape[0] :] = kv[...]


def second_kernel(
    info, x, q, kv, halo, gain, bias, w_proj, w_in, w_back, gain_next, bias_next, w_mix_next,
    z_out, q_next, kv_next, o_out, lse_out, active_out, slope_out, mid_out, squares, ext,
):
    step = pl.program_id(0)
    qw = q.shape[1]
    n = kv.shape[0]

    @pl.when(step == 0)
    def _():
        load_extended(halo, kv, ext)
        squares[...] = jnp.zeros_like(squares)

    limit = info[1]
    start = step * TB
    base = info[0] * n + start
    outs = []
    for sub in range(TB // WIN):
        near = pl.ds(pl.multiple_of(start + sub * WIN, WIN), 2 * WIN)
        keys = ext[near, :qw]
        values = ext[near, qw:]
        queries = q[sub * WIN : (sub + 1) * WIN]
        out, largest, total, _ = near_forward(queries, keys, values, base + sub * WIN, limit)
        inverse = 1.0 / total
        lse_out[sub * WIN : (sub + 1) * WIN] = spread_stat(largest + jnp.log(total))
        outs.append(jnp.concatenate([out[0] * inverse[:WIN], out[1] * inverse[WIN:]], axis=1))
    attended = jnp.concatenate(outs, axis=0).astype(BF16)
    o_out[...] = attended
    stream = x[...].astype(F32)
    branch = dot(attended, w_proj[...])
    middle = stream + branch
    mid_out[...] = middle
    unit, _ = norm_parts(middle)
    normed = (unit * gain[1:2] + bias[1:2]).astype(BF16)
    active, slope = gelu_pair(dot(normed, w_in[...]))
    active = active.astype(BF16)
    active_out[...] = active
    slope_out[...] = slope.astype(BF16)
    feed = dot(active, w_back[...])
    z = (middle + feed).astype(BF16)
    z_out[...] = z
    squares[0] += masked_squares(stream, base, limit)
    squares[1] += masked_squares(branch, base, limit)
    squares[2] += masked_squares(feed, base, limit)
    unit, _ = norm_parts(z.astype(F32))
    normed = (unit * gain_next[0:1] + bias_next[0:1]).astype(BF16)
    mixed = dot(normed, w_mix_next[...])
    q_next[...] = (mixed[:, :qw] * score_scale(qw)).astype(BF16)
    kv_next[...] = mixed[:, qw:].astype(BF16)


def far_mask(grid_q, grid_k, part_grid, residues):
    shape = (HEADS * residues * grid_q, residues * grid_k)
    row = lax.broadcasted_iota(jnp.int32, shape, 0)
    col = lax.broadcasted_iota(jnp.int32, shape, 1)
    row = jnp.where(row >= residues * grid_q, row - residues * grid_q, row)
    row_res = jnp.zeros(shape, jnp.int32)
    col_res = jnp.zeros(shape, jnp.int32)
    for r in range(1, residues):
        row_res += (row >= r * grid_q).astype(jnp.int32)
        col_res += (col >= r * grid_k).astype(jnp.int32)
    row_grid = row - row_res * grid_q + part_grid
    col_grid = col - col_res * grid_k
    allowed = (row_res == col_res) & (col_grid < row_grid)
    return allowed, col_grid * STRIDE + col_res


def far_forward_kernel(info, q, kv, other, qr, kr, vr, o_far, lse_far, q_s, k_s, v_s, o_s, lse_s):
    n, qw = q.shape
    grid_q = n // STRIDE
    grid_k = 2 * grid_q
    part = info[0]
    limit = info[1]

    def place(g, _):
        at = pl.ds(pl.multiple_of(g * STRIDE, STRIDE), STRIDE)
        own = kv[at].astype(F32)
        early = jnp.where(part == 0, own, other[at].astype(F32))
        q_s[pl.ds(g, STRIDE, stride=grid_q), :] = q[at].astype(F32)
        k_s[pl.ds(g, STRIDE, stride=grid_k), :] = early[:, :qw]
        k_s[pl.ds(g + grid_q, STRIDE, stride=grid_k), :] = own[:, :qw]
        hd = v_s.shape[1]
        for h in range(HEADS):
            v_s[h, pl.ds(g, STRIDE, stride=grid_k), :] = early[:, qw + h * 128 : qw + (h + 1) * 128]
            v_s[h, pl.ds(g + grid_q, STRIDE, stride=grid_k), :] = own[:, qw + h * 128 : qw + (h + 1) * 128]
        return 0

    lax.fori_loop(0, grid_q, place, 0)
    base_mask, key_pos = far_mask(grid_q, grid_k, part * grid_q, RES)
    rows_q = RES * grid_q
    rows_k = RES * grid_k

    def one(i):
        at_q = pl.ds(pl.multiple_of(i * rows_q, rows_q), rows_q)
        at_k = pl.ds(pl.multiple_of(i * rows_k, rows_k), rows_k)
        queries = q_s[at_q].astype(BF16)
        keys = k_s[at_k].astype(BF16)
        values = [v_s[h, at_k].astype(BF16) for h in range(HEADS)]
        qr[at_q] = queries
        kr[at_k] = keys
        for h in range(HEADS):
            vr[at_k, h * 128 : (h + 1) * 128] = values[h]
        allowed = base_mask & (key_pos + i * RES < limit)
        scores = jnp.where(allowed, dot_t(head_split(queries), keys), NEG)
        largest = jnp.max(scores, axis=-1, keepdims=True)
        powers = jnp.where(allowed, jnp.exp(scores - largest), 0.0)
        total = jnp.sum(powers, axis=-1, keepdims=True)
        safe = jnp.maximum(total, 1e-30)
        weights = (powers * (1.0 / safe)).astype(BF16)
        lse = jnp.where(total > 0.0, largest + jnp.log(safe), NEG)
        lse_s[at_q] = spread_stat(lse)
        for h in range(HEADS):
            o_s[h, at_q] = dot(weights[h * rows_q : (h + 1) * rows_q], values[h])

    def group(i, _):
        for u in range(UNROLL):
            one(i * UNROLL + u)
        return 0

    lax.fori_loop(0, STRIDE // RES // UNROLL, group, 0)

    def back(g, _):
        at = pl.ds(pl.multiple_of(g * STRIDE, STRIDE), STRIDE)
        pick = pl.ds(g, STRIDE, stride=grid_q)
        lse_far[at] = lse_s[pick, :]
        for h in range(HEADS):
            o_far[at, h * 128 : (h + 1) * 128] = o_s[h, pick, :]
        return 0

    lax.fori_loop(0, grid_q, back, 0)


def third_kernel(
    info, *refs,
):
    pieces = refs[:4]
    (q, kv, halo, o_far, lse_far, z, gain, bias, w_proj, w_in, w_back,
     cross0, cross1, local0, local1, go_out, stat_out, gq_out, gk_out, gv_out, gmid_out, keep, send,
     d_gain, d_bias, squares, ext, cot, slab, sems) = refs[4:]
    step = pl.program_id(0)
    qw = q.shape[1]
    n = kv.shape[0]

    @pl.when(step == 0)
    def _():
        gather_pieces(info, pieces, cot, sems, False)
        load_extended(halo, kv, ext)
        for ref in (squares, gk_out, gv_out, slab, d_gain, d_bias):
            ref[...] = jnp.zeros_like(ref)

    limit = info[1]
    start = pl.multiple_of(step * TB, TB)
    base = info[0] * n + start
    outs = []
    logs = []
    weights = []
    for sub in range(TB // WIN):
        rows = slice(sub * WIN, (sub + 1) * WIN)
        near = pl.ds(pl.multiple_of(start + sub * WIN, WIN), 2 * WIN)
        out, largest, total, powers = near_forward(q[rows], ext[near, :qw], ext[near, qw:], base + sub * WIN, limit)
        far_log = stack_stat(lse_far[rows])
        top = jnp.maximum(largest, far_log)
        near_share = jnp.exp(largest - top)
        far_share = jnp.exp(far_log - top)
        whole = total * near_share + far_share
        inverse = 1.0 / whole
        near_share = near_share * inverse
        far_share = far_share * inverse
        weights.append(powers * near_share)
        logs.append(top + jnp.log(whole))
        far = o_far[rows]
        outs.append(
            jnp.concatenate(
                [
                    out[h] * near_share[h * WIN : (h + 1) * WIN]
                    + far[:, h * 128 : (h + 1) * 128] * far_share[h * WIN : (h + 1) * WIN]
                    for h in range(HEADS)
                ],
                axis=1,
            )
        )
    attended_wide = jnp.concatenate(outs, axis=0)
    attended = attended_wide.astype(BF16)
    stream = z[...].astype(F32)
    branch = dot(attended, w_proj[...])
    middle = stream + branch
    unit, scale = norm_parts(middle)
    normed = (unit * gain[1:2] + bias[1:2]).astype(BF16)
    active, slope = gelu_pair(dot(normed, w_in[...]))
    active = active.astype(BF16)
    feed = dot(active, w_back[...])
    number = step * (TB // WIN)
    emit_rows(info, number, z[...], True, (cross0, cross1), (local0, local1))
    emit_rows(info, number, (middle + feed).astype(BF16), False, (cross0, cross1), (local0, local1))
    squares[0] += masked_squares(stream, base, limit)
    squares[1] += masked_squares(branch, base, limit)
    squares[2] += masked_squares(feed, base, limit)

    pos = base + lax.broadcasted_iota(jnp.int32, (TB, 1), 0)
    upstream = jnp.where(pos < limit, cot[pl.ds(start, TB)].astype(F32), 0.0)
    grad_out, grad_mid = feed_backward(
        upstream, active, slope, normed, unit, scale, attended, gain, w_proj, w_in, w_back, slab, 0, d_gain, d_bias
    )
    gmid_out[...] = grad_mid
    go_out[...] = grad_out
    weighted = grad_out.astype(F32) * attended_wide
    for sub in range(TB // WIN):
        rows = slice(sub * WIN, (sub + 1) * WIN)
        near = pl.ds(pl.multiple_of(start + sub * WIN, WIN), 2 * WIN)
        delta = jnp.concatenate(
            [jnp.sum(weighted[rows, h * 128 : (h + 1) * 128], axis=-1, keepdims=True) for h in range(HEADS)], axis=0
        )
        stat_out[rows] = pack_stats(logs[sub], delta)
        gq, gk, gv = near_backward(
            q[rows], ext[near, :qw], ext[near, qw:], grad_out[rows], logs[sub], delta, base + sub * WIN, limit,
            weights[sub],
        )
        gq_out[rows] = gq
        gk_out[near] += gk
        gv_out[near] += gv

    @pl.when(step == pl.num_programs(0) - 1)
    def _():
        split_slab(info, slab, keep, send)


def pack_stats(lse, delta):
    half = lse.shape[0] // 2
    lane = lax.broadcasted_iota(jnp.int32, (half, 128), 1)
    low = jnp.where(lane < 32, lse[:half], lse[half:])
    high = jnp.where(lane < 96, delta[:half], delta[half:])
    return jnp.where(lane < 64, low, high)


def add_columns(slab, at, grad):
    rows, cols = grad.shape
    width = slab.shape[1]
    for i in range(cols // width):
        slab[at + i * rows : at + (i + 1) * rows] += grad[:, i * width : (i + 1) * width]


def feed_backward(
    upstream, active, slope, normed, unit, scale, attended, gain, w_proj, w_in, w_back, slab, at, d_gain, d_bias,
):
    low = upstream.astype(BF16)
    width = low.shape[1]
    hidden = active.shape[1]
    slab[at + width + hidden : at + width + 2 * hidden] += t_dot(active, low)
    grad_hidden = (dot_t(low, w_back[...]) * slope).astype(BF16)
    add_columns(slab, at + width, t_dot(normed, grad_hidden))
    grad_normed = dot_t(grad_hidden, w_in[...])
    d_gain[...] += col_sum(grad_normed * unit)
    d_bias[...] += col_sum(grad_normed)
    grad_mid = upstream + norm_back(grad_normed, unit, scale, gain[1:2])
    branch_low = grad_mid.astype(BF16)
    slab[at : at + width] += t_dot(attended, branch_low)
    grad_out = dot_t(branch_low, w_proj[...]).astype(BF16)
    return grad_out, grad_mid


def far_backward_kernel(
    info, qr, kr, vr, go, stat, gq_near, gk_near, gv_near, gq_out, gkv_own, gkv_send,
    go_s, stat_s, gq_s, gk_s, gv_s,
):
    n, qw = gq_near.shape
    grid_q = n // STRIDE
    grid_k = 2 * grid_q
    part = info[0]
    limit = info[1]

    def place(g, _):
        at = pl.ds(pl.multiple_of(g * STRIDE, STRIDE), STRIDE)
        pick = pl.ds(g, STRIDE, stride=grid_q)
        rows = go[at].astype(F32)
        for h in range(HEADS):
            go_s[h, pick, :] = rows[:, h * 128 : (h + 1) * 128]
        stat_s[pick, :] = stat[at]
        return 0

    lax.fori_loop(0, grid_q, place, 0)
    base_mask, key_pos = far_mask(grid_q, grid_k, part * grid_q, RES_BACK)
    rows_q = RES_BACK * grid_q
    rows_k = RES_BACK * grid_k

    def one(i):
        at_q = pl.ds(pl.multiple_of(i * rows_q, rows_q), rows_q)
        at_k = pl.ds(pl.multiple_of(i * rows_k, rows_k), rows_k)
        keys = kr[at_k]
        split_q = head_split(qr[at_q])
        grads = [go_s[h, at_q].astype(BF16) for h in range(HEADS)]
        stats = stat_s[at_q]
        lse = jnp.concatenate([stats[:, 0:1], stats[:, 32:33]], axis=0)
        delta = jnp.concatenate([stats[:, 64:65], stats[:, 96:97]], axis=0)
        allowed = base_mask & (key_pos + i * RES_BACK < limit)
        weights = jnp.exp(jnp.where(allowed, dot_t(split_q, keys), NEG) - lse)
        pull = jnp.concatenate([dot_t(grads[h], vr[at_k, h * 128 : (h + 1) * 128]) for h in range(HEADS)], axis=0)
        slope = (weights * (pull - delta)).astype(BF16)
        weights = weights.astype(BF16)
        gq_s[at_q] = head_join(dot(slope, keys))
        gk_s[at_k] = t_dot(slope, split_q)
        for h in range(HEADS):
            gv_s[h, at_k] = t_dot(weights[h * rows_q : (h + 1) * rows_q], grads[h])

    def group(i, _):
        for u in range(UNROLL_BACK):
            one(i * UNROLL_BACK + u)
        return 0

    lax.fori_loop(0, STRIDE // RES_BACK // UNROLL_BACK, group, 0)

    def back(g, _):
        at = pl.ds(pl.multiple_of(g * STRIDE, STRIDE), STRIDE)
        shifted = pl.ds(pl.multiple_of(g * STRIDE + WIN, STRIDE), STRIDE)
        gq_out[at] = gq_near[at] + gq_s[pl.ds(g, STRIDE, stride=grid_q), :]
        mine = pl.ds(g + part * grid_q, STRIDE, stride=grid_k)
        sent = pl.ds(g, STRIDE, stride=grid_k)
        last = jnp.where(g == grid_q - 1, 1.0, 0.0)
        gkv_own[at, :qw] = gk_near[shifted] + gk_s[mine, :]
        gkv_send[at, :qw] = (gk_s[sent, :] + last * gk_near[:WIN]).astype(BF16)
        for h in range(HEADS):
            cols = slice(h * 128, (h + 1) * 128)
            wide = slice(qw + h * 128, qw + (h + 1) * 128)
            gkv_own[at, wide] = gv_near[shifted, cols] + gv_s[h, mine, :]
            gkv_send[at, wide] = (gv_s[h, sent, :] + last * gv_near[:WIN, cols]).astype(BF16)
        return 0

    lax.fori_loop(0, grid_q, back, 0)


def mix_backward(grad_q, grad_kv, rows, gain, bias, w_mix, slab, d_gain, d_bias, carried):
    grad_mixed = jnp.concatenate([grad_q * score_scale(grad_q.shape[1]), grad_kv], axis=1).astype(BF16)
    unit, scale = norm_parts(rows)
    normed = (unit * gain[0:1] + bias[0:1]).astype(BF16)
    add_columns(slab, 0, t_dot(normed, grad_mixed))
    grad_normed = dot_t(grad_mixed, w_mix[...])
    d_gain[...] += col_sum(grad_normed * unit)
    d_bias[...] += col_sum(grad_normed)
    return carried + norm_back(grad_normed, unit, scale, gain[0:1])


def fourth_kernel(
    info, gq, gkv, got, z, gmid, gain_next, bias_next, w_mix_next,
    q, kv, halo, o, lse, active, slope, mid, x, gain, bias, w_mix, w_proj, w_in, w_back,
    cross0, cross1, local0, local1, gq_last, gkv_last, gmid_last, halo_out, keep, send, slab_last,
    dn_gain, dn_bias, d_gain, d_bias, d_gain_first, d_bias_first,
    ext, slab, gq_ext, gk_ext, gv_ext, gmid_ext,
):
    step = pl.program_id(0)
    qw = q.shape[1]
    n = kv.shape[0]

    @pl.when(step == 0)
    def _():
        load_extended(halo, kv, ext)
        for ref in (
            slab, slab_last, dn_gain, dn_bias, d_gain, d_bias, d_gain_first, d_bias_first, gq_ext, gk_ext, gv_ext, gmid_ext
        ):
            ref[...] = jnp.zeros_like(ref)

    limit = info[1]
    start = pl.multiple_of(step * TB, TB)
    base = info[0] * n + start
    grad_kv = gkv[...] + got[...].astype(F32)
    grad_z = mix_backward(
        gq[...], grad_kv, z[...].astype(F32), gain_next, bias_next, w_mix_next, slab, dn_gain, dn_bias, gmid[...]
    )
    grad_low = grad_z.astype(BF16)
    emit_rows(info, step * (TB // WIN), grad_low, False, (cross0, cross1), (local0, local1))
    unit, scale = norm_parts(mid[...])
    normed = (unit * gain[1:2] + bias[1:2]).astype(BF16)
    attended = o[...]
    grad_out, grad_mid = feed_backward(
        grad_low.astype(F32), active[...], slope[...].astype(F32), normed, unit, scale, attended, gain,
        w_proj, w_in, w_back, slab, w_mix_next.size // w_proj.shape[1], d_gain, d_bias,
    )
    shifted = pl.ds(pl.multiple_of(start + WIN, WIN), TB)
    gmid_ext[shifted] = grad_mid
    weighted = grad_out.astype(F32) * attended.astype(F32)
    for sub in range(TB // WIN):
        rows = slice(sub * WIN, (sub + 1) * WIN)
        near = pl.ds(pl.multiple_of(start + sub * WIN, WIN), 2 * WIN)
        delta = jnp.concatenate(
            [jnp.sum(weighted[rows, h * 128 : (h + 1) * 128], axis=-1, keepdims=True) for h in range(HEADS)], axis=0
        )
        g_q, g_k, g_v = near_backward(
            q[rows], ext[near, :qw], ext[near, qw:], grad_out[rows], stack_stat(lse[rows]), delta,
            base + sub * WIN, limit,
        )
        gq_ext[pl.ds(pl.multiple_of(start + (sub + 1) * WIN, WIN), WIN)] = g_q
        gk_ext[near] += g_k
        gv_ext[near] += g_v

    @pl.when(step == 0)
    def _():
        halo_out[...] = jnp.concatenate([gk_ext[:WIN], gv_ext[:WIN]], axis=1).astype(BF16)
        gk_ext[:WIN] = jnp.zeros((WIN, gk_ext.shape[1]), F32)
        gv_ext[:WIN] = jnp.zeros((WIN, gv_ext.shape[1]), F32)

    whole_rows = pl.ds(start, TB)
    grad_x = mix_backward(
        gq_ext[whole_rows], jnp.concatenate([gk_ext[whole_rows], gv_ext[whole_rows]], axis=1),
        x[whole_rows].astype(F32), gain, bias, w_mix, slab_last, d_gain_first, d_bias_first, gmid_ext[whole_rows],
    )
    emit_rows(info, step * (TB // WIN) - 1, grad_x.astype(BF16), True, (cross0, cross1), (local0, local1))

    @pl.when(step == pl.num_programs(0) - 1)
    def _():
        gq_last[...] = gq_ext[n:]
        gkv_last[...] = jnp.concatenate([gk_ext[n:], gv_ext[n:]], axis=1)
        gmid_last[...] = gmid_ext[n:]
        split_slab(info, slab, keep, send)


def fifth_kernel(info, gq, gkv, got, x, gmid, gain, bias, w_mix, slab_in, *refs):
    vectors, squares = refs[:8], refs[8:10]
    cross, local, (keep, send, small, slab, d_gain, d_bias) = refs[-10:-8], refs[-8:-6], refs[-6:]
    slab[...] = slab_in[...]
    d_gain[...] = vectors[0][...]
    d_bias[...] = vectors[4][...]
    n = x.shape[0] - WIN
    grad_x = mix_backward(
        gq[...], gkv[...] + got[...].astype(F32), x[n:].astype(F32), gain, bias, w_mix, slab, d_gain, d_bias, gmid[...]
    )
    emit_rows(info, n // WIN - 1, grad_x.astype(BF16), True, cross, local)
    split_slab(info, slab, keep, send)
    small_rows(info, (d_gain,) + vectors[1:4] + (d_bias,) + vectors[5:], squares, small)
    put_riders(small[...], send, keep.shape[0])


def put_riders(rows, send, at):
    count = rows.shape[0]
    coarse = rows.astype(BF16)
    send[at : at + count] = coarse
    send[at + count :] = (rows - coarse.astype(F32)).astype(BF16)


def riders_of(got, at):
    count = (got.shape[0] - at) // 2
    return got[at : at + count].astype(F32) + got[at + count :].astype(F32)


def stage_kernel(digits, *refs, groups, ways, stage, riders):
    refs = list(refs)
    parts = [(refs.pop(0), [refs.pop(0) for _ in range(count)]) for count in groups]
    small = refs.pop(0) if riders else None
    messages = [refs.pop(0) for _ in range(max(ways - 1, 1))]
    kept_out = refs.pop(0) if ways > 1 else None
    small_out = refs.pop(0) if riders else None
    total = refs.pop(0)
    vectors = small[...] if riders else None
    at = 0
    for kept, got in parts:
        rows = kept.shape[0]
        value = kept[...]
        for g in got:
            value = value + g[:rows].astype(F32)
            if g.shape[0] > rows:
                vectors = vectors + riders_of(g, rows)
        total[at : at + rows] = value
        at += rows
    chunk = at // ways

    def piece(which):
        return total[pl.ds(pl.multiple_of(which * chunk, 16), chunk)]

    mine = digits[9 + stage] if ways > 1 else 0
    for i, message in enumerate(messages):
        message[:chunk] = piece(mine ^ (i + 1) if ways > 1 else 0).astype(BF16)
        if riders:
            put_riders(vectors, message, chunk)
    if ways > 1:
        kept_out[...] = piece(mine)
    if riders:
        small_out[...] = vectors


def exchange_kernel(digits, mine, theirs, rows_out, small_out):
    count = rows_out.shape[0]
    rows_out[...] = (mine[:count].astype(F32) + theirs[:count].astype(F32)).astype(BF16)
    small_out[...] = riders_of(mine, count) + riders_of(theirs, count)


def again_kernel(digits, rows, small, message):
    message[: rows.shape[0]] = rows[...]
    put_riders(small[...], message, rows.shape[0])


def order_kernel(digits, *refs, stage):
    pieces, out = refs[:-1], refs[-1]
    rows = pieces[0].shape[0]
    for c, piece in enumerate(pieces):
        out[pl.ds(pl.multiple_of((digits[9 + stage] ^ c) * rows, 16), rows)] = piece[...]


def assemble_kernel(info, *refs):
    own, other, out, wide, sems = refs[:4], *refs[4:]
    core = info[0]
    rows = out.shape[1]

    def leave(t):
        column = core if t < 4 else 1 - core
        image = (info[5] ^ (t % 4 // 2)) * 4 + column * 2 + (info[4] ^ (t % 2))
        return pltpu.make_async_copy(wide.at[t], out.at[image], sems.at[t])

    for t in range(8):
        if t < 4:
            block = own[t][pl.ds(pl.multiple_of(core * rows, rows), rows)]
        else:
            block = other[t - 4]
        wide[t] = block.astype(F32)
        leave(t).start()
    for t in range(8):
        leave(t).wait()


def hold_kernel(info, first, second, *refs):
    refs[-2][...] = first[...]
    refs[-1][...] = second[...]


def small_rows(info, vectors, squares, out):
    width = out.shape[1]
    once = jnp.where(info[7] == 0, 1.0, 0.0)
    lane = lax.broadcasted_iota(jnp.int32, (1, width), 1)
    out[...] = jnp.zeros_like(out)
    for i, vector in enumerate(vectors):
        out[i : i + 1] = jnp.sum(vector[...], axis=0, keepdims=True) * once
    for i in range(6):
        total = jnp.sum(jnp.sum(squares[i // 3][i % 3], axis=0, keepdims=True), axis=1, keepdims=True)
        out[8 + i : 9 + i] = jnp.where(lane == info[6], total * once, 0.0)


def trade_kernel(info, *refs):
    pieces, out = refs[:4], refs[-1]
    rows = out.shape[1]
    for t in range(4):
        out[t] = pieces[t][pl.ds(pl.multiple_of((1 - info[0]) * rows, rows), rows)]


def unpack_kernel(info, mine, theirs, small, counted, mix, proj, up, down, gain, bias, rms, wide, *, sizes):
    core = info[9]
    wide[core] = mine[...].astype(F32)
    wide[1 - core] = theirs[...].astype(F32)
    rows_a, rows_b, rows_c, ways = sizes
    early = rows_a // 2 // ways
    late = (rows_b + rows_c) // 2 // ways
    rows_mix = rows_c

    def pieces(slab, start, stop):
        total = {"a": rows_a, "b": rows_b, "c": rows_c}[slab] // 2
        size, shift, skip = {"a": (early, 0, 0), "b": (late, early, 0), "c": (late, early, rows_b // 2)}[slab]
        at = start
        while at < stop:
            half, row = at // total, at % total
            along = row + skip
            count = min(stop - at, total - row, size - along % size)
            yield at - start, half, along // size * (early + late) + shift + along % size, count
            at += count

    width = wide.shape[2]
    places = {0: (("c", 0), ("b", rows_mix)), 1: (("b", 0), ("a", 0))}
    for layer in range(2):
        (slab, at), (feed, feed_at) = places[layer]
        for out, name in ((mix, slab), (proj, feed), (up, feed), (down, feed)):
            if name == feed and out is not mix:
                at = feed_at
            rows, cols = out.shape[1:]
            for i in range(cols // width):
                for offset, half, row, count in pieces(name, at + i * rows, at + (i + 1) * rows):
                    out[layer, offset : offset + count, i * width : (i + 1) * width] = wide[half, row : row + count]
            if out is not mix:
                feed_at = at + rows * cols // width
    for layer in range(2):
        for norm in range(2):
            gain[layer, norm : norm + 1] = small[2 * layer + norm : 2 * layer + norm + 1]
            bias[layer, norm : norm + 1] = small[4 + 2 * layer + norm : 5 + 2 * layer + norm]
    images = rms.shape[1]
    sums = pltpu.roll(small[8:16], small.shape[1] - (info[6] - info[6] % images), 1)
    rms[...] = jnp.sqrt(sums[: rms.shape[0], :images] / counted[...])


VMEM = pl.BlockSpec(memory_space=pltpu.VMEM)


def call(kernel, info, operands, specs, outs, out_specs, scratch=(), grid=(), work=0, aliases={}):
    moved = sum(math.prod(a.shape) * a.dtype.itemsize for a in list(operands) + jax.tree.leaves(outs))
    single = not isinstance(outs, list)
    views = list(specs) + ([out_specs] if single else list(out_specs))

    def body_of(info, *refs):
        seen = [view(ref) if callable(view) else ref for view, ref in zip(views, refs)]
        kernel(info, *seen, *refs[len(views) :])

    def plain(view):
        return VMEM if callable(view) else view

    return pl.pallas_call(
        body_of,
        grid_spec=pltpu.PrefetchScalarGridSpec(
            num_scalar_prefetch=1,
            grid=grid,
            in_specs=[plain(v) for v in specs],
            out_specs=plain(out_specs) if single else [plain(v) for v in out_specs],
            scratch_shapes=list(scratch),
        ),
        out_shape=outs,
        input_output_aliases=aliases,
        compiler_params=pltpu.CompilerParams(vmem_limit_bytes=VMEM_LIMIT),
        cost_estimate=pl.CostEstimate(flops=int(work * 1.15e9), bytes_accessed=moved, transcendentals=0),
    )(info, *operands)


def whole(array):
    return VMEM


def tiled(array):
    return lambda ref: ref.at[pl.ds(pl.multiple_of(pl.program_id(0) * TB, TB), TB)]


def tiled_after_window(ref):
    return ref.at[pl.ds(pl.multiple_of(pl.program_id(0) * TB + WIN, WIN), TB)]


def last_rows(ref):
    return ref.at[pl.ds(ref.shape[0] - WIN, WIN)]


ANY = pl.BlockSpec(memory_space=pl.ANY)


def shape(dims, kind):
    return jax.ShapeDtypeStruct(dims, kind)


def after(value, *others):
    return lax.optimization_barrier((value, others))[0]


def body(edge_rows, lengths, norm_gain, norm_bias, w_qkv, w_out, w_up, w_down):
    sections = lax.axis_size("section")
    index = lax.axis_index("section")
    images, rows_dev, width = edge_rows.shape
    seats = 2 * images
    rep = sections // seats
    seat = index // rep
    twin = index % rep
    rows_piece = rows_dev * rep
    qw = (w_qkv.shape[2] - width) // 2
    kvw = w_qkv.shape[2] - qw
    hidden = w_up.shape[2]
    n = rows_piece * images // 2
    quarter = images // 2
    steps = (n // TB,)

    def route(pairs):
        return [(s * rep + e, d * rep + e) for s, d in pairs for e in range(rep)]

    if rep > 1:
        groups = [[s * rep + e for e in range(rep)] for s in range(seats)]
        edge_rows = lax.all_gather(edge_rows, "section", axis_index_groups=groups, axis=1, tiled=True)

    chip = seat // 2
    part = seat % 2
    fz, fl, fy = chip // 4, (chip // 2) % 2, chip % 2
    limit = lengths[chip]
    spot = lax.axis_index("dp") * images + chip
    dp_count = lax.axis_size("dp")
    dp_index = lax.axis_index("dp")

    def partners(masks):
        total = dp_count * sections
        spot = dp_index * sections + index
        digit = sum(((spot // m) % 2) << i for i, m in enumerate(masks))
        routes = []
        for c in range(1, 1 << len(masks)):
            flips = sum(m for i, m in enumerate(masks) if (c >> i) & 1)
            routes.append((c, [(s, s ^ flips) for s in range(total)]))
        return digit, routes

    dp_masks = [sections << b for b in range(dp_count.bit_length() - 1)]
    section_masks = [1 << b for b in range(1, sections.bit_length() - 1)]
    plane = [dp_masks[0], section_masks[0]]
    rest = section_masks[1:] + dp_masks[1:]
    digits = [partners(masks)[0] for masks in [[1], plane] + [[m] for m in rest]]
    counted = (lengths.astype(F32) * width)[None, :]
    info = jnp.stack([part, limit, chip % quarter, fz, fy, fz, spot, twin, index % 2] + digits).astype(jnp.int32)
    swap = route([(s, s ^ 1) for s in range(seats)])

    def bits(s):
        return s // 8, (s // 4) % 2, (s // 2) % 2, s % 2

    by_column = edge_rows.reshape(2, 2, 2, rows_piece, width)
    traded = lax.dynamic_index_in_dim(by_column, 1 - part, 1, keepdims=False).reshape(4, rows_piece, width)
    traded = lax.ppermute(traded, "section", swap)
    column = lax.dynamic_index_in_dim(by_column, part, 1, keepdims=False).reshape(4, rows_piece, width)
    received = [None] * 4
    for t in (2, 3, 0, 1):
        tz, ty = t // 2, t % 2
        image = (fz ^ tz) * 2 + (fy ^ ty)
        own = lax.dynamic_index_in_dim(column, image, 0, keepdims=False)
        got = lax.dynamic_index_in_dim(traded, image, 0, keepdims=False)
        message = jnp.where(part == 0, jnp.concatenate([own, got]), jnp.concatenate([got, own]))
        pairs = []
        for s in range(seats):
            z, l, y, k = bits(s)
            pairs.append((s, ((z ^ tz) * 4 + k * 2 + (y ^ ty)) * 2 + l))
        received[t] = lax.ppermute(message, "section", route(pairs))

    def send_back(message, tz, ty):
        pairs = []
        for s in range(seats):
            z, l, y, p = bits(s)
            pairs.append((s, ((z ^ tz) * 4 + p * 2 + (y ^ ty)) * 2 + l))
        return lax.ppermute(message, "section", route(pairs))

    def trade(got, *awaited):
        out = shape((4, rows_piece, width), BF16)
        send = call(trade_kernel, info, got + list(awaited), [VMEM] * 4 + [ANY] * len(awaited), out, VMEM)
        return lax.ppermute(send, "section", swap)

    first_to_second = route([(2 * c, 2 * c + 1) for c in range(images)])
    second_to_first = route([(2 * c + 1, 2 * c) for c in range(images)])

    dma = pltpu.SemaphoreType.DMA
    rows_q = shape((n, qw), BF16)
    rows_kv = shape((n, kvw), BF16)
    rows_low = shape((n, width), BF16)
    rows_wide = shape((n, width), F32)
    rows_stat = shape((n, 128), F32)
    rows_hidden = shape((n, hidden), BF16)
    grad_k_shape = shape((n + WIN, qw), F32)
    grad_v_shape = shape((n + WIN, width), F32)
    mix_rows = w_qkv.shape[1] * w_qkv.shape[2] // width
    feed_rows = (w_out[0].size + w_up[0].size + w_down[0].size) // width
    vec_shape = shape((8, width), F32)
    squares_shape = shape((3, 8, width), F32)
    ext = pltpu.VMEM((n + WIN, kvw), BF16)

    g0, g1, b0, b1 = norm_gain[0], norm_gain[1], norm_bias[0], norm_bias[1]

    halo_shape = shape((WIN, kvw), BF16)
    outs = [shape((n + WIN, width), BF16), rows_q, rows_kv, halo_shape]
    x, q0, kv0, halo0 = call(
        first_kernel, info, received + [g0, b0, w_qkv[0]], [ANY] * 4 + [whole(g0), whole(b0), whole(w_qkv[0])],
        outs, [whole(o) for o in outs], [dma((2,))], work=6,
    )
    halo0 = lax.ppermute(halo0, "section", first_to_second)

    outs = [rows_low, rows_q, rows_kv, rows_low, rows_stat, rows_hidden, rows_hidden, rows_wide, squares_shape]
    z, q1, kv1, o0, lse0, active0, slope0, mid0, squares0 = call(
        second_kernel, info, [x, q0, kv0, halo0, g0, b0, w_out[0], w_up[0], w_down[0], g1, b1, w_qkv[1]],
        [tiled_after_window, tiled(q0)] + [whole(a) for a in (kv0, halo0, g0, b0, w_out[0], w_up[0], w_down[0], g1, b1, w_qkv[1])],
        outs, [tiled(o) for o in outs[:-1]] + [whole(outs[-1])], [ext], steps, work=15,
    )
    kv_other = lax.ppermute(kv1, "section", first_to_second)

    rows_k_all = shape((2 * n, qw), BF16)
    rows_v_all = shape((2 * n, width), BF16)
    outs = [rows_q, rows_k_all, rows_v_all, rows_wide, rows_stat]
    qr, kr, vr, o_far, lse_far = call(
        far_forward_kernel, info, [q1, kv1, kv_other], [whole(a) for a in (q1, kv1, kv_other)],
        outs, [whole(o) for o in outs],
        [pltpu.VMEM((n, qw), F32), pltpu.VMEM((2 * n, qw), F32), pltpu.VMEM((HEADS, 2 * n, 128), F32),
         pltpu.VMEM((HEADS, n, 128), F32), pltpu.VMEM((n, 128), F32)], work=14,
    )

    message = shape((2 * rows_piece, width), BF16)
    outs = [message] * 4 + [rows_low, rows_stat, shape((n, qw), F32), grad_k_shape, grad_v_shape, rows_wide,
            shape((feed_rows // 2, width), F32), shape((feed_rows // 2, width), BF16),
            vec_shape, vec_shape, squares_shape]
    (cross0, cross1, local0, local1, go1, stat1, gq_near, gk_near, gv_near, gmid1, keep_a, send_a,
     d_gain11, d_bias11, squares1) = call(
        third_kernel, info,
        received + [q1, kv1, kv_other, o_far, lse_far, z, g1, b1, w_out[1], w_up[1], w_down[1]],
        [ANY] * 4
        + [tiled(q1), whole(kv1), last_rows]
        + [tiled(o_far), tiled(lse_far), tiled(z)]
        + [whole(a) for a in (g1, b1, w_out[1], w_up[1], w_down[1])],
        outs,
        [whole(message)] * 4 + [tiled(o) for o in outs[4:7]] + [whole(outs[7]), whole(outs[8]), tiled(outs[9])]
        + [whole(o) for o in outs[10:]],
        [ext, pltpu.VMEM((n, width), BF16), pltpu.VMEM((feed_rows, width), F32), dma((2,))], steps, work=24,
    )
    forward_back = [None, None, send_back(cross0, 1, 0), None]

    outs = [shape((n, qw), F32), shape((n, kvw), F32), rows_kv]
    operands = [qr, kr, vr, go1, stat1, gq_near, gk_near, gv_near]
    gq1, gkv1, gkv_send = call(
        far_backward_kernel, info, operands, [whole(a) for a in operands], outs, [whole(o) for o in outs],
        [pltpu.VMEM((HEADS, n, 128), F32), pltpu.VMEM((n, 128), F32), pltpu.VMEM((n, qw), F32),
         pltpu.VMEM((2 * n, qw), F32), pltpu.VMEM((HEADS, 2 * n, 128), F32)], work=18,
    )
    def pair(message):
        return lax.ppermute(message, ("dp", "section"), partners([1])[1][0][1])

    def send_all(messages, masks):
        return [lax.ppermute(m, ("dp", "section"), way) for m, (_, way) in zip(messages, partners(masks)[1])]

    small_shape = shape((16, width), F32)
    rider_rows = 2 * small_shape.shape[0]

    def stage(groups, small, ways, number):
        operands = [a for kept, got in groups for a in [kept] + got] + ([] if small is None else [small])
        rows = sum(kept.shape[0] for kept, _ in groups)
        riders = small is not None
        outs = [shape((rows // ways + rider_rows * riders, width), BF16)] * max(ways - 1, 1)
        outs += [shape((rows // ways, width), F32)] * (ways > 1) + [small_shape] * riders
        kernel = functools.partial(
            stage_kernel, groups=[len(got) for _, got in groups], ways=ways, stage=number, riders=riders
        )
        made = call(
            kernel, info, operands, [VMEM] * len(operands), outs, [VMEM] * len(outs), [pltpu.VMEM((rows, width), F32)]
        )
        sent = max(ways - 1, 1)
        return made[:sent], made[sent] if ways > 1 else None, made[-1] if riders else None

    def gather(piece, masks, number):
        pieces = [piece] + [lax.ppermute(piece, ("dp", "section"), way) for _, way in partners(masks)[1]]
        out = shape((len(pieces) * piece.shape[0], width), BF16)
        return call(functools.partial(order_kernel, stage=number), info, pieces, [VMEM] * len(pieces), out, VMEM)

    messages, kept_a, _ = stage([(keep_a, [pair(send_a)])], None, 4, 1)
    got_a = send_all(messages, plane)
    gkv_got = lax.ppermute(after(gkv_send, forward_back[2], *got_a), "section", second_to_first)
    forward_back[3] = send_back(after(cross1, forward_back[2]), 1, 1)
    forward_back[0] = send_back(after(local0, forward_back[2]), 0, 0)
    forward_back[1] = send_back(after(local1, forward_back[2]), 0, 1)

    slab_rows = mix_rows + feed_rows
    early_shape = slab_rows // 2, width
    mix_slab = shape((mix_rows, width), F32)
    outs = [message] * 4 + [shape((WIN, qw), F32), shape((WIN, kvw), F32), shape((WIN, width), F32), halo_shape,
            shape(early_shape, F32), shape(early_shape, BF16), mix_slab] + [vec_shape] * 6
    operands = [gq1, gkv1, gkv_got, z, gmid1, g1, b1, w_qkv[1], q0, kv0, halo0, o0, lse0, active0, slope0, mid0, x, g0,
                b0, w_qkv[0], w_out[0], w_up[0], w_down[0]]
    (cross0, cross1, local0, local1, gq_last, gkv_last, gmid_last, halo_send, keep_early, send_early, slab_last,
     d_gain10, d_bias10, d_gain01, d_bias01, d_gain00, d_bias00) = call(
        fourth_kernel, info, operands,
        [tiled(a) for a in operands[:5]] + [VMEM] * 3 + [tiled(q0), VMEM, VMEM] + [tiled(a) for a in operands[11:16]]
        + [VMEM] * 7,
        outs, [VMEM] * len(outs),
        [ext, pltpu.VMEM((slab_rows, width), F32), pltpu.VMEM((n + WIN, qw), F32), pltpu.VMEM((n + WIN, qw), F32),
         pltpu.VMEM((n + WIN, width), F32), pltpu.VMEM((n + WIN, width), F32)], steps, work=20,
    )
    outs = [halo_shape, shape(early_shape, BF16)]
    halo_send, send_early = call(
        hold_kernel, info, [halo_send, send_early] + forward_back, [VMEM] * 2 + [ANY] * 4, outs, [VMEM] * 2
    )
    halo_got = lax.ppermute(halo_send, "section", second_to_first)

    got_early = pair(send_early)
    outs = [message] * 4 + [shape((mix_rows // 2, width), F32), shape((mix_rows // 2 + rider_rows, width), BF16), small_shape]
    operands = [gq_last, gkv_last, halo_got, x, gmid_last, g0, b0, w_qkv[0], slab_last]
    operands += [d_gain00, d_gain01, d_gain10, d_gain11, d_bias00, d_bias01, d_bias10, d_bias11, squares0, squares1]
    aliases = {1 + len(operands) + i: i for i in range(4)}
    operands += [cross0, cross1, local0, local1]
    cross0, cross1, local0, local1, keep_late, send_late, small = call(
        fifth_kernel, info, operands, [VMEM] * len(operands), outs, [VMEM] * len(outs),
        [pltpu.VMEM((mix_rows, width), F32), pltpu.VMEM((8, width), F32), pltpu.VMEM((8, width), F32)],
        aliases=aliases,
    )

    def assemble(own, other):
        out = call(
            assemble_kernel, info, own + [other], [VMEM] * 5, shape((images, rows_piece, width), F32), ANY,
            [pltpu.VMEM((images, rows_piece, width), F32), dma((images,))],
        )
        if rep > 1:
            out = lax.dynamic_slice_in_dim(out, twin * rows_dev, rows_dev, 1)
        return out

    backward_back = [send_back(local0, 0, 0), None, send_back(cross0, 1, 0), None]
    groups = [(keep_early, [got_early]), (keep_late, [pair(send_late)])]
    messages, kept, small = stage(groups, small, 4, 1)
    forward_trade = trade(forward_back, send_late)
    forward_rows = assemble(forward_back, forward_trade)
    groups = [(kept_a, got_a), (kept, send_all(messages, plane))]
    number = 2
    scattered = []
    while number - 1 < len(rest) and sum(kept.shape[0] for kept, _ in groups) % 32 == 0:
        messages, kept, small = stage(groups, small, 2, number)
        groups = [(kept, send_all(messages, [rest[number - 2]]))]
        scattered.append(number)
        number += 1
    scattered_rows = groups[-1][1]
    backward_back[3] = send_back(after(cross1, backward_back[2], *scattered_rows, forward_rows), 1, 1)
    backward_back[1] = send_back(after(local1, backward_back[2], *scattered_rows, forward_rows), 0, 1)
    (both,), _, small = stage(groups, small, 1, 0)
    both = after(both, backward_back[0], backward_back[2])
    rows_shape = shape((both.shape[0] - rider_rows, width), BF16)
    while number - 2 < len(rest):
        (got,) = send_all([both], [rest[number - 2]])
        rows, small = call(exchange_kernel, info, [both, got], [VMEM] * 2, [rows_shape, small_shape], [VMEM] * 2)
        number += 1
        if number - 2 < len(rest):
            both = call(again_kernel, info, [rows, small], [VMEM] * 2, shape(both.shape, BF16), VMEM)
    both = after(rows, backward_back[1], backward_back[3])
    for number in scattered[::-1]:
        both = gather(both, [rest[number - 2]], number)
    backward_trade = trade(backward_back, rows)
    both = gather(both, plane, 1)
    both = after(both, backward_trade)
    theirs = pair(both)
    backward_rows = assemble(backward_back, backward_trade)
    outs = [shape(w.shape, F32) for w in (w_qkv, w_out, w_up, w_down, norm_gain, norm_bias)] + [shape((6, images), F32)]
    sizes = (feed_rows, slab_rows, mix_rows, 1 << len(plane))
    grads = call(
        functools.partial(unpack_kernel, sizes=sizes), info, [both, theirs, small, counted],
        [VMEM] * 4, outs, [whole(o) for o in outs],
        [pltpu.VMEM((2,) + both.shape, F32)],
    )
    return (forward_rows, backward_rows, grads[6], grads[4], grads[5]) + tuple(grads[:4])


def solution(mesh):
    placed = (P("dp", "section", None), P("dp"), P(), P(), P(), P(), P(), P())
    return jax.shard_map(
        body,
        mesh=mesh,
        in_specs=placed,
        out_specs=(P("dp", "section", None), P("dp", "section", None), P(None, "dp"), P(), P(), P(), P(), P(), P()),
        check_vma=False,
    )
```

```python
import functools
import math

import jax
import jax.numpy as jnp
from jax import lax
from jax.experimental import pallas as pl
from jax.experimental.pallas import tpu as pltpu
from jax.sharding import PartitionSpec as P

HEADS = 2
WIN = 128
STRIDE = 128
NEG = -1e30
F32 = jnp.float32
BF16 = jnp.bfloat16
TB = 768
RES = 8
UNROLL = 16
RES_BACK = 16
UNROLL_BACK = 8
VMEM_LIMIT = 16 * 1024 * 1024


def dot(left, right):
    return lax.dot_general(left, right, (((1,), (0,)), ((), ())), preferred_element_type=F32)


def dot_t(left, right):
    return lax.dot_general(left, right, (((1,), (1,)), ((), ())), preferred_element_type=F32)


def t_dot(left, right):
    return lax.dot_general(left, right, (((0,), (0,)), ((), ())), preferred_element_type=F32)


def score_scale(query_width):
    return 1.0 / math.sqrt(query_width // HEADS)


def norm_parts(rows):
    centre = rows - jnp.mean(rows, axis=-1, keepdims=True)
    scale = lax.rsqrt(jnp.mean(centre * centre, axis=-1, keepdims=True) + 1e-05)
    return centre * scale, scale


def norm_back(grad, unit, scale, gain):
    scaled = grad * gain
    first = jnp.mean(scaled, axis=-1, keepdims=True)
    second = jnp.mean(scaled * unit, axis=-1, keepdims=True)
    return scale * (scaled - first - unit * second)


def col_sum(rows):
    return jnp.sum(rows.reshape(rows.shape[0] // 8, 8, rows.shape[1]), axis=0)


def gelu_pair(hidden):
    c0 = math.sqrt(2.0 / math.pi)
    square = hidden * hidden
    share = 0.5 + 0.5 * jnp.tanh(hidden * (c0 + (c0 * 0.044715) * square))
    active = hidden * share
    slope = share + active * (1.0 - share) * (2.0 * c0 + (6.0 * c0 * 0.044715) * square)
    return active, slope


def head_split(rows):
    lane = lax.broadcasted_iota(jnp.int32, rows.shape, 1)
    zero = jnp.zeros_like(rows)
    low = lane < rows.shape[1] // HEADS
    return jnp.concatenate([jnp.where(low, rows, zero), jnp.where(low, zero, rows)], axis=0)


def head_join(stacked):
    half = stacked.shape[0] // 2
    lane = lax.broadcasted_iota(jnp.int32, (half, stacked.shape[1]), 1)
    return jnp.where(lane < stacked.shape[1] // HEADS, stacked[:half], stacked[half:])


def near_masks(base, limit):
    row = lax.broadcasted_iota(jnp.int32, (2 * WIN, WIN), 0)
    row = jnp.where(row >= WIN, row - WIN, row)
    col = lax.broadcasted_iota(jnp.int32, (2 * WIN, WIN), 1)
    own = col <= row
    key = base + col - jnp.where(own, 0, WIN)
    allowed = (key >= 0) & ((key < limit) | (col == row))
    return own, allowed


def near_scores(split_q, keys, own, allowed):
    scores = dot_t(split_q, keys)
    folded = jnp.where(own, scores[:, WIN:], scores[:, :WIN])
    return jnp.where(allowed, folded, NEG)


def unfold(folded, own):
    return jnp.concatenate([jnp.where(own, 0.0, folded), jnp.where(own, folded, 0.0)], axis=1).astype(BF16)


def near_forward(queries, keys, values, base, limit):
    own, allowed = near_masks(base, limit)
    scores = near_scores(head_split(queries), keys, own, allowed)
    largest = jnp.max(scores, axis=-1, keepdims=True)
    powers = jnp.exp(scores - largest)
    total = jnp.sum(powers, axis=-1, keepdims=True)
    weights = unfold(powers, own)
    hd = values.shape[1] // HEADS
    out = [dot(weights[h * WIN : (h + 1) * WIN], values[:, h * hd : (h + 1) * hd]) for h in range(HEADS)]
    return out, largest, total, powers


def near_backward(queries, keys, values, grad_out, log_total, delta, base, limit, weights=None):
    own, allowed = near_masks(base, limit)
    split_q = head_split(queries)
    if weights is None:
        weights = jnp.exp(near_scores(split_q, keys, own, allowed) - log_total)
    hd = values.shape[1] // HEADS
    pull = jnp.concatenate(
        [dot_t(grad_out[:, h * hd : (h + 1) * hd], values[:, h * hd : (h + 1) * hd]) for h in range(HEADS)], axis=0
    )
    pull = jnp.where(own, pull[:, WIN:], pull[:, :WIN])
    slope = weights * (pull - delta)
    grad_q = head_join(dot(unfold(slope, own), keys))
    row = lax.broadcasted_iota(jnp.int32, (WIN, 2 * WIN), 0)
    col = lax.broadcasted_iota(jnp.int32, (WIN, 2 * WIN), 1)
    here = (row <= jnp.where(col >= WIN, col - WIN, col)).astype(F32).astype(BF16)

    def turned(folded):
        flat = folded.astype(BF16).T
        current = flat * here
        return jnp.concatenate([flat - current, current], axis=0)

    grad_k = dot(turned(slope), split_q)
    weights = turned(weights)
    grad_v = jnp.concatenate(
        [dot(weights[:, h * WIN : (h + 1) * WIN], grad_out[:, h * hd : (h + 1) * hd]) for h in range(HEADS)], axis=1
    )
    return grad_q, grad_k, grad_v


def stack_stat(stat, width=128):
    return jnp.concatenate([stat[:, 0:1], stat[:, width // 2 : width // 2 + 1]], axis=0)


def spread_stat(stacked, width=128):
    half = stacked.shape[0] // 2
    lane = lax.broadcasted_iota(jnp.int32, (half, width), 1)
    return jnp.where(lane < width // 2, stacked[:half], stacked[half:])


def masked_squares(rows, base, limit):
    pos = base + lax.broadcasted_iota(jnp.int32, (rows.shape[0], 1), 0)
    return col_sum(jnp.where(pos < limit, rows * rows, 0.0))


def pick_piece(info, pieces, low, block, target):
    for t, piece in enumerate(pieces):
        tz, ty = t // 2, t % 2

        @pl.when(((block ^ info[4]) == ty) & ((info[5] ^ (0 if low else 1)) == tz))
        def _():
            target[...] = piece[...]


def emit_block(info, block, rows, to_lower, first, cross, local):
    stays = info[5] == (0 if to_lower else 1)
    at = slice(first, first + rows.shape[0])
    for ty in range(2):
        fits = (block ^ info[4]) == ty

        @pl.when(fits & stays)
        def _():
            local[ty][at] = rows

        @pl.when(fits & jnp.logical_not(stays))
        def _():
            cross[ty][at] = rows


def emit_rows(info, first, rows, to_lower, cross, local):
    units = cross[0].shape[0] // WIN
    stays = info[5] == (0 if to_lower else 1)
    for sub in range(rows.shape[0] // WIN):
        number = first + sub
        block = number // units
        at = pl.ds(pl.multiple_of((number - block * units) * WIN, WIN), WIN)
        value = rows[sub * WIN : (sub + 1) * WIN]
        for ty in range(2):
            fits = (block ^ info[4]) == ty

            @pl.when(fits & stays)
            def _():
                local[ty][at] = value

            @pl.when(fits & jnp.logical_not(stays))
            def _():
                cross[ty][at] = value


def split_slab(info, slab, keep, send):
    once = jnp.where(info[7] == 0, 1.0, 0.0)
    half = keep.shape[0]
    mine = info[8]
    keep[...] = slab[pl.ds(pl.multiple_of(mine * half, 8), half)] * once
    send[:half] = (slab[pl.ds(pl.multiple_of((1 - mine) * half, 8), half)] * once).astype(BF16)


def first_kernel(info, *refs):
    pieces = refs[:4]
    gain, bias, w_mix, x_out, q_out, kv_out, halo_out = refs[4:]
    for half in range(2):
        pick_piece(info, pieces, True, half, x_out.at[pl.ds(WIN + half * pieces[0].shape[0], pieces[0].shape[0])])
    x_out[:WIN] = jnp.zeros((WIN, x_out.shape[1]), BF16)
    qw = q_out.shape[1]

    def block(i, _):
        at = pl.ds(pl.multiple_of(i * TB, TB), TB)
        unit, _ = norm_parts(x_out[pl.ds(pl.multiple_of(i * TB + WIN, WIN), TB)].astype(F32))
        normed = (unit * gain[0:1] + bias[0:1]).astype(BF16)
        mixed = dot(normed, w_mix[...])
        q_out[at] = (mixed[:, :qw] * score_scale(qw)).astype(BF16)
        kv_out[at] = mixed[:, qw:].astype(BF16)
        return 0

    lax.fori_loop(0, q_out.shape[0] // TB, block, 0)
    halo_out[...] = kv_out[kv_out.shape[0] - WIN :]


def load_extended(halo, kv, ext):
    ext[: halo.shape[0]] = halo[...]
    ext[halo.shape[0] :] = kv[...]


def second_kernel(
    info, x, q, kv, halo, gain, bias, w_proj, w_in, w_back, gain_next, bias_next, w_mix_next,
    z_out, q_next, kv_next, o_out, lse_out, active_out, slope_out, mid_out, squares, ext,
):
    step = pl.program_id(0)
    qw = q.shape[1]
    n = kv.shape[0]

    @pl.when(step == 0)
    def _():
        load_extended(halo, kv, ext)
        squares[...] = jnp.zeros_like(squares)

    limit = info[1]
    start = step * TB
    base = info[0] * n + start
    outs = []
    for sub in range(TB // WIN):
        near = pl.ds(pl.multiple_of(start + sub * WIN, WIN), 2 * WIN)
        keys = ext[near, :qw]
        values = ext[near, qw:]
        queries = q[sub * WIN : (sub + 1) * WIN]
        out, largest, total, _ = near_forward(queries, keys, values, base + sub * WIN, limit)
        inverse = 1.0 / total
        lse_out[sub * WIN : (sub + 1) * WIN] = spread_stat(largest + jnp.log(total))
        outs.append(jnp.concatenate([out[0] * inverse[:WIN], out[1] * inverse[WIN:]], axis=1))
    attended = jnp.concatenate(outs, axis=0).astype(BF16)
    o_out[...] = attended
    stream = x[...].astype(F32)
    branch = dot(attended, w_proj[...])
    middle = stream + branch
    mid_out[...] = middle
    unit, _ = norm_parts(middle)
    normed = (unit * gain[1:2] + bias[1:2]).astype(BF16)
    active, slope = gelu_pair(dot(normed, w_in[...]))
    active = active.astype(BF16)
    active_out[...] = active
    slope_out[...] = slope.astype(BF16)
    feed = dot(active, w_back[...])
    z = (middle + feed).astype(BF16)
    z_out[...] = z
    squares[0] += masked_squares(stream, base, limit)
    squares[1] += masked_squares(branch, base, limit)
    squares[2] += masked_squares(feed, base, limit)
    unit, _ = norm_parts(z.astype(F32))
    normed = (unit * gain_next[0:1] + bias_next[0:1]).astype(BF16)
    mixed = dot(normed, w_mix_next[...])
    q_next[...] = (mixed[:, :qw] * score_scale(qw)).astype(BF16)
    kv_next[...] = mixed[:, qw:].astype(BF16)


def far_mask(grid_q, grid_k, part_grid, residues):
    shape = (HEADS * residues * grid_q, residues * grid_k)
    row = lax.broadcasted_iota(jnp.int32, shape, 0)
    col = lax.broadcasted_iota(jnp.int32, shape, 1)
    row = jnp.where(row >= residues * grid_q, row - residues * grid_q, row)
    row_res = jnp.zeros(shape, jnp.int32)
    col_res = jnp.zeros(shape, jnp.int32)
    for r in range(1, residues):
        row_res += (row >= r * grid_q).astype(jnp.int32)
        col_res += (col >= r * grid_k).astype(jnp.int32)
    row_grid = row - row_res * grid_q + part_grid
    col_grid = col - col_res * grid_k
    allowed = (row_res == col_res) & (col_grid < row_grid)
    return allowed, col_grid * STRIDE + col_res


def far_forward_kernel(info, q, kv, other, qr, kr, vr, o_far, lse_far, q_s, k_s, v_s, o_s, lse_s):
    n, qw = q.shape
    grid_q = n // STRIDE
    grid_k = 2 * grid_q
    part = info[0]
    limit = info[1]

    def place(g, _):
        at = pl.ds(pl.multiple_of(g * STRIDE, STRIDE), STRIDE)
        own = kv[at].astype(F32)
        early = jnp.where(part == 0, own, other[at].astype(F32))
        q_s[pl.ds(g, STRIDE, stride=grid_q), :] = q[at].astype(F32)
        k_s[pl.ds(g, STRIDE, stride=grid_k), :] = early[:, :qw]
        k_s[pl.ds(g + grid_q, STRIDE, stride=grid_k), :] = own[:, :qw]
        hd = v_s.shape[1]
        for h in range(HEADS):
            v_s[h, pl.ds(g, STRIDE, stride=grid_k), :] = early[:, qw + h * 128 : qw + (h + 1) * 128]
            v_s[h, pl.ds(g + grid_q, STRIDE, stride=grid_k), :] = own[:, qw + h * 128 : qw + (h + 1) * 128]
        return 0

    lax.fori_loop(0, grid_q, place, 0)
    base_mask, key_pos = far_mask(grid_q, grid_k, part * grid_q, RES)
    rows_q = RES * grid_q
    rows_k = RES * grid_k

    def one(i):
        at_q = pl.ds(pl.multiple_of(i * rows_q, rows_q), rows_q)
        at_k = pl.ds(pl.multiple_of(i * rows_k, rows_k), rows_k)
        queries = q_s[at_q].astype(BF16)
        keys = k_s[at_k].astype(BF16)
        values = [v_s[h, at_k].astype(BF16) for h in range(HEADS)]
        qr[at_q] = queries
        kr[at_k] = keys
        for h in range(HEADS):
            vr[at_k, h * 128 : (h + 1) * 128] = values[h]
        allowed = base_mask & (key_pos + i * RES < limit)
        scores = jnp.where(allowed, dot_t(head_split(queries), keys), NEG)
        largest = jnp.max(scores, axis=-1, keepdims=True)
        powers = jnp.where(allowed, jnp.exp(scores - largest), 0.0)
        total = jnp.sum(powers, axis=-1, keepdims=True)
        safe = jnp.maximum(total, 1e-30)
        weights = (powers * (1.0 / safe)).astype(BF16)
        lse = jnp.where(total > 0.0, largest + jnp.log(safe), NEG)
        lse_s[at_q] = spread_stat(lse)
        for h in range(HEADS):
            o_s[h, at_q] = dot(weights[h * rows_q : (h + 1) * rows_q], values[h])

    def group(i, _):
        for u in range(UNROLL):
            one(i * UNROLL + u)
        return 0

    lax.fori_loop(0, STRIDE // RES // UNROLL, group, 0)

    def back(g, _):
        at = pl.ds(pl.multiple_of(g * STRIDE, STRIDE), STRIDE)
        pick = pl.ds(g, STRIDE, stride=grid_q)
        lse_far[at] = lse_s[pick, :]
        for h in range(HEADS):
            o_far[at, h * 128 : (h + 1) * 128] = o_s[h, pick, :]
        return 0

    lax.fori_loop(0, grid_q, back, 0)


def third_kernel(
    info, *refs,
):
    pieces = refs[:4]
    (q, kv, halo, o_far, lse_far, z, gain, bias, w_proj, w_in, w_back,
     cross0, cross1, local0, local1, go_out, stat_out, gq_out, gk_out, gv_out, gmid_out, keep, send,
     d_gain, d_bias, squares, ext, cot, slab) = refs[4:]
    step = pl.program_id(0)
    qw = q.shape[1]
    n = kv.shape[0]

    @pl.when(step == 0)
    def _():
        load_extended(halo, kv, ext)
        for ref in (squares, gk_out, gv_out, slab, d_gain, d_bias):
            ref[...] = jnp.zeros_like(ref)

    limit = info[1]
    start = pl.multiple_of(step * TB, TB)
    base = info[0] * n + start
    outs = []
    logs = []
    weights = []
    for sub in range(TB // WIN):
        rows = slice(sub * WIN, (sub + 1) * WIN)
        near = pl.ds(pl.multiple_of(start + sub * WIN, WIN), 2 * WIN)
        out, largest, total, powers = near_forward(q[rows], ext[near, :qw], ext[near, qw:], base + sub * WIN, limit)
        far_log = stack_stat(lse_far[rows])
        top = jnp.maximum(largest, far_log)
        near_share = jnp.exp(largest - top)
        far_share = jnp.exp(far_log - top)
        whole = total * near_share + far_share
        inverse = 1.0 / whole
        near_share = near_share * inverse
        far_share = far_share * inverse
        weights.append(powers * near_share)
        logs.append(top + jnp.log(whole))
        far = o_far[rows]
        outs.append(
            jnp.concatenate(
                [
                    out[h] * near_share[h * WIN : (h + 1) * WIN]
                    + far[:, h * 128 : (h + 1) * 128] * far_share[h * WIN : (h + 1) * WIN]
                    for h in range(HEADS)
                ],
                axis=1,
            )
        )
    attended_wide = jnp.concatenate(outs, axis=0)
    attended = attended_wide.astype(BF16)
    stream = z[...].astype(F32)
    branch = dot(attended, w_proj[...])
    middle = stream + branch
    unit, scale = norm_parts(middle)
    normed = (unit * gain[1:2] + bias[1:2]).astype(BF16)
    active, slope = gelu_pair(dot(normed, w_in[...]))
    active = active.astype(BF16)
    feed = dot(active, w_back[...])
    emit_block(info, step, z[...], True, 0, (cross0, cross1), (local0, local1))
    emit_block(info, step, (middle + feed).astype(BF16), False, 0, (cross0, cross1), (local0, local1))
    pick_piece(info, pieces, False, step, cot)
    squares[0] += masked_squares(stream, base, limit)
    squares[1] += masked_squares(branch, base, limit)
    squares[2] += masked_squares(feed, base, limit)

    pos = base + lax.broadcasted_iota(jnp.int32, (TB, 1), 0)
    upstream = jnp.where(pos < limit, cot[...].astype(F32), 0.0)
    grad_out, grad_mid = feed_backward(
        upstream, active, slope, normed, unit, scale, attended, gain, w_proj, w_in, w_back, slab, 0, d_gain, d_bias
    )
    gmid_out[...] = grad_mid
    go_out[...] = grad_out
    weighted = grad_out.astype(F32) * attended_wide
    for sub in range(TB // WIN):
        rows = slice(sub * WIN, (sub + 1) * WIN)
        near = pl.ds(pl.multiple_of(start + sub * WIN, WIN), 2 * WIN)
        delta = jnp.concatenate(
            [jnp.sum(weighted[rows, h * 128 : (h + 1) * 128], axis=-1, keepdims=True) for h in range(HEADS)], axis=0
        )
        stat_out[rows] = pack_stats(logs[sub], delta)
        gq, gk, gv = near_backward(
            q[rows], ext[near, :qw], ext[near, qw:], grad_out[rows], logs[sub], delta, base + sub * WIN, limit,
            weights[sub],
        )
        gq_out[rows] = gq
        gk_out[near] += gk
        gv_out[near] += gv

    @pl.when(step == pl.num_programs(0) - 1)
    def _():
        split_slab(info, slab, keep, send)


def pack_stats(lse, delta):
    half = lse.shape[0] // 2
    lane = lax.broadcasted_iota(jnp.int32, (half, 128), 1)
    low = jnp.where(lane < 32, lse[:half], lse[half:])
    high = jnp.where(lane < 96, delta[:half], delta[half:])
    return jnp.where(lane < 64, low, high)


def add_columns(slab, at, grad):
    rows, cols = grad.shape
    width = slab.shape[1]
    for i in range(cols // width):
        slab[at + i * rows : at + (i + 1) * rows] += grad[:, i * width : (i + 1) * width]


def feed_backward(
    upstream, active, slope, normed, unit, scale, attended, gain, w_proj, w_in, w_back, slab, at, d_gain, d_bias,
):
    low = upstream.astype(BF16)
    width = low.shape[1]
    hidden = active.shape[1]
    slab[at + width + hidden : at + width + 2 * hidden] += t_dot(active, low)
    grad_hidden = (dot_t(low, w_back[...]) * slope).astype(BF16)
    add_columns(slab, at + width, t_dot(normed, grad_hidden))
    grad_normed = dot_t(grad_hidden, w_in[...])
    d_gain[...] += col_sum(grad_normed * unit)
    d_bias[...] += col_sum(grad_normed)
    grad_mid = upstream + norm_back(grad_normed, unit, scale, gain[1:2])
    branch_low = grad_mid.astype(BF16)
    slab[at : at + width] += t_dot(attended, branch_low)
    grad_out = dot_t(branch_low, w_proj[...]).astype(BF16)
    return grad_out, grad_mid


def far_backward_kernel(
    info, qr, kr, vr, go, stat, gq_near, gk_near, gv_near, gq_out, gkv_own, gkv_send,
    go_s, stat_s, gq_s, gk_s, gv_s,
):
    n, qw = gq_near.shape
    grid_q = n // STRIDE
    grid_k = 2 * grid_q
    part = info[0]
    limit = info[1]

    def place(g, _):
        at = pl.ds(pl.multiple_of(g * STRIDE, STRIDE), STRIDE)
        pick = pl.ds(g, STRIDE, stride=grid_q)
        rows = go[at].astype(F32)
        for h in range(HEADS):
            go_s[h, pick, :] = rows[:, h * 128 : (h + 1) * 128]
        stat_s[pick, :] = stat[at]
        return 0

    lax.fori_loop(0, grid_q, place, 0)
    base_mask, key_pos = far_mask(grid_q, grid_k, part * grid_q, RES_BACK)
    rows_q = RES_BACK * grid_q
    rows_k = RES_BACK * grid_k

    def one(i):
        at_q = pl.ds(pl.multiple_of(i * rows_q, rows_q), rows_q)
        at_k = pl.ds(pl.multiple_of(i * rows_k, rows_k), rows_k)
        keys = kr[at_k]
        split_q = head_split(qr[at_q])
        grads = [go_s[h, at_q].astype(BF16) for h in range(HEADS)]
        stats = stat_s[at_q]
        lse = jnp.concatenate([stats[:, 0:1], stats[:, 32:33]], axis=0)
        delta = jnp.concatenate([stats[:, 64:65], stats[:, 96:97]], axis=0)
        allowed = base_mask & (key_pos + i * RES_BACK < limit)
        weights = jnp.exp(jnp.where(allowed, dot_t(split_q, keys), NEG) - lse)
        pull = jnp.concatenate([dot_t(grads[h], vr[at_k, h * 128 : (h + 1) * 128]) for h in range(HEADS)], axis=0)
        slope = (weights * (pull - delta)).astype(BF16)
        weights = weights.astype(BF16)
        gq_s[at_q] = head_join(dot(slope, keys))
        gk_s[at_k] = t_dot(slope, split_q)
        for h in range(HEADS):
            gv_s[h, at_k] = t_dot(weights[h * rows_q : (h + 1) * rows_q], grads[h])

    def group(i, _):
        for u in range(UNROLL_BACK):
            one(i * UNROLL_BACK + u)
        return 0

    lax.fori_loop(0, STRIDE // RES_BACK // UNROLL_BACK, group, 0)

    def back(g, _):
        at = pl.ds(pl.multiple_of(g * STRIDE, STRIDE), STRIDE)
        shifted = pl.ds(pl.multiple_of(g * STRIDE + WIN, STRIDE), STRIDE)
        gq_out[at] = gq_near[at] + gq_s[pl.ds(g, STRIDE, stride=grid_q), :]
        mine = pl.ds(g + part * grid_q, STRIDE, stride=grid_k)
        sent = pl.ds(g, STRIDE, stride=grid_k)
        last = jnp.where(g == grid_q - 1, 1.0, 0.0)
        gkv_own[at, :qw] = gk_near[shifted] + gk_s[mine, :]
        gkv_send[at, :qw] = (gk_s[sent, :] + last * gk_near[:WIN]).astype(BF16)
        for h in range(HEADS):
            cols = slice(h * 128, (h + 1) * 128)
            wide = slice(qw + h * 128, qw + (h + 1) * 128)
            gkv_own[at, wide] = gv_near[shifted, cols] + gv_s[h, mine, :]
            gkv_send[at, wide] = (gv_s[h, sent, :] + last * gv_near[:WIN, cols]).astype(BF16)
        return 0

    lax.fori_loop(0, grid_q, back, 0)


def mix_backward(grad_q, grad_kv, rows, gain, bias, w_mix, slab, d_gain, d_bias, carried):
    grad_mixed = jnp.concatenate([grad_q * score_scale(grad_q.shape[1]), grad_kv], axis=1).astype(BF16)
    unit, scale = norm_parts(rows)
    normed = (unit * gain[0:1] + bias[0:1]).astype(BF16)
    add_columns(slab, 0, t_dot(normed, grad_mixed))
    grad_normed = dot_t(grad_mixed, w_mix[...])
    d_gain[...] += col_sum(grad_normed * unit)
    d_bias[...] += col_sum(grad_normed)
    return carried + norm_back(grad_normed, unit, scale, gain[0:1])


def fourth_kernel(
    info, gq, gkv, got, z, gmid, gain_next, bias_next, w_mix_next,
    q, kv, halo, o, lse, active, slope, mid, x, gain, bias, w_mix, w_proj, w_in, w_back,
    cross0, cross1, local0, local1, gq_last, gkv_last, gmid_last, halo_out, keep, send, slab_last,
    dn_gain, dn_bias, d_gain, d_bias, d_gain_first, d_bias_first,
    ext, slab, gq_ext, gk_ext, gv_ext, gmid_ext,
):
    step = pl.program_id(0)
    qw = q.shape[1]
    n = kv.shape[0]

    @pl.when(step == 0)
    def _():
        load_extended(halo, kv, ext)
        for ref in (
            slab, slab_last, dn_gain, dn_bias, d_gain, d_bias, d_gain_first, d_bias_first, gq_ext, gk_ext, gv_ext, gmid_ext
        ):
            ref[...] = jnp.zeros_like(ref)

    limit = info[1]
    start = pl.multiple_of(step * TB, TB)
    base = info[0] * n + start
    grad_kv = gkv[...] + got[...].astype(F32)
    grad_z = mix_backward(
        gq[...], grad_kv, z[...].astype(F32), gain_next, bias_next, w_mix_next, slab, dn_gain, dn_bias, gmid[...]
    )
    grad_low = grad_z.astype(BF16)
    emit_block(info, step, grad_low, False, 0, (cross0, cross1), (local0, local1))
    unit, scale = norm_parts(mid[...])
    normed = (unit * gain[1:2] + bias[1:2]).astype(BF16)
    attended = o[...]
    grad_out, grad_mid = feed_backward(
        grad_low.astype(F32), active[...], slope[...].astype(F32), normed, unit, scale, attended, gain,
        w_proj, w_in, w_back, slab, w_mix_next.size // w_proj.shape[1], d_gain, d_bias,
    )
    shifted = pl.ds(pl.multiple_of(start + WIN, WIN), TB)
    gmid_ext[shifted] = grad_mid
    weighted = grad_out.astype(F32) * attended.astype(F32)
    for sub in range(TB // WIN):
        rows = slice(sub * WIN, (sub + 1) * WIN)
        near = pl.ds(pl.multiple_of(start + sub * WIN, WIN), 2 * WIN)
        delta = jnp.concatenate(
            [jnp.sum(weighted[rows, h * 128 : (h + 1) * 128], axis=-1, keepdims=True) for h in range(HEADS)], axis=0
        )
        g_q, g_k, g_v = near_backward(
            q[rows], ext[near, :qw], ext[near, qw:], grad_out[rows], stack_stat(lse[rows]), delta,
            base + sub * WIN, limit,
        )
        gq_ext[pl.ds(pl.multiple_of(start + (sub + 1) * WIN, WIN), WIN)] = g_q
        gk_ext[near] += g_k
        gv_ext[near] += g_v

    @pl.when(step == 0)
    def _():
        halo_out[...] = jnp.concatenate([gk_ext[:WIN], gv_ext[:WIN]], axis=1).astype(BF16)
        gk_ext[:WIN] = jnp.zeros((WIN, gk_ext.shape[1]), F32)
        gv_ext[:WIN] = jnp.zeros((WIN, gv_ext.shape[1]), F32)

    whole_rows = pl.ds(start, TB)
    grad_x = mix_backward(
        gq_ext[whole_rows], jnp.concatenate([gk_ext[whole_rows], gv_ext[whole_rows]], axis=1),
        x[whole_rows].astype(F32), gain, bias, w_mix, slab_last, d_gain_first, d_bias_first, gmid_ext[whole_rows],
    )
    grad_x = grad_x.astype(BF16)
    emit_block(info, step, grad_x[WIN:], True, 0, (cross0, cross1), (local0, local1))

    @pl.when(step > 0)
    def _():
        emit_rows(info, step * (TB // WIN) - 1, grad_x[:WIN], True, (cross0, cross1), (local0, local1))

    @pl.when(step == pl.num_programs(0) - 1)
    def _():
        gq_last[...] = gq_ext[n:]
        gkv_last[...] = jnp.concatenate([gk_ext[n:], gv_ext[n:]], axis=1)
        gmid_last[...] = gmid_ext[n:]
        split_slab(info, slab, keep, send)


def fifth_kernel(info, gq, gkv, got, x, gmid, gain, bias, w_mix, slab_in, *refs):
    vectors, squares = refs[:8], refs[8:10]
    cross, local, (keep, send, small, slab, d_gain, d_bias) = refs[-10:-8], refs[-8:-6], refs[-6:]
    slab[...] = slab_in[...]
    d_gain[...] = vectors[0][...]
    d_bias[...] = vectors[4][...]
    n = x.shape[0] - WIN
    grad_x = mix_backward(
        gq[...], gkv[...] + got[...].astype(F32), x[n:].astype(F32), gain, bias, w_mix, slab, d_gain, d_bias, gmid[...]
    )
    emit_rows(info, n // WIN - 1, grad_x.astype(BF16), True, cross, local)
    split_slab(info, slab, keep, send)
    small_rows(info, (d_gain,) + vectors[1:4] + (d_bias,) + vectors[5:], squares, small)
    put_riders(small[...], send, keep.shape[0])


def put_riders(rows, send, at):
    count = rows.shape[0]
    coarse = rows.astype(BF16)
    send[at : at + count] = coarse
    send[at + count :] = (rows - coarse.astype(F32)).astype(BF16)


def riders_of(got, at):
    count = (got.shape[0] - at) // 2
    return got[at : at + count].astype(F32) + got[at + count :].astype(F32)


def stage_kernel(digits, *refs, groups, ways, stage, riders):
    refs = list(refs)
    parts = [(refs.pop(0), [refs.pop(0) for _ in range(count)]) for count in groups]
    small = refs.pop(0) if riders else None
    messages = [refs.pop(0) for _ in range(max(ways - 1, 1))]
    kept_out = refs.pop(0) if ways > 1 else None
    small_out = refs.pop(0) if riders else None
    total = refs.pop(0)
    vectors = small[...] if riders else None
    at = 0
    for kept, got in parts:
        rows = kept.shape[0]
        value = kept[...]
        for g in got:
            value = value + g[:rows].astype(F32)
            if g.shape[0] > rows:
                vectors = vectors + riders_of(g, rows)
        total[at : at + rows] = value
        at += rows
    chunk = at // ways

    def piece(which):
        return total[pl.ds(pl.multiple_of(which * chunk, 16), chunk)]

    mine = digits[9 + stage] if ways > 1 else 0
    for i, message in enumerate(messages):
        message[:chunk] = piece(mine ^ (i + 1) if ways > 1 else 0).astype(BF16)
        if riders:
            put_riders(vectors, message, chunk)
    if ways > 1:
        kept_out[...] = piece(mine)
    if riders:
        small_out[...] = vectors


def exchange_kernel(digits, mine, theirs, rows_out, small_out):
    count = rows_out.shape[0]
    rows_out[...] = (mine[:count].astype(F32) + theirs[:count].astype(F32)).astype(BF16)
    small_out[...] = riders_of(mine, count) + riders_of(theirs, count)


def again_kernel(digits, rows, small, message):
    message[: rows.shape[0]] = rows[...]
    put_riders(small[...], message, rows.shape[0])


def order_kernel(digits, *refs, stage):
    pieces, out = refs[:-1], refs[-1]
    rows = pieces[0].shape[0]
    for c, piece in enumerate(pieces):
        out[pl.ds(pl.multiple_of((digits[9 + stage] ^ c) * rows, 16), rows)] = piece[...]


def assemble_kernel(info, *refs):
    own, other, out, wide, sems = refs[:4], *refs[4:]
    core = info[0]
    rows = out.shape[1]

    def leave(t):
        column = core if t < 4 else 1 - core
        image = (info[5] ^ (t % 4 // 2)) * 4 + column * 2 + (info[4] ^ (t % 2))
        return pltpu.make_async_copy(wide.at[t], out.at[image], sems.at[t])

    for t in range(8):
        if t < 4:
            block = own[t][pl.ds(pl.multiple_of(core * rows, rows), rows)]
        else:
            block = other[t - 4]
        wide[t] = block.astype(F32)
        leave(t).start()
    for t in range(8):
        leave(t).wait()


def hold_kernel(info, first, second, *refs):
    refs[-2][...] = first[...]
    refs[-1][...] = second[...]


def small_rows(info, vectors, squares, out):
    width = out.shape[1]
    once = jnp.where(info[7] == 0, 1.0, 0.0)
    lane = lax.broadcasted_iota(jnp.int32, (1, width), 1)
    out[...] = jnp.zeros_like(out)
    for i, vector in enumerate(vectors):
        out[i : i + 1] = jnp.sum(vector[...], axis=0, keepdims=True) * once
    for i in range(6):
        total = jnp.sum(jnp.sum(squares[i // 3][i % 3], axis=0, keepdims=True), axis=1, keepdims=True)
        out[8 + i : 9 + i] = jnp.where(lane == info[6], total * once, 0.0)


def trade_kernel(info, *refs):
    pieces, out = refs[:4], refs[-1]
    rows = out.shape[1]
    for t in range(4):
        out[t] = pieces[t][pl.ds(pl.multiple_of((1 - info[0]) * rows, rows), rows)]


def unpack_kernel(info, mine, theirs, small, counted, mix, proj, up, down, gain, bias, rms, wide, *, sizes):
    core = info[9]
    wide[core] = mine[...].astype(F32)
    wide[1 - core] = theirs[...].astype(F32)
    rows_a, rows_b, rows_c, ways = sizes
    early = rows_a // 2 // ways
    late = (rows_b + rows_c) // 2 // ways
    rows_mix = rows_c

    def pieces(slab, start, stop):
        total = {"a": rows_a, "b": rows_b, "c": rows_c}[slab] // 2
        size, shift, skip = {"a": (early, 0, 0), "b": (late, early, 0), "c": (late, early, rows_b // 2)}[slab]
        at = start
        while at < stop:
            half, row = at // total, at % total
            along = row + skip
            count = min(stop - at, total - row, size - along % size)
            yield at - start, half, along // size * (early + late) + shift + along % size, count
            at += count

    width = wide.shape[2]
    places = {0: (("c", 0), ("b", rows_mix)), 1: (("b", 0), ("a", 0))}
    for layer in range(2):
        (slab, at), (feed, feed_at) = places[layer]
        for out, name in ((mix, slab), (proj, feed), (up, feed), (down, feed)):
            if name == feed and out is not mix:
                at = feed_at
            rows, cols = out.shape[1:]
            for i in range(cols // width):
                for offset, half, row, count in pieces(name, at + i * rows, at + (i + 1) * rows):
                    out[layer, offset : offset + count, i * width : (i + 1) * width] = wide[half, row : row + count]
            if out is not mix:
                feed_at = at + rows * cols // width
    for layer in range(2):
        for norm in range(2):
            gain[layer, norm : norm + 1] = small[2 * layer + norm : 2 * layer + norm + 1]
            bias[layer, norm : norm + 1] = small[4 + 2 * layer + norm : 5 + 2 * layer + norm]
    images = rms.shape[1]
    sums = pltpu.roll(small[8:16], small.shape[1] - (info[6] - info[6] % images), 1)
    rms[...] = jnp.sqrt(sums[: rms.shape[0], :images] / counted[...])


VMEM = pl.BlockSpec(memory_space=pltpu.VMEM)


def call(kernel, info, operands, specs, outs, out_specs, scratch=(), grid=(), work=0, aliases={}):
    moved = sum(math.prod(a.shape) * a.dtype.itemsize for a in list(operands) + jax.tree.leaves(outs))
    single = not isinstance(outs, list)
    views = list(specs) + ([out_specs] if single else list(out_specs))

    def body_of(info, *refs):
        seen = [view(ref) if callable(view) else ref for view, ref in zip(views, refs)]
        kernel(info, *seen, *refs[len(views) :])

    def plain(view):
        return VMEM if callable(view) else view

    return pl.pallas_call(
        body_of,
        grid_spec=pltpu.PrefetchScalarGridSpec(
            num_scalar_prefetch=1,
            grid=grid,
            in_specs=[plain(v) for v in specs],
            out_specs=plain(out_specs) if single else [plain(v) for v in out_specs],
            scratch_shapes=list(scratch),
        ),
        out_shape=outs,
        input_output_aliases=aliases,
        compiler_params=pltpu.CompilerParams(vmem_limit_bytes=VMEM_LIMIT),
        cost_estimate=pl.CostEstimate(flops=int(work * 1.15e9), bytes_accessed=moved, transcendentals=0),
    )(info, *operands)


def whole(array):
    return VMEM


def tiled(array):
    return lambda ref: ref.at[pl.ds(pl.multiple_of(pl.program_id(0) * TB, TB), TB)]


def tiled_after_window(ref):
    return ref.at[pl.ds(pl.multiple_of(pl.program_id(0) * TB + WIN, WIN), TB)]


def last_rows(ref):
    return ref.at[pl.ds(ref.shape[0] - WIN, WIN)]


ANY = pl.BlockSpec(memory_space=pl.ANY)


def shape(dims, kind):
    return jax.ShapeDtypeStruct(dims, kind)


def after(value, *others):
    return lax.optimization_barrier((value, others))[0]


def body(edge_rows, lengths, norm_gain, norm_bias, w_qkv, w_out, w_up, w_down):
    sections = lax.axis_size("section")
    index = lax.axis_index("section")
    images, rows_dev, width = edge_rows.shape
    seats = 2 * images
    rep = sections // seats
    seat = index // rep
    twin = index % rep
    rows_piece = rows_dev * rep
    qw = (w_qkv.shape[2] - width) // 2
    kvw = w_qkv.shape[2] - qw
    hidden = w_up.shape[2]
    n = rows_piece * images // 2
    if n != 2 * TB:
        raise ValueError("block size")
    quarter = images // 2
    steps = (n // TB,)

    def route(pairs):
        return [(s * rep + e, d * rep + e) for s, d in pairs for e in range(rep)]

    if rep > 1:
        groups = [[s * rep + e for e in range(rep)] for s in range(seats)]
        edge_rows = lax.all_gather(edge_rows, "section", axis_index_groups=groups, axis=1, tiled=True)

    chip = seat // 2
    part = seat % 2
    fz, fl, fy = chip // 4, (chip // 2) % 2, chip % 2
    limit = lengths[chip]
    spot = lax.axis_index("dp") * images + chip
    dp_count = lax.axis_size("dp")
    dp_index = lax.axis_index("dp")

    def partners(masks):
        total = dp_count * sections
        spot = dp_index * sections + index
        digit = sum(((spot // m) % 2) << i for i, m in enumerate(masks))
        routes = []
        for c in range(1, 1 << len(masks)):
            flips = sum(m for i, m in enumerate(masks) if (c >> i) & 1)
            routes.append((c, [(s, s ^ flips) for s in range(total)]))
        return digit, routes

    dp_masks = [sections << b for b in range(dp_count.bit_length() - 1)]
    section_masks = [1 << b for b in range(1, sections.bit_length() - 1)]
    plane = [dp_masks[0], section_masks[0]]
    rest = section_masks[1:] + dp_masks[1:]
    digits = [partners(masks)[0] for masks in [[1], plane] + [[m] for m in rest]]
    counted = (lengths.astype(F32) * width)[None, :]
    info = jnp.stack([part, limit, chip % quarter, fz, fy, fz, spot, twin, index % 2] + digits).astype(jnp.int32)
    swap = route([(s, s ^ 1) for s in range(seats)])

    def bits(s):
        return s // 8, (s // 4) % 2, (s // 2) % 2, s % 2

    by_column = edge_rows.reshape(2, 2, 2, rows_piece, width)
    traded = lax.dynamic_index_in_dim(by_column, 1 - part, 1, keepdims=False).reshape(4, rows_piece, width)
    traded = lax.ppermute(traded, "section", swap)
    column = lax.dynamic_index_in_dim(by_column, part, 1, keepdims=False).reshape(4, rows_piece, width)
    received = [None] * 4
    for t in (2, 3, 0, 1):
        tz, ty = t // 2, t % 2
        image = (fz ^ tz) * 2 + (fy ^ ty)
        own = lax.dynamic_index_in_dim(column, image, 0, keepdims=False)
        got = lax.dynamic_index_in_dim(traded, image, 0, keepdims=False)
        message = jnp.where(part == 0, jnp.concatenate([own, got]), jnp.concatenate([got, own]))
        pairs = []
        for s in range(seats):
            z, l, y, k = bits(s)
            pairs.append((s, ((z ^ tz) * 4 + k * 2 + (y ^ ty)) * 2 + l))
        received[t] = lax.ppermute(message, "section", route(pairs))

    def send_back(message, tz, ty):
        pairs = []
        for s in range(seats):
            z, l, y, p = bits(s)
            pairs.append((s, ((z ^ tz) * 4 + p * 2 + (y ^ ty)) * 2 + l))
        return lax.ppermute(message, "section", route(pairs))

    def trade(got, *awaited):
        out = shape((4, rows_piece, width), BF16)
        send = call(trade_kernel, info, got + list(awaited), [VMEM] * 4 + [ANY] * len(awaited), out, VMEM)
        return lax.ppermute(send, "section", swap)

    first_to_second = route([(2 * c, 2 * c + 1) for c in range(images)])
    second_to_first = route([(2 * c + 1, 2 * c) for c in range(images)])

    dma = pltpu.SemaphoreType.DMA
    rows_q = shape((n, qw), BF16)
    rows_kv = shape((n, kvw), BF16)
    rows_low = shape((n, width), BF16)
    rows_wide = shape((n, width), F32)
    rows_stat = shape((n, 128), F32)
    rows_hidden = shape((n, hidden), BF16)
    grad_k_shape = shape((n + WIN, qw), F32)
    grad_v_shape = shape((n + WIN, width), F32)
    mix_rows = w_qkv.shape[1] * w_qkv.shape[2] // width
    feed_rows = (w_out[0].size + w_up[0].size + w_down[0].size) // width
    vec_shape = shape((8, width), F32)
    squares_shape = shape((3, 8, width), F32)
    ext = pltpu.VMEM((n + WIN, kvw), BF16)

    g0, g1, b0, b1 = norm_gain[0], norm_gain[1], norm_bias[0], norm_bias[1]

    halo_shape = shape((WIN, kvw), BF16)
    outs = [shape((n + WIN, width), BF16), rows_q, rows_kv, halo_shape]
    x, q0, kv0, halo0 = call(
        first_kernel, info, received + [g0, b0, w_qkv[0]], [VMEM] * 7,
        outs, [whole(o) for o in outs], work=6,
    )
    halo0 = lax.ppermute(halo0, "section", first_to_second)

    outs = [rows_low, rows_q, rows_kv, rows_low, rows_stat, rows_hidden, rows_hidden, rows_wide, squares_shape]
    z, q1, kv1, o0, lse0, active0, slope0, mid0, squares0 = call(
        second_kernel, info, [x, q0, kv0, halo0, g0, b0, w_out[0], w_up[0], w_down[0], g1, b1, w_qkv[1]],
        [tiled_after_window, tiled(q0)] + [whole(a) for a in (kv0, halo0, g0, b0, w_out[0], w_up[0], w_down[0], g1, b1, w_qkv[1])],
        outs, [tiled(o) for o in outs[:-1]] + [whole(outs[-1])], [ext], steps, work=15,
    )
    kv_other = lax.ppermute(kv1, "section", first_to_second)

    rows_k_all = shape((2 * n, qw), BF16)
    rows_v_all = shape((2 * n, width), BF16)
    outs = [rows_q, rows_k_all, rows_v_all, rows_wide, rows_stat]
    qr, kr, vr, o_far, lse_far = call(
        far_forward_kernel, info, [q1, kv1, kv_other], [whole(a) for a in (q1, kv1, kv_other)],
        outs, [whole(o) for o in outs],
        [pltpu.VMEM((n, qw), F32), pltpu.VMEM((2 * n, qw), F32), pltpu.VMEM((HEADS, 2 * n, 128), F32),
         pltpu.VMEM((HEADS, n, 128), F32), pltpu.VMEM((n, 128), F32)], work=14,
    )

    message = shape((2 * rows_piece, width), BF16)
    outs = [message] * 4 + [rows_low, rows_stat, shape((n, qw), F32), grad_k_shape, grad_v_shape, rows_wide,
            shape((feed_rows // 2, width), F32), shape((feed_rows // 2, width), BF16),
            vec_shape, vec_shape, squares_shape]
    (cross0, cross1, local0, local1, go1, stat1, gq_near, gk_near, gv_near, gmid1, keep_a, send_a,
     d_gain11, d_bias11, squares1) = call(
        third_kernel, info,
        received + [q1, kv1, kv_other, o_far, lse_far, z, g1, b1, w_out[1], w_up[1], w_down[1]],
        [VMEM] * 4
        + [tiled(q1), whole(kv1), last_rows]
        + [tiled(o_far), tiled(lse_far), tiled(z)]
        + [whole(a) for a in (g1, b1, w_out[1], w_up[1], w_down[1])],
        outs,
        [whole(message)] * 4 + [tiled(o) for o in outs[4:7]] + [whole(outs[7]), whole(outs[8]), tiled(outs[9])]
        + [whole(o) for o in outs[10:]],
        [ext, pltpu.VMEM((TB, width), BF16), pltpu.VMEM((feed_rows, width), F32)], steps, work=24,
    )
    forward_back = [None, None, send_back(cross0, 1, 0), None]

    outs = [shape((n, qw), F32), shape((n, kvw), F32), rows_kv]
    operands = [qr, kr, vr, go1, stat1, gq_near, gk_near, gv_near]
    gq1, gkv1, gkv_send = call(
        far_backward_kernel, info, operands, [whole(a) for a in operands], outs, [whole(o) for o in outs],
        [pltpu.VMEM((HEADS, n, 128), F32), pltpu.VMEM((n, 128), F32), pltpu.VMEM((n, qw), F32),
         pltpu.VMEM((2 * n, qw), F32), pltpu.VMEM((HEADS, 2 * n, 128), F32)], work=18,
    )
    def pair(message):
        return lax.ppermute(message, ("dp", "section"), partners([1])[1][0][1])

    def send_all(messages, masks):
        return [lax.ppermute(m, ("dp", "section"), way) for m, (_, way) in zip(messages, partners(masks)[1])]

    small_shape = shape((16, width), F32)
    rider_rows = 2 * small_shape.shape[0]

    def stage(groups, small, ways, number):
        operands = [a for kept, got in groups for a in [kept] + got] + ([] if small is None else [small])
        rows = sum(kept.shape[0] for kept, _ in groups)
        riders = small is not None
        outs = [shape((rows // ways + rider_rows * riders, width), BF16)] * max(ways - 1, 1)
        outs += [shape((rows // ways, width), F32)] * (ways > 1) + [small_shape] * riders
        kernel = functools.partial(
            stage_kernel, groups=[len(got) for _, got in groups], ways=ways, stage=number, riders=riders
        )
        made = call(
            kernel, info, operands, [VMEM] * len(operands), outs, [VMEM] * len(outs), [pltpu.VMEM((rows, width), F32)]
        )
        sent = max(ways - 1, 1)
        return made[:sent], made[sent] if ways > 1 else None, made[-1] if riders else None

    def gather(piece, masks, number):
        pieces = [piece] + [lax.ppermute(piece, ("dp", "section"), way) for _, way in partners(masks)[1]]
        out = shape((len(pieces) * piece.shape[0], width), BF16)
        return call(functools.partial(order_kernel, stage=number), info, pieces, [VMEM] * len(pieces), out, VMEM)

    messages, kept_a, _ = stage([(keep_a, [pair(send_a)])], None, 4, 1)
    got_a = send_all(messages, plane)
    gkv_got = lax.ppermute(after(gkv_send, forward_back[2], *got_a), "section", second_to_first)
    forward_back[3] = send_back(after(cross1, forward_back[2]), 1, 1)
    forward_back[0] = send_back(after(local0, forward_back[2]), 0, 0)
    forward_back[1] = send_back(after(local1, forward_back[2]), 0, 1)

    slab_rows = mix_rows + feed_rows
    early_shape = slab_rows // 2, width
    mix_slab = shape((mix_rows, width), F32)
    outs = [message] * 4 + [shape((WIN, qw), F32), shape((WIN, kvw), F32), shape((WIN, width), F32), halo_shape,
            shape(early_shape, F32), shape(early_shape, BF16), mix_slab] + [vec_shape] * 6
    operands = [gq1, gkv1, gkv_got, z, gmid1, g1, b1, w_qkv[1], q0, kv0, halo0, o0, lse0, active0, slope0, mid0, x, g0,
                b0, w_qkv[0], w_out[0], w_up[0], w_down[0]]
    (cross0, cross1, local0, local1, gq_last, gkv_last, gmid_last, halo_send, keep_early, send_early, slab_last,
     d_gain10, d_bias10, d_gain01, d_bias01, d_gain00, d_bias00) = call(
        fourth_kernel, info, operands,
        [tiled(a) for a in operands[:5]] + [VMEM] * 3 + [tiled(q0), VMEM, VMEM] + [tiled(a) for a in operands[11:16]]
        + [VMEM] * 7,
        outs, [VMEM] * len(outs),
        [ext, pltpu.VMEM((slab_rows, width), F32), pltpu.VMEM((n + WIN, qw), F32), pltpu.VMEM((n + WIN, qw), F32),
         pltpu.VMEM((n + WIN, width), F32), pltpu.VMEM((n + WIN, width), F32)], steps, work=20,
    )
    outs = [halo_shape, shape(early_shape, BF16)]
    halo_send, send_early = call(
        hold_kernel, info, [halo_send, send_early] + forward_back, [VMEM] * 2 + [ANY] * 4, outs, [VMEM] * 2
    )
    halo_got = lax.ppermute(halo_send, "section", second_to_first)

    got_early = pair(send_early)
    outs = [message] * 4 + [shape((mix_rows // 2, width), F32), shape((mix_rows // 2 + rider_rows, width), BF16), small_shape]
    operands = [gq_last, gkv_last, halo_got, x, gmid_last, g0, b0, w_qkv[0], slab_last]
    operands += [d_gain00, d_gain01, d_gain10, d_gain11, d_bias00, d_bias01, d_bias10, d_bias11, squares0, squares1]
    aliases = {1 + len(operands) + i: i for i in range(4)}
    operands += [cross0, cross1, local0, local1]
    cross0, cross1, local0, local1, keep_late, send_late, small = call(
        fifth_kernel, info, operands, [VMEM] * len(operands), outs, [VMEM] * len(outs),
        [pltpu.VMEM((mix_rows, width), F32), pltpu.VMEM((8, width), F32), pltpu.VMEM((8, width), F32)],
        aliases=aliases,
    )

    def assemble(own, other):
        out = call(
            assemble_kernel, info, own + [other], [VMEM] * 5, shape((images, rows_piece, width), F32), ANY,
            [pltpu.VMEM((images, rows_piece, width), F32), dma((images,))],
        )
        if rep > 1:
            out = lax.dynamic_slice_in_dim(out, twin * rows_dev, rows_dev, 1)
        return out

    backward_back = [send_back(local0, 0, 0), None, send_back(cross0, 1, 0), None]
    groups = [(keep_early, [got_early]), (keep_late, [pair(send_late)])]
    messages, kept, small = stage(groups, small, 4, 1)
    forward_trade = trade(forward_back, send_late)
    forward_rows = assemble(forward_back, forward_trade)
    groups = [(kept_a, got_a), (kept, send_all(messages, plane))]
    number = 2
    scattered = []
    while number - 1 < len(rest) and sum(kept.shape[0] for kept, _ in groups) % 32 == 0:
        messages, kept, small = stage(groups, small, 2, number)
        groups = [(kept, send_all(messages, [rest[number - 2]]))]
        scattered.append(number)
        number += 1
    scattered_rows = groups[-1][1]
    backward_back[3] = send_back(after(cross1, backward_back[2], *scattered_rows, forward_rows), 1, 1)
    backward_back[1] = send_back(after(local1, backward_back[2], *scattered_rows, forward_rows), 0, 1)
    (both,), _, small = stage(groups, small, 1, 0)
    both = after(both, backward_back[0], backward_back[2])
    rows_shape = shape((both.shape[0] - rider_rows, width), BF16)
    while number - 2 < len(rest):
        (got,) = send_all([both], [rest[number - 2]])
        rows, small = call(exchange_kernel, info, [both, got], [VMEM] * 2, [rows_shape, small_shape], [VMEM] * 2)
        number += 1
        if number - 2 < len(rest):
            both = call(again_kernel, info, [rows, small], [VMEM] * 2, shape(both.shape, BF16), VMEM)
    both = after(rows, backward_back[1], backward_back[3])
    for number in scattered[::-1]:
        both = gather(both, [rest[number - 2]], number)
    backward_trade = trade(backward_back, rows)
    both = gather(both, plane, 1)
    both = after(both, backward_trade)
    theirs = pair(both)
    backward_rows = assemble(backward_back, backward_trade)
    outs = [shape(w.shape, F32) for w in (w_qkv, w_out, w_up, w_down, norm_gain, norm_bias)] + [shape((6, images), F32)]
    sizes = (feed_rows, slab_rows, mix_rows, 1 << len(plane))
    grads = call(
        functools.partial(unpack_kernel, sizes=sizes), info, [both, theirs, small, counted],
        [VMEM] * 4, outs, [whole(o) for o in outs],
        [pltpu.VMEM((2,) + both.shape, F32)],
    )
    return (forward_rows, backward_rows, grads[6], grads[4], grads[5]) + tuple(grads[:4])


def solution(mesh):
    placed = (P("dp", "section", None), P("dp"), P(), P(), P(), P(), P(), P())
    return jax.shard_map(
        body,
        mesh=mesh,
        in_specs=placed,
        out_specs=(P("dp", "section", None), P("dp", "section", None), P(None, "dp"), P(), P(), P(), P(), P(), P()),
        check_vma=False,
    )
```

```python
import functools
import math

import jax
import jax.numpy as jnp
from jax import lax
from jax.experimental import pallas as pl
from jax.experimental.pallas import tpu as pltpu
from jax.sharding import PartitionSpec as P

HEADS = 2
WIN = 128
STRIDE = 128
NEG = -1e30
F32 = jnp.float32
BF16 = jnp.bfloat16
TB = 768
RES = 8
UNROLL = 16
RES_BACK = 16
UNROLL_BACK = 8
VMEM_LIMIT = 16 * 1024 * 1024


def dot(left, right):
    return lax.dot_general(left, right, (((1,), (0,)), ((), ())), preferred_element_type=F32)


def dot_t(left, right):
    return lax.dot_general(left, right, (((1,), (1,)), ((), ())), preferred_element_type=F32)


def t_dot(left, right):
    return lax.dot_general(left, right, (((0,), (0,)), ((), ())), preferred_element_type=F32)


def score_scale(query_width):
    return 1.0 / math.sqrt(query_width // HEADS)


def norm_parts(rows):
    centre = rows - jnp.mean(rows, axis=-1, keepdims=True)
    scale = lax.rsqrt(jnp.mean(centre * centre, axis=-1, keepdims=True) + 1e-05)
    return centre * scale, scale


def norm_back(grad, unit, scale, gain):
    scaled = grad * gain
    first = jnp.mean(scaled, axis=-1, keepdims=True)
    second = jnp.mean(scaled * unit, axis=-1, keepdims=True)
    return scale * (scaled - first - unit * second)


def col_sum(rows):
    return jnp.sum(rows.reshape(rows.shape[0] // 8, 8, rows.shape[1]), axis=0)


def gelu_pair(hidden):
    c0 = math.sqrt(2.0 / math.pi)
    square = hidden * hidden
    share = 0.5 + 0.5 * jnp.tanh(hidden * (c0 + (c0 * 0.044715) * square))
    active = hidden * share
    slope = share + active * (1.0 - share) * (2.0 * c0 + (6.0 * c0 * 0.044715) * square)
    return active, slope


def head_split(rows):
    lane = lax.broadcasted_iota(jnp.int32, rows.shape, 1)
    zero = jnp.zeros_like(rows)
    low = lane < rows.shape[1] // HEADS
    return jnp.concatenate([jnp.where(low, rows, zero), jnp.where(low, zero, rows)], axis=0)


def head_join(stacked):
    half = stacked.shape[0] // 2
    lane = lax.broadcasted_iota(jnp.int32, (half, stacked.shape[1]), 1)
    return jnp.where(lane < stacked.shape[1] // HEADS, stacked[:half], stacked[half:])


def near_masks(base, limit):
    row = lax.broadcasted_iota(jnp.int32, (2 * WIN, WIN), 0)
    row = jnp.where(row >= WIN, row - WIN, row)
    col = lax.broadcasted_iota(jnp.int32, (2 * WIN, WIN), 1)
    own = col <= row
    key = base + col - jnp.where(own, 0, WIN)
    allowed = (key >= 0) & ((key < limit) | (col == row))
    return own, allowed


def near_scores(split_q, keys, own, allowed):
    scores = dot_t(split_q, keys)
    folded = jnp.where(own, scores[:, WIN:], scores[:, :WIN])
    return jnp.where(allowed, folded, NEG)


def unfold(folded, own):
    return jnp.concatenate([jnp.where(own, 0.0, folded), jnp.where(own, folded, 0.0)], axis=1).astype(BF16)


def near_forward(queries, keys, values, base, limit):
    own, allowed = near_masks(base, limit)
    scores = near_scores(head_split(queries), keys, own, allowed)
    largest = jnp.max(scores, axis=-1, keepdims=True)
    powers = jnp.exp(scores - largest)
    total = jnp.sum(powers, axis=-1, keepdims=True)
    weights = unfold(powers, own)
    hd = values.shape[1] // HEADS
    out = [dot(weights[h * WIN : (h + 1) * WIN], values[:, h * hd : (h + 1) * hd]) for h in range(HEADS)]
    return out, largest, total, powers


def near_backward(queries, keys, values, grad_out, log_total, delta, base, limit, weights=None):
    own, allowed = near_masks(base, limit)
    split_q = head_split(queries)
    if weights is None:
        weights = jnp.exp(near_scores(split_q, keys, own, allowed) - log_total)
    hd = values.shape[1] // HEADS
    pull = jnp.concatenate(
        [dot_t(grad_out[:, h * hd : (h + 1) * hd], values[:, h * hd : (h + 1) * hd]) for h in range(HEADS)], axis=0
    )
    pull = jnp.where(own, pull[:, WIN:], pull[:, :WIN])
    slope = weights * (pull - delta)
    grad_q = head_join(dot(unfold(slope, own), keys))
    row = lax.broadcasted_iota(jnp.int32, (WIN, 2 * WIN), 0)
    col = lax.broadcasted_iota(jnp.int32, (WIN, 2 * WIN), 1)
    here = (row <= jnp.where(col >= WIN, col - WIN, col)).astype(F32).astype(BF16)

    def turned(folded):
        flat = folded.astype(BF16).T
        current = flat * here
        return jnp.concatenate([flat - current, current], axis=0)

    grad_k = dot(turned(slope), split_q)
    weights = turned(weights)
    grad_v = jnp.concatenate(
        [dot(weights[:, h * WIN : (h + 1) * WIN], grad_out[:, h * hd : (h + 1) * hd]) for h in range(HEADS)], axis=1
    )
    return grad_q, grad_k, grad_v


def stack_stat(stat, width=128):
    return jnp.concatenate([stat[:, 0:1], stat[:, width // 2 : width // 2 + 1]], axis=0)


def spread_stat(stacked, width=128):
    half = stacked.shape[0] // 2
    lane = lax.broadcasted_iota(jnp.int32, (half, width), 1)
    return jnp.where(lane < width // 2, stacked[:half], stacked[half:])


def masked_squares(rows, base, limit):
    pos = base + lax.broadcasted_iota(jnp.int32, (rows.shape[0], 1), 0)
    return col_sum(jnp.where(pos < limit, rows * rows, 0.0))


def pick_piece(info, pieces, low, block, target):
    for t, piece in enumerate(pieces):
        tz, ty = t // 2, t % 2

        @pl.when(((block ^ info[4]) == ty) & ((info[5] ^ (0 if low else 1)) == tz))
        def _():
            target[...] = piece[...]


def emit_block(info, block, rows, to_lower, first, cross, local):
    stays = info[5] == (0 if to_lower else 1)
    at = slice(first, first + rows.shape[0])
    for ty in range(2):
        fits = (block ^ info[4]) == ty

        @pl.when(fits & stays)
        def _():
            local[ty][at] = rows

        @pl.when(fits & jnp.logical_not(stays))
        def _():
            cross[ty][at] = rows


def emit_rows(info, first, rows, to_lower, cross, local):
    units = cross[0].shape[0] // WIN
    stays = info[5] == (0 if to_lower else 1)
    for sub in range(rows.shape[0] // WIN):
        number = first + sub
        block = number // units
        at = pl.ds(pl.multiple_of((number - block * units) * WIN, WIN), WIN)
        value = rows[sub * WIN : (sub + 1) * WIN]
        for ty in range(2):
            fits = (block ^ info[4]) == ty

            @pl.when(fits & stays)
            def _():
                local[ty][at] = value

            @pl.when(fits & jnp.logical_not(stays))
            def _():
                cross[ty][at] = value


def split_slab(info, slab, keep, send):
    once = jnp.where(info[7] == 0, 1.0, 0.0)
    half = keep.shape[0]
    mine = info[8]
    keep[...] = slab[pl.ds(pl.multiple_of(mine * half, 8), half)] * once
    send[:half] = (slab[pl.ds(pl.multiple_of((1 - mine) * half, 8), half)] * once).astype(BF16)


def first_kernel(info, *refs):
    pieces = refs[:4]
    gain, bias, w_mix, x_out, q_out, kv_out, halo_out = refs[4:]
    for half in range(2):
        pick_piece(info, pieces, True, half, x_out.at[pl.ds(WIN + half * pieces[0].shape[0], pieces[0].shape[0])])
    x_out[:WIN] = jnp.zeros((WIN, x_out.shape[1]), BF16)
    qw = q_out.shape[1]

    def block(i, _):
        at = pl.ds(pl.multiple_of(i * TB, TB), TB)
        unit, _ = norm_parts(x_out[pl.ds(pl.multiple_of(i * TB + WIN, WIN), TB)].astype(F32))
        normed = (unit * gain[0:1] + bias[0:1]).astype(BF16)
        mixed = dot(normed, w_mix[...])
        q_out[at] = (mixed[:, :qw] * score_scale(qw)).astype(BF16)
        kv_out[at] = mixed[:, qw:].astype(BF16)
        return 0

    lax.fori_loop(0, q_out.shape[0] // TB, block, 0)
    halo_out[...] = kv_out[kv_out.shape[0] - WIN :]


def load_extended(halo, kv, ext):
    ext[: halo.shape[0]] = halo[...]
    ext[halo.shape[0] :] = kv[...]


def second_kernel(
    info, x, q, kv, halo, gain, bias, w_proj, w_in, w_back, gain_next, bias_next, w_mix_next,
    z_out, q_next, kv_next, o_out, lse_out, active_out, slope_out, mid_out, squares, ext,
):
    step = pl.program_id(0)
    qw = q.shape[1]
    n = kv.shape[0]

    @pl.when(step == 0)
    def _():
        load_extended(halo, kv, ext)
        squares[...] = jnp.zeros_like(squares)

    limit = info[1]
    count = q.shape[0]
    start = step * count
    base = info[0] * n + start
    outs = []
    for sub in range(count // WIN):
        near = pl.ds(pl.multiple_of(start + sub * WIN, WIN), 2 * WIN)
        keys = ext[near, :qw]
        values = ext[near, qw:]
        queries = q[sub * WIN : (sub + 1) * WIN]
        out, largest, total, _ = near_forward(queries, keys, values, base + sub * WIN, limit)
        inverse = 1.0 / total
        lse_out[sub * WIN : (sub + 1) * WIN] = spread_stat(largest + jnp.log(total))
        outs.append(jnp.concatenate([out[0] * inverse[:WIN], out[1] * inverse[WIN:]], axis=1))
    attended = jnp.concatenate(outs, axis=0).astype(BF16)
    o_out[...] = attended
    stream = x[...].astype(F32)
    branch = dot(attended, w_proj[...])
    middle = stream + branch
    mid_out[...] = middle
    unit, _ = norm_parts(middle)
    normed = (unit * gain[1:2] + bias[1:2]).astype(BF16)
    active, slope = gelu_pair(dot(normed, w_in[...]))
    active = active.astype(BF16)
    active_out[...] = active
    slope_out[...] = slope.astype(BF16)
    feed = dot(active, w_back[...])
    z = (middle + feed).astype(BF16)
    z_out[...] = z
    squares[0] += masked_squares(stream, base, limit)
    squares[1] += masked_squares(branch, base, limit)
    squares[2] += masked_squares(feed, base, limit)
    unit, _ = norm_parts(z.astype(F32))
    normed = (unit * gain_next[0:1] + bias_next[0:1]).astype(BF16)
    mixed = dot(normed, w_mix_next[...])
    q_next[...] = (mixed[:, :qw] * score_scale(qw)).astype(BF16)
    kv_next[...] = mixed[:, qw:].astype(BF16)


def far_mask(grid_q, grid_k, part_grid, residues):
    shape = (HEADS * residues * grid_q, residues * grid_k)
    row = lax.broadcasted_iota(jnp.int32, shape, 0)
    col = lax.broadcasted_iota(jnp.int32, shape, 1)
    row = jnp.where(row >= residues * grid_q, row - residues * grid_q, row)
    row_res = jnp.zeros(shape, jnp.int32)
    col_res = jnp.zeros(shape, jnp.int32)
    for r in range(1, residues):
        row_res += (row >= r * grid_q).astype(jnp.int32)
        col_res += (col >= r * grid_k).astype(jnp.int32)
    row_grid = row - row_res * grid_q + part_grid
    col_grid = col - col_res * grid_k
    allowed = (row_res == col_res) & (col_grid < row_grid)
    return allowed, col_grid * STRIDE + col_res


def far_forward_kernel(info, q, kv, other, qr, kr, vr, o_far, lse_far, q_s, k_s, v_s, o_s, lse_s):
    n, qw = q.shape
    grid_q = n // STRIDE
    grid_k = 2 * grid_q
    part = info[0]
    limit = info[1]

    def place(g, _):
        at = pl.ds(pl.multiple_of(g * STRIDE, STRIDE), STRIDE)
        own = kv[at].astype(F32)
        early = jnp.where(part == 0, own, other[at].astype(F32))
        q_s[pl.ds(g, STRIDE, stride=grid_q), :] = q[at].astype(F32)
        k_s[pl.ds(g, STRIDE, stride=grid_k), :] = early[:, :qw]
        k_s[pl.ds(g + grid_q, STRIDE, stride=grid_k), :] = own[:, :qw]
        hd = v_s.shape[1]
        for h in range(HEADS):
            v_s[h, pl.ds(g, STRIDE, stride=grid_k), :] = early[:, qw + h * 128 : qw + (h + 1) * 128]
            v_s[h, pl.ds(g + grid_q, STRIDE, stride=grid_k), :] = own[:, qw + h * 128 : qw + (h + 1) * 128]
        return 0

    lax.fori_loop(0, grid_q, place, 0)
    base_mask, key_pos = far_mask(grid_q, grid_k, part * grid_q, RES)
    rows_q = RES * grid_q
    rows_k = RES * grid_k

    def one(i):
        at_q = pl.ds(pl.multiple_of(i * rows_q, rows_q), rows_q)
        at_k = pl.ds(pl.multiple_of(i * rows_k, rows_k), rows_k)
        queries = q_s[at_q].astype(BF16)
        keys = k_s[at_k].astype(BF16)
        values = [v_s[h, at_k].astype(BF16) for h in range(HEADS)]
        qr[at_q] = queries
        kr[at_k] = keys
        for h in range(HEADS):
            vr[at_k, h * 128 : (h + 1) * 128] = values[h]
        allowed = base_mask & (key_pos + i * RES < limit)
        scores = jnp.where(allowed, dot_t(head_split(queries), keys), NEG)
        largest = jnp.max(scores, axis=-1, keepdims=True)
        powers = jnp.where(allowed, jnp.exp(scores - largest), 0.0)
        total = jnp.sum(powers, axis=-1, keepdims=True)
        safe = jnp.maximum(total, 1e-30)
        weights = (powers * (1.0 / safe)).astype(BF16)
        lse = jnp.where(total > 0.0, largest + jnp.log(safe), NEG)
        lse_s[at_q] = spread_stat(lse)
        for h in range(HEADS):
            o_s[h, at_q] = dot(weights[h * rows_q : (h + 1) * rows_q], values[h])

    def group(i, _):
        for u in range(UNROLL):
            one(i * UNROLL + u)
        return 0

    lax.fori_loop(0, STRIDE // RES // UNROLL, group, 0)

    def back(g, _):
        at = pl.ds(pl.multiple_of(g * STRIDE, STRIDE), STRIDE)
        pick = pl.ds(g, STRIDE, stride=grid_q)
        lse_far[at] = lse_s[pick, :]
        for h in range(HEADS):
            o_far[at, h * 128 : (h + 1) * 128] = o_s[h, pick, :]
        return 0

    lax.fori_loop(0, grid_q, back, 0)


def third_kernel(
    info, *refs,
):
    pieces = refs[:4]
    (q, kv, halo, o_far, lse_far, z, gain, bias, w_proj, w_in, w_back,
     cross0, cross1, local0, local1, go_out, stat_out, gq_out, gk_out, gv_out, gmid_out, keep, send,
     d_gain, d_bias, squares, ext, cot, slab) = refs[4:]
    step = pl.program_id(0)
    qw = q.shape[1]
    n = kv.shape[0]

    @pl.when(step == 0)
    def _():
        load_extended(halo, kv, ext)
        for ref in (squares, gk_out, gv_out, slab, d_gain, d_bias):
            ref[...] = jnp.zeros_like(ref)

    limit = info[1]
    start = pl.multiple_of(step * TB, TB)
    base = info[0] * n + start
    outs = []
    logs = []
    weights = []
    for sub in range(TB // WIN):
        rows = slice(sub * WIN, (sub + 1) * WIN)
        near = pl.ds(pl.multiple_of(start + sub * WIN, WIN), 2 * WIN)
        out, largest, total, powers = near_forward(q[rows], ext[near, :qw], ext[near, qw:], base + sub * WIN, limit)
        far_log = stack_stat(lse_far[rows])
        top = jnp.maximum(largest, far_log)
        near_share = jnp.exp(largest - top)
        far_share = jnp.exp(far_log - top)
        whole = total * near_share + far_share
        inverse = 1.0 / whole
        near_share = near_share * inverse
        far_share = far_share * inverse
        weights.append(powers * near_share)
        logs.append(top + jnp.log(whole))
        far = o_far[rows]
        outs.append(
            jnp.concatenate(
                [
                    out[h] * near_share[h * WIN : (h + 1) * WIN]
                    + far[:, h * 128 : (h + 1) * 128] * far_share[h * WIN : (h + 1) * WIN]
                    for h in range(HEADS)
                ],
                axis=1,
            )
        )
    attended_wide = jnp.concatenate(outs, axis=0)
    attended = attended_wide.astype(BF16)
    stream = z[...].astype(F32)
    branch = dot(attended, w_proj[...])
    middle = stream + branch
    unit, scale = norm_parts(middle)
    normed = (unit * gain[1:2] + bias[1:2]).astype(BF16)
    active, slope = gelu_pair(dot(normed, w_in[...]))
    active = active.astype(BF16)
    feed = dot(active, w_back[...])
    emit_block(info, step, z[...], True, 0, (cross0, cross1), (local0, local1))
    emit_block(info, step, (middle + feed).astype(BF16), False, 0, (cross0, cross1), (local0, local1))
    pick_piece(info, pieces, False, step, cot)
    squares[0] += masked_squares(stream, base, limit)
    squares[1] += masked_squares(branch, base, limit)
    squares[2] += masked_squares(feed, base, limit)

    pos = base + lax.broadcasted_iota(jnp.int32, (TB, 1), 0)
    upstream = jnp.where(pos < limit, cot[...].astype(F32), 0.0)
    grad_out, grad_mid = feed_backward(
        upstream, active, slope, normed, unit, scale, attended, gain, w_proj, w_in, w_back, slab, 0, d_gain, d_bias
    )
    gmid_out[...] = grad_mid
    go_out[...] = grad_out
    weighted = grad_out.astype(F32) * attended_wide
    for sub in range(TB // WIN):
        rows = slice(sub * WIN, (sub + 1) * WIN)
        near = pl.ds(pl.multiple_of(start + sub * WIN, WIN), 2 * WIN)
        delta = jnp.concatenate(
            [jnp.sum(weighted[rows, h * 128 : (h + 1) * 128], axis=-1, keepdims=True) for h in range(HEADS)], axis=0
        )
        stat_out[rows] = pack_stats(logs[sub], delta)
        gq, gk, gv = near_backward(
            q[rows], ext[near, :qw], ext[near, qw:], grad_out[rows], logs[sub], delta, base + sub * WIN, limit,
            weights[sub],
        )
        gq_out[rows] = gq
        gk_out[near] += gk
        gv_out[near] += gv

    @pl.when(step == pl.num_programs(0) - 1)
    def _():
        split_slab(info, slab, keep, send)


def pack_stats(lse, delta):
    half = lse.shape[0] // 2
    lane = lax.broadcasted_iota(jnp.int32, (half, 128), 1)
    low = jnp.where(lane < 32, lse[:half], lse[half:])
    high = jnp.where(lane < 96, delta[:half], delta[half:])
    return jnp.where(lane < 64, low, high)


def add_columns(slab, at, grad):
    rows, cols = grad.shape
    width = slab.shape[1]
    for i in range(cols // width):
        slab[at + i * rows : at + (i + 1) * rows] += grad[:, i * width : (i + 1) * width]


def feed_backward(
    upstream, active, slope, normed, unit, scale, attended, gain, w_proj, w_in, w_back, slab, at, d_gain, d_bias,
):
    low = upstream.astype(BF16)
    width = low.shape[1]
    hidden = active.shape[1]
    slab[at + width + hidden : at + width + 2 * hidden] += t_dot(active, low)
    grad_hidden = (dot_t(low, w_back[...]) * slope).astype(BF16)
    add_columns(slab, at + width, t_dot(normed, grad_hidden))
    grad_normed = dot_t(grad_hidden, w_in[...])
    d_gain[...] += col_sum(grad_normed * unit)
    d_bias[...] += col_sum(grad_normed)
    grad_mid = upstream + norm_back(grad_normed, unit, scale, gain[1:2])
    branch_low = grad_mid.astype(BF16)
    slab[at : at + width] += t_dot(attended, branch_low)
    grad_out = dot_t(branch_low, w_proj[...]).astype(BF16)
    return grad_out, grad_mid


def far_backward_kernel(
    info, qr, kr, vr, go, stat, gq_near, gk_near, gv_near, gq_out, gkv_own, gkv_send,
    go_s, stat_s, gq_s, gk_s, gv_s,
):
    n, qw = gq_near.shape
    grid_q = n // STRIDE
    grid_k = 2 * grid_q
    part = info[0]
    limit = info[1]

    def place(g, _):
        at = pl.ds(pl.multiple_of(g * STRIDE, STRIDE), STRIDE)
        pick = pl.ds(g, STRIDE, stride=grid_q)
        rows = go[at].astype(F32)
        for h in range(HEADS):
            go_s[h, pick, :] = rows[:, h * 128 : (h + 1) * 128]
        stat_s[pick, :] = stat[at]
        return 0

    lax.fori_loop(0, grid_q, place, 0)
    base_mask, key_pos = far_mask(grid_q, grid_k, part * grid_q, RES_BACK)
    rows_q = RES_BACK * grid_q
    rows_k = RES_BACK * grid_k

    def one(i):
        at_q = pl.ds(pl.multiple_of(i * rows_q, rows_q), rows_q)
        at_k = pl.ds(pl.multiple_of(i * rows_k, rows_k), rows_k)
        keys = kr[at_k]
        split_q = head_split(qr[at_q])
        grads = [go_s[h, at_q].astype(BF16) for h in range(HEADS)]
        stats = stat_s[at_q]
        lse = jnp.concatenate([stats[:, 0:1], stats[:, 32:33]], axis=0)
        delta = jnp.concatenate([stats[:, 64:65], stats[:, 96:97]], axis=0)
        allowed = base_mask & (key_pos + i * RES_BACK < limit)
        weights = jnp.exp(jnp.where(allowed, dot_t(split_q, keys), NEG) - lse)
        pull = jnp.concatenate([dot_t(grads[h], vr[at_k, h * 128 : (h + 1) * 128]) for h in range(HEADS)], axis=0)
        slope = (weights * (pull - delta)).astype(BF16)
        weights = weights.astype(BF16)
        gq_s[at_q] = head_join(dot(slope, keys))
        gk_s[at_k] = t_dot(slope, split_q)
        for h in range(HEADS):
            gv_s[h, at_k] = t_dot(weights[h * rows_q : (h + 1) * rows_q], grads[h])

    def group(i, _):
        for u in range(UNROLL_BACK):
            one(i * UNROLL_BACK + u)
        return 0

    lax.fori_loop(0, STRIDE // RES_BACK // UNROLL_BACK, group, 0)

    def back(g, _):
        at = pl.ds(pl.multiple_of(g * STRIDE, STRIDE), STRIDE)
        shifted = pl.ds(pl.multiple_of(g * STRIDE + WIN, STRIDE), STRIDE)
        gq_out[at] = gq_near[at] + gq_s[pl.ds(g, STRIDE, stride=grid_q), :]
        mine = pl.ds(g + part * grid_q, STRIDE, stride=grid_k)
        sent = pl.ds(g, STRIDE, stride=grid_k)
        last = jnp.where(g == grid_q - 1, 1.0, 0.0)
        gkv_own[at, :qw] = gk_near[shifted] + gk_s[mine, :]
        gkv_send[at, :qw] = (gk_s[sent, :] + last * gk_near[:WIN]).astype(BF16)
        for h in range(HEADS):
            cols = slice(h * 128, (h + 1) * 128)
            wide = slice(qw + h * 128, qw + (h + 1) * 128)
            gkv_own[at, wide] = gv_near[shifted, cols] + gv_s[h, mine, :]
            gkv_send[at, wide] = (gv_s[h, sent, :] + last * gv_near[:WIN, cols]).astype(BF16)
        return 0

    lax.fori_loop(0, grid_q, back, 0)


def mix_backward(grad_q, grad_kv, rows, gain, bias, w_mix, slab, d_gain, d_bias, carried):
    grad_mixed = jnp.concatenate([grad_q * score_scale(grad_q.shape[1]), grad_kv], axis=1).astype(BF16)
    unit, scale = norm_parts(rows)
    normed = (unit * gain[0:1] + bias[0:1]).astype(BF16)
    add_columns(slab, 0, t_dot(normed, grad_mixed))
    grad_normed = dot_t(grad_mixed, w_mix[...])
    d_gain[...] += col_sum(grad_normed * unit)
    d_bias[...] += col_sum(grad_normed)
    return carried + norm_back(grad_normed, unit, scale, gain[0:1])


def fourth_kernel(
    info, gq, gkv, got, z, gmid, gain_next, bias_next, w_mix_next,
    q, kv, halo, o, lse, active, slope, mid, x, gain, bias, w_mix, w_proj, w_in, w_back,
    cross0, cross1, local0, local1, gq_last, gkv_last, gmid_last, halo_out, keep, send, slab_last,
    dn_gain, dn_bias, d_gain, d_bias, d_gain_first, d_bias_first,
    ext, slab, gq_ext, gk_ext, gv_ext, gmid_ext,
):
    step = pl.program_id(0)
    qw = q.shape[1]
    n = kv.shape[0]

    @pl.when(step == 0)
    def _():
        load_extended(halo, kv, ext)
        for ref in (
            slab, slab_last, dn_gain, dn_bias, d_gain, d_bias, d_gain_first, d_bias_first, gq_ext, gk_ext, gv_ext, gmid_ext
        ):
            ref[...] = jnp.zeros_like(ref)

    limit = info[1]
    start = pl.multiple_of(step * TB, TB)
    base = info[0] * n + start
    grad_kv = gkv[...] + got[...].astype(F32)
    grad_z = mix_backward(
        gq[...], grad_kv, z[...].astype(F32), gain_next, bias_next, w_mix_next, slab, dn_gain, dn_bias, gmid[...]
    )
    grad_low = grad_z.astype(BF16)
    emit_block(info, step, grad_low, False, 0, (cross0, cross1), (local0, local1))
    unit, scale = norm_parts(mid[...])
    normed = (unit * gain[1:2] + bias[1:2]).astype(BF16)
    attended = o[...]
    grad_out, grad_mid = feed_backward(
        grad_low.astype(F32), active[...], slope[...].astype(F32), normed, unit, scale, attended, gain,
        w_proj, w_in, w_back, slab, w_mix_next.size // w_proj.shape[1], d_gain, d_bias,
    )
    shifted = pl.ds(pl.multiple_of(start + WIN, WIN), TB)
    gmid_ext[shifted] = grad_mid
    weighted = grad_out.astype(F32) * attended.astype(F32)
    for sub in range(TB // WIN):
        rows = slice(sub * WIN, (sub + 1) * WIN)
        near = pl.ds(pl.multiple_of(start + sub * WIN, WIN), 2 * WIN)
        delta = jnp.concatenate(
            [jnp.sum(weighted[rows, h * 128 : (h + 1) * 128], axis=-1, keepdims=True) for h in range(HEADS)], axis=0
        )
        g_q, g_k, g_v = near_backward(
            q[rows], ext[near, :qw], ext[near, qw:], grad_out[rows], stack_stat(lse[rows]), delta,
            base + sub * WIN, limit,
        )
        gq_ext[pl.ds(pl.multiple_of(start + (sub + 1) * WIN, WIN), WIN)] = g_q
        gk_ext[near] += g_k
        gv_ext[near] += g_v

    @pl.when(step == 0)
    def _():
        halo_out[...] = jnp.concatenate([gk_ext[:WIN], gv_ext[:WIN]], axis=1).astype(BF16)
        gk_ext[:WIN] = jnp.zeros((WIN, gk_ext.shape[1]), F32)
        gv_ext[:WIN] = jnp.zeros((WIN, gv_ext.shape[1]), F32)

    whole_rows = pl.ds(start, TB)
    grad_x = mix_backward(
        gq_ext[whole_rows], jnp.concatenate([gk_ext[whole_rows], gv_ext[whole_rows]], axis=1),
        x[whole_rows].astype(F32), gain, bias, w_mix, slab_last, d_gain_first, d_bias_first, gmid_ext[whole_rows],
    )
    grad_x = grad_x.astype(BF16)
    emit_block(info, step, grad_x[WIN:], True, 0, (cross0, cross1), (local0, local1))

    @pl.when(step > 0)
    def _():
        emit_rows(info, step * (TB // WIN) - 1, grad_x[:WIN], True, (cross0, cross1), (local0, local1))

    @pl.when(step == pl.num_programs(0) - 1)
    def _():
        gq_last[...] = gq_ext[n:]
        gkv_last[...] = jnp.concatenate([gk_ext[n:], gv_ext[n:]], axis=1)
        gmid_last[...] = gmid_ext[n:]
        split_slab(info, slab, keep, send)


def fifth_kernel(info, gq, gkv, got, x, gmid, gain, bias, w_mix, slab_in, *refs):
    vectors, squares = refs[:8], refs[8:10]
    cross, local, (keep, send, small, slab, d_gain, d_bias) = refs[-10:-8], refs[-8:-6], refs[-6:]
    slab[...] = slab_in[...]
    d_gain[...] = vectors[0][...]
    d_bias[...] = vectors[4][...]
    n = x.shape[0] - WIN
    grad_x = mix_backward(
        gq[...], gkv[...] + got[...].astype(F32), x[n:].astype(F32), gain, bias, w_mix, slab, d_gain, d_bias, gmid[...]
    )
    emit_rows(info, n // WIN - 1, grad_x.astype(BF16), True, cross, local)
    split_slab(info, slab, keep, send)
    small_rows(info, (d_gain,) + vectors[1:4] + (d_bias,) + vectors[5:], squares, small)
    put_riders(small[...], send, keep.shape[0])


def put_riders(rows, send, at):
    count = rows.shape[0]
    coarse = rows.astype(BF16)
    send[at : at + count] = coarse
    send[at + count :] = (rows - coarse.astype(F32)).astype(BF16)


def riders_of(got, at):
    count = (got.shape[0] - at) // 2
    return got[at : at + count].astype(F32) + got[at + count :].astype(F32)


def stage_kernel(digits, *refs, groups, ways, stage, riders):
    refs = list(refs)
    parts = [(refs.pop(0), [refs.pop(0) for _ in range(count)]) for count in groups]
    small = refs.pop(0) if riders else None
    messages = [refs.pop(0) for _ in range(max(ways - 1, 1))]
    kept_out = refs.pop(0) if ways > 1 else None
    small_out = refs.pop(0) if riders else None
    total = refs.pop(0)
    vectors = small[...] if riders else None
    at = 0
    for kept, got in parts:
        rows = kept.shape[0]
        value = kept[...]
        for g in got:
            value = value + g[:rows].astype(F32)
            if g.shape[0] > rows:
                vectors = vectors + riders_of(g, rows)
        total[at : at + rows] = value
        at += rows
    chunk = at // ways

    def piece(which):
        return total[pl.ds(pl.multiple_of(which * chunk, 16), chunk)]

    mine = digits[9 + stage] if ways > 1 else 0
    for i, message in enumerate(messages):
        message[:chunk] = piece(mine ^ (i + 1) if ways > 1 else 0).astype(BF16)
        if riders:
            put_riders(vectors, message, chunk)
    if ways > 1:
        kept_out[...] = piece(mine)
    if riders:
        small_out[...] = vectors


def exchange_kernel(digits, mine, theirs, rows_out, small_out):
    count = rows_out.shape[0]
    rows_out[...] = (mine[:count].astype(F32) + theirs[:count].astype(F32)).astype(BF16)
    small_out[...] = riders_of(mine, count) + riders_of(theirs, count)


def again_kernel(digits, rows, small, message):
    message[: rows.shape[0]] = rows[...]
    put_riders(small[...], message, rows.shape[0])


def order_kernel(digits, *refs, stage, count):
    pieces, out = refs[:count], refs[-1]
    rows = pieces[0].shape[0]
    for c, piece in enumerate(pieces):
        out[pl.ds(pl.multiple_of((digits[9 + stage] ^ c) * rows, 16), rows)] = piece[...]


def assemble_kernel(info, *refs):
    own, other, out, token, wide, sems = refs[:4], *refs[4:]
    token[...] = jnp.zeros_like(token)
    core = info[0]
    rows = out.shape[1]

    def leave(t):
        column = core if t < 4 else 1 - core
        image = (info[5] ^ (t % 4 // 2)) * 4 + column * 2 + (info[4] ^ (t % 2))
        return pltpu.make_async_copy(wide.at[t], out.at[image], sems.at[t])

    for t in range(8):
        if t < 4:
            block = own[t][pl.ds(pl.multiple_of(core * rows, rows), rows)]
        else:
            block = other[t - 4]
        wide[t] = block.astype(F32)
        leave(t).start()
    for t in range(8):
        leave(t).wait()


def hold_kernel(info, first, second, *refs):
    refs[-2][...] = first[...]
    refs[-1][...] = second[...]


def small_rows(info, vectors, squares, out):
    width = out.shape[1]
    once = jnp.where(info[7] == 0, 1.0, 0.0)
    lane = lax.broadcasted_iota(jnp.int32, (1, width), 1)
    out[...] = jnp.zeros_like(out)
    for i, vector in enumerate(vectors):
        out[i : i + 1] = jnp.sum(vector[...], axis=0, keepdims=True) * once
    for i in range(6):
        total = jnp.sum(jnp.sum(squares[i // 3][i % 3], axis=0, keepdims=True), axis=1, keepdims=True)
        out[8 + i : 9 + i] = jnp.where(lane == info[6], total * once, 0.0)


def trade_kernel(info, *refs):
    pieces, out = refs[:4], refs[-1]
    rows = out.shape[1]
    for t in range(4):
        out[t] = pieces[t][pl.ds(pl.multiple_of((1 - info[0]) * rows, rows), rows)]


def unpack_kernel(info, mine, theirs, small, counted, mix, proj, up, down, gain, bias, rms, wide, *, sizes):
    core = info[9]
    wide[core] = mine[...].astype(F32)
    wide[1 - core] = theirs[...].astype(F32)
    rows_a, rows_b, rows_c, ways = sizes
    early = rows_a // 2 // ways
    late = (rows_b + rows_c) // 2 // ways
    rows_mix = rows_c

    def pieces(slab, start, stop):
        total = {"a": rows_a, "b": rows_b, "c": rows_c}[slab] // 2
        size, shift, skip = {"a": (early, 0, 0), "b": (late, early, 0), "c": (late, early, rows_b // 2)}[slab]
        at = start
        while at < stop:
            half, row = at // total, at % total
            along = row + skip
            count = min(stop - at, total - row, size - along % size)
            yield at - start, half, along // size * (early + late) + shift + along % size, count
            at += count

    width = wide.shape[2]
    places = {0: (("c", 0), ("b", rows_mix)), 1: (("b", 0), ("a", 0))}
    for layer in range(2):
        (slab, at), (feed, feed_at) = places[layer]
        for out, name in ((mix, slab), (proj, feed), (up, feed), (down, feed)):
            if name == feed and out is not mix:
                at = feed_at
            rows, cols = out.shape[1:]
            for i in range(cols // width):
                for offset, half, row, count in pieces(name, at + i * rows, at + (i + 1) * rows):
                    out[layer, offset : offset + count, i * width : (i + 1) * width] = wide[half, row : row + count]
            if out is not mix:
                feed_at = at + rows * cols // width
    for layer in range(2):
        for norm in range(2):
            gain[layer, norm : norm + 1] = small[2 * layer + norm : 2 * layer + norm + 1]
            bias[layer, norm : norm + 1] = small[4 + 2 * layer + norm : 5 + 2 * layer + norm]
    images = rms.shape[1]
    sums = pltpu.roll(small[8:16], small.shape[1] - (info[6] - info[6] % images), 1)
    rms[...] = jnp.sqrt(sums[: rms.shape[0], :images] / counted[...])


VMEM = pl.BlockSpec(memory_space=pltpu.VMEM)


def call(kernel, info, operands, specs, outs, out_specs, scratch=(), grid=(), work=0, aliases={}, limit=VMEM_LIMIT):
    moved = sum(math.prod(a.shape) * a.dtype.itemsize for a in list(operands) + jax.tree.leaves(outs))
    single = not isinstance(outs, list)
    views = list(specs) + ([out_specs] if single else list(out_specs))

    def body_of(info, *refs):
        seen = [view(ref) if callable(view) else ref for view, ref in zip(views, refs)]
        kernel(info, *seen, *refs[len(views) :])

    def plain(view):
        return VMEM if callable(view) else view

    return pl.pallas_call(
        body_of,
        grid_spec=pltpu.PrefetchScalarGridSpec(
            num_scalar_prefetch=1,
            grid=grid,
            in_specs=[plain(v) for v in specs],
            out_specs=plain(out_specs) if single else [plain(v) for v in out_specs],
            scratch_shapes=list(scratch),
        ),
        out_shape=outs,
        input_output_aliases=aliases,
        compiler_params=pltpu.CompilerParams(vmem_limit_bytes=limit),
        cost_estimate=pl.CostEstimate(flops=int(work * 1.15e9), bytes_accessed=moved, transcendentals=0),
    )(info, *operands)


def whole(array):
    return VMEM


def tiled(array):
    return lambda ref: ref.at[pl.ds(pl.multiple_of(pl.program_id(0) * TB, TB), TB)]


def after_window(ref):
    return ref.at[pl.ds(WIN, ref.shape[0] - WIN)]


def last_rows(ref):
    return ref.at[pl.ds(ref.shape[0] - WIN, WIN)]


ANY = pl.BlockSpec(memory_space=pl.ANY)


def shape(dims, kind):
    return jax.ShapeDtypeStruct(dims, kind)


def after(value, *others):
    return lax.optimization_barrier((value, others))[0]


def body(edge_rows, lengths, norm_gain, norm_bias, w_qkv, w_out, w_up, w_down):
    sections = lax.axis_size("section")
    index = lax.axis_index("section")
    images, rows_dev, width = edge_rows.shape
    seats = 2 * images
    rep = sections // seats
    seat = index // rep
    twin = index % rep
    rows_piece = rows_dev * rep
    qw = (w_qkv.shape[2] - width) // 2
    kvw = w_qkv.shape[2] - qw
    hidden = w_up.shape[2]
    n = rows_piece * images // 2
    if n != 2 * TB:
        raise ValueError("block size")
    quarter = images // 2
    steps = (n // TB,)

    def route(pairs):
        return [(s * rep + e, d * rep + e) for s, d in pairs for e in range(rep)]

    if rep > 1:
        groups = [[s * rep + e for e in range(rep)] for s in range(seats)]
        edge_rows = lax.all_gather(edge_rows, "section", axis_index_groups=groups, axis=1, tiled=True)

    chip = seat // 2
    part = seat % 2
    fz, fl, fy = chip // 4, (chip // 2) % 2, chip % 2
    limit = lengths[chip]
    spot = lax.axis_index("dp") * images + chip
    dp_count = lax.axis_size("dp")
    dp_index = lax.axis_index("dp")

    def partners(masks):
        total = dp_count * sections
        spot = dp_index * sections + index
        digit = sum(((spot // m) % 2) << i for i, m in enumerate(masks))
        routes = []
        for c in range(1, 1 << len(masks)):
            flips = sum(m for i, m in enumerate(masks) if (c >> i) & 1)
            routes.append((c, [(s, s ^ flips) for s in range(total)]))
        return digit, routes

    dp_masks = [sections << b for b in range(dp_count.bit_length() - 1)]
    section_masks = [1 << b for b in range(1, sections.bit_length() - 1)]
    plane = [dp_masks[0], section_masks[0]]
    rest = section_masks[1:] + dp_masks[1:]
    digits = [partners(masks)[0] for masks in [[1], plane] + [[m] for m in rest]]
    counted = (lengths.astype(F32) * width)[None, :]
    info = jnp.stack([part, limit, chip % quarter, fz, fy, fz, spot, twin, index % 2] + digits).astype(jnp.int32)
    swap = route([(s, s ^ 1) for s in range(seats)])

    def bits(s):
        return s // 8, (s // 4) % 2, (s // 2) % 2, s % 2

    by_column = edge_rows.reshape(2, 2, 2, rows_piece, width)
    traded = lax.dynamic_index_in_dim(by_column, 1 - part, 1, keepdims=False).reshape(4, rows_piece, width)
    traded = lax.ppermute(traded, "section", swap)
    column = lax.dynamic_index_in_dim(by_column, part, 1, keepdims=False).reshape(4, rows_piece, width)
    received = [None] * 4
    for t in (2, 3, 0, 1):
        tz, ty = t // 2, t % 2
        image = (fz ^ tz) * 2 + (fy ^ ty)
        own = lax.dynamic_index_in_dim(column, image, 0, keepdims=False)
        got = lax.dynamic_index_in_dim(traded, image, 0, keepdims=False)
        message = jnp.where(part == 0, jnp.concatenate([own, got]), jnp.concatenate([got, own]))
        pairs = []
        for s in range(seats):
            z, l, y, k = bits(s)
            pairs.append((s, ((z ^ tz) * 4 + k * 2 + (y ^ ty)) * 2 + l))
        received[t] = lax.ppermute(message, "section", route(pairs))

    def send_back(message, tz, ty):
        pairs = []
        for s in range(seats):
            z, l, y, p = bits(s)
            pairs.append((s, ((z ^ tz) * 4 + p * 2 + (y ^ ty)) * 2 + l))
        return lax.ppermute(message, "section", route(pairs))

    def trade(got, *awaited):
        out = shape((4, rows_piece, width), BF16)
        send = call(trade_kernel, info, got + list(awaited), [VMEM] * 4 + [ANY] * len(awaited), out, VMEM)
        return lax.ppermute(send, "section", swap)

    first_to_second = route([(2 * c, 2 * c + 1) for c in range(images)])
    second_to_first = route([(2 * c + 1, 2 * c) for c in range(images)])

    dma = pltpu.SemaphoreType.DMA
    rows_q = shape((n, qw), BF16)
    rows_kv = shape((n, kvw), BF16)
    rows_low = shape((n, width), BF16)
    rows_wide = shape((n, width), F32)
    rows_stat = shape((n, 128), F32)
    rows_hidden = shape((n, hidden), BF16)
    grad_k_shape = shape((n + WIN, qw), F32)
    grad_v_shape = shape((n + WIN, width), F32)
    mix_rows = w_qkv.shape[1] * w_qkv.shape[2] // width
    feed_rows = (w_out[0].size + w_up[0].size + w_down[0].size) // width
    vec_shape = shape((8, width), F32)
    squares_shape = shape((3, 8, width), F32)
    ext = pltpu.VMEM((n + WIN, kvw), BF16)

    g0, g1, b0, b1 = norm_gain[0], norm_gain[1], norm_bias[0], norm_bias[1]

    halo_shape = shape((WIN, kvw), BF16)
    outs = [shape((n + WIN, width), BF16), rows_q, rows_kv, halo_shape]
    x, q0, kv0, halo0 = call(
        first_kernel, info, received + [g0, b0, w_qkv[0]], [VMEM] * 7,
        outs, [whole(o) for o in outs], work=6,
    )
    halo0 = lax.ppermute(halo0, "section", first_to_second)

    outs = [rows_low, rows_q, rows_kv, rows_low, rows_stat, rows_hidden, rows_hidden, rows_wide, squares_shape]
    z, q1, kv1, o0, lse0, active0, slope0, mid0, squares0 = call(
        second_kernel, info, [x, q0, kv0, halo0, g0, b0, w_out[0], w_up[0], w_down[0], g1, b1, w_qkv[1]],
        [after_window] + [VMEM] * 11, outs, [VMEM] * len(outs), [ext], (1,), work=15,
        limit=2 * VMEM_LIMIT,
    )
    kv_other = lax.ppermute(kv1, "section", first_to_second)

    rows_k_all = shape((2 * n, qw), BF16)
    rows_v_all = shape((2 * n, width), BF16)
    outs = [rows_q, rows_k_all, rows_v_all, rows_wide, rows_stat]
    qr, kr, vr, o_far, lse_far = call(
        far_forward_kernel, info, [q1, kv1, kv_other], [whole(a) for a in (q1, kv1, kv_other)],
        outs, [whole(o) for o in outs],
        [pltpu.VMEM((n, qw), F32), pltpu.VMEM((2 * n, qw), F32), pltpu.VMEM((HEADS, 2 * n, 128), F32),
         pltpu.VMEM((HEADS, n, 128), F32), pltpu.VMEM((n, 128), F32)], work=14,
    )

    message = shape((2 * rows_piece, width), BF16)
    outs = [message] * 4 + [rows_low, rows_stat, shape((n, qw), F32), grad_k_shape, grad_v_shape, rows_wide,
            shape((feed_rows // 2, width), F32), shape((feed_rows // 2, width), BF16),
            vec_shape, vec_shape, squares_shape]
    (cross0, cross1, local0, local1, go1, stat1, gq_near, gk_near, gv_near, gmid1, keep_a, send_a,
     d_gain11, d_bias11, squares1) = call(
        third_kernel, info,
        received + [q1, kv1, kv_other, o_far, lse_far, z, g1, b1, w_out[1], w_up[1], w_down[1]],
        [VMEM] * 4
        + [tiled(q1), whole(kv1), last_rows]
        + [tiled(o_far), tiled(lse_far), tiled(z)]
        + [whole(a) for a in (g1, b1, w_out[1], w_up[1], w_down[1])],
        outs,
        [whole(message)] * 4 + [tiled(o) for o in outs[4:7]] + [whole(outs[7]), whole(outs[8]), tiled(outs[9])]
        + [whole(o) for o in outs[10:]],
        [ext, pltpu.VMEM((TB, width), BF16), pltpu.VMEM((feed_rows, width), F32)], steps, work=24,
    )
    forward_back = [None, None, send_back(cross0, 1, 0), None]

    outs = [shape((n, qw), F32), shape((n, kvw), F32), rows_kv]
    operands = [qr, kr, vr, go1, stat1, gq_near, gk_near, gv_near]
    gq1, gkv1, gkv_send = call(
        far_backward_kernel, info, operands, [whole(a) for a in operands], outs, [whole(o) for o in outs],
        [pltpu.VMEM((HEADS, n, 128), F32), pltpu.VMEM((n, 128), F32), pltpu.VMEM((n, qw), F32),
         pltpu.VMEM((2 * n, qw), F32), pltpu.VMEM((HEADS, 2 * n, 128), F32)], work=18,
    )
    def pair(message):
        return lax.ppermute(message, ("dp", "section"), partners([1])[1][0][1])

    def send_all(messages, masks):
        return [lax.ppermute(m, ("dp", "section"), way) for m, (_, way) in zip(messages, partners(masks)[1])]

    small_shape = shape((16, width), F32)
    rider_rows = 2 * small_shape.shape[0]

    def stage(groups, small, ways, number):
        operands = [a for kept, got in groups for a in [kept] + got] + ([] if small is None else [small])
        rows = sum(kept.shape[0] for kept, _ in groups)
        riders = small is not None
        outs = [shape((rows // ways + rider_rows * riders, width), BF16)] * max(ways - 1, 1)
        outs += [shape((rows // ways, width), F32)] * (ways > 1) + [small_shape] * riders
        kernel = functools.partial(
            stage_kernel, groups=[len(got) for _, got in groups], ways=ways, stage=number, riders=riders
        )
        made = call(
            kernel, info, operands, [VMEM] * len(operands), outs, [VMEM] * len(outs), [pltpu.VMEM((rows, width), F32)]
        )
        sent = max(ways - 1, 1)
        return made[:sent], made[sent] if ways > 1 else None, made[-1] if riders else None

    def gather(piece, masks, number):
        return in_order([piece] + [lax.ppermute(piece, ("dp", "section"), way) for _, way in partners(masks)[1]], number)

    def in_order(pieces, number, awaited=()):
        out = shape((len(pieces) * pieces[0].shape[0], width), BF16)
        kernel = functools.partial(order_kernel, stage=number, count=len(pieces))
        return call(kernel, info, pieces + list(awaited), [VMEM] * len(pieces) + [ANY] * len(awaited), out, VMEM)

    messages, kept_a, _ = stage([(keep_a, [pair(send_a)])], None, 4, 1)
    got_a = send_all(messages, plane)
    gkv_got = lax.ppermute(after(gkv_send, forward_back[2], *got_a), "section", second_to_first)
    forward_back[3] = send_back(after(cross1, forward_back[2]), 1, 1)
    forward_back[0] = send_back(after(local0, forward_back[2]), 0, 0)
    forward_back[1] = send_back(after(local1, forward_back[2]), 0, 1)

    slab_rows = mix_rows + feed_rows
    early_shape = slab_rows // 2, width
    mix_slab = shape((mix_rows, width), F32)
    outs = [message] * 4 + [shape((WIN, qw), F32), shape((WIN, kvw), F32), shape((WIN, width), F32), halo_shape,
            shape(early_shape, F32), shape(early_shape, BF16), mix_slab] + [vec_shape] * 6
    operands = [gq1, gkv1, gkv_got, z, gmid1, g1, b1, w_qkv[1], q0, kv0, halo0, o0, lse0, active0, slope0, mid0, x, g0,
                b0, w_qkv[0], w_out[0], w_up[0], w_down[0]]
    (cross0, cross1, local0, local1, gq_last, gkv_last, gmid_last, halo_send, keep_early, send_early, slab_last,
     d_gain10, d_bias10, d_gain01, d_bias01, d_gain00, d_bias00) = call(
        fourth_kernel, info, operands,
        [tiled(a) for a in operands[:5]] + [VMEM] * 3 + [tiled(q0), VMEM, VMEM] + [tiled(a) for a in operands[11:16]]
        + [VMEM] * 7,
        outs, [VMEM] * len(outs),
        [ext, pltpu.VMEM((slab_rows, width), F32), pltpu.VMEM((n + WIN, qw), F32), pltpu.VMEM((n + WIN, qw), F32),
         pltpu.VMEM((n + WIN, width), F32), pltpu.VMEM((n + WIN, width), F32)], steps, work=20,
    )
    outs = [halo_shape, shape(early_shape, BF16)]
    halo_send, send_early = call(
        hold_kernel, info, [halo_send, send_early] + forward_back, [VMEM] * 2 + [ANY] * 4, outs, [VMEM] * 2
    )
    halo_got = lax.ppermute(halo_send, "section", second_to_first)

    got_early = pair(send_early)
    outs = [message] * 4 + [shape((mix_rows // 2, width), F32), shape((mix_rows // 2 + rider_rows, width), BF16), small_shape]
    operands = [gq_last, gkv_last, halo_got, x, gmid_last, g0, b0, w_qkv[0], slab_last]
    operands += [d_gain00, d_gain01, d_gain10, d_gain11, d_bias00, d_bias01, d_bias10, d_bias11, squares0, squares1]
    aliases = {1 + len(operands) + i: i for i in range(4)}
    operands += [cross0, cross1, local0, local1]
    cross0, cross1, local0, local1, keep_late, send_late, small = call(
        fifth_kernel, info, operands, [VMEM] * len(operands), outs, [VMEM] * len(outs),
        [pltpu.VMEM((mix_rows, width), F32), pltpu.VMEM((8, width), F32), pltpu.VMEM((8, width), F32)],
        aliases=aliases,
    )

    def assemble(own, other):
        outs = [shape((images, rows_piece, width), F32), shape((8, 128), F32)]
        out, token = call(
            assemble_kernel, info, own + [other], [VMEM] * 5, outs, [ANY, VMEM],
            [pltpu.VMEM((images, rows_piece, width), F32), dma((images,))],
        )
        if rep > 1:
            out = lax.dynamic_slice_in_dim(out, twin * rows_dev, rows_dev, 1)
        return out, token

    backward_back = [send_back(local0, 0, 0), None, send_back(cross0, 1, 0), None]
    got_late = pair(send_late)
    groups = [(keep_early, [got_early]), (keep_late, [got_late])]
    messages, kept, small = stage(groups, small, 4, 1)
    forward_trade = trade(forward_back, send_late)
    forward_rows, forward_token = assemble(forward_back, forward_trade)
    groups = [(kept_a, got_a), (kept, send_all(messages, plane))]
    number = 2
    scattered = []
    while number - 1 < len(rest) and sum(kept.shape[0] for kept, _ in groups) % 32 == 0:
        messages, kept, small = stage(groups, small, 2, number)
        groups = [(kept, send_all(messages, [rest[number - 2]]))]
        scattered.append(number)
        number += 1
    scattered_rows = groups[-1][1]
    backward_back[3] = send_back(after(cross1, backward_back[2]), 1, 1)
    backward_back[1] = send_back(after(local1, backward_back[2], *scattered_rows), 0, 1)
    (both,), _, small = stage(groups, small, 1, 0)
    both = after(both, backward_back[0], backward_back[2])
    rows_shape = shape((both.shape[0] - rider_rows, width), BF16)
    while number - 2 < len(rest):
        (got,) = send_all([both], [rest[number - 2]])
        rows, small = call(exchange_kernel, info, [both, got], [VMEM] * 2, [rows_shape, small_shape], [VMEM] * 2)
        number += 1
        if number - 2 < len(rest):
            both = call(again_kernel, info, [rows, small], [VMEM] * 2, shape(both.shape, BF16), VMEM)
    both = after(rows, backward_back[1], backward_back[3])
    for number in scattered[::-1]:
        both = gather(both, [rest[number - 2]], number)
    backward_trade = trade(backward_back, rows)
    backward_rows, backward_token = assemble(backward_back, backward_trade)
    both = in_order([both] + send_all([both] * 3, plane), 1, [backward_token, forward_token])
    theirs = pair(both)
    outs = [shape(w.shape, F32) for w in (w_qkv, w_out, w_up, w_down, norm_gain, norm_bias)] + [shape((6, images), F32)]
    sizes = (feed_rows, slab_rows, mix_rows, 1 << len(plane))
    grads = call(
        functools.partial(unpack_kernel, sizes=sizes), info, [both, theirs, small, counted],
        [VMEM] * 4, outs, [whole(o) for o in outs],
        [pltpu.VMEM((2,) + both.shape, F32)],
    )
    return (forward_rows, backward_rows, grads[6], grads[4], grads[5]) + tuple(grads[:4])


def solution(mesh):
    placed = (P("dp", "section", None), P("dp"), P(), P(), P(), P(), P(), P())
    return jax.shard_map(
        body,
        mesh=mesh,
        in_specs=placed,
        out_specs=(P("dp", "section", None), P("dp", "section", None), P(None, "dp"), P(), P(), P(), P(), P(), P()),
        check_vma=False,
    )
```

```python
import functools
import math

import jax
import jax.numpy as jnp
from jax import lax
from jax.experimental import pallas as pl
from jax.experimental.pallas import tpu as pltpu
from jax.sharding import PartitionSpec as P

HEADS = 2
WIN = 128
STRIDE = 128
NEG = -1e30
F32 = jnp.float32
BF16 = jnp.bfloat16
TB = 768
RES = 8
UNROLL = 16
RES_BACK = 16
UNROLL_BACK = 8
VMEM_LIMIT = 16 * 1024 * 1024


def dot(left, right):
    return lax.dot_general(left, right, (((1,), (0,)), ((), ())), preferred_element_type=F32)


def dot_t(left, right):
    return lax.dot_general(left, right, (((1,), (1,)), ((), ())), preferred_element_type=F32)


def t_dot(left, right):
    return lax.dot_general(left, right, (((0,), (0,)), ((), ())), preferred_element_type=F32)


def score_scale(query_width):
    return 1.0 / math.sqrt(query_width // HEADS)


def norm_parts(rows):
    centre = rows - jnp.mean(rows, axis=-1, keepdims=True)
    scale = lax.rsqrt(jnp.mean(centre * centre, axis=-1, keepdims=True) + 1e-05)
    return centre * scale, scale


def norm_back(grad, unit, scale, gain):
    scaled = grad * gain
    first = jnp.mean(scaled, axis=-1, keepdims=True)
    second = jnp.mean(scaled * unit, axis=-1, keepdims=True)
    return scale * (scaled - first - unit * second)


def col_sum(rows):
    return jnp.sum(rows.reshape(rows.shape[0] // 8, 8, rows.shape[1]), axis=0)


def gelu_pair(hidden):
    c0 = math.sqrt(2.0 / math.pi)
    square = hidden * hidden
    share = 0.5 + 0.5 * jnp.tanh(hidden * (c0 + (c0 * 0.044715) * square))
    active = hidden * share
    slope = share + active * (1.0 - share) * (2.0 * c0 + (6.0 * c0 * 0.044715) * square)
    return active, slope


def head_split(rows):
    lane = lax.broadcasted_iota(jnp.int32, rows.shape, 1)
    zero = jnp.zeros_like(rows)
    low = lane < rows.shape[1] // HEADS
    return jnp.concatenate([jnp.where(low, rows, zero), jnp.where(low, zero, rows)], axis=0)


def head_join(stacked):
    half = stacked.shape[0] // 2
    lane = lax.broadcasted_iota(jnp.int32, (half, stacked.shape[1]), 1)
    return jnp.where(lane < stacked.shape[1] // HEADS, stacked[:half], stacked[half:])


def near_masks(base, limit):
    row = lax.broadcasted_iota(jnp.int32, (2 * WIN, WIN), 0)
    row = jnp.where(row >= WIN, row - WIN, row)
    col = lax.broadcasted_iota(jnp.int32, (2 * WIN, WIN), 1)
    own = col <= row
    key = base + col - jnp.where(own, 0, WIN)
    allowed = (key >= 0) & ((key < limit) | (col == row))
    return own, allowed


def near_scores(split_q, keys, own, allowed):
    scores = dot_t(split_q, keys)
    folded = jnp.where(own, scores[:, WIN:], scores[:, :WIN])
    return jnp.where(allowed, folded, NEG)


def unfold(folded, own):
    return jnp.concatenate([jnp.where(own, 0.0, folded), jnp.where(own, folded, 0.0)], axis=1).astype(BF16)


def near_forward(queries, keys, values, base, limit):
    own, allowed = near_masks(base, limit)
    scores = near_scores(head_split(queries), keys, own, allowed)
    largest = jnp.max(scores, axis=-1, keepdims=True)
    powers = jnp.exp(scores - largest)
    total = jnp.sum(powers, axis=-1, keepdims=True)
    weights = unfold(powers, own)
    hd = values.shape[1] // HEADS
    out = [dot(weights[h * WIN : (h + 1) * WIN], values[:, h * hd : (h + 1) * hd]) for h in range(HEADS)]
    return out, largest, total, powers


def near_backward(queries, keys, values, grad_out, log_total, delta, base, limit, weights=None):
    own, allowed = near_masks(base, limit)
    split_q = head_split(queries)
    if weights is None:
        weights = jnp.exp(near_scores(split_q, keys, own, allowed) - log_total)
    hd = values.shape[1] // HEADS
    pull = jnp.concatenate(
        [dot_t(grad_out[:, h * hd : (h + 1) * hd], values[:, h * hd : (h + 1) * hd]) for h in range(HEADS)], axis=0
    )
    pull = jnp.where(own, pull[:, WIN:], pull[:, :WIN])
    slope = weights * (pull - delta)
    grad_q = head_join(dot(unfold(slope, own), keys))
    row = lax.broadcasted_iota(jnp.int32, (WIN, 2 * WIN), 0)
    col = lax.broadcasted_iota(jnp.int32, (WIN, 2 * WIN), 1)
    here = (row <= jnp.where(col >= WIN, col - WIN, col)).astype(F32).astype(BF16)

    def turned(folded):
        flat = folded.astype(BF16).T
        current = flat * here
        return jnp.concatenate([flat - current, current], axis=0)

    grad_k = dot(turned(slope), split_q)
    weights = turned(weights)
    grad_v = jnp.concatenate(
        [dot(weights[:, h * WIN : (h + 1) * WIN], grad_out[:, h * hd : (h + 1) * hd]) for h in range(HEADS)], axis=1
    )
    return grad_q, grad_k, grad_v


def stack_stat(stat, width=128):
    return jnp.concatenate([stat[:, 0:1], stat[:, width // 2 : width // 2 + 1]], axis=0)


def spread_stat(stacked, width=128):
    half = stacked.shape[0] // 2
    lane = lax.broadcasted_iota(jnp.int32, (half, width), 1)
    return jnp.where(lane < width // 2, stacked[:half], stacked[half:])


def masked_squares(rows, base, limit):
    pos = base + lax.broadcasted_iota(jnp.int32, (rows.shape[0], 1), 0)
    return col_sum(jnp.where(pos < limit, rows * rows, 0.0))


def pick_piece(info, pieces, low, block, target):
    for t, piece in enumerate(pieces):
        tz, ty = t // 2, t % 2

        @pl.when(((block ^ info[4]) == ty) & ((info[5] ^ (0 if low else 1)) == tz))
        def _():
            target[...] = piece[...]


def emit_block(info, block, rows, to_lower, first, cross, local):
    stays = info[5] == (0 if to_lower else 1)
    at = slice(first, first + rows.shape[0])
    for ty in range(2):
        fits = (block ^ info[4]) == ty

        @pl.when(fits & stays)
        def _():
            local[ty][at] = rows

        @pl.when(fits & jnp.logical_not(stays))
        def _():
            cross[ty][at] = rows


def emit_rows(info, first, rows, to_lower, cross, local):
    units = cross[0].shape[0] // WIN
    stays = info[5] == (0 if to_lower else 1)
    for sub in range(rows.shape[0] // WIN):
        number = first + sub
        block = number // units
        at = pl.ds(pl.multiple_of((number - block * units) * WIN, WIN), WIN)
        value = rows[sub * WIN : (sub + 1) * WIN]
        for ty in range(2):
            fits = (block ^ info[4]) == ty

            @pl.when(fits & stays)
            def _():
                local[ty][at] = value

            @pl.when(fits & jnp.logical_not(stays))
            def _():
                cross[ty][at] = value


def split_slab(info, slab, keep, send):
    once = jnp.where(info[7] == 0, 1.0, 0.0)
    half = keep.shape[0]
    mine = info[8]
    keep[...] = slab[pl.ds(pl.multiple_of(mine * half, 8), half)] * once
    send[:half] = (slab[pl.ds(pl.multiple_of((1 - mine) * half, 8), half)] * once).astype(BF16)


def first_kernel(info, *refs):
    pieces = refs[:4]
    gain, bias, w_mix, x_out, q_out, kv_out, halo_out = refs[4:]
    for half in range(2):
        pick_piece(info, pieces, True, half, x_out.at[pl.ds(WIN + half * pieces[0].shape[0], pieces[0].shape[0])])
    x_out[:WIN] = jnp.zeros((WIN, x_out.shape[1]), BF16)
    qw = q_out.shape[1]

    def block(i, _):
        at = pl.ds(pl.multiple_of(i * TB, TB), TB)
        unit, _ = norm_parts(x_out[pl.ds(pl.multiple_of(i * TB + WIN, WIN), TB)].astype(F32))
        normed = (unit * gain[0:1] + bias[0:1]).astype(BF16)
        mixed = dot(normed, w_mix[...])
        q_out[at] = (mixed[:, :qw] * score_scale(qw)).astype(BF16)
        kv_out[at] = mixed[:, qw:].astype(BF16)
        return 0

    lax.fori_loop(0, q_out.shape[0] // TB, block, 0)
    halo_out[...] = kv_out[kv_out.shape[0] - WIN :]


def load_extended(halo, kv, ext):
    ext[: halo.shape[0]] = halo[...]
    ext[halo.shape[0] :] = kv[...]


def second_kernel(
    info, x, q, kv, halo, gain, bias, w_proj, w_in, w_back, gain_next, bias_next, w_mix_next,
    z_out, q_next, kv_next, o_out, lse_out, active_out, slope_out, mid_out, squares, ext,
):
    step = pl.program_id(0)
    qw = q.shape[1]
    n = kv.shape[0]

    @pl.when(step == 0)
    def _():
        load_extended(halo, kv, ext)
        squares[...] = jnp.zeros_like(squares)

    limit = info[1]
    count = q.shape[0]
    start = step * count
    base = info[0] * n + start
    outs = []
    for sub in range(count // WIN):
        near = pl.ds(pl.multiple_of(start + sub * WIN, WIN), 2 * WIN)
        keys = ext[near, :qw]
        values = ext[near, qw:]
        queries = q[sub * WIN : (sub + 1) * WIN]
        out, largest, total, _ = near_forward(queries, keys, values, base + sub * WIN, limit)
        inverse = 1.0 / total
        lse_out[sub * WIN : (sub + 1) * WIN] = spread_stat(largest + jnp.log(total))
        outs.append(jnp.concatenate([out[0] * inverse[:WIN], out[1] * inverse[WIN:]], axis=1))
    attended = jnp.concatenate(outs, axis=0).astype(BF16)
    o_out[...] = attended
    stream = x[...].astype(F32)
    branch = dot(attended, w_proj[...])
    middle = stream + branch
    mid_out[...] = middle
    unit, _ = norm_parts(middle)
    normed = (unit * gain[1:2] + bias[1:2]).astype(BF16)
    active, slope = gelu_pair(dot(normed, w_in[...]))
    active = active.astype(BF16)
    active_out[...] = active
    slope_out[...] = slope.astype(BF16)
    feed = dot(active, w_back[...])
    z = (middle + feed).astype(BF16)
    z_out[...] = z
    squares[0] += masked_squares(stream, base, limit)
    squares[1] += masked_squares(branch, base, limit)
    squares[2] += masked_squares(feed, base, limit)
    unit, _ = norm_parts(z.astype(F32))
    normed = (unit * gain_next[0:1] + bias_next[0:1]).astype(BF16)
    mixed = dot(normed, w_mix_next[...])
    q_next[...] = (mixed[:, :qw] * score_scale(qw)).astype(BF16)
    kv_next[...] = mixed[:, qw:].astype(BF16)


def far_mask(grid_q, grid_k, part_grid, residues):
    shape = (HEADS * residues * grid_q, residues * grid_k)
    row = lax.broadcasted_iota(jnp.int32, shape, 0)
    col = lax.broadcasted_iota(jnp.int32, shape, 1)
    row = jnp.where(row >= residues * grid_q, row - residues * grid_q, row)
    row_res = jnp.zeros(shape, jnp.int32)
    col_res = jnp.zeros(shape, jnp.int32)
    for r in range(1, residues):
        row_res += (row >= r * grid_q).astype(jnp.int32)
        col_res += (col >= r * grid_k).astype(jnp.int32)
    row_grid = row - row_res * grid_q + part_grid
    col_grid = col - col_res * grid_k
    allowed = (row_res == col_res) & (col_grid < row_grid)
    return allowed, col_grid * STRIDE + col_res


def far_forward_kernel(info, q, kv, other, qr, kr, vr, o_far, lse_far, q_s, k_s, v_s, o_s, lse_s):
    n, qw = q.shape
    grid_q = n // STRIDE
    grid_k = 2 * grid_q
    part = info[0]
    limit = info[1]

    def place(g, _):
        at = pl.ds(pl.multiple_of(g * STRIDE, STRIDE), STRIDE)
        own = kv[at].astype(F32)
        early = jnp.where(part == 0, own, other[at].astype(F32))
        q_s[pl.ds(g, STRIDE, stride=grid_q), :] = q[at].astype(F32)
        k_s[pl.ds(g, STRIDE, stride=grid_k), :] = early[:, :qw]
        k_s[pl.ds(g + grid_q, STRIDE, stride=grid_k), :] = own[:, :qw]
        hd = v_s.shape[1]
        for h in range(HEADS):
            v_s[h, pl.ds(g, STRIDE, stride=grid_k), :] = early[:, qw + h * 128 : qw + (h + 1) * 128]
            v_s[h, pl.ds(g + grid_q, STRIDE, stride=grid_k), :] = own[:, qw + h * 128 : qw + (h + 1) * 128]
        return 0

    lax.fori_loop(0, grid_q, place, 0)
    base_mask, key_pos = far_mask(grid_q, grid_k, part * grid_q, RES)
    rows_q = RES * grid_q
    rows_k = RES * grid_k

    def one(i):
        at_q = pl.ds(pl.multiple_of(i * rows_q, rows_q), rows_q)
        at_k = pl.ds(pl.multiple_of(i * rows_k, rows_k), rows_k)
        queries = q_s[at_q].astype(BF16)
        keys = k_s[at_k].astype(BF16)
        values = [v_s[h, at_k].astype(BF16) for h in range(HEADS)]
        qr[at_q] = queries
        kr[at_k] = keys
        for h in range(HEADS):
            vr[at_k, h * 128 : (h + 1) * 128] = values[h]
        allowed = base_mask & (key_pos + i * RES < limit)
        scores = jnp.where(allowed, dot_t(head_split(queries), keys), NEG)
        largest = jnp.max(scores, axis=-1, keepdims=True)
        powers = jnp.where(allowed, jnp.exp(scores - largest), 0.0)
        total = jnp.sum(powers, axis=-1, keepdims=True)
        safe = jnp.maximum(total, 1e-30)
        weights = (powers * (1.0 / safe)).astype(BF16)
        lse = jnp.where(total > 0.0, largest + jnp.log(safe), NEG)
        lse_s[at_q] = spread_stat(lse)
        for h in range(HEADS):
            o_s[h, at_q] = dot(weights[h * rows_q : (h + 1) * rows_q], values[h])

    def group(i, _):
        for u in range(UNROLL):
            one(i * UNROLL + u)
        return 0

    lax.fori_loop(0, STRIDE // RES // UNROLL, group, 0)

    def back(g, _):
        at = pl.ds(pl.multiple_of(g * STRIDE, STRIDE), STRIDE)
        pick = pl.ds(g, STRIDE, stride=grid_q)
        lse_far[at] = lse_s[pick, :]
        for h in range(HEADS):
            o_far[at, h * 128 : (h + 1) * 128] = o_s[h, pick, :]
        return 0

    lax.fori_loop(0, grid_q, back, 0)


def third_kernel(
    info, *refs,
):
    pieces = refs[:4]
    (q, kv, halo, o_far, lse_far, z, gain, bias, w_proj, w_in, w_back,
     cross0, cross1, local0, local1, go_out, stat_out, gq_out, gk_out, gv_out, gmid_out, keep, send,
     d_gain, d_bias, squares, ext, cot, slab) = refs[4:]
    step = pl.program_id(0)
    qw = q.shape[1]
    n = kv.shape[0]

    @pl.when(step == 0)
    def _():
        load_extended(halo, kv, ext)
        for ref in (squares, gk_out, gv_out, slab, d_gain, d_bias):
            ref[...] = jnp.zeros_like(ref)

    limit = info[1]
    start = pl.multiple_of(step * TB, TB)
    base = info[0] * n + start
    outs = []
    logs = []
    weights = []
    for sub in range(TB // WIN):
        rows = slice(sub * WIN, (sub + 1) * WIN)
        near = pl.ds(pl.multiple_of(start + sub * WIN, WIN), 2 * WIN)
        out, largest, total, powers = near_forward(q[rows], ext[near, :qw], ext[near, qw:], base + sub * WIN, limit)
        far_log = stack_stat(lse_far[rows])
        top = jnp.maximum(largest, far_log)
        near_share = jnp.exp(largest - top)
        far_share = jnp.exp(far_log - top)
        whole = total * near_share + far_share
        inverse = 1.0 / whole
        near_share = near_share * inverse
        far_share = far_share * inverse
        weights.append(powers * near_share)
        logs.append(top + jnp.log(whole))
        far = o_far[rows]
        outs.append(
            jnp.concatenate(
                [
                    out[h] * near_share[h * WIN : (h + 1) * WIN]
                    + far[:, h * 128 : (h + 1) * 128] * far_share[h * WIN : (h + 1) * WIN]
                    for h in range(HEADS)
                ],
                axis=1,
            )
        )
    attended_wide = jnp.concatenate(outs, axis=0)
    attended = attended_wide.astype(BF16)
    stream = z[...].astype(F32)
    branch = dot(attended, w_proj[...])
    middle = stream + branch
    unit, scale = norm_parts(middle)
    normed = (unit * gain[1:2] + bias[1:2]).astype(BF16)
    active, slope = gelu_pair(dot(normed, w_in[...]))
    active = active.astype(BF16)
    feed = dot(active, w_back[...])
    emit_block(info, step, z[...], True, 0, (cross0, cross1), (local0, local1))
    emit_block(info, step, (middle + feed).astype(BF16), False, 0, (cross0, cross1), (local0, local1))
    pick_piece(info, pieces, False, step, cot)
    squares[0] += masked_squares(stream, base, limit)
    squares[1] += masked_squares(branch, base, limit)
    squares[2] += masked_squares(feed, base, limit)

    pos = base + lax.broadcasted_iota(jnp.int32, (TB, 1), 0)
    upstream = jnp.where(pos < limit, cot[...].astype(F32), 0.0)
    grad_out, grad_mid = feed_backward(
        upstream, active, slope, normed, unit, scale, attended, gain, w_proj, w_in, w_back, slab, 0, d_gain, d_bias
    )
    gmid_out[...] = grad_mid
    go_out[...] = grad_out
    weighted = grad_out.astype(F32) * attended_wide
    for sub in range(TB // WIN):
        rows = slice(sub * WIN, (sub + 1) * WIN)
        near = pl.ds(pl.multiple_of(start + sub * WIN, WIN), 2 * WIN)
        delta = jnp.concatenate(
            [jnp.sum(weighted[rows, h * 128 : (h + 1) * 128], axis=-1, keepdims=True) for h in range(HEADS)], axis=0
        )
        stat_out[rows] = pack_stats(logs[sub], delta)
        gq, gk, gv = near_backward(
            q[rows], ext[near, :qw], ext[near, qw:], grad_out[rows], logs[sub], delta, base + sub * WIN, limit,
            weights[sub],
        )
        gq_out[rows] = gq
        gk_out[near] += gk
        gv_out[near] += gv

    @pl.when(step == pl.num_programs(0) - 1)
    def _():
        split_slab(info, slab, keep, send)


def pack_stats(lse, delta):
    half = lse.shape[0] // 2
    lane = lax.broadcasted_iota(jnp.int32, (half, 128), 1)
    low = jnp.where(lane < 32, lse[:half], lse[half:])
    high = jnp.where(lane < 96, delta[:half], delta[half:])
    return jnp.where(lane < 64, low, high)


def add_columns(slab, at, grad):
    rows, cols = grad.shape
    width = slab.shape[1]
    for i in range(cols // width):
        slab[at + i * rows : at + (i + 1) * rows] += grad[:, i * width : (i + 1) * width]


def feed_backward(
    upstream, active, slope, normed, unit, scale, attended, gain, w_proj, w_in, w_back, slab, at, d_gain, d_bias,
):
    low = upstream.astype(BF16)
    width = low.shape[1]
    hidden = active.shape[1]
    slab[at + width + hidden : at + width + 2 * hidden] += t_dot(active, low)
    grad_hidden = (dot_t(low, w_back[...]) * slope).astype(BF16)
    add_columns(slab, at + width, t_dot(normed, grad_hidden))
    grad_normed = dot_t(grad_hidden, w_in[...])
    d_gain[...] += col_sum(grad_normed * unit)
    d_bias[...] += col_sum(grad_normed)
    grad_mid = upstream + norm_back(grad_normed, unit, scale, gain[1:2])
    branch_low = grad_mid.astype(BF16)
    slab[at : at + width] += t_dot(attended, branch_low)
    grad_out = dot_t(branch_low, w_proj[...]).astype(BF16)
    return grad_out, grad_mid


def far_backward_kernel(
    info, qr, kr, vr, go, stat, gq_near, gk_near, gv_near, gq_out, gkv_own, gkv_send,
    go_s, stat_s, gq_s, gk_s, gv_s,
):
    n, qw = gq_near.shape
    grid_q = n // STRIDE
    grid_k = 2 * grid_q
    part = info[0]
    limit = info[1]

    def place(g, _):
        at = pl.ds(pl.multiple_of(g * STRIDE, STRIDE), STRIDE)
        pick = pl.ds(g, STRIDE, stride=grid_q)
        rows = go[at].astype(F32)
        for h in range(HEADS):
            go_s[h, pick, :] = rows[:, h * 128 : (h + 1) * 128]
        stat_s[pick, :] = stat[at]
        return 0

    lax.fori_loop(0, grid_q, place, 0)
    base_mask, key_pos = far_mask(grid_q, grid_k, part * grid_q, RES_BACK)
    rows_q = RES_BACK * grid_q
    rows_k = RES_BACK * grid_k

    def one(i):
        at_q = pl.ds(pl.multiple_of(i * rows_q, rows_q), rows_q)
        at_k = pl.ds(pl.multiple_of(i * rows_k, rows_k), rows_k)
        keys = kr[at_k]
        split_q = head_split(qr[at_q])
        grads = [go_s[h, at_q].astype(BF16) for h in range(HEADS)]
        stats = stat_s[at_q]
        lse = jnp.concatenate([stats[:, 0:1], stats[:, 32:33]], axis=0)
        delta = jnp.concatenate([stats[:, 64:65], stats[:, 96:97]], axis=0)
        allowed = base_mask & (key_pos + i * RES_BACK < limit)
        weights = jnp.exp(jnp.where(allowed, dot_t(split_q, keys), NEG) - lse)
        pull = jnp.concatenate([dot_t(grads[h], vr[at_k, h * 128 : (h + 1) * 128]) for h in range(HEADS)], axis=0)
        slope = (weights * (pull - delta)).astype(BF16)
        weights = weights.astype(BF16)
        gq_s[at_q] = head_join(dot(slope, keys))
        gk_s[at_k] = t_dot(slope, split_q)
        for h in range(HEADS):
            gv_s[h, at_k] = t_dot(weights[h * rows_q : (h + 1) * rows_q], grads[h])

    def group(i, _):
        for u in range(UNROLL_BACK):
            one(i * UNROLL_BACK + u)
        return 0

    lax.fori_loop(0, STRIDE // RES_BACK // UNROLL_BACK, group, 0)

    def back(g, _):
        at = pl.ds(pl.multiple_of(g * STRIDE, STRIDE), STRIDE)
        shifted = pl.ds(pl.multiple_of(g * STRIDE + WIN, STRIDE), STRIDE)
        gq_out[at] = gq_near[at] + gq_s[pl.ds(g, STRIDE, stride=grid_q), :]
        mine = pl.ds(g + part * grid_q, STRIDE, stride=grid_k)
        sent = pl.ds(g, STRIDE, stride=grid_k)
        last = jnp.where(g == grid_q - 1, 1.0, 0.0)
        gkv_own[at, :qw] = gk_near[shifted] + gk_s[mine, :]
        gkv_send[at, :qw] = (gk_s[sent, :] + last * gk_near[:WIN]).astype(BF16)
        for h in range(HEADS):
            cols = slice(h * 128, (h + 1) * 128)
            wide = slice(qw + h * 128, qw + (h + 1) * 128)
            gkv_own[at, wide] = gv_near[shifted, cols] + gv_s[h, mine, :]
            gkv_send[at, wide] = (gv_s[h, sent, :] + last * gv_near[:WIN, cols]).astype(BF16)
        return 0

    lax.fori_loop(0, grid_q, back, 0)


def mix_backward(grad_q, grad_kv, rows, gain, bias, w_mix, slab, d_gain, d_bias, carried):
    grad_mixed = jnp.concatenate([grad_q * score_scale(grad_q.shape[1]), grad_kv], axis=1).astype(BF16)
    unit, scale = norm_parts(rows)
    normed = (unit * gain[0:1] + bias[0:1]).astype(BF16)
    add_columns(slab, 0, t_dot(normed, grad_mixed))
    grad_normed = dot_t(grad_mixed, w_mix[...])
    d_gain[...] += col_sum(grad_normed * unit)
    d_bias[...] += col_sum(grad_normed)
    return carried + norm_back(grad_normed, unit, scale, gain[0:1])


def fourth_kernel(
    info, gq, gkv, got, z, gmid, gain_next, bias_next, w_mix_next,
    q, kv, halo, o, lse, active, slope, mid, x, gain, bias, w_mix, w_proj, w_in, w_back,
    cross0, cross1, local0, local1, gq_last, gkv_last, gmid_last, halo_out, keep, send, slab_last,
    dn_gain, dn_bias, d_gain, d_bias, d_gain_first, d_bias_first,
    ext, slab, gq_ext, gk_ext, gv_ext, gmid_ext,
):
    step = pl.program_id(0)
    qw = q.shape[1]
    n = kv.shape[0]

    @pl.when(step == 0)
    def _():
        load_extended(halo, kv, ext)
        for ref in (
            slab, slab_last, dn_gain, dn_bias, d_gain, d_bias, d_gain_first, d_bias_first, gq_ext, gk_ext, gv_ext, gmid_ext
        ):
            ref[...] = jnp.zeros_like(ref)

    limit = info[1]
    start = pl.multiple_of(step * TB, TB)
    base = info[0] * n + start
    grad_kv = gkv[...] + got[...].astype(F32)
    grad_z = mix_backward(
        gq[...], grad_kv, z[...].astype(F32), gain_next, bias_next, w_mix_next, slab, dn_gain, dn_bias, gmid[...]
    )
    grad_low = grad_z.astype(BF16)
    emit_block(info, step, grad_low, False, 0, (cross0, cross1), (local0, local1))
    unit, scale = norm_parts(mid[...])
    normed = (unit * gain[1:2] + bias[1:2]).astype(BF16)
    attended = o[...]
    grad_out, grad_mid = feed_backward(
        grad_low.astype(F32), active[...], slope[...].astype(F32), normed, unit, scale, attended, gain,
        w_proj, w_in, w_back, slab, w_mix_next.size // w_proj.shape[1], d_gain, d_bias,
    )
    shifted = pl.ds(pl.multiple_of(start + WIN, WIN), TB)
    gmid_ext[shifted] = grad_mid
    weighted = grad_out.astype(F32) * attended.astype(F32)
    for sub in range(TB // WIN):
        rows = slice(sub * WIN, (sub + 1) * WIN)
        near = pl.ds(pl.multiple_of(start + sub * WIN, WIN), 2 * WIN)
        delta = jnp.concatenate(
            [jnp.sum(weighted[rows, h * 128 : (h + 1) * 128], axis=-1, keepdims=True) for h in range(HEADS)], axis=0
        )
        g_q, g_k, g_v = near_backward(
            q[rows], ext[near, :qw], ext[near, qw:], grad_out[rows], stack_stat(lse[rows]), delta,
            base + sub * WIN, limit,
        )
        gq_ext[pl.ds(pl.multiple_of(start + (sub + 1) * WIN, WIN), WIN)] = g_q
        gk_ext[near] += g_k
        gv_ext[near] += g_v

    @pl.when(step == 0)
    def _():
        halo_out[...] = jnp.concatenate([gk_ext[:WIN], gv_ext[:WIN]], axis=1).astype(BF16)
        gk_ext[:WIN] = jnp.zeros((WIN, gk_ext.shape[1]), F32)
        gv_ext[:WIN] = jnp.zeros((WIN, gv_ext.shape[1]), F32)

    whole_rows = pl.ds(start, TB)
    grad_x = mix_backward(
        gq_ext[whole_rows], jnp.concatenate([gk_ext[whole_rows], gv_ext[whole_rows]], axis=1),
        x[whole_rows].astype(F32), gain, bias, w_mix, slab_last, d_gain_first, d_bias_first, gmid_ext[whole_rows],
    )
    grad_x = grad_x.astype(BF16)
    emit_block(info, step, grad_x[WIN:], True, 0, (cross0, cross1), (local0, local1))

    @pl.when(step > 0)
    def _():
        emit_rows(info, step * (TB // WIN) - 1, grad_x[:WIN], True, (cross0, cross1), (local0, local1))

    @pl.when(step == pl.num_programs(0) - 1)
    def _():
        gq_last[...] = gq_ext[n:]
        gkv_last[...] = jnp.concatenate([gk_ext[n:], gv_ext[n:]], axis=1)
        gmid_last[...] = gmid_ext[n:]
        split_slab(info, slab, keep, send)


def fifth_kernel(info, gq, gkv, got, x, gmid, gain, bias, w_mix, slab_in, *refs):
    vectors, squares = refs[:8], refs[8:10]
    cross, local, (keep, send, small, slab, d_gain, d_bias) = refs[-10:-8], refs[-8:-6], refs[-6:]
    slab[...] = slab_in[...]
    d_gain[...] = vectors[0][...]
    d_bias[...] = vectors[4][...]
    n = x.shape[0] - WIN
    grad_x = mix_backward(
        gq[...], gkv[...] + got[...].astype(F32), x[n:].astype(F32), gain, bias, w_mix, slab, d_gain, d_bias, gmid[...]
    )
    emit_rows(info, n // WIN - 1, grad_x.astype(BF16), True, cross, local)
    split_slab(info, slab, keep, send)
    small_rows(info, (d_gain,) + vectors[1:4] + (d_bias,) + vectors[5:], squares, small)
    put_riders(small[...], send, keep.shape[0])


def put_riders(rows, send, at):
    count = rows.shape[0]
    coarse = rows.astype(BF16)
    send[at : at + count] = coarse
    send[at + count :] = (rows - coarse.astype(F32)).astype(BF16)


def riders_of(got, at):
    count = (got.shape[0] - at) // 2
    return got[at : at + count].astype(F32) + got[at + count :].astype(F32)


def stage_kernel(digits, *refs, groups, ways, stage, riders):
    refs = list(refs)
    parts = [(refs.pop(0), [refs.pop(0) for _ in range(count)]) for count in groups]
    small = refs.pop(0) if riders else None
    messages = [refs.pop(0) for _ in range(max(ways - 1, 1))]
    kept_out = refs.pop(0) if ways > 1 else None
    small_out = refs.pop(0) if riders else None
    total = refs.pop(0)
    vectors = small[...] if riders else None
    at = 0
    for kept, got in parts:
        rows = kept.shape[0]
        value = kept[...]
        for g in got:
            value = value + g[:rows].astype(F32)
            if g.shape[0] > rows:
                vectors = vectors + riders_of(g, rows)
        total[at : at + rows] = value
        at += rows
    chunk = at // ways

    def piece(which):
        return total[pl.ds(pl.multiple_of(which * chunk, 16), chunk)]

    mine = digits[9 + stage] if ways > 1 else 0
    for i, message in enumerate(messages):
        message[:chunk] = piece(mine ^ (i + 1) if ways > 1 else 0).astype(BF16)
        if riders:
            put_riders(vectors, message, chunk)
    if ways > 1:
        kept_out[...] = piece(mine)
    if riders:
        small_out[...] = vectors


def exchange_kernel(digits, mine, theirs, rows_out, small_out):
    count = rows_out.shape[0]
    rows_out[...] = (mine[:count].astype(F32) + theirs[:count].astype(F32)).astype(BF16)
    small_out[...] = riders_of(mine, count) + riders_of(theirs, count)


def again_kernel(digits, rows, small, message):
    message[: rows.shape[0]] = rows[...]
    put_riders(small[...], message, rows.shape[0])


def order_kernel(digits, *refs, stage, count):
    pieces, out = refs[:count], refs[-1]
    rows = pieces[0].shape[0]
    for c, piece in enumerate(pieces):
        out[pl.ds(pl.multiple_of((digits[9 + stage] ^ c) * rows, 16), rows)] = piece[...]


def assemble_kernel(info, *refs):
    own, other, out, token, wide, sems = refs[:4], *refs[4:]
    token[...] = jnp.zeros_like(token)
    core = info[0]
    rows = out.shape[1]

    def leave(t):
        column = core if t < 4 else 1 - core
        image = (info[5] ^ (t % 4 // 2)) * 4 + column * 2 + (info[4] ^ (t % 2))
        return pltpu.make_async_copy(wide.at[t], out.at[image], sems.at[t])

    for t in range(8):
        if t < 4:
            block = own[t][pl.ds(pl.multiple_of(core * rows, rows), rows)]
        else:
            block = other[t - 4]
        wide[t] = block.astype(F32)
        leave(t).start()
    for t in range(8):
        leave(t).wait()


def hold_kernel(info, first, second, *refs):
    refs[-2][...] = first[...]
    refs[-1][...] = second[...]


def small_rows(info, vectors, squares, out):
    width = out.shape[1]
    once = jnp.where(info[7] == 0, 1.0, 0.0)
    lane = lax.broadcasted_iota(jnp.int32, (1, width), 1)
    out[...] = jnp.zeros_like(out)
    for i, vector in enumerate(vectors):
        out[i : i + 1] = jnp.sum(vector[...], axis=0, keepdims=True) * once
    for i in range(6):
        total = jnp.sum(jnp.sum(squares[i // 3][i % 3], axis=0, keepdims=True), axis=1, keepdims=True)
        out[8 + i : 9 + i] = jnp.where(lane == info[6], total * once, 0.0)


def trade_kernel(info, *refs):
    pieces, out = refs[:4], refs[-1]
    rows = out.shape[1]
    for t in range(4):
        out[t] = pieces[t][pl.ds(pl.multiple_of((1 - info[0]) * rows, rows), rows)]


def unpack_kernel(info, mine, theirs, small, counted, mix, proj, up, down, gain, bias, rms, wide, *, sizes):
    core = info[9]
    wide[core] = mine[...].astype(F32)
    wide[1 - core] = theirs[...].astype(F32)
    rows_a, rows_b, rows_c, ways = sizes
    early = rows_a // 2 // ways
    late = (rows_b + rows_c) // 2 // ways
    rows_mix = rows_c

    def pieces(slab, start, stop):
        total = {"a": rows_a, "b": rows_b, "c": rows_c}[slab] // 2
        size, shift, skip = {"a": (early, 0, 0), "b": (late, early, 0), "c": (late, early, rows_b // 2)}[slab]
        at = start
        while at < stop:
            half, row = at // total, at % total
            along = row + skip
            count = min(stop - at, total - row, size - along % size)
            yield at - start, half, along // size * (early + late) + shift + along % size, count
            at += count

    width = wide.shape[2]
    places = {0: (("c", 0), ("b", rows_mix)), 1: (("b", 0), ("a", 0))}
    for layer in range(2):
        (slab, at), (feed, feed_at) = places[layer]
        for out, name in ((mix, slab), (proj, feed), (up, feed), (down, feed)):
            if name == feed and out is not mix:
                at = feed_at
            rows, cols = out.shape[1:]
            for i in range(cols // width):
                for offset, half, row, count in pieces(name, at + i * rows, at + (i + 1) * rows):
                    out[layer, offset : offset + count, i * width : (i + 1) * width] = wide[half, row : row + count]
            if out is not mix:
                feed_at = at + rows * cols // width
    for layer in range(2):
        for norm in range(2):
            gain[layer, norm : norm + 1] = small[2 * layer + norm : 2 * layer + norm + 1]
            bias[layer, norm : norm + 1] = small[4 + 2 * layer + norm : 5 + 2 * layer + norm]
    images = rms.shape[1]
    sums = pltpu.roll(small[8:16], small.shape[1] - (info[6] - info[6] % images), 1)
    rms[...] = jnp.sqrt(sums[: rms.shape[0], :images] / counted[...])


VMEM = pl.BlockSpec(memory_space=pltpu.VMEM)


def call(kernel, info, operands, specs, outs, out_specs, scratch=(), grid=(), work=0, aliases={}, limit=VMEM_LIMIT):
    moved = sum(math.prod(a.shape) * a.dtype.itemsize for a in list(operands) + jax.tree.leaves(outs))
    single = not isinstance(outs, list)
    views = list(specs) + ([out_specs] if single else list(out_specs))

    def body_of(info, *refs):
        seen = [view(ref) if callable(view) else ref for view, ref in zip(views, refs)]
        kernel(info, *seen, *refs[len(views) :])

    def plain(view):
        return VMEM if callable(view) else view

    return pl.pallas_call(
        body_of,
        grid_spec=pltpu.PrefetchScalarGridSpec(
            num_scalar_prefetch=1,
            grid=grid,
            in_specs=[plain(v) for v in specs],
            out_specs=plain(out_specs) if single else [plain(v) for v in out_specs],
            scratch_shapes=list(scratch),
        ),
        out_shape=outs,
        input_output_aliases=aliases,
        compiler_params=pltpu.CompilerParams(vmem_limit_bytes=limit),
        cost_estimate=pl.CostEstimate(flops=int(work * 1.15e9), bytes_accessed=moved, transcendentals=0),
    )(info, *operands)


def whole(array):
    return VMEM


def tiled(array):
    return lambda ref: ref.at[pl.ds(pl.multiple_of(pl.program_id(0) * TB, TB), TB)]


def after_window(ref):
    return ref.at[pl.ds(WIN, ref.shape[0] - WIN)]


def last_rows(ref):
    return ref.at[pl.ds(ref.shape[0] - WIN, WIN)]


ANY = pl.BlockSpec(memory_space=pl.ANY)


def shape(dims, kind):
    return jax.ShapeDtypeStruct(dims, kind)


def after(value, *others):
    return lax.optimization_barrier((value, others))[0]


def body(edge_rows, lengths, norm_gain, norm_bias, w_qkv, w_out, w_up, w_down):
    sections = lax.axis_size("section")
    index = lax.axis_index("section")
    images, rows_dev, width = edge_rows.shape
    seats = 2 * images
    rep = sections // seats
    seat = index // rep
    twin = index % rep
    rows_piece = rows_dev * rep
    qw = (w_qkv.shape[2] - width) // 2
    kvw = w_qkv.shape[2] - qw
    hidden = w_up.shape[2]
    n = rows_piece * images // 2
    if n != 2 * TB:
        raise ValueError("block size")
    quarter = images // 2
    steps = (n // TB,)

    def route(pairs):
        return [(s * rep + e, d * rep + e) for s, d in pairs for e in range(rep)]

    if rep > 1:
        groups = [[s * rep + e for e in range(rep)] for s in range(seats)]
        edge_rows = lax.all_gather(edge_rows, "section", axis_index_groups=groups, axis=1, tiled=True)

    chip = seat // 2
    part = seat % 2
    fz, fl, fy = chip // 4, (chip // 2) % 2, chip % 2
    limit = lengths[chip]
    spot = lax.axis_index("dp") * images + chip
    dp_count = lax.axis_size("dp")
    dp_index = lax.axis_index("dp")

    def partners(masks):
        total = dp_count * sections
        spot = dp_index * sections + index
        digit = sum(((spot // m) % 2) << i for i, m in enumerate(masks))
        routes = []
        for c in range(1, 1 << len(masks)):
            flips = sum(m for i, m in enumerate(masks) if (c >> i) & 1)
            routes.append((c, [(s, s ^ flips) for s in range(total)]))
        return digit, routes

    dp_masks = [sections << b for b in range(dp_count.bit_length() - 1)]
    section_masks = [1 << b for b in range(1, sections.bit_length() - 1)]
    plane = [dp_masks[0], section_masks[0]]
    rest = section_masks[1:] + dp_masks[1:]
    digits = [partners(masks)[0] for masks in [[1], plane] + [[m] for m in rest]]
    counted = (lengths.astype(F32) * width)[None, :]
    info = jnp.stack([part, limit, chip % quarter, fz, fy, fz, spot, twin, index % 2] + digits).astype(jnp.int32)
    swap = route([(s, s ^ 1) for s in range(seats)])

    def bits(s):
        return s // 8, (s // 4) % 2, (s // 2) % 2, s % 2

    by_column = edge_rows.reshape(2, 2, 2, rows_piece, width)
    traded = lax.dynamic_index_in_dim(by_column, 1 - part, 1, keepdims=False).reshape(4, rows_piece, width)
    traded = lax.ppermute(traded, "section", swap)
    column = lax.dynamic_index_in_dim(by_column, part, 1, keepdims=False).reshape(4, rows_piece, width)
    received = [None] * 4
    for t in (2, 3, 0, 1):
        tz, ty = t // 2, t % 2
        image = (fz ^ tz) * 2 + (fy ^ ty)
        own = lax.dynamic_index_in_dim(column, image, 0, keepdims=False)
        got = lax.dynamic_index_in_dim(traded, image, 0, keepdims=False)
        message = jnp.where(part == 0, jnp.concatenate([own, got]), jnp.concatenate([got, own]))
        pairs = []
        for s in range(seats):
            z, l, y, k = bits(s)
            pairs.append((s, ((z ^ tz) * 4 + k * 2 + (y ^ ty)) * 2 + l))
        received[t] = lax.ppermute(message, "section", route(pairs))

    def send_back(message, tz, ty):
        pairs = []
        for s in range(seats):
            z, l, y, p = bits(s)
            pairs.append((s, ((z ^ tz) * 4 + p * 2 + (y ^ ty)) * 2 + l))
        return lax.ppermute(message, "section", route(pairs))

    def trade(got, *awaited):
        out = shape((4, rows_piece, width), BF16)
        send = call(trade_kernel, info, got + list(awaited), [VMEM] * 4 + [ANY] * len(awaited), out, VMEM)
        return lax.ppermute(send, "section", swap)

    first_to_second = route([(2 * c, 2 * c + 1) for c in range(images)])
    second_to_first = route([(2 * c + 1, 2 * c) for c in range(images)])

    dma = pltpu.SemaphoreType.DMA
    rows_q = shape((n, qw), BF16)
    rows_kv = shape((n, kvw), BF16)
    rows_low = shape((n, width), BF16)
    rows_wide = shape((n, width), F32)
    rows_stat = shape((n, 128), F32)
    rows_hidden = shape((n, hidden), BF16)
    grad_k_shape = shape((n + WIN, qw), F32)
    grad_v_shape = shape((n + WIN, width), F32)
    mix_rows = w_qkv.shape[1] * w_qkv.shape[2] // width
    feed_rows = (w_out[0].size + w_up[0].size + w_down[0].size) // width
    vec_shape = shape((8, width), F32)
    squares_shape = shape((3, 8, width), F32)
    ext = pltpu.VMEM((n + WIN, kvw), BF16)

    g0, g1, b0, b1 = norm_gain[0], norm_gain[1], norm_bias[0], norm_bias[1]

    halo_shape = shape((WIN, kvw), BF16)
    outs = [shape((n + WIN, width), BF16), rows_q, rows_kv, halo_shape]
    x, q0, kv0, halo0 = call(
        first_kernel, info, received + [g0, b0, w_qkv[0]], [VMEM] * 7,
        outs, [whole(o) for o in outs], work=6,
    )
    halo0 = lax.ppermute(halo0, "section", first_to_second)

    outs = [rows_low, rows_q, rows_kv, rows_low, rows_stat, rows_hidden, rows_hidden, rows_wide, squares_shape]
    z, q1, kv1, o0, lse0, active0, slope0, mid0, squares0 = call(
        second_kernel, info, [x, q0, kv0, halo0, g0, b0, w_out[0], w_up[0], w_down[0], g1, b1, w_qkv[1]],
        [after_window] + [VMEM] * 11, outs, [VMEM] * len(outs), [ext], (1,), work=15,
        limit=2 * VMEM_LIMIT,
    )
    kv_other = lax.ppermute(kv1, "section", first_to_second)

    pad = 2 * n // STRIDE
    rows_k_all = shape((2 * n, qw), BF16)
    rows_v_all = shape((2 * n, width), BF16)
    outs = [rows_q, rows_k_all, rows_v_all, rows_wide, rows_stat]
    qr, kr, vr, o_far, lse_far = call(
        far_forward_kernel, info, [q1, kv1, kv_other], [whole(a) for a in (q1, kv1, kv_other)],
        outs, [whole(o) for o in outs],
        [pltpu.VMEM((n + pad, qw), F32), pltpu.VMEM((2 * n + pad, qw), F32), pltpu.VMEM((HEADS, 2 * n + pad, 128), F32),
         pltpu.VMEM((HEADS, n + pad, 128), F32), pltpu.VMEM((n + pad, 128), F32)], work=14,
    )

    message = shape((2 * rows_piece, width), BF16)
    outs = [message] * 4 + [rows_low, rows_stat, shape((n, qw), F32), grad_k_shape, grad_v_shape, rows_wide,
            shape((feed_rows // 2, width), F32), shape((feed_rows // 2, width), BF16),
            vec_shape, vec_shape, squares_shape]
    (cross0, cross1, local0, local1, go1, stat1, gq_near, gk_near, gv_near, gmid1, keep_a, send_a,
     d_gain11, d_bias11, squares1) = call(
        third_kernel, info,
        received + [q1, kv1, kv_other, o_far, lse_far, z, g1, b1, w_out[1], w_up[1], w_down[1]],
        [VMEM] * 4
        + [tiled(q1), whole(kv1), last_rows]
        + [tiled(o_far), tiled(lse_far), tiled(z)]
        + [whole(a) for a in (g1, b1, w_out[1], w_up[1], w_down[1])],
        outs,
        [whole(message)] * 4 + [tiled(o) for o in outs[4:7]] + [whole(outs[7]), whole(outs[8]), tiled(outs[9])]
        + [whole(o) for o in outs[10:]],
        [ext, pltpu.VMEM((TB, width), BF16), pltpu.VMEM((feed_rows, width), F32)], steps, work=24,
    )
    forward_back = [None, None, send_back(cross0, 1, 0), None]

    outs = [shape((n, qw), F32), shape((n, kvw), F32), rows_kv]
    operands = [qr, kr, vr, go1, stat1, gq_near, gk_near, gv_near]
    gq1, gkv1, gkv_send = call(
        far_backward_kernel, info, operands, [whole(a) for a in operands], outs, [whole(o) for o in outs],
        [pltpu.VMEM((HEADS, n + pad, 128), F32), pltpu.VMEM((n + pad, 128), F32), pltpu.VMEM((n + pad, qw), F32),
         pltpu.VMEM((2 * n + pad, qw), F32), pltpu.VMEM((HEADS, 2 * n + pad, 128), F32)], work=18,
    )
    def pair(message):
        return lax.ppermute(message, ("dp", "section"), partners([1])[1][0][1])

    def send_all(messages, masks):
        return [lax.ppermute(m, ("dp", "section"), way) for m, (_, way) in zip(messages, partners(masks)[1])]

    small_shape = shape((16, width), F32)
    rider_rows = 2 * small_shape.shape[0]

    def stage(groups, small, ways, number):
        operands = [a for kept, got in groups for a in [kept] + got] + ([] if small is None else [small])
        rows = sum(kept.shape[0] for kept, _ in groups)
        riders = small is not None
        outs = [shape((rows // ways + rider_rows * riders, width), BF16)] * max(ways - 1, 1)
        outs += [shape((rows // ways, width), F32)] * (ways > 1) + [small_shape] * riders
        kernel = functools.partial(
            stage_kernel, groups=[len(got) for _, got in groups], ways=ways, stage=number, riders=riders
        )
        made = call(
            kernel, info, operands, [VMEM] * len(operands), outs, [VMEM] * len(outs), [pltpu.VMEM((rows, width), F32)]
        )
        sent = max(ways - 1, 1)
        return made[:sent], made[sent] if ways > 1 else None, made[-1] if riders else None

    def gather(piece, masks, number):
        return in_order([piece] + [lax.ppermute(piece, ("dp", "section"), way) for _, way in partners(masks)[1]], number)

    def in_order(pieces, number, awaited=()):
        out = shape((len(pieces) * pieces[0].shape[0], width), BF16)
        kernel = functools.partial(order_kernel, stage=number, count=len(pieces))
        return call(kernel, info, pieces + list(awaited), [VMEM] * len(pieces) + [ANY] * len(awaited), out, VMEM)

    messages, kept_a, _ = stage([(keep_a, [pair(send_a)])], None, 4, 1)
    got_a = send_all(messages, plane)
    gkv_got = lax.ppermute(after(gkv_send, forward_back[2], *got_a), "section", second_to_first)
    forward_back[3] = send_back(after(cross1, forward_back[2]), 1, 1)
    forward_back[0] = send_back(after(local0, forward_back[2]), 0, 0)
    forward_back[1] = send_back(after(local1, forward_back[2]), 0, 1)

    slab_rows = mix_rows + feed_rows
    early_shape = slab_rows // 2, width
    mix_slab = shape((mix_rows, width), F32)
    outs = [message] * 4 + [shape((WIN, qw), F32), shape((WIN, kvw), F32), shape((WIN, width), F32), halo_shape,
            shape(early_shape, F32), shape(early_shape, BF16), mix_slab] + [vec_shape] * 6
    operands = [gq1, gkv1, gkv_got, z, gmid1, g1, b1, w_qkv[1], q0, kv0, halo0, o0, lse0, active0, slope0, mid0, x, g0,
                b0, w_qkv[0], w_out[0], w_up[0], w_down[0]]
    (cross0, cross1, local0, local1, gq_last, gkv_last, gmid_last, halo_send, keep_early, send_early, slab_last,
     d_gain10, d_bias10, d_gain01, d_bias01, d_gain00, d_bias00) = call(
        fourth_kernel, info, operands,
        [tiled(a) for a in operands[:5]] + [VMEM] * 3 + [tiled(q0), VMEM, VMEM] + [tiled(a) for a in operands[11:16]]
        + [VMEM] * 7,
        outs, [VMEM] * len(outs),
        [ext, pltpu.VMEM((slab_rows, width), F32), pltpu.VMEM((n + WIN, qw), F32), pltpu.VMEM((n + WIN, qw), F32),
         pltpu.VMEM((n + WIN, width), F32), pltpu.VMEM((n + WIN, width), F32)], steps, work=20,
    )
    outs = [halo_shape, shape(early_shape, BF16)]
    halo_send, send_early = call(
        hold_kernel, info, [halo_send, send_early] + forward_back, [VMEM] * 2 + [ANY] * 4, outs, [VMEM] * 2
    )
    halo_got = lax.ppermute(halo_send, "section", second_to_first)

    got_early = pair(send_early)
    outs = [message] * 4 + [shape((mix_rows // 2, width), F32), shape((mix_rows // 2 + rider_rows, width), BF16), small_shape]
    operands = [gq_last, gkv_last, halo_got, x, gmid_last, g0, b0, w_qkv[0], slab_last]
    operands += [d_gain00, d_gain01, d_gain10, d_gain11, d_bias00, d_bias01, d_bias10, d_bias11, squares0, squares1]
    aliases = {1 + len(operands) + i: i for i in range(4)}
    operands += [cross0, cross1, local0, local1]
    cross0, cross1, local0, local1, keep_late, send_late, small = call(
        fifth_kernel, info, operands, [VMEM] * len(operands), outs, [VMEM] * len(outs),
        [pltpu.VMEM((mix_rows, width), F32), pltpu.VMEM((8, width), F32), pltpu.VMEM((8, width), F32)],
        aliases=aliases,
    )

    def assemble(own, other):
        outs = [shape((images, rows_piece, width), F32), shape((8, 128), F32)]
        out, token = call(
            assemble_kernel, info, own + [other], [VMEM] * 5, outs, [ANY, VMEM],
            [pltpu.VMEM((images, rows_piece, width), F32), dma((images,))],
        )
        if rep > 1:
            out = lax.dynamic_slice_in_dim(out, twin * rows_dev, rows_dev, 1)
        return out, token

    backward_back = [send_back(local0, 0, 0), None, send_back(cross0, 1, 0), None]
    got_late = pair(send_late)
    groups = [(keep_early, [got_early]), (keep_late, [got_late])]
    messages, kept, small = stage(groups, small, 4, 1)
    forward_trade = trade(forward_back, send_late)
    forward_rows, forward_token = assemble(forward_back, forward_trade)
    groups = [(kept_a, got_a), (kept, send_all(messages, plane))]
    number = 2
    scattered = []
    while number - 1 < len(rest) and sum(kept.shape[0] for kept, _ in groups) % 32 == 0:
        messages, kept, small = stage(groups, small, 2, number)
        groups = [(kept, send_all(messages, [rest[number - 2]]))]
        scattered.append(number)
        number += 1
    scattered_rows = groups[-1][1]
    backward_back[3] = send_back(after(cross1, backward_back[2]), 1, 1)
    backward_back[1] = send_back(after(local1, backward_back[2], *scattered_rows), 0, 1)
    (both,), _, small = stage(groups, small, 1, 0)
    both = after(both, backward_back[0], backward_back[2])
    rows_shape = shape((both.shape[0] - rider_rows, width), BF16)
    while number - 2 < len(rest):
        (got,) = send_all([both], [rest[number - 2]])
        rows, small = call(exchange_kernel, info, [both, got], [VMEM] * 2, [rows_shape, small_shape], [VMEM] * 2)
        number += 1
        if number - 2 < len(rest):
            both = call(again_kernel, info, [rows, small], [VMEM] * 2, shape(both.shape, BF16), VMEM)
    both = after(rows, backward_back[1], backward_back[3])
    for number in scattered[::-1]:
        both = gather(both, [rest[number - 2]], number)
    backward_trade = trade(backward_back, rows)
    backward_rows, backward_token = assemble(backward_back, backward_trade)
    both = in_order([both] + send_all([both] * 3, plane), 1, [backward_token, forward_token])
    theirs = pair(both)
    outs = [shape(w.shape, F32) for w in (w_qkv, w_out, w_up, w_down, norm_gain, norm_bias)] + [shape((6, images), F32)]
    sizes = (feed_rows, slab_rows, mix_rows, 1 << len(plane))
    grads = call(
        functools.partial(unpack_kernel, sizes=sizes), info, [both, theirs, small, counted],
        [VMEM] * 4, outs, [whole(o) for o in outs],
        [pltpu.VMEM((2,) + both.shape, F32)],
    )
    return (forward_rows, backward_rows, grads[6], grads[4], grads[5]) + tuple(grads[:4])


def solution(mesh):
    placed = (P("dp", "section", None), P("dp"), P(), P(), P(), P(), P(), P())
    return jax.shard_map(
        body,
        mesh=mesh,
        in_specs=placed,
        out_specs=(P("dp", "section", None), P("dp", "section", None), P(None, "dp"), P(), P(), P(), P(), P(), P()),
        check_vma=False,
    )
```

```python
import functools
import math

import jax
import jax.numpy as jnp
from jax import lax
from jax.experimental import pallas as pl
from jax.experimental.pallas import tpu as pltpu
from jax.sharding import PartitionSpec as P

HEADS = 2
WIN = 128
STRIDE = 128
NEG = -1e30
F32 = jnp.float32
BF16 = jnp.bfloat16
TB = 768
RES = 8
UNROLL = 16
RES_BACK = 16
UNROLL_BACK = 8
VMEM_LIMIT = 16 * 1024 * 1024


def dot(left, right):
    return lax.dot_general(left, right, (((1,), (0,)), ((), ())), preferred_element_type=F32)


def dot_t(left, right):
    return lax.dot_general(left, right, (((1,), (1,)), ((), ())), preferred_element_type=F32)


def t_dot(left, right):
    return lax.dot_general(left, right, (((0,), (0,)), ((), ())), preferred_element_type=F32)


def score_scale(query_width):
    return 1.0 / math.sqrt(query_width // HEADS)


def norm_parts(rows):
    centre = rows - jnp.mean(rows, axis=-1, keepdims=True)
    scale = lax.rsqrt(jnp.mean(centre * centre, axis=-1, keepdims=True) + 1e-05)
    return centre * scale, scale


def norm_back(grad, unit, scale, gain):
    scaled = grad * gain
    first = jnp.mean(scaled, axis=-1, keepdims=True)
    second = jnp.mean(scaled * unit, axis=-1, keepdims=True)
    return scale * (scaled - first - unit * second)


def col_sum(rows):
    return jnp.sum(rows.reshape(rows.shape[0] // 8, 8, rows.shape[1]), axis=0)


def gelu_pair(hidden):
    c0 = math.sqrt(2.0 / math.pi)
    square = hidden * hidden
    share = 0.5 + 0.5 * jnp.tanh(hidden * (c0 + (c0 * 0.044715) * square))
    active = hidden * share
    slope = share + active * (1.0 - share) * (2.0 * c0 + (6.0 * c0 * 0.044715) * square)
    return active, slope


def head_split(rows):
    lane = lax.broadcasted_iota(jnp.int32, rows.shape, 1)
    zero = jnp.zeros_like(rows)
    low = lane < rows.shape[1] // HEADS
    return jnp.concatenate([jnp.where(low, rows, zero), jnp.where(low, zero, rows)], axis=0)


def head_join(stacked):
    half = stacked.shape[0] // 2
    lane = lax.broadcasted_iota(jnp.int32, (half, stacked.shape[1]), 1)
    return jnp.where(lane < stacked.shape[1] // HEADS, stacked[:half], stacked[half:])


def near_masks(base, limit):
    row = lax.broadcasted_iota(jnp.int32, (2 * WIN, WIN), 0)
    row = jnp.where(row >= WIN, row - WIN, row)
    col = lax.broadcasted_iota(jnp.int32, (2 * WIN, WIN), 1)
    own = col <= row
    key = base + col - jnp.where(own, 0, WIN)
    allowed = (key >= 0) & ((key < limit) | (col == row))
    return own, allowed


def near_scores(split_q, keys, own, allowed):
    scores = dot_t(split_q, keys)
    folded = jnp.where(own, scores[:, WIN:], scores[:, :WIN])
    return jnp.where(allowed, folded, NEG)


def unfold(folded, own):
    return jnp.concatenate([jnp.where(own, 0.0, folded), jnp.where(own, folded, 0.0)], axis=1).astype(BF16)


def near_forward(queries, keys, values, base, limit):
    own, allowed = near_masks(base, limit)
    scores = near_scores(head_split(queries), keys, own, allowed)
    largest = jnp.max(scores, axis=-1, keepdims=True)
    powers = jnp.exp(scores - largest)
    total = jnp.sum(powers, axis=-1, keepdims=True)
    weights = unfold(powers, own)
    hd = values.shape[1] // HEADS
    out = [dot(weights[h * WIN : (h + 1) * WIN], values[:, h * hd : (h + 1) * hd]) for h in range(HEADS)]
    return out, largest, total, powers


def near_backward(queries, keys, values, grad_out, log_total, delta, base, limit, weights=None):
    own, allowed = near_masks(base, limit)
    split_q = head_split(queries)
    if weights is None:
        weights = jnp.exp(near_scores(split_q, keys, own, allowed) - log_total)
    hd = values.shape[1] // HEADS
    pull = jnp.concatenate(
        [dot_t(grad_out[:, h * hd : (h + 1) * hd], values[:, h * hd : (h + 1) * hd]) for h in range(HEADS)], axis=0
    )
    pull = jnp.where(own, pull[:, WIN:], pull[:, :WIN])
    slope = weights * (pull - delta)
    grad_q = head_join(dot(unfold(slope, own), keys))
    row = lax.broadcasted_iota(jnp.int32, (WIN, 2 * WIN), 0)
    col = lax.broadcasted_iota(jnp.int32, (WIN, 2 * WIN), 1)
    here = (row <= jnp.where(col >= WIN, col - WIN, col)).astype(F32).astype(BF16)

    def turned(folded):
        flat = folded.astype(BF16).T
        current = flat * here
        return jnp.concatenate([flat - current, current], axis=0)

    grad_k = dot(turned(slope), split_q)
    weights = turned(weights)
    grad_v = jnp.concatenate(
        [dot(weights[:, h * WIN : (h + 1) * WIN], grad_out[:, h * hd : (h + 1) * hd]) for h in range(HEADS)], axis=1
    )
    return grad_q, grad_k, grad_v


def stack_stat(stat, width=128):
    return jnp.concatenate([stat[:, 0:1], stat[:, width // 2 : width // 2 + 1]], axis=0)


def spread_stat(stacked, width=128):
    half = stacked.shape[0] // 2
    lane = lax.broadcasted_iota(jnp.int32, (half, width), 1)
    return jnp.where(lane < width // 2, stacked[:half], stacked[half:])


def masked_squares(rows, base, limit):
    pos = base + lax.broadcasted_iota(jnp.int32, (rows.shape[0], 1), 0)
    return col_sum(jnp.where(pos < limit, rows * rows, 0.0))


def pick_piece(info, pieces, low, block, target):
    for t, piece in enumerate(pieces):
        tz, ty = t // 2, t % 2

        @pl.when(((block ^ info[4]) == ty) & ((info[5] ^ (0 if low else 1)) == tz))
        def _():
            target[...] = piece[...]


def emit_block(info, block, rows, to_lower, first, cross, local):
    stays = info[5] == (0 if to_lower else 1)
    at = slice(first, first + rows.shape[0])
    for ty in range(2):
        fits = (block ^ info[4]) == ty

        @pl.when(fits & stays)
        def _():
            local[ty][at] = rows

        @pl.when(fits & jnp.logical_not(stays))
        def _():
            cross[ty][at] = rows


def emit_rows(info, first, rows, to_lower, cross, local):
    units = cross[0].shape[0] // WIN
    stays = info[5] == (0 if to_lower else 1)
    for sub in range(rows.shape[0] // WIN):
        number = first + sub
        block = number // units
        at = pl.ds(pl.multiple_of((number - block * units) * WIN, WIN), WIN)
        value = rows[sub * WIN : (sub + 1) * WIN]
        for ty in range(2):
            fits = (block ^ info[4]) == ty

            @pl.when(fits & stays)
            def _():
                local[ty][at] = value

            @pl.when(fits & jnp.logical_not(stays))
            def _():
                cross[ty][at] = value


def split_slab(info, slab, keep, send):
    once = jnp.where(info[7] == 0, 1.0, 0.0)
    half = keep.shape[0]
    mine = info[8]
    keep[...] = slab[pl.ds(pl.multiple_of(mine * half, 8), half)] * once
    send[:half] = (slab[pl.ds(pl.multiple_of((1 - mine) * half, 8), half)] * once).astype(BF16)


def first_kernel(info, *refs):
    pieces = refs[:4]
    gain, bias, w_mix, x_out, q_out, kv_out, halo_out = refs[4:]
    for half in range(2):
        pick_piece(info, pieces, True, half, x_out.at[pl.ds(WIN + half * pieces[0].shape[0], pieces[0].shape[0])])
    x_out[:WIN] = jnp.zeros((WIN, x_out.shape[1]), BF16)
    qw = q_out.shape[1]

    def block(i, _):
        at = pl.ds(pl.multiple_of(i * TB, TB), TB)
        unit, _ = norm_parts(x_out[pl.ds(pl.multiple_of(i * TB + WIN, WIN), TB)].astype(F32))
        normed = (unit * gain[0:1] + bias[0:1]).astype(BF16)
        mixed = dot(normed, w_mix[...])
        q_out[at] = (mixed[:, :qw] * score_scale(qw)).astype(BF16)
        kv_out[at] = mixed[:, qw:].astype(BF16)
        return 0

    lax.fori_loop(0, q_out.shape[0] // TB, block, 0)
    halo_out[...] = kv_out[kv_out.shape[0] - WIN :]


def load_extended(halo, kv, ext):
    ext[: halo.shape[0]] = halo[...]
    ext[halo.shape[0] :] = kv[...]


def second_kernel(
    info, x, q, kv, halo, gain, bias, w_proj, w_in, w_back, gain_next, bias_next, w_mix_next,
    z_out, q_next, kv_next, o_out, lse_out, active_out, slope_out, mid_out, squares, ext,
):
    step = pl.program_id(0)
    qw = q.shape[1]
    n = kv.shape[0]

    @pl.when(step == 0)
    def _():
        load_extended(halo, kv, ext)
        squares[...] = jnp.zeros_like(squares)

    limit = info[1]
    count = q.shape[0]
    start = step * count
    base = info[0] * n + start
    outs = []
    for sub in range(count // WIN):
        near = pl.ds(pl.multiple_of(start + sub * WIN, WIN), 2 * WIN)
        keys = ext[near, :qw]
        values = ext[near, qw:]
        queries = q[sub * WIN : (sub + 1) * WIN]
        out, largest, total, _ = near_forward(queries, keys, values, base + sub * WIN, limit)
        inverse = 1.0 / total
        lse_out[sub * WIN : (sub + 1) * WIN] = spread_stat(largest + jnp.log(total))
        outs.append(jnp.concatenate([out[0] * inverse[:WIN], out[1] * inverse[WIN:]], axis=1))
    attended = jnp.concatenate(outs, axis=0).astype(BF16)
    o_out[...] = attended
    stream = x[...].astype(F32)
    branch = dot(attended, w_proj[...])
    middle = stream + branch
    mid_out[...] = middle
    unit, _ = norm_parts(middle)
    normed = (unit * gain[1:2] + bias[1:2]).astype(BF16)
    active, slope = gelu_pair(dot(normed, w_in[...]))
    active = active.astype(BF16)
    active_out[...] = active
    slope_out[...] = slope.astype(BF16)
    feed = dot(active, w_back[...])
    z = (middle + feed).astype(BF16)
    z_out[...] = z
    squares[0] += masked_squares(stream, base, limit)
    squares[1] += masked_squares(branch, base, limit)
    squares[2] += masked_squares(feed, base, limit)
    unit, _ = norm_parts(z.astype(F32))
    normed = (unit * gain_next[0:1] + bias_next[0:1]).astype(BF16)
    mixed = dot(normed, w_mix_next[...])
    q_next[...] = (mixed[:, :qw] * score_scale(qw)).astype(BF16)
    kv_next[...] = mixed[:, qw:].astype(BF16)


def far_mask(grid_q, grid_k, part_grid, residues):
    shape = (HEADS * residues * grid_q, residues * grid_k)
    row = lax.broadcasted_iota(jnp.int32, shape, 0)
    col = lax.broadcasted_iota(jnp.int32, shape, 1)
    row = jnp.where(row >= residues * grid_q, row - residues * grid_q, row)
    row_res = jnp.zeros(shape, jnp.int32)
    col_res = jnp.zeros(shape, jnp.int32)
    for r in range(1, residues):
        row_res += (row >= r * grid_q).astype(jnp.int32)
        col_res += (col >= r * grid_k).astype(jnp.int32)
    row_grid = row - row_res * grid_q + part_grid
    col_grid = col - col_res * grid_k
    allowed = (row_res == col_res) & (col_grid < row_grid)
    return allowed, col_grid * STRIDE + col_res


def far_forward_kernel(info, q, kv, other, qr, kr, vr, o_far, lse_far, q_s, k_s, v_s, o_s, lse_s):
    n, qw = q.shape
    grid_q = n // STRIDE
    grid_k = 2 * grid_q
    part = info[0]
    limit = info[1]

    def place(g, _):
        at = pl.ds(pl.multiple_of(g * STRIDE, STRIDE), STRIDE)
        own = kv[at].astype(F32)
        early = jnp.where(part == 0, own, other[at].astype(F32))
        q_s[pl.ds(g, STRIDE, stride=grid_q), :] = q[at].astype(F32)
        k_s[pl.ds(g, STRIDE, stride=grid_k), :] = early[:, :qw]
        k_s[pl.ds(g + grid_q, STRIDE, stride=grid_k), :] = own[:, :qw]
        hd = v_s.shape[1]
        for h in range(HEADS):
            v_s[h, pl.ds(g, STRIDE, stride=grid_k), :] = early[:, qw + h * 128 : qw + (h + 1) * 128]
            v_s[h, pl.ds(g + grid_q, STRIDE, stride=grid_k), :] = own[:, qw + h * 128 : qw + (h + 1) * 128]
        return 0

    lax.fori_loop(0, grid_q, place, 0)
    base_mask, key_pos = far_mask(grid_q, grid_k, part * grid_q, RES)
    rows_q = RES * grid_q
    rows_k = RES * grid_k

    def one(i):
        at_q = pl.ds(pl.multiple_of(i * rows_q, rows_q), rows_q)
        at_k = pl.ds(pl.multiple_of(i * rows_k, rows_k), rows_k)
        queries = q_s[at_q].astype(BF16)
        keys = k_s[at_k].astype(BF16)
        values = [v_s[h, at_k].astype(BF16) for h in range(HEADS)]
        qr[at_q] = queries
        kr[at_k] = keys
        for h in range(HEADS):
            vr[at_k, h * 128 : (h + 1) * 128] = values[h]
        allowed = base_mask & (key_pos + i * RES < limit)
        scores = jnp.where(allowed, dot_t(head_split(queries), keys), NEG)
        largest = jnp.max(scores, axis=-1, keepdims=True)
        powers = jnp.where(allowed, jnp.exp(scores - largest), 0.0)
        total = jnp.sum(powers, axis=-1, keepdims=True)
        safe = jnp.maximum(total, 1e-30)
        weights = (powers * (1.0 / safe)).astype(BF16)
        lse = jnp.where(total > 0.0, largest + jnp.log(safe), NEG)
        lse_s[at_q] = spread_stat(lse)
        for h in range(HEADS):
            o_s[h, at_q] = dot(weights[h * rows_q : (h + 1) * rows_q], values[h])

    def group(i, _):
        for u in range(UNROLL):
            one(i * UNROLL + u)
        return 0

    lax.fori_loop(0, STRIDE // RES // UNROLL, group, 0)

    def back(g, _):
        at = pl.ds(pl.multiple_of(g * STRIDE, STRIDE), STRIDE)
        pick = pl.ds(g, STRIDE, stride=grid_q)
        lse_far[at] = lse_s[pick, :]
        for h in range(HEADS):
            o_far[at, h * 128 : (h + 1) * 128] = o_s[h, pick, :]
        return 0

    lax.fori_loop(0, grid_q, back, 0)


def third_kernel(
    info, *refs,
):
    pieces = refs[:4]
    (q, kv, halo, o_far, lse_far, z, gain, bias, w_proj, w_in, w_back,
     cross0, cross1, local0, local1, go_out, stat_out, gq_out, gk_out, gv_out, gmid_out, keep, send,
     d_gain, d_bias, squares, ext, cot, slab) = refs[4:]
    step = pl.program_id(0)
    qw = q.shape[1]
    n = kv.shape[0]

    @pl.when(step == 0)
    def _():
        load_extended(halo, kv, ext)
        for ref in (squares, gk_out, gv_out, slab, d_gain, d_bias):
            ref[...] = jnp.zeros_like(ref)

    limit = info[1]
    start = pl.multiple_of(step * TB, TB)
    base = info[0] * n + start
    outs = []
    logs = []
    weights = []
    for sub in range(TB // WIN):
        rows = slice(sub * WIN, (sub + 1) * WIN)
        near = pl.ds(pl.multiple_of(start + sub * WIN, WIN), 2 * WIN)
        out, largest, total, powers = near_forward(q[rows], ext[near, :qw], ext[near, qw:], base + sub * WIN, limit)
        far_log = stack_stat(lse_far[rows])
        top = jnp.maximum(largest, far_log)
        near_share = jnp.exp(largest - top)
        far_share = jnp.exp(far_log - top)
        whole = total * near_share + far_share
        inverse = 1.0 / whole
        near_share = near_share * inverse
        far_share = far_share * inverse
        weights.append(powers * near_share)
        logs.append(top + jnp.log(whole))
        far = o_far[rows]
        outs.append(
            jnp.concatenate(
                [
                    out[h] * near_share[h * WIN : (h + 1) * WIN]
                    + far[:, h * 128 : (h + 1) * 128] * far_share[h * WIN : (h + 1) * WIN]
                    for h in range(HEADS)
                ],
                axis=1,
            )
        )
    attended_wide = jnp.concatenate(outs, axis=0)
    attended = attended_wide.astype(BF16)
    stream = z[...].astype(F32)
    branch = dot(attended, w_proj[...])
    middle = stream + branch
    unit, scale = norm_parts(middle)
    normed = (unit * gain[1:2] + bias[1:2]).astype(BF16)
    active, slope = gelu_pair(dot(normed, w_in[...]))
    active = active.astype(BF16)
    feed = dot(active, w_back[...])
    emit_block(info, step, z[...], True, 0, (cross0, cross1), (local0, local1))
    emit_block(info, step, (middle + feed).astype(BF16), False, 0, (cross0, cross1), (local0, local1))
    pick_piece(info, pieces, False, step, cot)
    squares[0] += masked_squares(stream, base, limit)
    squares[1] += masked_squares(branch, base, limit)
    squares[2] += masked_squares(feed, base, limit)

    pos = base + lax.broadcasted_iota(jnp.int32, (TB, 1), 0)
    upstream = jnp.where(pos < limit, cot[...].astype(F32), 0.0)
    grad_out, grad_mid = feed_backward(
        upstream, active, slope, normed, unit, scale, attended, gain, w_proj, w_in, w_back, slab, 0, d_gain, d_bias
    )
    gmid_out[...] = grad_mid
    go_out[...] = grad_out
    weighted = grad_out.astype(F32) * attended_wide
    for sub in range(TB // WIN):
        rows = slice(sub * WIN, (sub + 1) * WIN)
        near = pl.ds(pl.multiple_of(start + sub * WIN, WIN), 2 * WIN)
        delta = jnp.concatenate(
            [jnp.sum(weighted[rows, h * 128 : (h + 1) * 128], axis=-1, keepdims=True) for h in range(HEADS)], axis=0
        )
        stat_out[rows] = pack_stats(logs[sub], delta)
        gq, gk, gv = near_backward(
            q[rows], ext[near, :qw], ext[near, qw:], grad_out[rows], logs[sub], delta, base + sub * WIN, limit,
            weights[sub],
        )
        gq_out[rows] = gq
        gk_out[near] += gk
        gv_out[near] += gv

    @pl.when(step == pl.num_programs(0) - 1)
    def _():
        split_slab(info, slab, keep, send)


def pack_stats(lse, delta):
    half = lse.shape[0] // 2
    lane = lax.broadcasted_iota(jnp.int32, (half, 128), 1)
    low = jnp.where(lane < 32, lse[:half], lse[half:])
    high = jnp.where(lane < 96, delta[:half], delta[half:])
    return jnp.where(lane < 64, low, high)


def add_columns(slab, at, grad):
    rows, cols = grad.shape
    width = slab.shape[1]
    for i in range(cols // width):
        slab[at + i * rows : at + (i + 1) * rows] += grad[:, i * width : (i + 1) * width]


def feed_backward(
    upstream, active, slope, normed, unit, scale, attended, gain, w_proj, w_in, w_back, slab, at, d_gain, d_bias,
):
    low = upstream.astype(BF16)
    width = low.shape[1]
    hidden = active.shape[1]
    slab[at + width + hidden : at + width + 2 * hidden] += t_dot(active, low)
    grad_hidden = (dot_t(low, w_back[...]) * slope).astype(BF16)
    add_columns(slab, at + width, t_dot(normed, grad_hidden))
    grad_normed = dot_t(grad_hidden, w_in[...])
    d_gain[...] += col_sum(grad_normed * unit)
    d_bias[...] += col_sum(grad_normed)
    grad_mid = upstream + norm_back(grad_normed, unit, scale, gain[1:2])
    branch_low = grad_mid.astype(BF16)
    slab[at : at + width] += t_dot(attended, branch_low)
    grad_out = dot_t(branch_low, w_proj[...]).astype(BF16)
    return grad_out, grad_mid


def far_backward_kernel(
    info, qr, kr, vr, go, stat, gq_near, gk_near, gv_near, gq_out, gkv_own, gkv_send,
    go_s, stat_s, gq_s, gk_s, gv_s,
):
    n, qw = gq_near.shape
    grid_q = n // STRIDE
    grid_k = 2 * grid_q
    part = info[0]
    limit = info[1]

    def place(g, _):
        at = pl.ds(pl.multiple_of(g * STRIDE, STRIDE), STRIDE)
        pick = pl.ds(g, STRIDE, stride=grid_q)
        rows = go[at].astype(F32)
        for h in range(HEADS):
            go_s[h, pick, :] = rows[:, h * 128 : (h + 1) * 128]
        stat_s[pick, :] = stat[at]
        return 0

    lax.fori_loop(0, grid_q, place, 0)
    base_mask, key_pos = far_mask(grid_q, grid_k, part * grid_q, RES_BACK)
    rows_q = RES_BACK * grid_q
    rows_k = RES_BACK * grid_k

    def one(i):
        at_q = pl.ds(pl.multiple_of(i * rows_q, rows_q), rows_q)
        at_k = pl.ds(pl.multiple_of(i * rows_k, rows_k), rows_k)
        keys = kr[at_k]
        split_q = head_split(qr[at_q])
        grads = [go_s[h, at_q].astype(BF16) for h in range(HEADS)]
        stats = stat_s[at_q]
        lse = jnp.concatenate([stats[:, 0:1], stats[:, 32:33]], axis=0)
        delta = jnp.concatenate([stats[:, 64:65], stats[:, 96:97]], axis=0)
        allowed = base_mask & (key_pos + i * RES_BACK < limit)
        weights = jnp.exp(jnp.where(allowed, dot_t(split_q, keys), NEG) - lse)
        pull = jnp.concatenate([dot_t(grads[h], vr[at_k, h * 128 : (h + 1) * 128]) for h in range(HEADS)], axis=0)
        slope = (weights * (pull - delta)).astype(BF16)
        weights = weights.astype(BF16)
        gq_s[at_q] = head_join(dot(slope, keys))
        gk_s[at_k] = t_dot(slope, split_q)
        for h in range(HEADS):
            gv_s[h, at_k] = t_dot(weights[h * rows_q : (h + 1) * rows_q], grads[h])

    def group(i, _):
        for u in range(UNROLL_BACK):
            one(i * UNROLL_BACK + u)
        return 0

    lax.fori_loop(0, STRIDE // RES_BACK // UNROLL_BACK, group, 0)

    def back(g, _):
        at = pl.ds(pl.multiple_of(g * STRIDE, STRIDE), STRIDE)
        shifted = pl.ds(pl.multiple_of(g * STRIDE + WIN, STRIDE), STRIDE)
        gq_out[at] = gq_near[at] + gq_s[pl.ds(g, STRIDE, stride=grid_q), :]
        mine = pl.ds(g + part * grid_q, STRIDE, stride=grid_k)
        sent = pl.ds(g, STRIDE, stride=grid_k)
        last = jnp.where(g == grid_q - 1, 1.0, 0.0)
        gkv_own[at, :qw] = gk_near[shifted] + gk_s[mine, :]
        gkv_send[at, :qw] = (gk_s[sent, :] + last * gk_near[:WIN]).astype(BF16)
        for h in range(HEADS):
            cols = slice(h * 128, (h + 1) * 128)
            wide = slice(qw + h * 128, qw + (h + 1) * 128)
            gkv_own[at, wide] = gv_near[shifted, cols] + gv_s[h, mine, :]
            gkv_send[at, wide] = (gv_s[h, sent, :] + last * gv_near[:WIN, cols]).astype(BF16)
        return 0

    lax.fori_loop(0, grid_q, back, 0)


def mix_backward(grad_q, grad_kv, rows, gain, bias, w_mix, slab, d_gain, d_bias, carried):
    grad_mixed = jnp.concatenate([grad_q * score_scale(grad_q.shape[1]), grad_kv], axis=1).astype(BF16)
    unit, scale = norm_parts(rows)
    normed = (unit * gain[0:1] + bias[0:1]).astype(BF16)
    add_columns(slab, 0, t_dot(normed, grad_mixed))
    grad_normed = dot_t(grad_mixed, w_mix[...])
    d_gain[...] += col_sum(grad_normed * unit)
    d_bias[...] += col_sum(grad_normed)
    return carried + norm_back(grad_normed, unit, scale, gain[0:1])


def fourth_kernel(
    info, gq, gkv, got, z, gmid, gain_next, bias_next, w_mix_next,
    q, kv, halo, o, lse, active, slope, mid, x, gain, bias, w_mix, w_proj, w_in, w_back,
    cross0, cross1, local0, local1, gq_last, gkv_last, gmid_last, halo_out, keep, send, slab_last,
    dn_gain, dn_bias, d_gain, d_bias, d_gain_first, d_bias_first,
    ext, slab, gq_ext, gk_ext, gv_ext, gmid_ext,
):
    step = pl.program_id(0)
    qw = q.shape[1]
    n = kv.shape[0]

    @pl.when(step == 0)
    def _():
        load_extended(halo, kv, ext)
        for ref in (
            slab, slab_last, dn_gain, dn_bias, d_gain, d_bias, d_gain_first, d_bias_first, gq_ext, gk_ext, gv_ext, gmid_ext
        ):
            ref[...] = jnp.zeros_like(ref)

    limit = info[1]
    start = pl.multiple_of(step * TB, TB)
    base = info[0] * n + start
    grad_kv = gkv[...] + got[...].astype(F32)
    grad_z = mix_backward(
        gq[...], grad_kv, z[...].astype(F32), gain_next, bias_next, w_mix_next, slab, dn_gain, dn_bias, gmid[...]
    )
    grad_low = grad_z.astype(BF16)
    emit_block(info, step, grad_low, False, 0, (cross0, cross1), (local0, local1))
    unit, scale = norm_parts(mid[...])
    normed = (unit * gain[1:2] + bias[1:2]).astype(BF16)
    attended = o[...]
    grad_out, grad_mid = feed_backward(
        grad_low.astype(F32), active[...], slope[...].astype(F32), normed, unit, scale, attended, gain,
        w_proj, w_in, w_back, slab, w_mix_next.size // w_proj.shape[1], d_gain, d_bias,
    )
    shifted = pl.ds(pl.multiple_of(start + WIN, WIN), TB)
    gmid_ext[shifted] = grad_mid
    weighted = grad_out.astype(F32) * attended.astype(F32)
    for sub in range(TB // WIN):
        rows = slice(sub * WIN, (sub + 1) * WIN)
        near = pl.ds(pl.multiple_of(start + sub * WIN, WIN), 2 * WIN)
        delta = jnp.concatenate(
            [jnp.sum(weighted[rows, h * 128 : (h + 1) * 128], axis=-1, keepdims=True) for h in range(HEADS)], axis=0
        )
        g_q, g_k, g_v = near_backward(
            q[rows], ext[near, :qw], ext[near, qw:], grad_out[rows], stack_stat(lse[rows]), delta,
            base + sub * WIN, limit,
        )
        gq_ext[pl.ds(pl.multiple_of(start + (sub + 1) * WIN, WIN), WIN)] = g_q
        gk_ext[near] += g_k
        gv_ext[near] += g_v

    @pl.when(step == 0)
    def _():
        halo_out[...] = jnp.concatenate([gk_ext[:WIN], gv_ext[:WIN]], axis=1).astype(BF16)
        gk_ext[:WIN] = jnp.zeros((WIN, gk_ext.shape[1]), F32)
        gv_ext[:WIN] = jnp.zeros((WIN, gv_ext.shape[1]), F32)

    whole_rows = pl.ds(start, TB)
    grad_x = mix_backward(
        gq_ext[whole_rows], jnp.concatenate([gk_ext[whole_rows], gv_ext[whole_rows]], axis=1),
        x[whole_rows].astype(F32), gain, bias, w_mix, slab_last, d_gain_first, d_bias_first, gmid_ext[whole_rows],
    )
    grad_x = grad_x.astype(BF16)
    emit_block(info, step, grad_x[WIN:], True, 0, (cross0, cross1), (local0, local1))

    @pl.when(step > 0)
    def _():
        emit_rows(info, step * (TB // WIN) - 1, grad_x[:WIN], True, (cross0, cross1), (local0, local1))

    @pl.when(step == pl.num_programs(0) - 1)
    def _():
        gq_last[...] = gq_ext[n:]
        gkv_last[...] = jnp.concatenate([gk_ext[n:], gv_ext[n:]], axis=1)
        gmid_last[...] = gmid_ext[n:]
        split_slab(info, slab, keep, send)


def fifth_kernel(info, gq, gkv, got, x, gmid, gain, bias, w_mix, slab_in, *refs):
    vectors, squares = refs[:8], refs[8:10]
    cross, local, (keep, send, small, slab, d_gain, d_bias) = refs[-10:-8], refs[-8:-6], refs[-6:]
    slab[...] = slab_in[...]
    d_gain[...] = vectors[0][...]
    d_bias[...] = vectors[4][...]
    n = x.shape[0] - WIN
    grad_x = mix_backward(
        gq[...], gkv[...] + got[...].astype(F32), x[n:].astype(F32), gain, bias, w_mix, slab, d_gain, d_bias, gmid[...]
    )
    emit_rows(info, n // WIN - 1, grad_x.astype(BF16), True, cross, local)
    split_slab(info, slab, keep, send)
    small_rows(info, (d_gain,) + vectors[1:4] + (d_bias,) + vectors[5:], squares, small)
    put_riders(small[...], send, keep.shape[0])


def put_riders(rows, send, at):
    count = rows.shape[0]
    coarse = rows.astype(BF16)
    send[at : at + count] = coarse
    send[at + count :] = (rows - coarse.astype(F32)).astype(BF16)


def riders_of(got, at):
    count = (got.shape[0] - at) // 2
    return got[at : at + count].astype(F32) + got[at + count :].astype(F32)


def stage_kernel(digits, *refs, groups, ways, stage, riders):
    refs = list(refs)
    parts = [(refs.pop(0), [refs.pop(0) for _ in range(count)]) for count in groups]
    small = refs.pop(0) if riders else None
    messages = [refs.pop(0) for _ in range(max(ways - 1, 1))]
    kept_out = refs.pop(0) if ways > 1 else None
    small_out = refs.pop(0) if riders else None
    total = refs.pop(0)
    vectors = small[...] if riders else None
    at = 0
    for kept, got in parts:
        rows = kept.shape[0]
        value = kept[...]
        for g in got:
            value = value + g[:rows].astype(F32)
            if g.shape[0] > rows:
                vectors = vectors + riders_of(g, rows)
        total[at : at + rows] = value
        at += rows
    chunk = at // ways

    def piece(which):
        return total[pl.ds(pl.multiple_of(which * chunk, 16), chunk)]

    mine = digits[9 + stage] if ways > 1 else 0
    for i, message in enumerate(messages):
        message[:chunk] = piece(mine ^ (i + 1) if ways > 1 else 0).astype(BF16)
        if riders:
            put_riders(vectors, message, chunk)
    if ways > 1:
        kept_out[...] = piece(mine)
    if riders:
        small_out[...] = vectors


def exchange_kernel(digits, mine, theirs, rows_out, small_out):
    count = rows_out.shape[0]
    rows_out[...] = (mine[:count].astype(F32) + theirs[:count].astype(F32)).astype(BF16)
    small_out[...] = riders_of(mine, count) + riders_of(theirs, count)


def again_kernel(digits, rows, small, message):
    message[: rows.shape[0]] = rows[...]
    put_riders(small[...], message, rows.shape[0])


def order_kernel(digits, *refs, stage, count):
    pieces, out = refs[:count], refs[-1]
    rows = pieces[0].shape[0]
    for c, piece in enumerate(pieces):
        out[pl.ds(pl.multiple_of((digits[9 + stage] ^ c) * rows, 16), rows)] = piece[...]


def assemble_kernel(info, *refs):
    own, other, out, token, wide, sems = refs[:4], *refs[4:]
    token[...] = jnp.zeros_like(token)
    core = info[0]
    rows = out.shape[1]

    def leave(t):
        column = core if t < 4 else 1 - core
        image = (info[5] ^ (t % 4 // 2)) * 4 + column * 2 + (info[4] ^ (t % 2))
        return pltpu.make_async_copy(wide.at[t], out.at[image], sems.at[t])

    for t in range(8):
        if t < 4:
            block = own[t][pl.ds(pl.multiple_of(core * rows, rows), rows)]
        else:
            block = other[t - 4]
        wide[t] = block.astype(F32)
        leave(t).start()
    for t in range(8):
        leave(t).wait()


def hold_kernel(info, first, second, *refs):
    refs[-2][...] = first[...]
    refs[-1][...] = second[...]


def small_rows(info, vectors, squares, out):
    width = out.shape[1]
    once = jnp.where(info[7] == 0, 1.0, 0.0)
    lane = lax.broadcasted_iota(jnp.int32, (1, width), 1)
    out[...] = jnp.zeros_like(out)
    for i, vector in enumerate(vectors):
        out[i : i + 1] = jnp.sum(vector[...], axis=0, keepdims=True) * once
    for i in range(6):
        total = jnp.sum(jnp.sum(squares[i // 3][i % 3], axis=0, keepdims=True), axis=1, keepdims=True)
        out[8 + i : 9 + i] = jnp.where(lane == info[6], total * once, 0.0)


def trade_kernel(info, *refs):
    pieces, out = refs[:4], refs[-1]
    rows = out.shape[1]
    for t in range(4):
        out[t] = pieces[t][pl.ds(pl.multiple_of((1 - info[0]) * rows, rows), rows)]


def unpack_kernel(info, mine, theirs, small, counted, mix, proj, up, down, gain, bias, rms, wide, *, sizes):
    core = info[9]
    wide[core] = mine[...].astype(F32)
    wide[1 - core] = theirs[...].astype(F32)
    rows_a, rows_b, rows_c, ways = sizes
    early = rows_a // 2 // ways
    late = (rows_b + rows_c) // 2 // ways
    rows_mix = rows_c

    def pieces(slab, start, stop):
        total = {"a": rows_a, "b": rows_b, "c": rows_c}[slab] // 2
        size, shift, skip = {"a": (early, 0, 0), "b": (late, early, 0), "c": (late, early, rows_b // 2)}[slab]
        at = start
        while at < stop:
            half, row = at // total, at % total
            along = row + skip
            count = min(stop - at, total - row, size - along % size)
            yield at - start, half, along // size * (early + late) + shift + along % size, count
            at += count

    width = wide.shape[2]
    places = {0: (("c", 0), ("b", rows_mix)), 1: (("b", 0), ("a", 0))}
    for layer in range(2):
        (slab, at), (feed, feed_at) = places[layer]
        for out, name in ((mix, slab), (proj, feed), (up, feed), (down, feed)):
            if name == feed and out is not mix:
                at = feed_at
            rows, cols = out.shape[1:]
            for i in range(cols // width):
                for offset, half, row, count in pieces(name, at + i * rows, at + (i + 1) * rows):
                    out[layer, offset : offset + count, i * width : (i + 1) * width] = wide[half, row : row + count]
            if out is not mix:
                feed_at = at + rows * cols // width
    for layer in range(2):
        for norm in range(2):
            gain[layer, norm : norm + 1] = small[2 * layer + norm : 2 * layer + norm + 1]
            bias[layer, norm : norm + 1] = small[4 + 2 * layer + norm : 5 + 2 * layer + norm]
    images = rms.shape[1]
    sums = pltpu.roll(small[8:16], small.shape[1] - (info[6] - info[6] % images), 1)
    rms[...] = jnp.sqrt(sums[: rms.shape[0], :images] / counted[...])


VMEM = pl.BlockSpec(memory_space=pltpu.VMEM)


def call(kernel, info, operands, specs, outs, out_specs, scratch=(), grid=(), work=0, aliases={}, limit=VMEM_LIMIT):
    moved = sum(math.prod(a.shape) * a.dtype.itemsize for a in list(operands) + jax.tree.leaves(outs))
    single = not isinstance(outs, list)
    views = list(specs) + ([out_specs] if single else list(out_specs))

    def body_of(info, *refs):
        seen = [view(ref) if callable(view) else ref for view, ref in zip(views, refs)]
        kernel(info, *seen, *refs[len(views) :])

    def plain(view):
        return VMEM if callable(view) else view

    return pl.pallas_call(
        body_of,
        grid_spec=pltpu.PrefetchScalarGridSpec(
            num_scalar_prefetch=1,
            grid=grid,
            in_specs=[plain(v) for v in specs],
            out_specs=plain(out_specs) if single else [plain(v) for v in out_specs],
            scratch_shapes=list(scratch),
        ),
        out_shape=outs,
        input_output_aliases=aliases,
        compiler_params=pltpu.CompilerParams(vmem_limit_bytes=limit),
        cost_estimate=pl.CostEstimate(flops=int(work * 1.15e9), bytes_accessed=moved, transcendentals=0),
    )(info, *operands)


def whole(array):
    return VMEM


def tiled(array):
    return lambda ref: ref.at[pl.ds(pl.multiple_of(pl.program_id(0) * TB, TB), TB)]


def after_window(ref):
    return ref.at[pl.ds(WIN, ref.shape[0] - WIN)]


def last_rows(ref):
    return ref.at[pl.ds(ref.shape[0] - WIN, WIN)]


ANY = pl.BlockSpec(memory_space=pl.ANY)


def shape(dims, kind):
    return jax.ShapeDtypeStruct(dims, kind)


def after(value, *others):
    return lax.optimization_barrier((value, others))[0]


def body(edge_rows, lengths, norm_gain, norm_bias, w_qkv, w_out, w_up, w_down):
    sections = lax.axis_size("section")
    index = lax.axis_index("section")
    images, rows_dev, width = edge_rows.shape
    seats = 2 * images
    rep = sections // seats
    seat = index // rep
    twin = index % rep
    rows_piece = rows_dev * rep
    qw = (w_qkv.shape[2] - width) // 2
    kvw = w_qkv.shape[2] - qw
    hidden = w_up.shape[2]
    n = rows_piece * images // 2
    if n != 2 * TB:
        raise ValueError("block size")
    quarter = images // 2
    steps = (n // TB,)

    def route(pairs):
        return [(s * rep + e, d * rep + e) for s, d in pairs for e in range(rep)]

    if rep > 1:
        groups = [[s * rep + e for e in range(rep)] for s in range(seats)]
        edge_rows = lax.all_gather(edge_rows, "section", axis_index_groups=groups, axis=1, tiled=True)

    chip = seat // 2
    part = seat % 2
    fz, fl, fy = chip // 4, (chip // 2) % 2, chip % 2
    limit = lengths[chip]
    spot = lax.axis_index("dp") * images + chip
    dp_count = lax.axis_size("dp")
    dp_index = lax.axis_index("dp")

    def partners(masks):
        total = dp_count * sections
        spot = dp_index * sections + index
        digit = sum(((spot // m) % 2) << i for i, m in enumerate(masks))
        routes = []
        for c in range(1, 1 << len(masks)):
            flips = sum(m for i, m in enumerate(masks) if (c >> i) & 1)
            routes.append((c, [(s, s ^ flips) for s in range(total)]))
        return digit, routes

    dp_masks = [sections << b for b in range(dp_count.bit_length() - 1)]
    section_masks = [1 << b for b in range(1, sections.bit_length() - 1)]
    plane = [dp_masks[0], section_masks[0]]
    rest = section_masks[1:] + dp_masks[1:]
    digits = [partners(masks)[0] for masks in [[1], plane] + [[m] for m in rest]]
    counted = (lengths.astype(F32) * width)[None, :]
    info = jnp.stack([part, limit, chip % quarter, fz, fy, fz, spot, twin, index % 2] + digits).astype(jnp.int32)
    swap = route([(s, s ^ 1) for s in range(seats)])

    def bits(s):
        return s // 8, (s // 4) % 2, (s // 2) % 2, s % 2

    by_column = edge_rows.reshape(2, 2, 2, rows_piece, width)
    traded = lax.dynamic_index_in_dim(by_column, 1 - part, 1, keepdims=False).reshape(4, rows_piece, width)
    traded = lax.ppermute(traded, "section", swap)
    column = lax.dynamic_index_in_dim(by_column, part, 1, keepdims=False).reshape(4, rows_piece, width)
    received = [None] * 4
    for t in (2, 3, 0, 1):
        tz, ty = t // 2, t % 2
        image = (fz ^ tz) * 2 + (fy ^ ty)
        own = lax.dynamic_index_in_dim(column, image, 0, keepdims=False)
        got = lax.dynamic_index_in_dim(traded, image, 0, keepdims=False)
        message = jnp.where(part == 0, jnp.concatenate([own, got]), jnp.concatenate([got, own]))
        pairs = []
        for s in range(seats):
            z, l, y, k = bits(s)
            pairs.append((s, ((z ^ tz) * 4 + k * 2 + (y ^ ty)) * 2 + l))
        received[t] = lax.ppermute(message, "section", route(pairs))

    def send_back(message, tz, ty):
        pairs = []
        for s in range(seats):
            z, l, y, p = bits(s)
            pairs.append((s, ((z ^ tz) * 4 + p * 2 + (y ^ ty)) * 2 + l))
        return lax.ppermute(message, "section", route(pairs))

    def trade(got, *awaited):
        out = shape((4, rows_piece, width), BF16)
        send = call(trade_kernel, info, got + list(awaited), [VMEM] * 4 + [ANY] * len(awaited), out, VMEM)
        return lax.ppermute(send, "section", swap)

    first_to_second = route([(2 * c, 2 * c + 1) for c in range(images)])
    second_to_first = route([(2 * c + 1, 2 * c) for c in range(images)])

    dma = pltpu.SemaphoreType.DMA
    rows_q = shape((n, qw), BF16)
    rows_kv = shape((n, kvw), BF16)
    rows_low = shape((n, width), BF16)
    rows_wide = shape((n, width), F32)
    rows_stat = shape((n, 128), F32)
    rows_hidden = shape((n, hidden), BF16)
    grad_k_shape = shape((n + WIN, qw), F32)
    grad_v_shape = shape((n + WIN, width), F32)
    mix_rows = w_qkv.shape[1] * w_qkv.shape[2] // width
    feed_rows = (w_out[0].size + w_up[0].size + w_down[0].size) // width
    vec_shape = shape((8, width), F32)
    squares_shape = shape((3, 8, width), F32)
    ext = pltpu.VMEM((n + WIN, kvw), BF16)

    g0, g1, b0, b1 = norm_gain[0], norm_gain[1], norm_bias[0], norm_bias[1]

    halo_shape = shape((WIN, kvw), BF16)
    outs = [shape((n + WIN, width), BF16), rows_q, rows_kv, halo_shape]
    x, q0, kv0, halo0 = call(
        first_kernel, info, received + [g0, b0, w_qkv[0]], [VMEM] * 7,
        outs, [whole(o) for o in outs], work=6,
    )
    halo0 = lax.ppermute(halo0, "section", first_to_second)

    outs = [rows_low, rows_q, rows_kv, rows_low, rows_stat, rows_hidden, rows_hidden, rows_wide, squares_shape]
    z, q1, kv1, o0, lse0, active0, slope0, mid0, squares0 = call(
        second_kernel, info, [x, q0, kv0, halo0, g0, b0, w_out[0], w_up[0], w_down[0], g1, b1, w_qkv[1]],
        [after_window] + [VMEM] * 11, outs, [VMEM] * len(outs), [ext], (1,), work=15,
        limit=2 * VMEM_LIMIT,
    )
    kv_other = lax.ppermute(kv1, "section", first_to_second)

    pad = 2 * n // STRIDE
    rows_k_all = shape((2 * n, qw), BF16)
    rows_v_all = shape((2 * n, width), BF16)
    outs = [rows_q, rows_k_all, rows_v_all, rows_wide, rows_stat]
    qr, kr, vr, o_far, lse_far = call(
        far_forward_kernel, info, [q1, kv1, kv_other], [whole(a) for a in (q1, kv1, kv_other)],
        outs, [whole(o) for o in outs],
        [pltpu.VMEM((n + pad, qw), F32), pltpu.VMEM((2 * n + pad, qw), F32), pltpu.VMEM((HEADS, 2 * n + pad, 128), F32),
         pltpu.VMEM((HEADS, n + pad, 128), F32), pltpu.VMEM((n + pad, 128), F32)], work=14,
    )

    message = shape((2 * rows_piece, width), BF16)
    outs = [message] * 4 + [rows_low, rows_stat, shape((n, qw), F32), grad_k_shape, grad_v_shape, rows_wide,
            shape((feed_rows // 2, width), F32), shape((feed_rows // 2, width), BF16),
            vec_shape, vec_shape, squares_shape]
    (cross0, cross1, local0, local1, go1, stat1, gq_near, gk_near, gv_near, gmid1, keep_a, send_a,
     d_gain11, d_bias11, squares1) = call(
        third_kernel, info,
        received + [q1, kv1, kv_other, o_far, lse_far, z, g1, b1, w_out[1], w_up[1], w_down[1]],
        [VMEM] * 4
        + [tiled(q1), whole(kv1), last_rows]
        + [tiled(o_far), tiled(lse_far), tiled(z)]
        + [whole(a) for a in (g1, b1, w_out[1], w_up[1], w_down[1])],
        outs,
        [whole(message)] * 4 + [tiled(o) for o in outs[4:7]] + [whole(outs[7]), whole(outs[8]), tiled(outs[9])]
        + [whole(o) for o in outs[10:]],
        [ext, pltpu.VMEM((TB, width), BF16), pltpu.VMEM((feed_rows, width), F32)], steps, work=24,
    )
    forward_back = [None, None, send_back(cross0, 1, 0), None]

    outs = [shape((n, qw), F32), shape((n, kvw), F32), rows_kv]
    operands = [qr, kr, vr, go1, stat1, gq_near, gk_near, gv_near]
    gq1, gkv1, gkv_send = call(
        far_backward_kernel, info, operands, [whole(a) for a in operands], outs, [whole(o) for o in outs],
        [pltpu.VMEM((HEADS, n + pad, 128), F32), pltpu.VMEM((n + pad, 128), F32), pltpu.VMEM((n + pad, qw), F32),
         pltpu.VMEM((2 * n + pad, qw), F32), pltpu.VMEM((HEADS, 2 * n + pad, 128), F32)], work=18,
    )
    def pair(message):
        return lax.ppermute(message, ("dp", "section"), partners([1])[1][0][1])

    def send_all(messages, masks):
        return [lax.ppermute(m, ("dp", "section"), way) for m, (_, way) in zip(messages, partners(masks)[1])]

    small_shape = shape((16, width), F32)
    rider_rows = 2 * small_shape.shape[0]

    def stage(groups, small, ways, number):
        operands = [a for kept, got in groups for a in [kept] + got] + ([] if small is None else [small])
        rows = sum(kept.shape[0] for kept, _ in groups)
        riders = small is not None
        outs = [shape((rows // ways + rider_rows * riders, width), BF16)] * max(ways - 1, 1)
        outs += [shape((rows // ways, width), F32)] * (ways > 1) + [small_shape] * riders
        kernel = functools.partial(
            stage_kernel, groups=[len(got) for _, got in groups], ways=ways, stage=number, riders=riders
        )
        made = call(
            kernel, info, operands, [VMEM] * len(operands), outs, [VMEM] * len(outs), [pltpu.VMEM((rows, width), F32)]
        )
        sent = max(ways - 1, 1)
        return made[:sent], made[sent] if ways > 1 else None, made[-1] if riders else None

    def gather(piece, masks, number):
        return in_order([piece] + [lax.ppermute(piece, ("dp", "section"), way) for _, way in partners(masks)[1]], number)

    def in_order(pieces, number, awaited=()):
        out = shape((len(pieces) * pieces[0].shape[0], width), BF16)
        kernel = functools.partial(order_kernel, stage=number, count=len(pieces))
        return call(kernel, info, pieces + list(awaited), [VMEM] * len(pieces) + [ANY] * len(awaited), out, VMEM)

    messages, kept_a, _ = stage([(keep_a, [pair(send_a)])], None, 4, 1)
    got_a = send_all(messages, plane)
    gkv_got = lax.ppermute(after(gkv_send, forward_back[2], *got_a), "section", second_to_first)
    forward_back[3] = send_back(after(cross1, forward_back[2]), 1, 1)
    forward_back[0] = send_back(after(local0, forward_back[2]), 0, 0)
    forward_back[1] = send_back(after(local1, forward_back[2]), 0, 1)

    slab_rows = mix_rows + feed_rows
    early_shape = slab_rows // 2, width
    mix_slab = shape((mix_rows, width), F32)
    outs = [message] * 4 + [shape((WIN, qw), F32), shape((WIN, kvw), F32), shape((WIN, width), F32), halo_shape,
            shape(early_shape, F32), shape(early_shape, BF16), mix_slab] + [vec_shape] * 6
    operands = [gq1, gkv1, gkv_got, z, gmid1, g1, b1, w_qkv[1], q0, kv0, halo0, o0, lse0, active0, slope0, mid0, x, g0,
                b0, w_qkv[0], w_out[0], w_up[0], w_down[0]]
    (cross0, cross1, local0, local1, gq_last, gkv_last, gmid_last, halo_send, keep_early, send_early, slab_last,
     d_gain10, d_bias10, d_gain01, d_bias01, d_gain00, d_bias00) = call(
        fourth_kernel, info, operands,
        [tiled(a) for a in operands[:5]] + [VMEM] * 3 + [tiled(q0), VMEM, VMEM] + [tiled(a) for a in operands[11:16]]
        + [VMEM] * 7,
        outs, [VMEM] * len(outs),
        [ext, pltpu.VMEM((slab_rows, width), F32), pltpu.VMEM((n + WIN, qw), F32), pltpu.VMEM((n + WIN, qw), F32),
         pltpu.VMEM((n + WIN, width), F32), pltpu.VMEM((n + WIN, width), F32)], steps, work=20,
    )
    halo_send, _ = call(
        hold_kernel, info, [halo_send, halo_send] + forward_back, [VMEM] * 2 + [ANY] * 4, [halo_shape] * 2, [VMEM] * 2
    )
    halo_got = lax.ppermute(halo_send, "section", second_to_first)

    got_early = pair(send_early)
    outs = [message] * 4 + [shape((mix_rows // 2, width), F32), shape((mix_rows // 2 + rider_rows, width), BF16), small_shape]
    operands = [gq_last, gkv_last, halo_got, x, gmid_last, g0, b0, w_qkv[0], slab_last]
    operands += [d_gain00, d_gain01, d_gain10, d_gain11, d_bias00, d_bias01, d_bias10, d_bias11, squares0, squares1]
    aliases = {1 + len(operands) + i: i for i in range(4)}
    operands += [cross0, cross1, local0, local1]
    cross0, cross1, local0, local1, keep_late, send_late, small = call(
        fifth_kernel, info, operands, [VMEM] * len(operands), outs, [VMEM] * len(outs),
        [pltpu.VMEM((mix_rows, width), F32), pltpu.VMEM((8, width), F32), pltpu.VMEM((8, width), F32)],
        aliases=aliases,
    )

    def assemble(own, other):
        outs = [shape((images, rows_piece, width), F32), shape((8, 128), F32)]
        out, token = call(
            assemble_kernel, info, own + [other], [VMEM] * 5, outs, [ANY, VMEM],
            [pltpu.VMEM((images, rows_piece, width), F32), dma((images,))],
        )
        if rep > 1:
            out = lax.dynamic_slice_in_dim(out, twin * rows_dev, rows_dev, 1)
        return out, token

    backward_back = [send_back(local0, 0, 0), None, send_back(cross0, 1, 0), None]
    got_late = pair(send_late)
    groups = [(keep_early, [got_early]), (keep_late, [got_late])]
    messages, kept, small = stage(groups, small, 4, 1)
    forward_trade = trade(forward_back, send_late)
    forward_rows, forward_token = assemble(forward_back, forward_trade)
    groups = [(kept_a, got_a), (kept, send_all(messages, plane))]
    number = 2
    scattered = []
    while number - 1 < len(rest) and sum(kept.shape[0] for kept, _ in groups) % 32 == 0:
        messages, kept, small = stage(groups, small, 2, number)
        groups = [(kept, send_all(messages, [rest[number - 2]]))]
        scattered.append(number)
        number += 1
    scattered_rows = groups[-1][1]
    backward_back[3] = send_back(after(cross1, backward_back[2]), 1, 1)
    backward_back[1] = send_back(after(local1, backward_back[2], *scattered_rows), 0, 1)
    (both,), _, small = stage(groups, small, 1, 0)
    both = after(both, backward_back[0], backward_back[2])
    rows_shape = shape((both.shape[0] - rider_rows, width), BF16)
    while number - 2 < len(rest):
        (got,) = send_all([both], [rest[number - 2]])
        rows, small = call(exchange_kernel, info, [both, got], [VMEM] * 2, [rows_shape, small_shape], [VMEM] * 2)
        number += 1
        if number - 2 < len(rest):
            both = call(again_kernel, info, [rows, small], [VMEM] * 2, shape(both.shape, BF16), VMEM)
    both = after(rows, backward_back[1], backward_back[3])
    for number in scattered[::-1]:
        both = gather(both, [rest[number - 2]], number)
    backward_trade = trade(backward_back, rows)
    backward_rows, backward_token = assemble(backward_back, backward_trade)
    both = in_order([both] + send_all([both] * 3, plane), 1, [backward_token, forward_token])
    theirs = pair(both)
    outs = [shape(w.shape, F32) for w in (w_qkv, w_out, w_up, w_down, norm_gain, norm_bias)] + [shape((6, images), F32)]
    sizes = (feed_rows, slab_rows, mix_rows, 1 << len(plane))
    grads = call(
        functools.partial(unpack_kernel, sizes=sizes), info, [both, theirs, small, counted],
        [VMEM] * 4, outs, [whole(o) for o in outs],
        [pltpu.VMEM((2,) + both.shape, F32)],
    )
    return (forward_rows, backward_rows, grads[6], grads[4], grads[5]) + tuple(grads[:4])


def solution(mesh):
    placed = (P("dp", "section", None), P("dp"), P(), P(), P(), P(), P(), P())
    return jax.shard_map(
        body,
        mesh=mesh,
        in_specs=placed,
        out_specs=(P("dp", "section", None), P("dp", "section", None), P(None, "dp"), P(), P(), P(), P(), P(), P()),
        check_vma=False,
    )
```

```python
import functools
import math

import jax
import jax.numpy as jnp
from jax import lax
from jax.experimental import pallas as pl
from jax.experimental.pallas import tpu as pltpu
from jax.sharding import PartitionSpec as P

HEADS = 2
WIN = 128
STRIDE = 128
NEG = -1e30
F32 = jnp.float32
BF16 = jnp.bfloat16
TB = 768
RES = 8
UNROLL = 16
RES_BACK = 16
UNROLL_BACK = 8
VMEM_LIMIT = 16 * 1024 * 1024


def dot(left, right):
    return lax.dot_general(left, right, (((1,), (0,)), ((), ())), preferred_element_type=F32)


def dot_t(left, right):
    return lax.dot_general(left, right, (((1,), (1,)), ((), ())), preferred_element_type=F32)


def t_dot(left, right):
    return lax.dot_general(left, right, (((0,), (0,)), ((), ())), preferred_element_type=F32)


def score_scale(query_width):
    return 1.0 / math.sqrt(query_width // HEADS)


def norm_parts(rows):
    centre = rows - jnp.mean(rows, axis=-1, keepdims=True)
    scale = lax.rsqrt(jnp.mean(centre * centre, axis=-1, keepdims=True) + 1e-05)
    return centre * scale, scale


def norm_back(grad, unit, scale, gain):
    scaled = grad * gain
    first = jnp.mean(scaled, axis=-1, keepdims=True)
    second = jnp.mean(scaled * unit, axis=-1, keepdims=True)
    return scale * (scaled - first - unit * second)


def col_sum(rows):
    return jnp.sum(rows.reshape(rows.shape[0] // 8, 8, rows.shape[1]), axis=0)


def gelu_pair(hidden):
    c0 = math.sqrt(2.0 / math.pi)
    square = hidden * hidden
    share = 0.5 + 0.5 * jnp.tanh(hidden * (c0 + (c0 * 0.044715) * square))
    active = hidden * share
    slope = share + active * (1.0 - share) * (2.0 * c0 + (6.0 * c0 * 0.044715) * square)
    return active, slope


def head_split(rows):
    lane = lax.broadcasted_iota(jnp.int32, rows.shape, 1)
    zero = jnp.zeros_like(rows)
    low = lane < rows.shape[1] // HEADS
    return jnp.concatenate([jnp.where(low, rows, zero), jnp.where(low, zero, rows)], axis=0)


def head_join(stacked):
    half = stacked.shape[0] // 2
    lane = lax.broadcasted_iota(jnp.int32, (half, stacked.shape[1]), 1)
    return jnp.where(lane < stacked.shape[1] // HEADS, stacked[:half], stacked[half:])


def near_masks(base, limit):
    row = lax.broadcasted_iota(jnp.int32, (2 * WIN, WIN), 0)
    row = jnp.where(row >= WIN, row - WIN, row)
    col = lax.broadcasted_iota(jnp.int32, (2 * WIN, WIN), 1)
    own = col <= row
    key = base + col - jnp.where(own, 0, WIN)
    allowed = (key >= 0) & ((key < limit) | (col == row))
    return own, allowed


def near_scores(split_q, keys, own, allowed):
    scores = dot_t(split_q, keys)
    folded = jnp.where(own, scores[:, WIN:], scores[:, :WIN])
    return jnp.where(allowed, folded, NEG)


def unfold(folded, own):
    return jnp.concatenate([jnp.where(own, 0.0, folded), jnp.where(own, folded, 0.0)], axis=1).astype(BF16)


def near_forward(queries, keys, values, base, limit):
    own, allowed = near_masks(base, limit)
    scores = near_scores(head_split(queries), keys, own, allowed)
    largest = jnp.max(scores, axis=-1, keepdims=True)
    powers = jnp.exp(scores - largest)
    total = jnp.sum(powers, axis=-1, keepdims=True)
    weights = unfold(powers, own)
    hd = values.shape[1] // HEADS
    out = [dot(weights[h * WIN : (h + 1) * WIN], values[:, h * hd : (h + 1) * hd]) for h in range(HEADS)]
    return out, largest, total, powers


def near_backward(queries, keys, values, grad_out, log_total, delta, base, limit, weights=None):
    own, allowed = near_masks(base, limit)
    split_q = head_split(queries)
    if weights is None:
        weights = jnp.exp(near_scores(split_q, keys, own, allowed) - log_total)
    hd = values.shape[1] // HEADS
    pull = jnp.concatenate(
        [dot_t(grad_out[:, h * hd : (h + 1) * hd], values[:, h * hd : (h + 1) * hd]) for h in range(HEADS)], axis=0
    )
    pull = jnp.where(own, pull[:, WIN:], pull[:, :WIN])
    slope = weights * (pull - delta)
    grad_q = head_join(dot(unfold(slope, own), keys))
    row = lax.broadcasted_iota(jnp.int32, (WIN, 2 * WIN), 0)
    col = lax.broadcasted_iota(jnp.int32, (WIN, 2 * WIN), 1)
    here = (row <= jnp.where(col >= WIN, col - WIN, col)).astype(F32).astype(BF16)

    def turned(folded):
        flat = folded.astype(BF16).T
        current = flat * here
        return jnp.concatenate([flat - current, current], axis=0)

    grad_k = dot(turned(slope), split_q)
    weights = turned(weights)
    grad_v = jnp.concatenate(
        [dot(weights[:, h * WIN : (h + 1) * WIN], grad_out[:, h * hd : (h + 1) * hd]) for h in range(HEADS)], axis=1
    )
    return grad_q, grad_k, grad_v


def stack_stat(stat, width=128):
    return jnp.concatenate([stat[:, 0:1], stat[:, width // 2 : width // 2 + 1]], axis=0)


def spread_stat(stacked, width=128):
    half = stacked.shape[0] // 2
    lane = lax.broadcasted_iota(jnp.int32, (half, width), 1)
    return jnp.where(lane < width // 2, stacked[:half], stacked[half:])


def masked_squares(rows, base, limit):
    pos = base + lax.broadcasted_iota(jnp.int32, (rows.shape[0], 1), 0)
    return col_sum(jnp.where(pos < limit, rows * rows, 0.0))


def pick_piece(info, pieces, low, block, target):
    for t, piece in enumerate(pieces):
        tz, ty = t // 2, t % 2

        @pl.when(((block ^ info[4]) == ty) & ((info[5] ^ (0 if low else 1)) == tz))
        def _():
            target[...] = piece[...]


def emit_block(info, block, rows, to_lower, first, cross, local):
    stays = info[5] == (0 if to_lower else 1)
    at = slice(first, first + rows.shape[0])
    for ty in range(2):
        fits = (block ^ info[4]) == ty

        @pl.when(fits & stays)
        def _():
            local[ty][at] = rows

        @pl.when(fits & jnp.logical_not(stays))
        def _():
            cross[ty][at] = rows


def emit_rows(info, first, rows, to_lower, cross, local):
    units = cross[0].shape[0] // WIN
    stays = info[5] == (0 if to_lower else 1)
    for sub in range(rows.shape[0] // WIN):
        number = first + sub
        block = number // units
        at = pl.ds(pl.multiple_of((number - block * units) * WIN, WIN), WIN)
        value = rows[sub * WIN : (sub + 1) * WIN]
        for ty in range(2):
            fits = (block ^ info[4]) == ty

            @pl.when(fits & stays)
            def _():
                local[ty][at] = value

            @pl.when(fits & jnp.logical_not(stays))
            def _():
                cross[ty][at] = value


def split_slab(info, slab, keep, send):
    once = jnp.where(info[7] == 0, 1.0, 0.0)
    half = keep.shape[0]
    mine = info[8]
    keep[...] = slab[pl.ds(pl.multiple_of(mine * half, 8), half)] * once
    send[:half] = (slab[pl.ds(pl.multiple_of((1 - mine) * half, 8), half)] * once).astype(BF16)


def first_kernel(info, *refs):
    pieces = refs[:4]
    gain, bias, w_mix, x_out, q_out, kv_out, halo_out = refs[4:]
    for half in range(2):
        pick_piece(info, pieces, True, half, x_out.at[pl.ds(WIN + half * pieces[0].shape[0], pieces[0].shape[0])])
    x_out[:WIN] = jnp.zeros((WIN, x_out.shape[1]), BF16)
    qw = q_out.shape[1]

    def block(i, _):
        at = pl.ds(pl.multiple_of(i * TB, TB), TB)
        unit, _ = norm_parts(x_out[pl.ds(pl.multiple_of(i * TB + WIN, WIN), TB)].astype(F32))
        normed = (unit * gain[0:1] + bias[0:1]).astype(BF16)
        mixed = dot(normed, w_mix[...])
        q_out[at] = (mixed[:, :qw] * score_scale(qw)).astype(BF16)
        kv_out[at] = mixed[:, qw:].astype(BF16)
        return 0

    lax.fori_loop(0, q_out.shape[0] // TB, block, 0)
    halo_out[...] = kv_out[kv_out.shape[0] - WIN :]


def load_extended(halo, kv, ext):
    ext[: halo.shape[0]] = halo[...]
    ext[halo.shape[0] :] = kv[...]


def second_kernel(
    info, x, q, kv, halo, gain, bias, w_proj, w_in, w_back, gain_next, bias_next, w_mix_next,
    z_out, q_next, kv_next, o_out, lse_out, active_out, slope_out, mid_out, squares, ext,
):
    step = pl.program_id(0)
    qw = q.shape[1]
    n = kv.shape[0]

    @pl.when(step == 0)
    def _():
        load_extended(halo, kv, ext)
        squares[...] = jnp.zeros_like(squares)

    limit = info[1]
    count = q.shape[0]
    start = step * count
    base = info[0] * n + start
    outs = []
    for sub in range(count // WIN):
        near = pl.ds(pl.multiple_of(start + sub * WIN, WIN), 2 * WIN)
        keys = ext[near, :qw]
        values = ext[near, qw:]
        queries = q[sub * WIN : (sub + 1) * WIN]
        out, largest, total, _ = near_forward(queries, keys, values, base + sub * WIN, limit)
        inverse = 1.0 / total
        lse_out[sub * WIN : (sub + 1) * WIN] = spread_stat(largest + jnp.log(total))
        outs.append(jnp.concatenate([out[0] * inverse[:WIN], out[1] * inverse[WIN:]], axis=1))
    attended = jnp.concatenate(outs, axis=0).astype(BF16)
    o_out[...] = attended
    stream = x[...].astype(F32)
    branch = dot(attended, w_proj[...])
    middle = stream + branch
    mid_out[...] = middle
    unit, _ = norm_parts(middle)
    normed = (unit * gain[1:2] + bias[1:2]).astype(BF16)
    active, slope = gelu_pair(dot(normed, w_in[...]))
    active = active.astype(BF16)
    active_out[...] = active
    slope_out[...] = slope.astype(BF16)
    feed = dot(active, w_back[...])
    z = (middle + feed).astype(BF16)
    z_out[...] = z
    squares[0] += masked_squares(stream, base, limit)
    squares[1] += masked_squares(branch, base, limit)
    squares[2] += masked_squares(feed, base, limit)
    unit, _ = norm_parts(z.astype(F32))
    normed = (unit * gain_next[0:1] + bias_next[0:1]).astype(BF16)
    mixed = dot(normed, w_mix_next[...])
    q_next[...] = (mixed[:, :qw] * score_scale(qw)).astype(BF16)
    kv_next[...] = mixed[:, qw:].astype(BF16)


def far_mask(grid_q, grid_k, part_grid, residues):
    shape = (HEADS * residues * grid_q, residues * grid_k)
    row = lax.broadcasted_iota(jnp.int32, shape, 0)
    col = lax.broadcasted_iota(jnp.int32, shape, 1)
    row = jnp.where(row >= residues * grid_q, row - residues * grid_q, row)
    row_res = jnp.zeros(shape, jnp.int32)
    col_res = jnp.zeros(shape, jnp.int32)
    for r in range(1, residues):
        row_res += (row >= r * grid_q).astype(jnp.int32)
        col_res += (col >= r * grid_k).astype(jnp.int32)
    row_grid = row - row_res * grid_q + part_grid
    col_grid = col - col_res * grid_k
    allowed = (row_res == col_res) & (col_grid < row_grid)
    return allowed, col_grid * STRIDE + col_res


def far_forward_kernel(info, q, kv, other, qr, kr, vr, o_far, lse_far, q_s, k_s, v_s, o_s, lse_s):
    n, qw = q.shape
    grid_q = n // STRIDE
    grid_k = 2 * grid_q
    part = info[0]
    limit = info[1]

    def place(g, _):
        at = pl.ds(pl.multiple_of(g * STRIDE, STRIDE), STRIDE)
        own = kv[at].astype(F32)
        early = jnp.where(part == 0, own, other[at].astype(F32))
        q_s[pl.ds(g, STRIDE, stride=grid_q), :] = q[at].astype(F32)
        k_s[pl.ds(g, STRIDE, stride=grid_k), :] = early[:, :qw]
        k_s[pl.ds(g + grid_q, STRIDE, stride=grid_k), :] = own[:, :qw]
        hd = v_s.shape[1]
        for h in range(HEADS):
            v_s[h, pl.ds(g, STRIDE, stride=grid_k), :] = early[:, qw + h * 128 : qw + (h + 1) * 128]
            v_s[h, pl.ds(g + grid_q, STRIDE, stride=grid_k), :] = own[:, qw + h * 128 : qw + (h + 1) * 128]
        return 0

    lax.fori_loop(0, grid_q, place, 0)
    base_mask, key_pos = far_mask(grid_q, grid_k, part * grid_q, RES)
    rows_q = RES * grid_q
    rows_k = RES * grid_k

    def one(i):
        at_q = pl.ds(pl.multiple_of(i * rows_q, rows_q), rows_q)
        at_k = pl.ds(pl.multiple_of(i * rows_k, rows_k), rows_k)
        queries = q_s[at_q].astype(BF16)
        keys = k_s[at_k].astype(BF16)
        values = [v_s[h, at_k].astype(BF16) for h in range(HEADS)]
        qr[at_q] = queries
        kr[at_k] = keys
        for h in range(HEADS):
            vr[at_k, h * 128 : (h + 1) * 128] = values[h]
        allowed = base_mask & (key_pos + i * RES < limit)
        scores = jnp.where(allowed, dot_t(head_split(queries), keys), NEG)
        largest = jnp.max(scores, axis=-1, keepdims=True)
        powers = jnp.where(allowed, jnp.exp(scores - largest), 0.0)
        total = jnp.sum(powers, axis=-1, keepdims=True)
        safe = jnp.maximum(total, 1e-30)
        weights = (powers * (1.0 / safe)).astype(BF16)
        lse = jnp.where(total > 0.0, largest + jnp.log(safe), NEG)
        lse_s[at_q] = spread_stat(lse)
        for h in range(HEADS):
            o_s[h, at_q] = dot(weights[h * rows_q : (h + 1) * rows_q], values[h])

    def group(i, _):
        for u in range(UNROLL):
            one(i * UNROLL + u)
        return 0

    lax.fori_loop(0, STRIDE // RES // UNROLL, group, 0)

    def back(g, _):
        at = pl.ds(pl.multiple_of(g * STRIDE, STRIDE), STRIDE)
        pick = pl.ds(g, STRIDE, stride=grid_q)
        lse_far[at] = lse_s[pick, :]
        for h in range(HEADS):
            o_far[at, h * 128 : (h + 1) * 128] = o_s[h, pick, :]
        return 0

    lax.fori_loop(0, grid_q, back, 0)


def third_kernel(
    info, *refs,
):
    pieces = refs[:4]
    (q, kv, halo, o_far, lse_far, z, gain, bias, w_proj, w_in, w_back,
     cross0, cross1, local0, local1, go_out, stat_out, gq_out, gk_out, gv_out, gmid_out, keep, send,
     d_gain, d_bias, squares, ext, cot, slab) = refs[4:]
    step = pl.program_id(0)
    qw = q.shape[1]
    n = kv.shape[0]

    @pl.when(step == 0)
    def _():
        load_extended(halo, kv, ext)
        for ref in (squares, gk_out, gv_out, slab, d_gain, d_bias):
            ref[...] = jnp.zeros_like(ref)

    limit = info[1]
    start = pl.multiple_of(step * TB, TB)
    base = info[0] * n + start
    outs = []
    logs = []
    weights = []
    for sub in range(TB // WIN):
        rows = slice(sub * WIN, (sub + 1) * WIN)
        near = pl.ds(pl.multiple_of(start + sub * WIN, WIN), 2 * WIN)
        out, largest, total, powers = near_forward(q[rows], ext[near, :qw], ext[near, qw:], base + sub * WIN, limit)
        far_log = stack_stat(lse_far[rows])
        top = jnp.maximum(largest, far_log)
        near_share = jnp.exp(largest - top)
        far_share = jnp.exp(far_log - top)
        whole = total * near_share + far_share
        inverse = 1.0 / whole
        near_share = near_share * inverse
        far_share = far_share * inverse
        weights.append(powers * near_share)
        logs.append(top + jnp.log(whole))
        far = o_far[rows]
        outs.append(
            jnp.concatenate(
                [
                    out[h] * near_share[h * WIN : (h + 1) * WIN]
                    + far[:, h * 128 : (h + 1) * 128] * far_share[h * WIN : (h + 1) * WIN]
                    for h in range(HEADS)
                ],
                axis=1,
            )
        )
    attended_wide = jnp.concatenate(outs, axis=0)
    attended = attended_wide.astype(BF16)
    stream = z[...].astype(F32)
    branch = dot(attended, w_proj[...])
    middle = stream + branch
    unit, scale = norm_parts(middle)
    normed = (unit * gain[1:2] + bias[1:2]).astype(BF16)
    active, slope = gelu_pair(dot(normed, w_in[...]))
    active = active.astype(BF16)
    feed = dot(active, w_back[...])
    emit_block(info, step, z[...], True, 0, (cross0, cross1), (local0, local1))
    emit_block(info, step, (middle + feed).astype(BF16), False, 0, (cross0, cross1), (local0, local1))
    pick_piece(info, pieces, False, step, cot)
    squares[0] += masked_squares(stream, base, limit)
    squares[1] += masked_squares(branch, base, limit)
    squares[2] += masked_squares(feed, base, limit)

    pos = base + lax.broadcasted_iota(jnp.int32, (TB, 1), 0)
    upstream = jnp.where(pos < limit, cot[...].astype(F32), 0.0)
    grad_out, grad_mid = feed_backward(
        upstream, active, slope, normed, unit, scale, attended, gain, w_proj, w_in, w_back, slab, 0, d_gain, d_bias
    )
    gmid_out[...] = grad_mid
    go_out[...] = grad_out
    weighted = grad_out.astype(F32) * attended_wide
    for sub in range(TB // WIN):
        rows = slice(sub * WIN, (sub + 1) * WIN)
        near = pl.ds(pl.multiple_of(start + sub * WIN, WIN), 2 * WIN)
        delta = jnp.concatenate(
            [jnp.sum(weighted[rows, h * 128 : (h + 1) * 128], axis=-1, keepdims=True) for h in range(HEADS)], axis=0
        )
        stat_out[rows] = pack_stats(logs[sub], delta)
        gq, gk, gv = near_backward(
            q[rows], ext[near, :qw], ext[near, qw:], grad_out[rows], logs[sub], delta, base + sub * WIN, limit,
            weights[sub],
        )
        gq_out[rows] = gq
        gk_out[near] += gk
        gv_out[near] += gv

    @pl.when(step == pl.num_programs(0) - 1)
    def _():
        split_slab(info, slab, keep, send)


def pack_stats(lse, delta):
    half = lse.shape[0] // 2
    lane = lax.broadcasted_iota(jnp.int32, (half, 128), 1)
    low = jnp.where(lane < 32, lse[:half], lse[half:])
    high = jnp.where(lane < 96, delta[:half], delta[half:])
    return jnp.where(lane < 64, low, high)


def add_columns(slab, at, grad):
    rows, cols = grad.shape
    width = slab.shape[1]
    for i in range(cols // width):
        slab[at + i * rows : at + (i + 1) * rows] += grad[:, i * width : (i + 1) * width]


def feed_backward(
    upstream, active, slope, normed, unit, scale, attended, gain, w_proj, w_in, w_back, slab, at, d_gain, d_bias,
):
    low = upstream.astype(BF16)
    width = low.shape[1]
    hidden = active.shape[1]
    slab[at + width + hidden : at + width + 2 * hidden] += t_dot(active, low)
    grad_hidden = (dot_t(low, w_back[...]) * slope).astype(BF16)
    add_columns(slab, at + width, t_dot(normed, grad_hidden))
    grad_normed = dot_t(grad_hidden, w_in[...])
    d_gain[...] += col_sum(grad_normed * unit)
    d_bias[...] += col_sum(grad_normed)
    grad_mid = upstream + norm_back(grad_normed, unit, scale, gain[1:2])
    branch_low = grad_mid.astype(BF16)
    slab[at : at + width] += t_dot(attended, branch_low)
    grad_out = dot_t(branch_low, w_proj[...]).astype(BF16)
    return grad_out, grad_mid


def far_backward_kernel(
    info, qr, kr, vr, go, stat, gq_near, gk_near, gv_near, gq_out, gkv_own, gkv_send,
    go_s, stat_s, gq_s, gk_s, gv_s,
):
    n, qw = gq_near.shape
    grid_q = n // STRIDE
    grid_k = 2 * grid_q
    part = info[0]
    limit = info[1]

    def place(g, _):
        at = pl.ds(pl.multiple_of(g * STRIDE, STRIDE), STRIDE)
        pick = pl.ds(g, STRIDE, stride=grid_q)
        rows = go[at].astype(F32)
        for h in range(HEADS):
            go_s[h, pick, :] = rows[:, h * 128 : (h + 1) * 128]
        stat_s[pick, :] = stat[at]
        return 0

    lax.fori_loop(0, grid_q, place, 0)
    base_mask, key_pos = far_mask(grid_q, grid_k, part * grid_q, RES_BACK)
    rows_q = RES_BACK * grid_q
    rows_k = RES_BACK * grid_k

    def one(i):
        at_q = pl.ds(pl.multiple_of(i * rows_q, rows_q), rows_q)
        at_k = pl.ds(pl.multiple_of(i * rows_k, rows_k), rows_k)
        keys = kr[at_k]
        split_q = head_split(qr[at_q])
        grads = [go_s[h, at_q].astype(BF16) for h in range(HEADS)]
        stats = stat_s[at_q]
        lse = jnp.concatenate([stats[:, 0:1], stats[:, 32:33]], axis=0)
        delta = jnp.concatenate([stats[:, 64:65], stats[:, 96:97]], axis=0)
        allowed = base_mask & (key_pos + i * RES_BACK < limit)
        weights = jnp.exp(jnp.where(allowed, dot_t(split_q, keys), NEG) - lse)
        pull = jnp.concatenate([dot_t(grads[h], vr[at_k, h * 128 : (h + 1) * 128]) for h in range(HEADS)], axis=0)
        slope = (weights * (pull - delta)).astype(BF16)
        weights = weights.astype(BF16)
        gq_s[at_q] = head_join(dot(slope, keys))
        gk_s[at_k] = t_dot(slope, split_q)
        for h in range(HEADS):
            gv_s[h, at_k] = t_dot(weights[h * rows_q : (h + 1) * rows_q], grads[h])

    def group(i, _):
        for u in range(UNROLL_BACK):
            one(i * UNROLL_BACK + u)
        return 0

    lax.fori_loop(0, STRIDE // RES_BACK // UNROLL_BACK, group, 0)

    def back(g, _):
        at = pl.ds(pl.multiple_of(g * STRIDE, STRIDE), STRIDE)
        shifted = pl.ds(pl.multiple_of(g * STRIDE + WIN, STRIDE), STRIDE)
        gq_out[at] = gq_near[at] + gq_s[pl.ds(g, STRIDE, stride=grid_q), :]
        mine = pl.ds(g + part * grid_q, STRIDE, stride=grid_k)
        sent = pl.ds(g, STRIDE, stride=grid_k)
        last = jnp.where(g == grid_q - 1, 1.0, 0.0)
        gkv_own[at, :qw] = gk_near[shifted] + gk_s[mine, :]
        gkv_send[at, :qw] = (gk_s[sent, :] + last * gk_near[:WIN]).astype(BF16)
        for h in range(HEADS):
            cols = slice(h * 128, (h + 1) * 128)
            wide = slice(qw + h * 128, qw + (h + 1) * 128)
            gkv_own[at, wide] = gv_near[shifted, cols] + gv_s[h, mine, :]
            gkv_send[at, wide] = (gv_s[h, sent, :] + last * gv_near[:WIN, cols]).astype(BF16)
        return 0

    lax.fori_loop(0, grid_q, back, 0)


def mix_backward(grad_q, grad_kv, rows, gain, bias, w_mix, slab, d_gain, d_bias, carried):
    grad_mixed = jnp.concatenate([grad_q * score_scale(grad_q.shape[1]), grad_kv], axis=1).astype(BF16)
    unit, scale = norm_parts(rows)
    normed = (unit * gain[0:1] + bias[0:1]).astype(BF16)
    add_columns(slab, 0, t_dot(normed, grad_mixed))
    grad_normed = dot_t(grad_mixed, w_mix[...])
    d_gain[...] += col_sum(grad_normed * unit)
    d_bias[...] += col_sum(grad_normed)
    return carried + norm_back(grad_normed, unit, scale, gain[0:1])


def fourth_kernel(
    info, gq, gkv, got, z, gmid, gain_next, bias_next, w_mix_next,
    q, kv, halo, o, lse, active, slope, mid, x, gain, bias, w_mix, w_proj, w_in, w_back,
    cross0, cross1, local0, local1, gq_last, gkv_last, gmid_last, halo_out, keep, send, slab_last,
    dn_gain, dn_bias, d_gain, d_bias, d_gain_first, d_bias_first,
    ext, slab, gq_ext, gk_ext, gv_ext, gmid_ext,
):
    step = pl.program_id(0)
    qw = q.shape[1]
    n = kv.shape[0]

    @pl.when(step == 0)
    def _():
        load_extended(halo, kv, ext)
        for ref in (
            slab, slab_last, dn_gain, dn_bias, d_gain, d_bias, d_gain_first, d_bias_first, gq_ext, gk_ext, gv_ext, gmid_ext
        ):
            ref[...] = jnp.zeros_like(ref)

    limit = info[1]
    start = pl.multiple_of(step * TB, TB)
    base = info[0] * n + start
    grad_kv = gkv[...] + got[...].astype(F32)
    grad_z = mix_backward(
        gq[...], grad_kv, z[...].astype(F32), gain_next, bias_next, w_mix_next, slab, dn_gain, dn_bias, gmid[...]
    )
    grad_low = grad_z.astype(BF16)
    emit_block(info, step, grad_low, False, 0, (cross0, cross1), (local0, local1))
    unit, scale = norm_parts(mid[...])
    normed = (unit * gain[1:2] + bias[1:2]).astype(BF16)
    attended = o[...]
    grad_out, grad_mid = feed_backward(
        grad_low.astype(F32), active[...], slope[...].astype(F32), normed, unit, scale, attended, gain,
        w_proj, w_in, w_back, slab, w_mix_next.size // w_proj.shape[1], d_gain, d_bias,
    )
    shifted = pl.ds(pl.multiple_of(start + WIN, WIN), TB)
    gmid_ext[shifted] = grad_mid
    weighted = grad_out.astype(F32) * attended.astype(F32)
    for sub in range(TB // WIN):
        rows = slice(sub * WIN, (sub + 1) * WIN)
        near = pl.ds(pl.multiple_of(start + sub * WIN, WIN), 2 * WIN)
        delta = jnp.concatenate(
            [jnp.sum(weighted[rows, h * 128 : (h + 1) * 128], axis=-1, keepdims=True) for h in range(HEADS)], axis=0
        )
        g_q, g_k, g_v = near_backward(
            q[rows], ext[near, :qw], ext[near, qw:], grad_out[rows], stack_stat(lse[rows]), delta,
            base + sub * WIN, limit,
        )
        gq_ext[pl.ds(pl.multiple_of(start + (sub + 1) * WIN, WIN), WIN)] = g_q
        gk_ext[near] += g_k
        gv_ext[near] += g_v

    @pl.when(step == 0)
    def _():
        halo_out[...] = jnp.concatenate([gk_ext[:WIN], gv_ext[:WIN]], axis=1).astype(BF16)
        gk_ext[:WIN] = jnp.zeros((WIN, gk_ext.shape[1]), F32)
        gv_ext[:WIN] = jnp.zeros((WIN, gv_ext.shape[1]), F32)

    whole_rows = pl.ds(start, TB)
    grad_x = mix_backward(
        gq_ext[whole_rows], jnp.concatenate([gk_ext[whole_rows], gv_ext[whole_rows]], axis=1),
        x[whole_rows].astype(F32), gain, bias, w_mix, slab_last, d_gain_first, d_bias_first, gmid_ext[whole_rows],
    )
    grad_x = grad_x.astype(BF16)
    emit_block(info, step, grad_x[WIN:], True, 0, (cross0, cross1), (local0, local1))

    @pl.when(step > 0)
    def _():
        emit_rows(info, step * (TB // WIN) - 1, grad_x[:WIN], True, (cross0, cross1), (local0, local1))

    @pl.when(step == pl.num_programs(0) - 1)
    def _():
        gq_last[...] = gq_ext[n:]
        gkv_last[...] = jnp.concatenate([gk_ext[n:], gv_ext[n:]], axis=1)
        gmid_last[...] = gmid_ext[n:]
        split_slab(info, slab, keep, send)


def fifth_kernel(info, gq, gkv, got, x, gmid, gain, bias, w_mix, slab_in, *refs):
    vectors, squares = refs[:8], refs[8:10]
    cross, local, (keep, send, small, slab, d_gain, d_bias) = refs[-10:-8], refs[-8:-6], refs[-6:]
    slab[...] = slab_in[...]
    d_gain[...] = vectors[0][...]
    d_bias[...] = vectors[4][...]
    n = x.shape[0] - WIN
    grad_x = mix_backward(
        gq[...], gkv[...] + got[...].astype(F32), x[n:].astype(F32), gain, bias, w_mix, slab, d_gain, d_bias, gmid[...]
    )
    emit_rows(info, n // WIN - 1, grad_x.astype(BF16), True, cross, local)
    split_slab(info, slab, keep, send)
    small_rows(info, (d_gain,) + vectors[1:4] + (d_bias,) + vectors[5:], squares, small)
    put_riders(small[...], send, keep.shape[0])


def put_riders(rows, send, at):
    count = rows.shape[0]
    coarse = rows.astype(BF16)
    send[at : at + count] = coarse
    send[at + count :] = (rows - coarse.astype(F32)).astype(BF16)


def riders_of(got, at):
    count = (got.shape[0] - at) // 2
    return got[at : at + count].astype(F32) + got[at + count :].astype(F32)


def stage_kernel(digits, *refs, groups, ways, stage, riders):
    refs = list(refs)
    parts = [(refs.pop(0), [refs.pop(0) for _ in range(count)]) for count in groups]
    small = refs.pop(0) if riders else None
    messages = [refs.pop(0) for _ in range(max(ways - 1, 1))]
    kept_out = refs.pop(0) if ways > 1 else None
    small_out = refs.pop(0) if riders else None
    total = refs.pop(0)
    vectors = small[...] if riders else None
    at = 0
    for kept, got in parts:
        rows = kept.shape[0]
        value = kept[...]
        for g in got:
            value = value + g[:rows].astype(F32)
            if g.shape[0] > rows:
                vectors = vectors + riders_of(g, rows)
        total[at : at + rows] = value
        at += rows
    chunk = at // ways

    def piece(which):
        return total[pl.ds(pl.multiple_of(which * chunk, 16), chunk)]

    mine = digits[9 + stage] if ways > 1 else 0
    for i, message in enumerate(messages):
        message[:chunk] = piece(mine ^ (i + 1) if ways > 1 else 0).astype(BF16)
        if riders:
            put_riders(vectors, message, chunk)
    if ways > 1:
        kept_out[...] = piece(mine)
    if riders:
        small_out[...] = vectors


def exchange_kernel(digits, mine, theirs, rows_out, small_out):
    count = rows_out.shape[0]
    rows_out[...] = (mine[:count].astype(F32) + theirs[:count].astype(F32)).astype(BF16)
    small_out[...] = riders_of(mine, count) + riders_of(theirs, count)


def again_kernel(digits, rows, small, message):
    message[: rows.shape[0]] = rows[...]
    put_riders(small[...], message, rows.shape[0])


def order_kernel(digits, *refs, stage, count):
    pieces, out = refs[:count], refs[-1]
    rows = pieces[0].shape[0]
    for c, piece in enumerate(pieces):
        out[pl.ds(pl.multiple_of((digits[9 + stage] ^ c) * rows, 16), rows)] = piece[...]


def assemble_kernel(info, *refs):
    own, other, out, token, wide, sems = refs[:4], *refs[4:]
    token[...] = jnp.zeros_like(token)
    core = info[0]
    rows = out.shape[1]

    def leave(t):
        column = core if t < 4 else 1 - core
        image = (info[5] ^ (t % 4 // 2)) * 4 + column * 2 + (info[4] ^ (t % 2))
        return pltpu.make_async_copy(wide.at[t], out.at[image], sems.at[t])

    for t in range(8):
        if t < 4:
            block = own[t][pl.ds(pl.multiple_of(core * rows, rows), rows)]
        else:
            block = other[t - 4]
        wide[t] = block.astype(F32)
        leave(t).start()
    for t in range(8):
        leave(t).wait()


def hold_kernel(info, first, second, *refs):
    refs[-2][...] = first[...]
    refs[-1][...] = second[...]


def small_rows(info, vectors, squares, out):
    width = out.shape[1]
    once = jnp.where(info[7] == 0, 1.0, 0.0)
    lane = lax.broadcasted_iota(jnp.int32, (1, width), 1)
    out[...] = jnp.zeros_like(out)
    for i, vector in enumerate(vectors):
        out[i : i + 1] = jnp.sum(vector[...], axis=0, keepdims=True) * once
    for i in range(6):
        total = jnp.sum(jnp.sum(squares[i // 3][i % 3], axis=0, keepdims=True), axis=1, keepdims=True)
        out[8 + i : 9 + i] = jnp.where(lane == info[6], total * once, 0.0)


def trade_kernel(info, *refs):
    pieces, out = refs[:4], refs[-1]
    rows = out.shape[1]
    for t in range(4):
        out[t] = pieces[t][pl.ds(pl.multiple_of((1 - info[0]) * rows, rows), rows)]


def unpack_kernel(info, mine, theirs, small, counted, mix, proj, up, down, gain, bias, rms, wide, *, sizes):
    core = info[9]
    wide[core] = mine[...].astype(F32)
    wide[1 - core] = theirs[...].astype(F32)
    rows_a, rows_b, rows_c, ways = sizes
    early = rows_a // 2 // ways
    late = (rows_b + rows_c) // 2 // ways
    rows_mix = rows_c

    def pieces(slab, start, stop):
        total = {"a": rows_a, "b": rows_b, "c": rows_c}[slab] // 2
        size, shift, skip = {"a": (early, 0, 0), "b": (late, early, 0), "c": (late, early, rows_b // 2)}[slab]
        at = start
        while at < stop:
            half, row = at // total, at % total
            along = row + skip
            count = min(stop - at, total - row, size - along % size)
            yield at - start, half, along // size * (early + late) + shift + along % size, count
            at += count

    width = wide.shape[2]
    places = {0: (("c", 0), ("b", rows_mix)), 1: (("b", 0), ("a", 0))}
    for layer in range(2):
        (slab, at), (feed, feed_at) = places[layer]
        for out, name in ((mix, slab), (proj, feed), (up, feed), (down, feed)):
            if name == feed and out is not mix:
                at = feed_at
            rows, cols = out.shape[1:]
            for i in range(cols // width):
                for offset, half, row, count in pieces(name, at + i * rows, at + (i + 1) * rows):
                    out[layer, offset : offset + count, i * width : (i + 1) * width] = wide[half, row : row + count]
            if out is not mix:
                feed_at = at + rows * cols // width
    for layer in range(2):
        for norm in range(2):
            gain[layer, norm : norm + 1] = small[2 * layer + norm : 2 * layer + norm + 1]
            bias[layer, norm : norm + 1] = small[4 + 2 * layer + norm : 5 + 2 * layer + norm]
    images = rms.shape[1]
    sums = pltpu.roll(small[8:16], small.shape[1] - (info[6] - info[6] % images), 1)
    rms[...] = jnp.sqrt(sums[: rms.shape[0], :images] / counted[...])


VMEM = pl.BlockSpec(memory_space=pltpu.VMEM)


def call(kernel, info, operands, specs, outs, out_specs, scratch=(), grid=(), work=0, aliases={}, limit=VMEM_LIMIT):
    moved = sum(math.prod(a.shape) * a.dtype.itemsize for a in list(operands) + jax.tree.leaves(outs))
    single = not isinstance(outs, list)
    views = list(specs) + ([out_specs] if single else list(out_specs))

    def body_of(info, *refs):
        seen = [view(ref) if callable(view) else ref for view, ref in zip(views, refs)]
        kernel(info, *seen, *refs[len(views) :])

    def plain(view):
        return VMEM if callable(view) else view

    return pl.pallas_call(
        body_of,
        grid_spec=pltpu.PrefetchScalarGridSpec(
            num_scalar_prefetch=1,
            grid=grid,
            in_specs=[plain(v) for v in specs],
            out_specs=plain(out_specs) if single else [plain(v) for v in out_specs],
            scratch_shapes=list(scratch),
        ),
        out_shape=outs,
        input_output_aliases=aliases,
        compiler_params=pltpu.CompilerParams(vmem_limit_bytes=limit),
        cost_estimate=pl.CostEstimate(flops=int(work * 1.15e9), bytes_accessed=moved, transcendentals=0),
    )(info, *operands)


def whole(array):
    return VMEM


def tiled(array):
    return lambda ref: ref.at[pl.ds(pl.multiple_of(pl.program_id(0) * TB, TB), TB)]


def after_window(ref):
    return ref.at[pl.ds(WIN, ref.shape[0] - WIN)]


def last_rows(ref):
    return ref.at[pl.ds(ref.shape[0] - WIN, WIN)]


ANY = pl.BlockSpec(memory_space=pl.ANY)


def shape(dims, kind):
    return jax.ShapeDtypeStruct(dims, kind)


def after(value, *others):
    return lax.optimization_barrier((value, others))[0]


def body(edge_rows, lengths, norm_gain, norm_bias, w_qkv, w_out, w_up, w_down):
    sections = lax.axis_size("section")
    index = lax.axis_index("section")
    images, rows_dev, width = edge_rows.shape
    seats = 2 * images
    rep = sections // seats
    seat = index // rep
    twin = index % rep
    rows_piece = rows_dev * rep
    qw = (w_qkv.shape[2] - width) // 2
    kvw = w_qkv.shape[2] - qw
    hidden = w_up.shape[2]
    n = rows_piece * images // 2
    if n != 2 * TB:
        raise ValueError("block size")
    quarter = images // 2
    steps = (n // TB,)

    def route(pairs):
        return [(s * rep + e, d * rep + e) for s, d in pairs for e in range(rep)]

    if rep > 1:
        groups = [[s * rep + e for e in range(rep)] for s in range(seats)]
        edge_rows = lax.all_gather(edge_rows, "section", axis_index_groups=groups, axis=1, tiled=True)

    chip = seat // 2
    part = seat % 2
    fz, fl, fy = chip // 4, (chip // 2) % 2, chip % 2
    limit = lengths[chip]
    spot = lax.axis_index("dp") * images + chip
    dp_count = lax.axis_size("dp")
    dp_index = lax.axis_index("dp")

    def partners(masks):
        total = dp_count * sections
        spot = dp_index * sections + index
        digit = sum(((spot // m) % 2) << i for i, m in enumerate(masks))
        routes = []
        for c in range(1, 1 << len(masks)):
            flips = sum(m for i, m in enumerate(masks) if (c >> i) & 1)
            routes.append((c, [(s, s ^ flips) for s in range(total)]))
        return digit, routes

    dp_masks = [sections << b for b in range(dp_count.bit_length() - 1)]
    section_masks = [1 << b for b in range(1, sections.bit_length() - 1)]
    plane = [dp_masks[0], section_masks[0]]
    rest = section_masks[1:] + dp_masks[1:]
    digits = [partners(masks)[0] for masks in [[1], plane] + [[m] for m in rest]]
    counted = (lengths.astype(F32) * width)[None, :]
    info = jnp.stack([part, limit, chip % quarter, fz, fy, fz, spot, twin, index % 2] + digits).astype(jnp.int32)
    swap = route([(s, s ^ 1) for s in range(seats)])

    def bits(s):
        return s // 8, (s // 4) % 2, (s // 2) % 2, s % 2

    by_column = edge_rows.reshape(2, 2, 2, rows_piece, width)
    traded = lax.dynamic_index_in_dim(by_column, 1 - part, 1, keepdims=False).reshape(4, rows_piece, width)
    traded = lax.ppermute(traded, "section", swap)
    column = lax.dynamic_index_in_dim(by_column, part, 1, keepdims=False).reshape(4, rows_piece, width)
    received = [None] * 4
    for t in (2, 3, 0, 1):
        tz, ty = t // 2, t % 2
        image = (fz ^ tz) * 2 + (fy ^ ty)
        own = lax.dynamic_index_in_dim(column, image, 0, keepdims=False)
        got = lax.dynamic_index_in_dim(traded, image, 0, keepdims=False)
        message = jnp.where(part == 0, jnp.concatenate([own, got]), jnp.concatenate([got, own]))
        pairs = []
        for s in range(seats):
            z, l, y, k = bits(s)
            pairs.append((s, ((z ^ tz) * 4 + k * 2 + (y ^ ty)) * 2 + l))
        received[t] = lax.ppermute(message, "section", route(pairs))

    def send_back(message, tz, ty):
        pairs = []
        for s in range(seats):
            z, l, y, p = bits(s)
            pairs.append((s, ((z ^ tz) * 4 + p * 2 + (y ^ ty)) * 2 + l))
        return lax.ppermute(message, "section", route(pairs))

    def trade(got, *awaited):
        out = shape((4, rows_piece, width), BF16)
        send = call(trade_kernel, info, got + list(awaited), [VMEM] * 4 + [ANY] * len(awaited), out, VMEM)
        return lax.ppermute(send, "section", swap)

    first_to_second = route([(2 * c, 2 * c + 1) for c in range(images)])
    second_to_first = route([(2 * c + 1, 2 * c) for c in range(images)])

    dma = pltpu.SemaphoreType.DMA
    rows_q = shape((n, qw), BF16)
    rows_kv = shape((n, kvw), BF16)
    rows_low = shape((n, width), BF16)
    rows_wide = shape((n, width), F32)
    rows_stat = shape((n, 128), F32)
    rows_hidden = shape((n, hidden), BF16)
    grad_k_shape = shape((n + WIN, qw), F32)
    grad_v_shape = shape((n + WIN, width), F32)
    mix_rows = w_qkv.shape[1] * w_qkv.shape[2] // width
    feed_rows = (w_out[0].size + w_up[0].size + w_down[0].size) // width
    vec_shape = shape((8, width), F32)
    squares_shape = shape((3, 8, width), F32)
    ext = pltpu.VMEM((n + WIN, kvw), BF16)

    g0, g1, b0, b1 = norm_gain[0], norm_gain[1], norm_bias[0], norm_bias[1]

    halo_shape = shape((WIN, kvw), BF16)
    outs = [shape((n + WIN, width), BF16), rows_q, rows_kv, halo_shape]
    x, q0, kv0, halo0 = call(
        first_kernel, info, received + [g0, b0, w_qkv[0]], [VMEM] * 7,
        outs, [whole(o) for o in outs], work=6,
    )
    halo0 = lax.ppermute(halo0, "section", first_to_second)

    outs = [rows_low, rows_q, rows_kv, rows_low, rows_stat, rows_hidden, rows_hidden, rows_wide, squares_shape]
    z, q1, kv1, o0, lse0, active0, slope0, mid0, squares0 = call(
        second_kernel, info, [x, q0, kv0, halo0, g0, b0, w_out[0], w_up[0], w_down[0], g1, b1, w_qkv[1]],
        [after_window] + [VMEM] * 11, outs, [VMEM] * len(outs), [ext], (1,), work=15,
        limit=2 * VMEM_LIMIT,
    )
    kv_other = lax.ppermute(kv1, "section", first_to_second)

    pad = 2 * n // STRIDE
    rows_k_all = shape((2 * n, qw), BF16)
    rows_v_all = shape((2 * n, width), BF16)
    outs = [rows_q, rows_k_all, rows_v_all, rows_wide, rows_stat]
    qr, kr, vr, o_far, lse_far = call(
        far_forward_kernel, info, [q1, kv1, kv_other], [whole(a) for a in (q1, kv1, kv_other)],
        outs, [whole(o) for o in outs],
        [pltpu.VMEM((n + pad, qw), F32), pltpu.VMEM((2 * n + pad, qw), F32), pltpu.VMEM((HEADS, 2 * n + pad, 128), F32),
         pltpu.VMEM((HEADS, n + pad, 128), F32), pltpu.VMEM((n + pad, 128), F32)], work=14,
    )

    message = shape((2 * rows_piece, width), BF16)
    outs = [message] * 4 + [rows_low, rows_stat, shape((n, qw), F32), grad_k_shape, grad_v_shape, rows_wide,
            shape((feed_rows // 2, width), F32), shape((feed_rows // 2, width), BF16),
            vec_shape, vec_shape, squares_shape]
    (cross0, cross1, local0, local1, go1, stat1, gq_near, gk_near, gv_near, gmid1, keep_a, send_a,
     d_gain11, d_bias11, squares1) = call(
        third_kernel, info,
        received + [q1, kv1, kv_other, o_far, lse_far, z, g1, b1, w_out[1], w_up[1], w_down[1]],
        [VMEM] * 4
        + [tiled(q1), whole(kv1), last_rows]
        + [tiled(o_far), tiled(lse_far), tiled(z)]
        + [whole(a) for a in (g1, b1, w_out[1], w_up[1], w_down[1])],
        outs,
        [whole(message)] * 4 + [tiled(o) for o in outs[4:7]] + [whole(outs[7]), whole(outs[8]), tiled(outs[9])]
        + [whole(o) for o in outs[10:]],
        [ext, pltpu.VMEM((TB, width), BF16), pltpu.VMEM((feed_rows, width), F32)], steps, work=24,
    )
    forward_back = [None, None, send_back(cross0, 1, 0), None]

    outs = [shape((n, qw), F32), shape((n, kvw), F32), rows_kv]
    operands = [qr, kr, vr, go1, stat1, gq_near, gk_near, gv_near]
    gq1, gkv1, gkv_send = call(
        far_backward_kernel, info, operands, [whole(a) for a in operands], outs, [whole(o) for o in outs],
        [pltpu.VMEM((HEADS, n + pad, 128), F32), pltpu.VMEM((n + pad, 128), F32), pltpu.VMEM((n + pad, qw), F32),
         pltpu.VMEM((2 * n + pad, qw), F32), pltpu.VMEM((HEADS, 2 * n + pad, 128), F32)], work=18,
    )
    def pair(message):
        return lax.ppermute(message, ("dp", "section"), partners([1])[1][0][1])

    def send_all(messages, masks):
        return [lax.ppermute(m, ("dp", "section"), way) for m, (_, way) in zip(messages, partners(masks)[1])]

    small_shape = shape((16, width), F32)
    rider_rows = 2 * small_shape.shape[0]

    def stage(groups, small, ways, number):
        operands = [a for kept, got in groups for a in [kept] + got] + ([] if small is None else [small])
        rows = sum(kept.shape[0] for kept, _ in groups)
        riders = small is not None
        outs = [shape((rows // ways + rider_rows * riders, width), BF16)] * max(ways - 1, 1)
        outs += [shape((rows // ways, width), F32)] * (ways > 1) + [small_shape] * riders
        kernel = functools.partial(
            stage_kernel, groups=[len(got) for _, got in groups], ways=ways, stage=number, riders=riders
        )
        made = call(
            kernel, info, operands, [VMEM] * len(operands), outs, [VMEM] * len(outs), [pltpu.VMEM((rows, width), F32)]
        )
        sent = max(ways - 1, 1)
        return made[:sent], made[sent] if ways > 1 else None, made[-1] if riders else None

    def gather(piece, masks, number):
        return in_order([piece] + [lax.ppermute(piece, ("dp", "section"), way) for _, way in partners(masks)[1]], number)

    def in_order(pieces, number, awaited=()):
        out = shape((len(pieces) * pieces[0].shape[0], width), BF16)
        kernel = functools.partial(order_kernel, stage=number, count=len(pieces))
        return call(kernel, info, pieces + list(awaited), [VMEM] * len(pieces) + [ANY] * len(awaited), out, VMEM)

    messages, kept_a, _ = stage([(keep_a, [pair(send_a)])], None, 4, 1)
    got_a = send_all(messages, plane)
    gkv_got = lax.ppermute(after(gkv_send, forward_back[2], *got_a), "section", second_to_first)
    forward_back[3] = send_back(after(cross1, forward_back[2]), 1, 1)
    forward_back[0] = send_back(after(local0, forward_back[2]), 0, 0)
    forward_back[1] = send_back(after(local1, forward_back[2]), 0, 1)

    slab_rows = mix_rows + feed_rows
    early_shape = slab_rows // 2, width
    mix_slab = shape((mix_rows, width), F32)
    outs = [message] * 4 + [shape((WIN, qw), F32), shape((WIN, kvw), F32), shape((WIN, width), F32), halo_shape,
            shape(early_shape, F32), shape(early_shape, BF16), mix_slab] + [vec_shape] * 6
    operands = [gq1, gkv1, gkv_got, z, gmid1, g1, b1, w_qkv[1], q0, kv0, halo0, o0, lse0, active0, slope0, mid0, x, g0,
                b0, w_qkv[0], w_out[0], w_up[0], w_down[0]]
    (cross0, cross1, local0, local1, gq_last, gkv_last, gmid_last, halo_send, keep_early, send_early, slab_last,
     d_gain10, d_bias10, d_gain01, d_bias01, d_gain00, d_bias00) = call(
        fourth_kernel, info, operands,
        [tiled(a) for a in operands[:5]] + [VMEM] * 3 + [tiled(q0), VMEM, VMEM] + [tiled(a) for a in operands[11:16]]
        + [VMEM] * 7,
        outs, [VMEM] * len(outs),
        [ext, pltpu.VMEM((slab_rows, width), F32), pltpu.VMEM((n + WIN, qw), F32), pltpu.VMEM((n + WIN, qw), F32),
         pltpu.VMEM((n + WIN, width), F32), pltpu.VMEM((n + WIN, width), F32)], steps, work=20,
    )
    halo_send, _ = call(
        hold_kernel, info, [halo_send, halo_send] + forward_back[2:], [VMEM] * 2 + [ANY] * 2, [halo_shape] * 2, [VMEM] * 2
    )
    halo_got = lax.ppermute(halo_send, "section", second_to_first)

    got_early = pair(send_early)
    outs = [message] * 4 + [shape((mix_rows // 2, width), F32), shape((mix_rows // 2 + rider_rows, width), BF16), small_shape]
    operands = [gq_last, gkv_last, halo_got, x, gmid_last, g0, b0, w_qkv[0], slab_last]
    operands += [d_gain00, d_gain01, d_gain10, d_gain11, d_bias00, d_bias01, d_bias10, d_bias11, squares0, squares1]
    aliases = {1 + len(operands) + i: i for i in range(4)}
    operands += [cross0, cross1, local0, local1]
    cross0, cross1, local0, local1, keep_late, send_late, small = call(
        fifth_kernel, info, operands, [VMEM] * len(operands), outs, [VMEM] * len(outs),
        [pltpu.VMEM((mix_rows, width), F32), pltpu.VMEM((8, width), F32), pltpu.VMEM((8, width), F32)],
        aliases=aliases,
    )

    def assemble(own, other):
        outs = [shape((images, rows_piece, width), F32), shape((8, 128), F32)]
        out, token = call(
            assemble_kernel, info, own + [other], [VMEM] * 5, outs, [ANY, VMEM],
            [pltpu.VMEM((images, rows_piece, width), F32), dma((images,))],
        )
        if rep > 1:
            out = lax.dynamic_slice_in_dim(out, twin * rows_dev, rows_dev, 1)
        return out, token

    backward_back = [send_back(local0, 0, 0), None, send_back(cross0, 1, 0), None]
    got_late = pair(send_late)
    groups = [(keep_early, [got_early]), (keep_late, [got_late])]
    messages, kept, small = stage(groups, small, 4, 1)
    forward_trade = trade(forward_back, send_late)
    forward_rows, forward_token = assemble(forward_back, forward_trade)
    groups = [(kept_a, got_a), (kept, send_all(messages, plane))]
    number = 2
    scattered = []
    while number - 1 < len(rest) and sum(kept.shape[0] for kept, _ in groups) % 32 == 0:
        messages, kept, small = stage(groups, small, 2, number)
        groups = [(kept, send_all(messages, [rest[number - 2]]))]
        scattered.append(number)
        number += 1
    scattered_rows = groups[-1][1]
    backward_back[3] = send_back(after(cross1, backward_back[2]), 1, 1)
    backward_back[1] = send_back(after(local1, backward_back[2], *scattered_rows), 0, 1)
    (both,), _, small = stage(groups, small, 1, 0)
    both = after(both, backward_back[0], backward_back[2])
    rows_shape = shape((both.shape[0] - rider_rows, width), BF16)
    while number - 2 < len(rest):
        (got,) = send_all([both], [rest[number - 2]])
        rows, small = call(exchange_kernel, info, [both, got], [VMEM] * 2, [rows_shape, small_shape], [VMEM] * 2)
        number += 1
        if number - 2 < len(rest):
            both = call(again_kernel, info, [rows, small], [VMEM] * 2, shape(both.shape, BF16), VMEM)
    both = after(rows, backward_back[1], backward_back[3])
    for number in scattered[::-1]:
        both = gather(both, [rest[number - 2]], number)
    backward_trade = trade(backward_back, rows)
    backward_rows, backward_token = assemble(backward_back, backward_trade)
    both = in_order([both] + send_all([both] * 3, plane), 1, [backward_token, forward_token])
    theirs = pair(both)
    outs = [shape(w.shape, F32) for w in (w_qkv, w_out, w_up, w_down, norm_gain, norm_bias)] + [shape((6, images), F32)]
    sizes = (feed_rows, slab_rows, mix_rows, 1 << len(plane))
    grads = call(
        functools.partial(unpack_kernel, sizes=sizes), info, [both, theirs, small, counted],
        [VMEM] * 4, outs, [whole(o) for o in outs],
        [pltpu.VMEM((2,) + both.shape, F32)],
    )
    return (forward_rows, backward_rows, grads[6], grads[4], grads[5]) + tuple(grads[:4])


def solution(mesh):
    placed = (P("dp", "section", None), P("dp"), P(), P(), P(), P(), P(), P())
    return jax.shard_map(
        body,
        mesh=mesh,
        in_specs=placed,
        out_specs=(P("dp", "section", None), P("dp", "section", None), P(None, "dp"), P(), P(), P(), P(), P(), P()),
        check_vma=False,
    )
```
